256 devices in a mesh: gx: 16 (over y, x), gy: 16 (over z, core).
Axes of the slice: x: 4, y: 4, z: 8, core: 2. Of those that a mesh axis runs over, the one named last changes fastest.
Arguments:
- labels: int32 [32, 256, 2048], P(None, 'gx', 'gy'), may hold values from 0 to 1
- guess: float32 [3, 32, 256, 2048], P(None, None, 'gx', 'gy'), may hold values from -6 to 6
Outputs:
- solution: float32 [3, 32, 256, 2048], P(None, None, 'gx', 'gy')
The draws below stay inside these ranges and needn't reach their ends.
All inputs are finite; a program needn't handle non-finite values.
Results may differ from the reference program's by a relative error of at most 0.0003.
Values sent between devices are 32-bit elements; how exact they have to be, the bound alone decides.
No kernel may reach another device: no remote copies, remote signals or barrier semaphores. Data moves between devices by JAX's collectives and lax.ppermute only.
A program may use at most 128 MiB of HBM per device.

```python
import jax
import jax.numpy as jnp
from jax import lax

CX = 16
CY = 128
NZ = 32
LEVELS = 4
SWEEPS = 2
COARSE_SWEEPS = 6
NX = 256
NY = 2048


def draw_labels(key, part):
    key = jax.random.fold_in(key, 11)
    level_key, cell_key = jax.random.split(key)
    tiles = jax.random.randint(level_key, (NX // CX, NY // CY), 1, 10, dtype=jnp.int32)
    tiles = jnp.repeat(jnp.repeat(tiles, CX, axis=0), CY, axis=1)
    cells = jax.random.randint(cell_key, (NZ, NX, NY), 0, 10, dtype=jnp.int32)
    return (cells < tiles[None]).astype(jnp.int32)


def block_scale(own_key, shape, cuts, smallest, largest):
    factor_of, own = 1.0, jax.random.fold_in(own_key, 6)
    for position, blocks in cuts:
        heights = jnp.exp(jax.random.uniform(jax.random.fold_in(own, position), (blocks,), jnp.float32, smallest / len(cuts), largest / len(cuts)))
        factor_of = factor_of * jnp.repeat(heights, shape[position] // blocks).reshape([-1 if axis == position else 1 for axis in range(len(shape))])
    return factor_of


def noise(rng, shape, spread, most, cuts=(), kind=jnp.bfloat16):
    drawn = jax.random.normal(rng, shape, jnp.float32) * spread
    if len(cuts) > 0:
        drawn = block_scale(rng, shape, cuts, -0.22, 0.18) * drawn
    return jnp.clip(drawn, min=-most, max=most).astype(kind)


def setup_inputs(seed: int = 0) -> dict:
    keys = jax.random.split(jax.random.key(seed), 3)
    labels = draw_labels(jax.random.fold_in(keys[2], 71), 0)
    guess = noise(keys[1], (3, NZ, NX, NY), 1.0, 6.0, ((2, 16), (3, 16)), jnp.float32)
    return {"labels": labels, "guess": guess}


SOLID = 0.1
OMEGA = 0.8


def harmonic(first, second):
    return 2.0 * first * second / (first + second)


def face_weights(coef, scale):
    padded = jnp.pad(coef, 1, constant_values=1.0)
    return (scale * harmonic(coef, padded[1:-1, :-2, 1:-1]),
            scale * harmonic(coef, padded[1:-1, 2:, 1:-1]),
            scale * harmonic(coef, padded[1:-1, 1:-1, :-2]),
            scale * harmonic(coef, padded[1:-1, 1:-1, 2:]),
            scale * harmonic(coef, padded[:-2, 1:-1, 1:-1]),
            scale * harmonic(coef, padded[2:, 1:-1, 1:-1]))


def operate(weights, field):
    padded = jnp.pad(field, 1)
    total = weights[0] * (field - padded[1:-1, :-2, 1:-1])
    total = total + weights[1] * (field - padded[1:-1, 2:, 1:-1])
    total = total + weights[2] * (field - padded[1:-1, 1:-1, :-2])
    total = total + weights[3] * (field - padded[1:-1, 1:-1, 2:])
    total = total + weights[4] * (field - padded[:-2, 1:-1, 1:-1])
    total = total + weights[5] * (field - padded[2:, 1:-1, 1:-1])
    return total


def restrict(field):
    shape = field.shape
    blocks = field.reshape(shape[:-3] + (shape[-3] // 2, 2, shape[-2] // 2, 2, shape[-1] // 2, 2))
    return jnp.mean(blocks, axis=(-5, -3, -1))


def prolong(field):
    return jnp.repeat(jnp.repeat(jnp.repeat(field, 2, axis=-3), 2, axis=-2), 2, axis=-1)


def solve_field(field, which, coef_zero, weights_zero):
    source = jnp.where(which == 0, weights_zero[1] - weights_zero[0],
                       jnp.where(which == 1, weights_zero[3] - weights_zero[2], weights_zero[5] - weights_zero[4]))
    diag = sum(weights_zero)
    for step in range(SWEEPS):
        field = field + OMEGA * (source - operate(weights_zero, field)) / diag
    resid = source - operate(weights_zero, field)
    coef = coef_zero
    corrections = []
    for level in range(1, LEVELS + 1):
        coef = restrict(coef)
        rhs = restrict(resid)
        weights = face_weights(coef, 0.25 ** level)
        diag = sum(weights)
        count = SWEEPS if level < LEVELS else COARSE_SWEEPS
        correction = jnp.zeros_like(rhs)
        for step in range(count):
            correction = correction + OMEGA * (rhs - operate(weights, correction)) / diag
        if level < LEVELS:
            resid = rhs - operate(weights, correction)
        else:
            left = rhs - operate(weights, correction)
            correction = correction + jnp.sum(left) / jnp.sum(diag)
        corrections.append(correction)
    total = corrections[-1]
    for finer in reversed(corrections[:-1]):
        total = finer + prolong(total)
    return field + prolong(total)


def reference(labels, guess):
    coef_zero = jnp.where(labels == 1, 1.0, SOLID).astype(jnp.float32)
    weights_zero = face_weights(coef_zero, 1.0)
    which = jnp.arange(3, dtype=jnp.int32)
    return lax.map(lambda item: solve_field(item[0], item[1], coef_zero, weights_zero), (guess, which))
```

```python
import jax
import jax.numpy as jnp
from jax import lax
from jax.experimental import pallas as pl
from jax.experimental.pallas import tpu as pltpu
from jax.sharding import PartitionSpec as P


F32 = jnp.float32
NX, NY = 16, 16
BETWEEN = 2.0 * 0.1 / 1.1
ANY = pl.BlockSpec(memory_space=pltpu.HBM)


def dot(a, b):
    return jnp.dot(a, b, precision=lax.Precision.HIGHEST, preferred_element_type=F32)


def iota(shape, dim):
    return lax.broadcasted_iota(jnp.int32, shape, dim)


def roll(x, shift, axis=1):
    shift = shift % x.shape[axis]
    return x if shift == 0 else pltpu.roll(x, shift, axis)


def turn(x, shift):
    return pltpu.roll(x, lax.rem(shift + 256, 128), 1)


def recip(x):
    guess = pl.reciprocal(x, approx=True)
    return guess * (2.0 - x * guess)


def call(kernel, outs, scratch, flops=1_000_000, **kw):
    return pl.pallas_call(
        kernel,
        out_shape=[jax.ShapeDtypeStruct(s, F32) for s in outs],
        scratch_shapes=[pltpu.VMEM(s, F32) if isinstance(s, tuple) else s for s in scratch],
        compiler_params=pltpu.CompilerParams(vmem_limit_bytes=48 * 1024 * 1024),
        cost_estimate=pl.CostEstimate(flops=flops, bytes_accessed=4_000_000, transcendentals=0),
        **kw,
    )


def loop(count, body, unroll=1):
    def step(i, carry):
        body(i)
        return carry

    lax.fori_loop(0, count, step, 0, unroll=unroll)


def weigh(weights, values):
    parts = [w * v for w, v in zip(weights, values)]
    while len(parts) > 1:
        parts = [sum(parts[i : i + 2][1:], parts[i]) for i in range(0, len(parts), 2)]
    return parts[0]


def rows_kernel(guess, labels, up, down, own, phase, sems):
    copies = [pltpu.make_async_copy(labels, phase, sems.at[3])]
    for f in range(3):
        copies.append(pltpu.make_async_copy(guess.at[f], own.at[f], sems.at[f]))
    for copy in copies:
        copy.start()
    copies[0].wait()
    own[3] = jnp.where(phase[...] == 1, 0.0, 1.0).astype(F32)
    flat = own.reshape(4 * 32 * 16, 128)
    for ch in (3, 0, 1, 2):
        if ch < 3:
            copies[ch + 1].wait()
        for row in range(3):
            up[3 * ch + row] = flat[pl.ds(512 * ch + 13 + row, 32, stride=16), :]
            down[3 * ch + row] = flat[pl.ds(512 * ch + row, 32, stride=16), :]


def pack_kernel(own, before, after, near, far, held):
    first_core = lax.rem(lax.axis_index("gy"), 2) == 0
    flat = held.reshape(4 * 34 * 32, 128)
    for ch in range(4):
        first = (ch * 34 + 1) * 32
        for row in range(3):
            flat[pl.ds(first + row, 32, stride=32), :] = before[3 * ch + row]
            flat[pl.ds(first + 19 + row, 32, stride=32), :] = after[3 * ch + row]
        held[ch, 0] = jnp.zeros((32, 128), F32)
        held[ch, 33] = jnp.zeros((32, 128), F32)

    def plane(z):
        for ch in range(4):
            held[ch, z + 1, 3:19, :] = own[ch, z]

    loop(32, plane, 4)
    group = iota((24, 128), 1) // 16

    def some(low):
        for ch in range(4):
            to_right = jnp.zeros((24, 128), F32)
            to_left = jnp.zeros((24, 128), F32)
            for h in range(8):
                moved = roll(held[ch, 4 * h + low + 1, 0:24, :], 16 * h + 16)
                to_right = jnp.where(group == h, moved, to_right)
                to_left = jnp.where(group == (h + 1) % 8, moved, to_left)
            near[ch, low] = jnp.where(first_core, to_right, to_left)
            far[ch, low] = jnp.where(first_core, to_left, to_right)

    loop(4, some)


def six_of(ref, lead, z, first, count):
    own = ref[(*lead, z, pl.ds(first, count), slice(None))]
    return own, (
        ref[(*lead, z, pl.ds(first - 1, count), slice(None))],
        ref[(*lead, z, pl.ds(first + 1, count), slice(None))],
        roll(own, 1),
        roll(own, -1),
        ref[(*lead, z - 1, pl.ds(first, count), slice(None))],
        ref[(*lead, z + 1, pl.ds(first, count), slice(None))],
    )


def face(total):
    return jnp.where(total < 0.5, 1.0, jnp.where(total < 1.5, BETWEEN, 0.1))


def rows_inside(gx, shape):
    row = iota(shape, 0) + 1
    low, high = jnp.where(gx > 0, 1, 0), jnp.where(gx < NX - 1, 1, 0)
    return jnp.where(row < 3, low, jnp.where(row >= 19, high, 1))


def fine_sweeps(planes, start, share, one, two, weights, diags, halves, omega, wrap, keep, unroll):
    def first_sweep(z):
        own, six = six_of(share, (), z + 1, 1, 24)
        faces = [face(own + other) for other in six]
        diag = (faces[0] + faces[1]) + (faces[2] + faces[3]) + (faces[4] + faces[5])
        gain = omega * recip(diag)
        diags[z, 1:25, :] = 1.25 * diag
        w = [gain * value for value in faces]
        for i in range(6):
            weights[i, z, 1:25, :] = w[i]
        for f in range(3):
            own, six = six_of(start, (f,), z + 1, 1, 24)
            one[f, z + 1, 1:25, :] = (0.2 * own + (w[2 * f + 1] - w[2 * f])) + weigh(w, six)

    loop(planes, first_sweep, unroll)
    wrap(one)

    def second_sweep(z):
        w = [weights[i, z, 2:26, :] for i in range(6)]
        for f in range(3):
            own, six = six_of(one, (f,), z + 1, 2, 24)
            two[f, z + 1, 2:26, :] = (0.2 * own + (w[2 * f + 1] - w[2 * f])) + weigh(w, six)

    loop(planes, second_sweep, unroll)
    wrap(two)

    def residual(pair):
        sums = {}
        for k in range(2):
            z = 2 * pair + k
            w = [weights[i, z, 3:19, :] for i in range(6)]
            diag = diags[z, 3:19, :]
            for f in range(3):
                own, six = six_of(two, (f,), z + 1, 3, 16)
                keep[f, z] = own
                value = (((w[2 * f + 1] - w[2 * f]) - 0.8 * own) + weigh(w, six)) * diag
                sums[f] = value if k == 0 else sums[f] + value
            value = share[z + 1, 3:19, :]
            sums[3] = value if k == 0 else sums[3] + value
        for ch, value in sums.items():
            halves[ch, pair] = value

    loop(planes // 2, residual, unroll // 2)


def own_kernel(held, field, coarse, edges, one, two, weights, diags, halves, pooled):
    gx = lax.axis_index("gx")
    for ref in (one, two):
        for f in range(3):
            ref[f, 0] = jnp.zeros((32, 128), F32)
            ref[f, 33] = jnp.zeros((32, 128), F32)
    omega = 0.8 * rows_inside(gx, (24, 128)).astype(F32)
    fine_sweeps(
        32, held, held.at[3], one, two, weights, diags, halves, omega, lambda ref: None, field, 4
    )
    pool = jnp.where(iota((128, 128), 0) // 2 == iota((128, 128), 1), 0.125, 0.0)
    pooled[...] = dot(halves[...].reshape(1024, 128), pool)
    for ch in range(4):
        even = pooled[pl.ds(256 * ch, 128, stride=2), :]
        odd = pooled[pl.ds(256 * ch + 1, 128, stride=2), :]
        coarse[ch] = (even + odd).reshape(16, 8, 128)
    lane = iota((24, 128), 1)

    def edge(z):
        for ch in range(4):
            value = jnp.zeros((24, 128), F32)
            for half in range(2):
                source = held[ch, z + 16 * half + 1, 0:24, :]
                base = 64 * half
                value = jnp.where((lane >= base) & (lane < base + 7), roll(source, base + 7), value)
                value = jnp.where((lane >= base + 57) & (lane < base + 64), roll(source, base + 57), value)
            edges[ch, z] = value

    loop(16, edge)


def rim_kernel(
    edges, owned, near, far, field, coarse, packed,
    start, share, one, two, weights, diags, halves, pooled,
):
    gx, gy = lax.axis_index("gx"), lax.axis_index("gy")
    lane = iota((24, 128), 1)
    part = lane % 64
    is_after = (part >= 7) & (part < 22)
    is_before = (part >= 42) & (part < 57)
    first_core = lax.rem(gy, 2) == 0

    def unpack(low):
        for ch in range(4):
            target = start.at[ch] if ch < 3 else share
            from_right = jnp.where(first_core, near[ch, low], far[ch, low])
            from_left = jnp.where(first_core, far[ch, low], near[ch, low])
            for h in range(4):
                z = 4 * h + low
                after_y = roll(from_right, 7 - 16 * (h + 1))
                before_y = roll(from_left, 41 - 16 * h)
                target[z + 1, 0:24, :] = jnp.where(
                    is_after, after_y, jnp.where(is_before, before_y, edges[ch, z])
                )

    loop(4, unpack)

    def wrap_one(ref):
        ref[0, 0:24, :] = jnp.where(lane >= 64, roll(ref[16, 0:24, :], 64), 0.0)
        ref[17, 0:24, :] = jnp.where(lane < 64, roll(ref[1, 0:24, :], 64), 0.0)

    def wrap(ref):
        for f in range(3):
            wrap_one(ref.at[f])

    wrap_one(share)
    wrap(start)
    inside_y = jnp.where(
        part < 32,
        jnp.where((part < 7) | (gy < NY - 1), 1, 0),
        jnp.where((part >= 57) | (gy > 0), 1, 0),
    )
    omega = 0.8 * (rows_inside(gx, (24, 128)) * inside_y).astype(F32)
    fine_sweeps(16, start, share, one, two, weights, diags, halves, omega, wrap, field, 4)

    source, target = iota((128, 128), 0), iota((128, 128), 1)
    spot = source % 64
    column = jnp.where(spot < 32, 121 + spot, 128 + spot - 57)
    to = jnp.where(spot < 32, column // 2, (column // 2 + 64) % 128)
    from_rim = (iota((128, 128), 1) < 2) | (iota((128, 128), 1) >= 62)
    mixed = halves[...].reshape(512, 128)
    for half in range(2):
        pool = jnp.where((to == target) & (source // 64 == half), 0.125, 0.0)
        pooled[...] = dot(mixed, pool)
        for ch in range(4):
            even = pooled[pl.ds(128 * ch, 64, stride=2), :]
            odd = pooled[pl.ds(128 * ch + 1, 64, stride=2), :]
            at = pl.ds(8 * half, 8)
            rest = owned[ch, at].reshape(64, 128)
            coarse[ch, at] = jnp.where(from_rim[:64], even + odd, rest).reshape(8, 8, 128)

    lane = iota((8, 128), 1)
    for ch in range(4):
        for group in range(2):
            tiles = [None] * 5
            for k in range(8):
                moved = roll(coarse[ch, 8 * group + k], 8 + 80 * k)
                tile, off = divmod(80 * k, 128)
                tiles[tile] = moved if off == 0 else jnp.where(lane >= off, moved, tiles[tile])
                if off + 80 > 128:
                    tiles[tile + 1] = moved
            for tile in range(5):
                packed[ch, group, tile] = tiles[tile]


def patch_kernel(owned, rim, field):
    lane = iota((16, 128), 1)

    def plane(z):
        for f in range(3):
            value = rim[f, z]
            for half in range(2):
                base = 64 * half
                low = roll(value, -57 - base)
                high = roll(value, 121 - base)
                at = z + 16 * half
                field[f, at] = jnp.where(lane < 3, low, jnp.where(lane >= 125, high, owned[f, at]))

    loop(16, plane, 2)


def resist(share):
    return recip(1.0 - 0.9 * share)


def level_weights(own, six, omega):
    faces = [2.0 * recip(own + other) for other in six]
    diag = (faces[0] + faces[1]) + (faces[2] + faces[3]) + (faces[4] + faces[5])
    gain = omega * recip(diag)
    return gain, [gain * w for w in faces], diag


def middle_kernel(
    mine, before, after, sent, e_one, e_two,
    share, rest, rhs, first, second, weights, diags, halves, pooled,
    rest2, first2, second2, rhs2, share2, weights2, diags2,
):
    gx, gy = lax.axis_index("gx"), lax.axis_index("gy")
    low_x, high_x = jnp.where(gx > 0, 1, 0), jnp.where(gx < NX - 1, 1, 0)
    low_y, high_y = jnp.where(gy > 0, 1, 0), jnp.where(gy < NY - 1, 1, 0)

    for f in range(3):
        for ref in (first, second):
            ref[f, 0] = jnp.zeros((32, 128), F32)
            ref[f, 17] = jnp.zeros((32, 128), F32)
    for z in (0, 17):
        rest[z] = jnp.ones((32, 128), F32)
    lane = iota((8, 128), 1)

    def fill(group):
        for k in range(8):
            z = 8 * group + k
            tile, off = divmod(80 * k, 128)
            for ch in range(4):
                parts = []
                for ref in (before, after):
                    value = ref[ch, group, tile]
                    if off + 80 > 128:
                        value = jnp.where(lane >= off, value, ref[ch, group, tile + 1])
                    parts.append(roll(value, -8 - 80 * k))
                parts.insert(1, mine[ch, z])
                for i, value in enumerate(parts):
                    if ch < 3:
                        rhs[ch, z, 8 * i : 8 * i + 8, :] = value
                    else:
                        share[z, 8 * i : 8 * i + 8, :] = value
                        rest[z + 1, 8 * i : 8 * i + 8, :] = resist(value)
            rest[z + 1, 24:32, :] = jnp.ones((8, 128), F32)

    loop(2, fill)

    row, lane = iota((24, 128), 0) + 1, iota((24, 128), 1)
    in_x = jnp.where(row < 8, low_x, jnp.where(row >= 16, high_x, 1))
    in_y = jnp.where(lane < 64, 1, jnp.where(lane < 96, high_y, low_y))
    omega = 0.8 * (in_x * in_y).astype(F32)

    def start(z):
        own, six = six_of(rest, (), z + 1, 1, 24)
        gain, w, diag = level_weights(own, six, omega)
        for i in range(6):
            weights[i, z, 1:25, :] = w[i]
        diags[z, 1:25, :] = (1.25 * 0.25) * diag
        for f in range(3):
            first[f, z + 1, 1:25, :] = (4.0 * gain) * rhs[f, z, 1:25, :]

    loop(16, start, 2)

    def sweep(z):
        w = [weights[i, z, 3:27, :] for i in range(6)]
        for f in range(3):
            own, six = six_of(first, (f,), z + 1, 3, 24)
            second[f, z + 1, 3:27, :] = 1.2 * own + weigh(w, six)

    loop(16, sweep, 4)

    def left(pair):
        sums = {}
        for k in range(2):
            z = 2 * pair + k
            w = [weights[i, z, 4:20, :] for i in range(6)]
            diag = diags[z, 4:20, :]
            for f in range(3):
                own, six = six_of(second, (f,), z + 1, 4, 16)
                change = (first[f, z + 1, 4:20, :] - 0.8 * own) + weigh(w, six)
                value = change * diag
                sums[f] = value if k == 0 else sums[f] + value
                e_one[f, z] = second[f, z + 1, 8:16, :]
        for f in range(3):
            halves[f, pair, 0:16, :] = sums[f]
            halves[f, pair, 16:24, :] = jnp.zeros((8, 128), F32)
        halves[3, pair] = share[2 * pair] + share[2 * pair + 1]

    loop(8, left, 2)

    source, target = iota((128, 128), 0), iota((128, 128), 1)
    pool = jnp.where(source // 2 + jnp.where(source >= 96, 64, 0) == target, 0.125, 0.0)
    pooled[...] = dot(halves[...].reshape(4 * 8 * 24, 128), pool)
    for z in (0, 9):
        rest2[z] = jnp.ones((24, 128), F32)
        for f in range(3):
            first2[f, z] = jnp.zeros((24, 128), F32)
            second2[f, z] = jnp.zeros((24, 128), F32)
    for z in range(8):
        for f in range(3):
            base = (f * 8 + z) * 24
            rhs2[f, z] = pooled[pl.ds(base, 8, stride=2), :] + pooled[pl.ds(base + 1, 8, stride=2), :]
        base = (3 * 8 + z) * 24
        value = pooled[pl.ds(base + 2, 8, stride=2), :] + pooled[pl.ds(base + 3, 8, stride=2), :]
        rest2[z + 1, 0:8, :] = resist(value)
        value = pooled[pl.ds(base + 8, 8, stride=2), :] + pooled[pl.ds(base + 9, 8, stride=2), :]
        rest2[z + 1, 3:11, :] = resist(value)
        share2[z] = value

    row, lane = iota((8, 128), 0) + 1, iota((8, 128), 1)
    in_x = jnp.where(row < 3, low_x, jnp.where(row >= 7, high_x, 1))
    in_y = jnp.where(lane < 32, 1, jnp.where(lane < 96, high_y, low_y))
    omega2 = 0.8 * (in_x * in_y).astype(F32)

    def start2(z):
        own, six = six_of(rest2, (), z + 1, 1, 8)
        gain, w, diag = level_weights(own, six, omega2)
        for i in range(6):
            weights2[i, z, 1:9, :] = w[i]
        diags2[z, 1:9, :] = (1.25 * 0.0625) * diag
        for f in range(3):
            first2[f, z + 1, 1:9, :] = (16.0 * gain) * rhs2[f, z]

    loop(8, start2, 8)

    def sweep2(z):
        w = [weights2[i, z, 2:10, :] for i in range(6)]
        for f in range(3):
            own, six = six_of(first2, (f,), z + 1, 2, 8)
            second2[f, z + 1, 2:10, :] = 1.2 * own + weigh(w, six)

    loop(8, sweep2, 8)

    own_row = iota((8, 128), 0) < 4
    parts = []
    for pair in range(4):
        sums = {}
        for k in range(2):
            z = 2 * pair + k
            w = [weights2[i, z, 3:11, :] for i in range(6)]
            diag = diags2[z, 3:11, :]
            for f in range(3):
                own, six = six_of(second2, (f,), z + 1, 3, 8)
                e_two[f, z] = own
                change = (first2[f, z + 1, 3:11, :] - 0.8 * own) + weigh(w, six)
                value = jnp.where(own_row, change * diag, 0.0)
                sums[f] = value if k == 0 else sums[f] + value
            value = jnp.where(own_row, share2[z], 0.0)
            sums[3] = value if k == 0 else sums[3] + value
        parts.append(sums)

    pool = jnp.where((source < 32) & (source // 2 == target % 16), 0.125, 0.0)
    rows = jnp.concatenate([parts[pair][ch] for ch in range(4) for pair in range(4)], axis=0)
    spread = dot(rows, pool)
    at, to = iota((32, 128), 0), iota((32, 128), 1)
    keep = (at // 8 == to // 32) & ((at % 8) // 2 == (to // 16) % 2)
    result = jnp.concatenate(
        [
            jnp.sum(jnp.where(keep, spread[32 * ch : 32 * ch + 32], 0.0), axis=0, keepdims=True)
            for ch in range(4)
        ],
        axis=0,
    )
    for copy in range(NY):
        sent[copy] = result


def turn_kernel(column, sent):
    sub, group = iota((8, 128), 0), iota((8, 128), 1) // 16
    tiles = [column[8 * j : 8 * j + 8, :] for j in range(8)]
    moved = [[roll(tile, 16 * d) for d in range(8)] for tile in tiles]
    for q in range(8):
        for half in range(2):
            value = jnp.zeros((8, 128), F32)
            for j in range(4):
                for odd in range(2):
                    to = 2 * j + odd
                    mask = (sub // 4 == odd) & (group == to)
                    value = jnp.where(mask, moved[4 * half + j][(to - q) % 8], value)
            value = value + roll(value, 4, 0)
            row = (q * 2 + half) * 4
            for copy in range(NX):
                sent[copy, row : row + 4, :] = value[0:4]


def top_kernel(
    gathered, field, e_one, e_two, out,
    first, second, four, weights, diags, lefts, wide, final, sems,
):
    gx, gy = lax.axis_index("gx"), lax.axis_index("gy")
    lane, sub = iota((16, 128), 1), iota((16, 128), 0)
    cells = [(z, x, half) for z in range(4) for x in range(2) for half in range(2)]

    def plane(ch, z, x, half):
        return gathered[pl.ds(((z * 2 + x) * 2 + half) * 4 + ch, 16, stride=64), :]

    def neighbours(at, z, x, half, outside):
        own, other = at(z, x, half), at(z, 1 - x, half)
        beside = at(z, x, 1 - half)
        shifted = roll(other, 1 if x == 0 else -1, 0)
        low, high = (shifted, other) if x == 0 else (other, shifted)
        left, right = roll(own, 1), roll(own, -1)
        if half == 0:
            right = jnp.where(lane == 127, roll(beside, -1), right)
        else:
            left = jnp.where(lane == 0, roll(beside, 1), left)
        down = at(z - 1, x, half) if z > 0 else outside
        up = at(z + 1, x, half) if z < 3 else outside
        return own, [low, high, left, right, down, up]

    def edge_masks(x, half):
        return [
            sub > 0 if x == 0 else None,
            sub < 15 if x == 1 else None,
            lane > 0 if half == 0 else None,
            lane < 127 if half == 1 else None,
            None,
            None,
        ]

    def key(z, x, half):
        return (z * 2 + x) * 2 + half

    shares = {c: plane(3, *c) for c in cells}
    rests = {c: resist(shares[c]) for c in cells}
    ones, zeros = jnp.ones((16, 128), F32), jnp.zeros((16, 128), F32)
    for z, x, half in cells:
        own, six = neighbours(lambda *c: rests[c], z, x, half, ones)
        masks = edge_masks(x, half)
        six = [s if m is None else jnp.where(m, s, 1.0) for s, m in zip(six, masks)]
        gain, w, diag = level_weights(own, six, 0.8)
        at = key(z, x, half)
        for i in range(6):
            weights[i, at] = w[i] if masks[i] is None else jnp.where(masks[i], w[i], 0.0)
        diags[at] = (1.25 * 0.25**3) * diag
        for f in range(3):
            first[f, at] = (64.0 * gain) * plane(f, z, x, half)

    for z, x, half in cells:
        at = key(z, x, half)
        w = [weights[i, at] for i in range(6)]
        for f in range(3):
            own, six = neighbours(lambda *c: first[f, key(*c)], z, x, half, zeros)
            second[half, f, z * 2 + x] = 1.2 * own + weigh(w, six)

    for z4 in range(2):
        for half in range(2):
            sums = [None] * 4
            for z in (2 * z4, 2 * z4 + 1):
                for x in range(2):
                    at = key(z, x, half)
                    w = [weights[i, at] for i in range(6)]
                    diag = diags[at]
                    for f in range(3):
                        own, six = neighbours(
                            lambda c, d, e: second[e, f, c * 2 + d], z, x, half, zeros
                        )
                        value = ((first[f, at] - 0.8 * own) + weigh(w, six)) * diag
                        sums[f] = value if sums[f] is None else sums[f] + value
                    share = shares[z, x, half]
                    sums[3] = share if sums[3] is None else sums[3] + share
            for ch in range(4):
                lefts[ch, z4, :, 128 * half : 128 * half + 128] = sums[ch]

    pool = jnp.where(iota((256, 128), 0) // 2 == iota((256, 128), 1), 0.125, 0.0)
    level = dot(lefts[...].reshape(128, 256), pool)

    def coarsest(ch, z):
        return level[(ch * 2 + z) * 16 : (ch * 2 + z) * 16 + 16, :]

    masks = [sub > 0, sub < 15, lane > 0, lane < 127]
    resists = [resist(coarsest(3, z)) for z in range(2)]
    gains, ws, ds = [], [], []
    for z in range(2):
        own, other = resists[z], resists[1 - z]
        six = [roll(own, 1, 0), roll(own, -1, 0), roll(own, 1), roll(own, -1)]
        six = [jnp.where(m, s, 1.0) for m, s in zip(masks, six)] + [other, ones]
        gain, w, diag = level_weights(own, six, 0.8)
        gains.append(gain)
        ds.append(diag)
        ws.append([jnp.where(m, v, 0.0) for m, v in zip(masks, w)] + [w[4]])
    whole = jnp.sum(ds[0] + ds[1], keepdims=True)

    def around(values, z):
        own, other = values[z], values[1 - z]
        return weigh(ws[z], (roll(own, 1, 0), roll(own, -1, 0), roll(own, 1), roll(own, -1), other))

    begin = [[256.0 * gains[z] * coarsest(f, z) for z in range(2)] for f in range(3)]
    values = begin
    for step in range(5):
        values = [
            [(0.2 * values[f][z] + begin[f][z]) + around(values[f], z) for z in range(2)] for f in range(3)
        ]
    for f in range(3):
        change = [(begin[f][z] - 0.8 * values[f][z]) + around(values[f], z) for z in range(2)]
        total = jnp.sum(1.25 * (change[0] * ds[0] + change[1] * ds[1]), keepdims=True)
        for z in range(2):
            four[2 * f + z] = values[f][z] + total / whole

    copy = jnp.where(iota((128, 128), 0) == iota((128, 128), 1) // 2, 1.0, 0.0)
    rows = four.reshape(96, 128)[pl.ds(gx, 6, stride=16), :]
    rows = jnp.concatenate([jnp.broadcast_to(rows[i : i + 1], (4, 128)) for i in range(6)], axis=0)
    three = dot(turn(rows, -8 * gy), copy)
    flat = second.reshape(768, 128)
    halves = [flat[pl.ds(gx + 384 * half, 24, stride=16), :] for half in range(2)]
    three = three + turn(jnp.where(gy < 8, halves[0], halves[1]), -16 * lax.rem(gy, 8))

    three = dot(three, copy)
    low = iota((8, 128), 0) < 2
    tiles = []
    for f in range(3):
        for z in range(4):
            at = f * 8 + z * 2
            tile = jnp.where(
                low,
                jnp.broadcast_to(three[at : at + 1], (8, 128)),
                jnp.broadcast_to(three[at + 1 : at + 2], (8, 128)),
            )
            tiles += [e_two[f, 2 * z] + tile, e_two[f, 2 * z + 1] + tile]

    two = dot(jnp.concatenate(tiles, axis=0), copy)
    for block in range(24):
        value = two[8 * block : 8 * block + 4, :]
        wide[pl.ds(8 * block, 4, stride=2), :] = value
        wide[pl.ds(8 * block + 1, 4, stride=2), :] = value
    one = e_one[...].reshape(24, 2, 8, 128) + wide[...].reshape(24, 1, 8, 128)

    one = dot(one.reshape(384, 128), copy)
    flat_in = field.reshape(3 * 32 * 16, 128)
    flat_out = final.reshape(3 * 32 * 16, 128)
    copies = []
    for f in range(3):
        for block in range(16 * f, 16 * f + 16):
            value = one[8 * block : 8 * block + 8, :]
            for k in range(2):
                for half in range(2):
                    at = pl.ds(32 * block + 16 * k + half, 8, stride=2)
                    flat_out[at, :] = flat_in[at, :] + value
        copies.append(pltpu.make_async_copy(final.at[f], out.at[f], sems.at[f]))
        copies[-1].start()
    for copy in copies:
        copy.wait()


def local(labels, guess):
    up = [(i, i + 1) for i in range(NX - 1)]
    down = [(i + 1, i) for i in range(NX - 1)]
    to_up, to_down, own = call(
        rows_kernel,
        [(12, 32, 128)] * 2 + [(4, 32, 16, 128)],
        [pltpu.VMEM((32, 16, 128), jnp.int32), pltpu.SemaphoreType.DMA((4,))],
        in_specs=[ANY, ANY],
    )(pltpu.with_memory_space_constraint(guess, pltpu.HBM), pltpu.with_memory_space_constraint(labels, pltpu.HBM))
    before = lax.ppermute(to_up, "gx", up)
    after = lax.ppermute(to_down, "gx", down)
    swap_near = [(i, i ^ 1) for i in range(NY)]
    swap_far = [(i, j) for k in range(1, NY - 1, 2) for i, j in ((k, k + 1), (k + 1, k))]
    to_near, to_far, held = call(pack_kernel, [(4, 4, 24, 128)] * 2 + [(4, 34, 32, 128)], [])(
        own, before, after
    )
    from_far = lax.ppermute(to_far, "gy", swap_far)
    from_near = lax.ppermute(to_near, "gy", swap_near)
    owned, part, edges = call(
        own_kernel,
        [(3, 32, 16, 128), (4, 16, 8, 128), (4, 16, 24, 128)],
        [(3, 34, 32, 128)] * 2
        + [(6, 32, 32, 128), (32, 32, 128)]
        + [(4, 16, 16, 128), (1024, 128)],
        flops=20_000_000,
    )(held)
    rim, coarse, packed = call(
        rim_kernel,
        [(3, 16, 16, 128), (4, 16, 8, 128), (4, 2, 5, 8, 128)],
        [(3, 18, 32, 128), (18, 32, 128)]
        + [(3, 18, 32, 128)] * 2
        + [(6, 16, 32, 128), (16, 32, 128)]
        + [(4, 8, 16, 128), (512, 128)],
        flops=10_000_000,
    )(edges, part, from_near, from_far)
    before = lax.ppermute(packed, "gx", up)
    after = lax.ppermute(packed, "gx", down)
    (field,) = call(patch_kernel, [(3, 32, 16, 128)], [])(owned, rim)
    sent, e_one, e_two = call(
        middle_kernel,
        [(NY, 4, 128), (3, 16, 8, 128), (3, 8, 8, 128)],
        [(16, 24, 128), (18, 32, 128), (3, 16, 32, 128), (3, 18, 32, 128), (3, 18, 32, 128)]
        + [(6, 16, 32, 128), (16, 32, 128), (4, 8, 24, 128), (768, 128)]
        + [(10, 24, 128), (3, 10, 24, 128), (3, 10, 24, 128), (3, 8, 8, 128), (8, 8, 128)]
        + [(6, 8, 16, 128), (8, 16, 128)],
    )(coarse, before, after)
    column = lax.all_to_all(sent, "gy", split_axis=0, concat_axis=0, tiled=True).reshape(64, 128)
    (copies,) = call(turn_kernel, [(NX, 64, 128)], [])(column)
    gathered = lax.all_to_all(copies, "gx", split_axis=0, concat_axis=0, tiled=True).reshape(1024, 128)
    (out,) = call(
        top_kernel,
        [(3, 32, 16, 128)],
        [(3, 16, 16, 128), (2, 3, 8, 16, 128), (6, 16, 128), (6, 16, 16, 128), (16, 16, 128)]
        + [(4, 2, 16, 256), (192, 128), (3, 32, 16, 128), pltpu.SemaphoreType.DMA((3,))],
        out_specs=[ANY],
    )(gathered, field, e_one, e_two)
    return out


def solution(mesh):
    return jax.shard_map(
        local,
        mesh=mesh,
        in_specs=(P(None, "gx", "gy"), P(None, None, "gx", "gy")),
        out_specs=P(None, None, "gx", "gy"),
        check_vma=False,
    )
```

```python
import jax
import jax.numpy as jnp
from jax import lax
from jax.experimental import pallas as pl
from jax.experimental.pallas import tpu as pltpu
from jax.sharding import PartitionSpec as P


F32 = jnp.float32
NX, NY = 16, 16
BETWEEN = 2.0 * 0.1 / 1.1
ANY = pl.BlockSpec(memory_space=pltpu.HBM)


def dot(a, b):
    return jnp.dot(a, b, precision=lax.Precision.HIGHEST, preferred_element_type=F32)


def iota(shape, dim):
    return lax.broadcasted_iota(jnp.int32, shape, dim)


def roll(x, shift, axis=1):
    shift = shift % x.shape[axis]
    return x if shift == 0 else pltpu.roll(x, shift, axis)


def turn(x, shift):
    return pltpu.roll(x, lax.rem(shift + 256, 128), 1)


def recip(x):
    guess = pl.reciprocal(x, approx=True)
    return guess * (2.0 - x * guess)


def call(kernel, outs, scratch, flops=1_000_000, **kw):
    return pl.pallas_call(
        kernel,
        out_shape=[jax.ShapeDtypeStruct(s, F32) for s in outs],
        scratch_shapes=[pltpu.VMEM(s, F32) if isinstance(s, tuple) else s for s in scratch],
        compiler_params=pltpu.CompilerParams(vmem_limit_bytes=32 * 1024 * 1024),
        cost_estimate=pl.CostEstimate(flops=flops, bytes_accessed=4_000_000, transcendentals=0),
        **kw,
    )


def loop(count, body, unroll=1):
    def step(i, carry):
        body(i)
        return carry

    lax.fori_loop(0, count, step, 0, unroll=unroll)


def weigh(weights, values):
    parts = [w * v for w, v in zip(weights, values)]
    while len(parts) > 1:
        parts = [sum(parts[i : i + 2][1:], parts[i]) for i in range(0, len(parts), 2)]
    return parts[0]


def rows_kernel(guess, labels, near, far, own, phase, sems):
    even = lax.rem(lax.axis_index("gx"), 2) == 0
    near_row, far_row = jnp.where(even, 13, 0), jnp.where(even, 0, 13)
    copies = [pltpu.make_async_copy(labels, phase, sems.at[3])]
    for f in range(3):
        copies.append(pltpu.make_async_copy(guess.at[f], own.at[f], sems.at[f]))
    for copy in copies:
        copy.start()
    copies[0].wait()
    own[3] = jnp.where(phase[...] == 1, 0.0, 1.0).astype(F32)
    flat = own.reshape(4 * 32 * 16, 128)
    for ch in (3, 0, 1, 2):
        if ch < 3:
            copies[ch + 1].wait()
        for row in range(3):
            near[3 * ch + row] = flat[pl.ds(512 * ch + near_row + row, 32, stride=16), :]
            far[3 * ch + row] = flat[pl.ds(512 * ch + far_row + row, 32, stride=16), :]


def pack_kernel(to_right, to_left, x_near, x_far, near, far, rim):
    first_core = lax.rem(lax.axis_index("gy"), 2) == 0
    even = lax.rem(lax.axis_index("gx"), 2) == 0
    near_row, far_row = jnp.where(even, 0, 5), jnp.where(even, 5, 0)
    flat = rim.reshape(4 * 32 * 8, 128)
    for ch in range(4):
        for row in range(3):
            flat[pl.ds(256 * ch + near_row + row, 32, stride=8), :] = x_near[3 * ch + row]
            flat[pl.ds(256 * ch + far_row + row, 32, stride=8), :] = x_far[3 * ch + row]

    def some(low):
        for ch in range(4):
            right, left = pack_planes(lambda z: rim[ch, z], low, (8, 128))
            for at, right, left in (
                (slice(0, 16), to_right[ch, low], to_left[ch, low]),
                (slice(16, 24), right, left),
            ):
                near[ch, low, at, :] = jnp.where(first_core, right, left)
                far[ch, low, at, :] = jnp.where(first_core, left, right)

    loop(4, some)


def pack_planes(plane, low, shape):
    group = iota(shape, 1) // 16
    right = left = jnp.zeros(shape, F32)
    for h in range(8):
        moved = roll(plane(4 * h + low), 16 * h + 16)
        right = jnp.where(group == h, moved, right)
        left = jnp.where(group == (h + 1) % 8, moved, left)
    return right, left


def edge_columns(plane, z, shape):
    lane = iota(shape, 1)
    value = jnp.zeros(shape, F32)
    for half in range(2):
        source = plane(z + 16 * half)
        base = 64 * half
        value = jnp.where((lane >= base) & (lane < base + 7), roll(source, base + 7), value)
        value = jnp.where((lane >= base + 57) & (lane < base + 64), roll(source, base + 57), value)
    return value


def six_of(ref, lead, z, first, count):
    own = ref[(*lead, z, pl.ds(first, count), slice(None))]
    return own, (
        ref[(*lead, z, pl.ds(first - 1, count), slice(None))],
        ref[(*lead, z, pl.ds(first + 1, count), slice(None))],
        roll(own, 1),
        roll(own, -1),
        ref[(*lead, z - 1, pl.ds(first, count), slice(None))],
        ref[(*lead, z + 1, pl.ds(first, count), slice(None))],
    )


def face(total):
    return jnp.where(total < 0.5, 1.0, jnp.where(total < 1.5, BETWEEN, 0.1))


def fine_weights(own, six, omega):
    faces = [face(own + other) for other in six]
    diag = (faces[0] + faces[1]) + (faces[2] + faces[3]) + (faces[4] + faces[5])
    gain = omega * recip(diag)
    return [gain * value for value in faces], 1.25 * diag


def fine_sweep(w, f, own, six):
    return (0.2 * own + (w[2 * f + 1] - w[2 * f])) + weigh(w, six)


def fine_left(w, f, own, six, diag):
    return (((w[2 * f + 1] - w[2 * f]) - 0.8 * own) + weigh(w, six)) * diag


def fine_sweeps(planes, windows, start, share, one, two, weights, diags, halves, omega, wrap, keep):
    first, count = windows[0]

    def first_sweep(z):
        own, six = six_of(share, (), z + 1, first, count)
        w, diag = fine_weights(own, six, omega)
        diags[z, pl.ds(first, count), :] = diag
        for i in range(6):
            weights[i, z, pl.ds(first, count), :] = w[i]
        for f in range(3):
            own, six = six_of(start, (f,), z + 1, first, count)
            one[f, z + 1, pl.ds(first, count), :] = fine_sweep(w, f, own, six)

    loop(planes, first_sweep, 4)
    wrap(one)
    second, count2 = windows[1]

    def second_sweep(z):
        w = [weights[i, z, pl.ds(second, count2), :] for i in range(6)]
        for f in range(3):
            own, six = six_of(one, (f,), z + 1, second, count2)
            two[f, z + 1, pl.ds(second, count2), :] = fine_sweep(w, f, own, six)

    loop(planes, second_sweep, 4)
    wrap(two)

    def residual(pair):
        sums = {}
        for k in range(2):
            z = 2 * pair + k
            w = [weights[i, z, 8:24, :] for i in range(6)]
            diag = diags[z, 8:24, :]
            for f in range(3):
                own, six = six_of(two, (f,), z + 1, 8, 16)
                if keep is not None:
                    keep[f, z] = own
                value = fine_left(w, f, own, six, diag)
                sums[f] = value if k == 0 else sums[f] + value
            value = share[z + 1, 8:24, :]
            sums[3] = value if k == 0 else sums[3] + value
        for ch, value in sums.items():
            halves[ch, pair] = value

    loop(planes // 2, residual, 2)


def own_kernel(own, one, two, halves, to_right, to_left, edges, held, weights, diags):
    zero = jnp.zeros((32, 128), F32)
    for z in (0, 33):
        for ch in range(4):
            held[ch, z] = zero
        for ref in (one, two):
            for f in range(3):
                ref[f, z] = zero

    def plane(z):
        for ch in range(4):
            held[ch, z + 1, 8:24, :] = own[ch, z]

    loop(32, plane, 4)
    fine_sweeps(
        32, [(8, 16)] * 2, held, held.at[3], one, two, weights, diags, halves, 0.8, lambda ref: None, None
    )

    def some(low):
        for ch in range(4):
            to_right[ch, low], to_left[ch, low] = pack_planes(lambda z: own[ch, z], low, (16, 128))

    loop(4, some)

    def edge(z):
        for ch in range(4):
            edges[ch, z] = edge_columns(lambda at: own[ch, at], z, (16, 128))

    loop(16, edge, 2)


def rows_edge_kernel(own, rim, own_one, own_two, own_halves, two, coarse, edges, start, one, weights, diags, halves, pooled):
    gx = lax.axis_index("gx")
    zero = jnp.zeros((24, 128), F32)
    for z in (0, 33):
        for ch in range(4):
            start[ch, z] = zero
        for ref in (one, two):
            for f in range(3):
                ref[f, z] = zero

    def fill(z):
        for ch in range(4):
            start[ch, z + 1, 0:8, :] = own[ch, z, 8:16, :]
            start[ch, z + 1, 8:16, :] = rim[ch, z]
            start[ch, z + 1, 16:24, :] = own[ch, z, 0:8, :]
        for f in range(3):
            for ref, source in ((one, own_one), (two, own_two)):
                ref[f, z + 1, 0:8, :] = source[f, z + 1, 16:24, :]
                ref[f, z + 1, 16:24, :] = source[f, z + 1, 8:16, :]

    loop(32, fill, 4)
    upper = iota((8, 128), 0) < 4

    def both(ref, lead, step, shift=0):
        high = ref[(*lead, pl.ds(8 - step + shift, 8), slice(None))]
        low = ref[(*lead, pl.ds(8 + step + shift, 8), slice(None))]
        return jnp.where(upper, high, low)

    def six_both(ref, f, z, step):
        value = both(ref, (f, z), step)
        return value, (
            both(ref, (f, z), step, -1),
            both(ref, (f, z), step, 1),
            roll(value, 1),
            roll(value, -1),
            both(ref, (f, z - 1), step),
            both(ref, (f, z + 1), step),
        )

    def put(ref, f, z, step, value):
        ref[f, z, pl.ds(8 - step, 4), :] = value[0:4]
        ref[f, z, pl.ds(12 + step, 4), :] = value[4:8]

    row = iota((16, 128), 0) + 5
    low, high = jnp.where(gx > 0, 1, 0), jnp.where(gx < NX - 1, 1, 0)
    inside = jnp.where((row >= 8) & (row < 12), high, jnp.where((row >= 12) & (row < 16), low, 1))
    omega = 0.8 * inside.astype(F32)

    def weigh_all(z):
        value, six = six_of(start, (3,), z + 1, 5, 16)
        w, diag = fine_weights(value, six, omega)
        diags[z, 5:21, :] = diag
        for i in range(6):
            weights[i, z, 5:21, :] = w[i]

    loop(32, weigh_all, 4)

    for step, source, target in ((1, start, one), (2, one, two)):

        def sweep(z):
            w = [both(weights, (i, z), step) for i in range(6)]
            for f in range(3):
                value, six = six_both(source, f, z + 1, step)
                put(target, f, z + 1, step, fine_sweep(w, f, value, six))

        loop(32, sweep, 4)

    sub = iota((8, 128), 0)

    def residual(pair):
        sums = {}
        for k in range(2):
            z = 2 * pair + k
            w = [both(weights, (i, z), 3) for i in range(6)]
            diag = both(diags, (z,), 3)
            for f in range(3):
                value, six = six_both(two, f, z + 1, 3)
                value = fine_left(w, f, value, six, diag)
                sums[f] = value if k == 0 else sums[f] + value
        for f in range(3):
            halves[f, pair, 0:8, :] = jnp.where(sub < 3, roll(sums[f], 3, 0), own_halves[f, pair, 0:8, :])
            halves[f, pair, 8:16, :] = jnp.where(sub >= 5, roll(sums[f], 5, 0), own_halves[f, pair, 8:16, :])
        halves[3, pair] = own_halves[3, pair]

    loop(16, residual, 2)
    pool = jnp.where(iota((128, 128), 0) // 2 == iota((128, 128), 1), 0.125, 0.0)
    pooled[...] = dot(halves[...].reshape(1024, 128), pool)
    for ch in range(4):
        even = pooled[pl.ds(256 * ch, 128, stride=2), :]
        odd = pooled[pl.ds(256 * ch + 1, 128, stride=2), :]
        coarse[ch] = (even + odd).reshape(16, 8, 128)

    def edge(z):
        for ch in range(4):
            edges[ch, z] = edge_columns(lambda at: rim[ch, at], z, (8, 128))

    loop(16, edge, 2)


def rim_kernel(
    edges, edges_rim, owned, near, far, field, coarse, packed,
    start, share, one, two, weights, diags, halves, pooled,
):
    gx, gy = lax.axis_index("gx"), lax.axis_index("gy")
    lane = iota((24, 128), 1)
    part = lane % 64
    is_after = (part >= 7) & (part < 22)
    is_before = (part >= 42) & (part < 57)
    first_core = lax.rem(gy, 2) == 0

    def unpack(low):
        for ch in range(4):
            target = start.at[ch] if ch < 3 else share
            from_right = jnp.where(first_core, near[ch, low], far[ch, low])
            from_left = jnp.where(first_core, far[ch, low], near[ch, low])
            for h in range(4):
                z = 4 * h + low
                after_y = roll(from_right, 7 - 16 * (h + 1))
                before_y = roll(from_left, 41 - 16 * h)
                own = jnp.concatenate([edges[ch, z], edges_rim[ch, z]], axis=0)
                value = jnp.where(is_after, after_y, jnp.where(is_before, before_y, own))
                target[z + 1, 8:24, :] = value[0:16]
                target[z + 1, 0:8, :] = value[16:24]
                target[z + 1, 24:32, :] = value[16:24]

    loop(4, unpack)

    half_of = iota((32, 128), 1)

    def wrap_one(ref):
        ref[0] = jnp.where(half_of >= 64, roll(ref[16], 64), 0.0)
        ref[17] = jnp.where(half_of < 64, roll(ref[1], 64), 0.0)

    def wrap(ref):
        for f in range(3):
            wrap_one(ref.at[f])

    wrap_one(share)
    wrap(start)
    row = iota((24, 128), 0) + 6
    low, high = jnp.where(gx > 0, 1, 0), jnp.where(gx < NX - 1, 1, 0)
    inside_x = jnp.where(row < 8, low, jnp.where(row >= 24, high, 1))
    inside_y = jnp.where(
        part < 32,
        jnp.where((part < 7) | (gy < NY - 1), 1, 0),
        jnp.where((part >= 57) | (gy > 0), 1, 0),
    )
    omega = 0.8 * (inside_x * inside_y).astype(F32)
    fine_sweeps(
        16, [(6, 24), (7, 24)], start, share, one, two, weights, diags, halves, omega, wrap, field
    )

    source, target = iota((128, 128), 0), iota((128, 128), 1)
    spot = source % 64
    column = jnp.where(spot < 32, 121 + spot, 128 + spot - 57)
    to = jnp.where(spot < 32, column // 2, (column // 2 + 64) % 128)
    from_rim = (iota((64, 128), 1) < 2) | (iota((64, 128), 1) >= 62)
    mixed = halves[...].reshape(512, 128)
    for half in range(2):
        pool = jnp.where((to == target) & (source // 64 == half), 0.125, 0.0)
        pooled[...] = dot(mixed, pool)
        for ch in range(4):
            even = pooled[pl.ds(128 * ch, 64, stride=2), :]
            odd = pooled[pl.ds(128 * ch + 1, 64, stride=2), :]
            at = pl.ds(8 * half, 8)
            rest = owned[ch, at].reshape(64, 128)
            coarse[ch, at] = jnp.where(from_rim, even + odd, rest).reshape(8, 8, 128)

    lane = iota((8, 128), 1)
    for ch in range(4):
        for group in range(2):
            tiles = [None] * 5
            for k in range(8):
                moved = roll(coarse[ch, 8 * group + k], 8 + 80 * k)
                tile, off = divmod(80 * k, 128)
                tiles[tile] = moved if off == 0 else jnp.where(lane >= off, moved, tiles[tile])
                if off + 80 > 128:
                    tiles[tile + 1] = moved
            for tile in range(5):
                packed[ch, group, tile] = tiles[tile]


def patch_kernel(two, rim, field):
    lane = iota((16, 128), 1)

    def plane(z):
        for f in range(3):
            value = rim[f, z]
            for half in range(2):
                base = 64 * half
                low = roll(value, -57 - base)
                high = roll(value, 121 - base)
                at = z + 16 * half
                own = jnp.concatenate([two[f, at + 1, 16:24, :], two[f, at + 1, 0:8, :]], axis=0)
                field[f, at] = jnp.where(lane < 3, low, jnp.where(lane >= 125, high, own))

    loop(16, plane, 2)


def resist(share):
    return recip(1.0 - 0.9 * share)


def level_weights(own, six, omega):
    faces = [2.0 * recip(own + other) for other in six]
    diag = (faces[0] + faces[1]) + (faces[2] + faces[3]) + (faces[4] + faces[5])
    gain = omega * recip(diag)
    return gain, [gain * w for w in faces], diag


def middle_kernel(
    mine, near, far, sent, e_one, e_two,
    share, rest, rhs, first, second, weights, diags, halves, pooled,
    rest2, first2, second2, rhs2, share2, weights2, diags2,
):
    gx, gy = lax.axis_index("gx"), lax.axis_index("gy")
    low_x, high_x = jnp.where(gx > 0, 1, 0), jnp.where(gx < NX - 1, 1, 0)
    low_y, high_y = jnp.where(gy > 0, 1, 0), jnp.where(gy < NY - 1, 1, 0)

    for f in range(3):
        for ref in (first, second):
            ref[f, 0] = jnp.zeros((32, 128), F32)
            ref[f, 17] = jnp.zeros((32, 128), F32)
    for z in (0, 17):
        rest[z] = jnp.ones((32, 128), F32)
    lane = iota((8, 128), 1)
    even = lax.rem(gx, 2) == 0
    near_row, far_row = jnp.where(even, 16, 0), jnp.where(even, 0, 16)
    starts = (pl.multiple_of(near_row, 8), pl.multiple_of(far_row, 8), 8)

    def fill(group):
        for k in range(8):
            z = 8 * group + k
            tile, off = divmod(80 * k, 128)
            for ch in range(4):
                parts = []
                for ref in (near, far):
                    value = ref[ch, group, tile]
                    if off + 80 > 128:
                        value = jnp.where(lane >= off, value, ref[ch, group, tile + 1])
                    parts.append(roll(value, -8 - 80 * k))
                parts.append(mine[ch, z])
                for at, value in zip(starts, parts):
                    if ch < 3:
                        rhs[ch, z, pl.ds(at, 8), :] = value
                    else:
                        share[z, pl.ds(at, 8), :] = value
                        rest[z + 1, pl.ds(at, 8), :] = resist(value)
            rest[z + 1, 24:32, :] = jnp.ones((8, 128), F32)

    loop(2, fill)

    row, lane = iota((24, 128), 0) + 1, iota((24, 128), 1)
    in_x = jnp.where(row < 8, low_x, jnp.where(row >= 16, high_x, 1))
    in_y = jnp.where(lane < 64, 1, jnp.where(lane < 96, high_y, low_y))
    omega = 0.8 * (in_x * in_y).astype(F32)

    def start(z):
        own, six = six_of(rest, (), z + 1, 1, 24)
        gain, w, diag = level_weights(own, six, omega)
        for i in range(6):
            weights[i, z, 1:25, :] = w[i]
        diags[z, 1:25, :] = (1.25 * 0.25) * diag
        for f in range(3):
            first[f, z + 1, 1:25, :] = (4.0 * gain) * rhs[f, z, 1:25, :]

    loop(16, start, 2)

    def sweep(z):
        w = [weights[i, z, 3:27, :] for i in range(6)]
        for f in range(3):
            own, six = six_of(first, (f,), z + 1, 3, 24)
            second[f, z + 1, 3:27, :] = 1.2 * own + weigh(w, six)

    loop(16, sweep, 4)

    def left(pair):
        sums = {}
        for k in range(2):
            z = 2 * pair + k
            w = [weights[i, z, 4:20, :] for i in range(6)]
            diag = diags[z, 4:20, :]
            for f in range(3):
                own, six = six_of(second, (f,), z + 1, 4, 16)
                change = (first[f, z + 1, 4:20, :] - 0.8 * own) + weigh(w, six)
                value = change * diag
                sums[f] = value if k == 0 else sums[f] + value
                e_one[f, z] = second[f, z + 1, 8:16, :]
        for f in range(3):
            halves[f, pair, 0:16, :] = sums[f]
            halves[f, pair, 16:24, :] = jnp.zeros((8, 128), F32)
        halves[3, pair] = share[2 * pair] + share[2 * pair + 1]

    loop(8, left, 2)

    source, target = iota((128, 128), 0), iota((128, 128), 1)
    pool = jnp.where(source // 2 + jnp.where(source >= 96, 64, 0) == target, 0.125, 0.0)
    pooled[...] = dot(halves[...].reshape(4 * 8 * 24, 128), pool)
    for z in (0, 9):
        rest2[z] = jnp.ones((24, 128), F32)
        for f in range(3):
            first2[f, z] = jnp.zeros((24, 128), F32)
            second2[f, z] = jnp.zeros((24, 128), F32)
    for z in range(8):
        for f in range(3):
            base = (f * 8 + z) * 24
            rhs2[f, z] = pooled[pl.ds(base, 8, stride=2), :] + pooled[pl.ds(base + 1, 8, stride=2), :]
        base = (3 * 8 + z) * 24
        value = pooled[pl.ds(base + 2, 8, stride=2), :] + pooled[pl.ds(base + 3, 8, stride=2), :]
        rest2[z + 1, 0:8, :] = resist(value)
        value = pooled[pl.ds(base + 8, 8, stride=2), :] + pooled[pl.ds(base + 9, 8, stride=2), :]
        rest2[z + 1, 3:11, :] = resist(value)
        share2[z] = value

    row, lane = iota((8, 128), 0) + 1, iota((8, 128), 1)
    in_x = jnp.where(row < 3, low_x, jnp.where(row >= 7, high_x, 1))
    in_y = jnp.where(lane < 32, 1, jnp.where(lane < 96, high_y, low_y))
    omega2 = 0.8 * (in_x * in_y).astype(F32)

    def start2(z):
        own, six = six_of(rest2, (), z + 1, 1, 8)
        gain, w, diag = level_weights(own, six, omega2)
        for i in range(6):
            weights2[i, z, 1:9, :] = w[i]
        diags2[z, 1:9, :] = (1.25 * 0.0625) * diag
        for f in range(3):
            first2[f, z + 1, 1:9, :] = (16.0 * gain) * rhs2[f, z]

    loop(8, start2, 8)

    def sweep2(z):
        w = [weights2[i, z, 2:10, :] for i in range(6)]
        for f in range(3):
            own, six = six_of(first2, (f,), z + 1, 2, 8)
            second2[f, z + 1, 2:10, :] = 1.2 * own + weigh(w, six)

    loop(8, sweep2, 8)

    own_row = iota((8, 128), 0) < 4
    parts = []
    for pair in range(4):
        sums = {}
        for k in range(2):
            z = 2 * pair + k
            w = [weights2[i, z, 3:11, :] for i in range(6)]
            diag = diags2[z, 3:11, :]
            for f in range(3):
                own, six = six_of(second2, (f,), z + 1, 3, 8)
                e_two[f, z] = own
                change = (first2[f, z + 1, 3:11, :] - 0.8 * own) + weigh(w, six)
                value = jnp.where(own_row, change * diag, 0.0)
                sums[f] = value if k == 0 else sums[f] + value
            value = jnp.where(own_row, share2[z], 0.0)
            sums[3] = value if k == 0 else sums[3] + value
        parts.append(sums)

    pool = jnp.where((source < 32) & (source // 2 == target % 16), 0.125, 0.0)
    rows = jnp.concatenate([parts[pair][ch] for ch in range(4) for pair in range(4)], axis=0)
    spread = dot(rows, pool)
    at, to = iota((32, 128), 0), iota((32, 128), 1)
    keep = (at // 8 == to // 32) & ((at % 8) // 2 == (to // 16) % 2)
    result = jnp.concatenate(
        [
            jnp.sum(jnp.where(keep, spread[32 * ch : 32 * ch + 32], 0.0), axis=0, keepdims=True)
            for ch in range(4)
        ],
        axis=0,
    )
    for copy in range(NY):
        sent[copy] = result


def turn_kernel(column, sent):
    sub, group = iota((8, 128), 0), iota((8, 128), 1) // 16
    tiles = [column[8 * j : 8 * j + 8, :] for j in range(8)]
    moved = [[roll(tile, 16 * d) for d in range(8)] for tile in tiles]
    for q in range(8):
        halves = []
        for half in range(2):
            value = jnp.zeros((8, 128), F32)
            for j in range(4):
                for odd in range(2):
                    to = 2 * j + odd
                    mask = (sub // 4 == odd) & (group == to)
                    value = jnp.where(mask, moved[4 * half + j][(to - q) % 8], value)
            halves.append(value + roll(value, 4, 0))
        tile = jnp.where(sub < 4, halves[0], halves[1])
        for copy in range(NX):
            sent[copy, 8 * q : 8 * q + 8, :] = tile


def top_kernel(
    gathered, field, e_one, e_two, out,
    first, second, four, weights, diags, lefts, wide, final, sems,
):
    gx, gy = lax.axis_index("gx"), lax.axis_index("gy")
    lane, sub = iota((16, 128), 1), iota((16, 128), 0)
    cells = [(z, x, half) for z in range(4) for x in range(2) for half in range(2)]

    def plane(ch, z, x, half):
        return gathered[pl.ds(((z * 2 + x) * 2 + half) * 4 + ch, 16, stride=64), :]

    def neighbours(at, z, x, half, outside):
        own, other = at(z, x, half), at(z, 1 - x, half)
        beside = at(z, x, 1 - half)
        shifted = roll(other, 1 if x == 0 else -1, 0)
        low, high = (shifted, other) if x == 0 else (other, shifted)
        left, right = roll(own, 1), roll(own, -1)
        if half == 0:
            right = jnp.where(lane == 127, roll(beside, -1), right)
        else:
            left = jnp.where(lane == 0, roll(beside, 1), left)
        down = at(z - 1, x, half) if z > 0 else outside
        up = at(z + 1, x, half) if z < 3 else outside
        return own, [low, high, left, right, down, up]

    def edge_masks(x, half):
        return [
            sub > 0 if x == 0 else None,
            sub < 15 if x == 1 else None,
            lane > 0 if half == 0 else None,
            lane < 127 if half == 1 else None,
            None,
            None,
        ]

    def key(z, x, half):
        return (z * 2 + x) * 2 + half

    shares = {c: plane(3, *c) for c in cells}
    rests = {c: resist(shares[c]) for c in cells}
    ones, zeros = jnp.ones((16, 128), F32), jnp.zeros((16, 128), F32)
    for z, x, half in cells:
        own, six = neighbours(lambda *c: rests[c], z, x, half, ones)
        masks = edge_masks(x, half)
        six = [s if m is None else jnp.where(m, s, 1.0) for s, m in zip(six, masks)]
        gain, w, diag = level_weights(own, six, 0.8)
        at = key(z, x, half)
        for i in range(6):
            weights[i, at] = w[i] if masks[i] is None else jnp.where(masks[i], w[i], 0.0)
        diags[at] = (1.25 * 0.25**3) * diag
        for f in range(3):
            first[f, at] = (64.0 * gain) * plane(f, z, x, half)

    for z, x, half in cells:
        at = key(z, x, half)
        w = [weights[i, at] for i in range(6)]
        for f in range(3):
            own, six = neighbours(lambda *c: first[f, key(*c)], z, x, half, zeros)
            second[half, f, z * 2 + x] = 1.2 * own + weigh(w, six)

    for z4 in range(2):
        for half in range(2):
            sums = [None] * 4
            for z in (2 * z4, 2 * z4 + 1):
                for x in range(2):
                    at = key(z, x, half)
                    w = [weights[i, at] for i in range(6)]
                    diag = diags[at]
                    for f in range(3):
                        own, six = neighbours(
                            lambda c, d, e: second[e, f, c * 2 + d], z, x, half, zeros
                        )
                        value = ((first[f, at] - 0.8 * own) + weigh(w, six)) * diag
                        sums[f] = value if sums[f] is None else sums[f] + value
                    share = shares[z, x, half]
                    sums[3] = share if sums[3] is None else sums[3] + share
            for ch in range(4):
                lefts[ch, z4, :, 128 * half : 128 * half + 128] = sums[ch]

    pool = jnp.where(iota((256, 128), 0) // 2 == iota((256, 128), 1), 0.125, 0.0)
    level = dot(lefts[...].reshape(128, 256), pool)

    def coarsest(ch, z):
        return level[(ch * 2 + z) * 16 : (ch * 2 + z) * 16 + 16, :]

    masks = [sub > 0, sub < 15, lane > 0, lane < 127]
    resists = [resist(coarsest(3, z)) for z in range(2)]
    gains, ws, ds = [], [], []
    for z in range(2):
        own, other = resists[z], resists[1 - z]
        six = [roll(own, 1, 0), roll(own, -1, 0), roll(own, 1), roll(own, -1)]
        six = [jnp.where(m, s, 1.0) for m, s in zip(masks, six)] + [other, ones]
        gain, w, diag = level_weights(own, six, 0.8)
        gains.append(gain)
        ds.append(diag)
        ws.append([jnp.where(m, v, 0.0) for m, v in zip(masks, w)] + [w[4]])
    whole = jnp.sum(ds[0] + ds[1], keepdims=True)

    def around(values, z):
        own, other = values[z], values[1 - z]
        return weigh(ws[z], (roll(own, 1, 0), roll(own, -1, 0), roll(own, 1), roll(own, -1), other))

    begin = [[256.0 * gains[z] * coarsest(f, z) for z in range(2)] for f in range(3)]
    values = begin
    for step in range(5):
        values = [
            [(0.2 * values[f][z] + begin[f][z]) + around(values[f], z) for z in range(2)] for f in range(3)
        ]
    for f in range(3):
        change = [(begin[f][z] - 0.8 * values[f][z]) + around(values[f], z) for z in range(2)]
        total = jnp.sum(1.25 * (change[0] * ds[0] + change[1] * ds[1]), keepdims=True)
        for z in range(2):
            four[2 * f + z] = values[f][z] + total / whole

    copy = jnp.where(iota((128, 128), 0) == iota((128, 128), 1) // 2, 1.0, 0.0)
    rows = four.reshape(96, 128)[pl.ds(gx, 6, stride=16), :]
    rows = jnp.concatenate([jnp.broadcast_to(rows[i : i + 1], (4, 128)) for i in range(6)], axis=0)
    three = dot(turn(rows, -8 * gy), copy)
    flat = second.reshape(768, 128)
    halves = [flat[pl.ds(gx + 384 * half, 24, stride=16), :] for half in range(2)]
    three = three + turn(jnp.where(gy < 8, halves[0], halves[1]), -16 * lax.rem(gy, 8))

    three = dot(three, copy)
    low = iota((8, 128), 0) < 2
    tiles = []
    for f in range(3):
        for z in range(4):
            at = f * 8 + z * 2
            tile = jnp.where(
                low,
                jnp.broadcast_to(three[at : at + 1], (8, 128)),
                jnp.broadcast_to(three[at + 1 : at + 2], (8, 128)),
            )
            tiles += [e_two[f, 2 * z] + tile, e_two[f, 2 * z + 1] + tile]

    two = dot(jnp.concatenate(tiles, axis=0), copy)
    for block in range(24):
        value = two[8 * block : 8 * block + 4, :]
        wide[pl.ds(8 * block, 4, stride=2), :] = value
        wide[pl.ds(8 * block + 1, 4, stride=2), :] = value
    one = e_one[...].reshape(24, 2, 8, 128) + wide[...].reshape(24, 1, 8, 128)

    one = dot(one.reshape(384, 128), copy)
    flat_in = field.reshape(3 * 32 * 16, 128)
    flat_out = final.reshape(3 * 32 * 16, 128)
    copies = []
    for f in range(3):
        for block in range(16 * f, 16 * f + 16):
            value = one[8 * block : 8 * block + 8, :]
            for k in range(2):
                for half in range(2):
                    at = pl.ds(32 * block + 16 * k + half, 8, stride=2)
                    flat_out[at, :] = flat_in[at, :] + value
            if block % 8 == 7:
                part = (f, pl.ds(2 * (block % 16) - 14, 16))
                copy = pltpu.make_async_copy(final.at[part], out.at[part], sems.at[len(copies)])
                copy.start()
                copies.append(copy)
    for copy in copies:
        copy.wait()


def local(labels, guess):
    swap_near = [(i, i ^ 1) for i in range(NY)]
    swap_far = [(i, j) for k in range(1, NY - 1, 2) for i, j in ((k, k + 1), (k + 1, k))]
    to_near, to_far, own = call(
        rows_kernel,
        [(12, 32, 128)] * 2 + [(4, 32, 16, 128)],
        [pltpu.VMEM((32, 16, 128), jnp.int32), pltpu.SemaphoreType.DMA((4,))],
        in_specs=[ANY, ANY],
    )(pltpu.with_memory_space_constraint(guess, pltpu.HBM), pltpu.with_memory_space_constraint(labels, pltpu.HBM))
    from_near = lax.ppermute(to_near, "gx", swap_near)
    from_far = lax.ppermute(to_far, "gx", swap_far)
    own_one, own_two, halves, to_right, to_left, edges = call(
        own_kernel,
        [(3, 34, 32, 128)] * 2 + [(4, 16, 16, 128)] + [(4, 4, 16, 128)] * 2 + [(4, 16, 16, 128)],
        [(4, 34, 32, 128), (6, 32, 32, 128), (32, 32, 128)],
        flops=20_000_000,
    )(own)
    to_near, to_far, rim_rows = call(pack_kernel, [(4, 4, 24, 128)] * 2 + [(4, 32, 8, 128)], [])(
        to_right, to_left, from_near, from_far
    )
    from_far = lax.ppermute(to_far, "gy", swap_far)
    from_near = lax.ppermute(to_near, "gy", swap_near)
    two, part, edges_rim = call(
        rows_edge_kernel,
        [(3, 34, 24, 128), (4, 16, 8, 128), (4, 16, 8, 128)],
        [(4, 34, 24, 128), (3, 34, 24, 128), (6, 32, 24, 128), (32, 24, 128)]
        + [(4, 16, 16, 128), (1024, 128)],
        flops=10_000_000,
    )(own, rim_rows, own_one, own_two, halves)
    rim, coarse, packed = call(
        rim_kernel,
        [(3, 16, 16, 128), (4, 16, 8, 128), (4, 2, 5, 8, 128)],
        [(3, 18, 32, 128), (18, 32, 128)]
        + [(3, 18, 32, 128)] * 2
        + [(6, 16, 32, 128), (16, 32, 128)]
        + [(4, 8, 16, 128), (512, 128)],
        flops=10_000_000,
    )(edges, edges_rim, part, from_near, from_far)
    from_near = lax.ppermute(packed, "gx", swap_near)
    from_far = lax.ppermute(packed, "gx", swap_far)
    (field,) = call(patch_kernel, [(3, 32, 16, 128)], [])(two, rim)
    sent, e_one, e_two = call(
        middle_kernel,
        [(NY, 4, 128), (3, 16, 8, 128), (3, 8, 8, 128)],
        [(16, 24, 128), (18, 32, 128), (3, 16, 32, 128), (3, 18, 32, 128), (3, 18, 32, 128)]
        + [(6, 16, 32, 128), (16, 32, 128), (4, 8, 24, 128), (768, 128)]
        + [(10, 24, 128), (3, 10, 24, 128), (3, 10, 24, 128), (3, 8, 8, 128), (8, 8, 128)]
        + [(6, 8, 16, 128), (8, 16, 128)],
    )(coarse, from_near, from_far)
    column = lax.all_to_all(sent, "gy", split_axis=0, concat_axis=0, tiled=True).reshape(64, 128)
    (copies,) = call(turn_kernel, [(NX, 64, 128)], [])(column)
    gathered = lax.all_to_all(copies, "gx", split_axis=0, concat_axis=0, tiled=True).reshape(1024, 128)
    (out,) = call(
        top_kernel,
        [(3, 32, 16, 128)],
        [(3, 16, 16, 128), (2, 3, 8, 16, 128), (6, 16, 128), (6, 16, 16, 128), (16, 16, 128)]
        + [(4, 2, 16, 256), (192, 128), (3, 32, 16, 128), pltpu.SemaphoreType.DMA((6,))],
        out_specs=[ANY],
    )(gathered, field, e_one, e_two)
    return out


def solution(mesh):
    return jax.shard_map(
        local,
        mesh=mesh,
        in_specs=(P(None, "gx", "gy"), P(None, None, "gx", "gy")),
        out_specs=P(None, None, "gx", "gy"),
        check_vma=False,
    )
```

```python
import jax
import jax.numpy as jnp
from jax import lax
from jax.experimental import pallas as pl
from jax.experimental.pallas import tpu as pltpu
from jax.sharding import PartitionSpec as P


F32 = jnp.float32
NX, NY, CHIPS = 16, 16, 128
BETWEEN = 2.0 * 0.1 / 1.1
ANY = pl.BlockSpec(memory_space=pltpu.HBM)


def dot(a, b):
    return jnp.dot(a, b, precision=lax.Precision.HIGHEST, preferred_element_type=F32)


def iota(shape, dim):
    return lax.broadcasted_iota(jnp.int32, shape, dim)


def roll(x, shift, axis=1):
    shift = shift % x.shape[axis]
    return x if shift == 0 else pltpu.roll(x, shift, axis)


def turn(x, shift):
    return pltpu.roll(x, lax.rem(shift + 256, 128), 1)


def recip(x):
    guess = pl.reciprocal(x, approx=True)
    return guess * (2.0 - x * guess)


def call(kernel, outs, scratch, flops=1_000_000, **kw):
    return pl.pallas_call(
        kernel,
        out_shape=[jax.ShapeDtypeStruct(s, F32) for s in outs],
        scratch_shapes=[pltpu.VMEM(s, F32) if isinstance(s, tuple) else s for s in scratch],
        compiler_params=pltpu.CompilerParams(vmem_limit_bytes=32 * 1024 * 1024),
        cost_estimate=pl.CostEstimate(flops=flops, bytes_accessed=4_000_000, transcendentals=0),
        **kw,
    )


def loop(count, body, unroll=1):
    def step(i, carry):
        body(i)
        return carry

    lax.fori_loop(0, count, step, 0, unroll=unroll)


def weigh(weights, values):
    parts = [w * v for w, v in zip(weights, values)]
    while len(parts) > 1:
        parts = [sum(parts[i : i + 2][1:], parts[i]) for i in range(0, len(parts), 2)]
    return parts[0]


def rows_kernel(guess, labels, near, far, own, phase, sems):
    even = lax.rem(lax.axis_index("gx"), 2) == 0
    near_row, far_row = jnp.where(even, 13, 0), jnp.where(even, 0, 13)
    copies = [pltpu.make_async_copy(labels, phase, sems.at[3])]
    for f in range(3):
        copies.append(pltpu.make_async_copy(guess.at[f], own.at[f], sems.at[f]))
    for copy in copies:
        copy.start()
    copies[0].wait()
    own[3] = jnp.where(phase[...] == 1, 0.0, 1.0).astype(F32)
    flat = own.reshape(4 * 32 * 16, 128)
    for ch in (3, 0, 1, 2):
        if ch < 3:
            copies[ch + 1].wait()
        for row in range(3):
            near[3 * ch + row] = flat[pl.ds(512 * ch + near_row + row, 32, stride=16), :]
            far[3 * ch + row] = flat[pl.ds(512 * ch + far_row + row, 32, stride=16), :]


def pack_kernel(to_right, to_left, x_near, x_far, near, far, rim):
    first_core = lax.rem(lax.axis_index("gy"), 2) == 0
    even = lax.rem(lax.axis_index("gx"), 2) == 0
    near_row, far_row = jnp.where(even, 0, 5), jnp.where(even, 5, 0)
    flat = rim.reshape(4 * 32 * 8, 128)
    for ch in range(4):
        for row in range(3):
            flat[pl.ds(256 * ch + near_row + row, 32, stride=8), :] = x_near[3 * ch + row]
            flat[pl.ds(256 * ch + far_row + row, 32, stride=8), :] = x_far[3 * ch + row]

    def some(low):
        for ch in range(4):
            right, left = pack_planes(lambda z: rim[ch, z], low, (8, 128))
            for at, right, left in (
                (slice(0, 16), to_right[ch, low], to_left[ch, low]),
                (slice(16, 24), right, left),
            ):
                near[ch, low, at, :] = jnp.where(first_core, right, left)
                far[ch, low, at, :] = jnp.where(first_core, left, right)

    loop(4, some)


def pack_planes(plane, low, shape):
    group = iota(shape, 1) // 16
    right = left = jnp.zeros(shape, F32)
    for h in range(8):
        moved = roll(plane(4 * h + low), 16 * h + 16)
        right = jnp.where(group == h, moved, right)
        left = jnp.where(group == (h + 1) % 8, moved, left)
    return right, left


def edge_columns(plane, z, shape):
    lane = iota(shape, 1)
    value = jnp.zeros(shape, F32)
    for half in range(2):
        source = plane(z + 16 * half)
        base = 64 * half
        value = jnp.where((lane >= base) & (lane < base + 7), roll(source, base + 7), value)
        value = jnp.where((lane >= base + 57) & (lane < base + 64), roll(source, base + 57), value)
    return value


def six_of(ref, lead, z, first, count):
    own = ref[(*lead, z, pl.ds(first, count), slice(None))]
    return own, (
        ref[(*lead, z, pl.ds(first - 1, count), slice(None))],
        ref[(*lead, z, pl.ds(first + 1, count), slice(None))],
        roll(own, 1),
        roll(own, -1),
        ref[(*lead, z - 1, pl.ds(first, count), slice(None))],
        ref[(*lead, z + 1, pl.ds(first, count), slice(None))],
    )


def face(total):
    return jnp.where(total < 0.5, 1.0, jnp.where(total < 1.5, BETWEEN, 0.1))


def fine_weights(own, six, omega):
    faces = [face(own + other) for other in six]
    diag = (faces[0] + faces[1]) + (faces[2] + faces[3]) + (faces[4] + faces[5])
    gain = omega * recip(diag)
    return [gain * value for value in faces], 1.25 * diag


def fine_sweep(w, f, own, six):
    return (0.2 * own + (w[2 * f + 1] - w[2 * f])) + weigh(w, six)


def fine_left(w, f, own, six, diag):
    return (((w[2 * f + 1] - w[2 * f]) - 0.8 * own) + weigh(w, six)) * diag


def fine_sweeps(planes, windows, start, share, one, two, weights, diags, halves, omega, wrap, keep):
    first, count = windows[0]

    def first_sweep(z):
        own, six = six_of(share, (), z + 1, first, count)
        w, diag = fine_weights(own, six, omega)
        diags[z, pl.ds(first, count), :] = diag
        for i in range(6):
            weights[i, z, pl.ds(first, count), :] = w[i]
        for f in range(3):
            own, six = six_of(start, (f,), z + 1, first, count)
            one[f, z + 1, pl.ds(first, count), :] = fine_sweep(w, f, own, six)

    loop(planes, first_sweep, 4)
    wrap(one)
    second, count2 = windows[1]

    def second_sweep(z):
        w = [weights[i, z, pl.ds(second, count2), :] for i in range(6)]
        for f in range(3):
            own, six = six_of(one, (f,), z + 1, second, count2)
            two[f, z + 1, pl.ds(second, count2), :] = fine_sweep(w, f, own, six)

    loop(planes, second_sweep, 4)
    wrap(two)

    def residual(pair):
        sums = {}
        for k in range(2):
            z = 2 * pair + k
            w = [weights[i, z, 8:24, :] for i in range(6)]
            diag = diags[z, 8:24, :]
            for f in range(3):
                own, six = six_of(two, (f,), z + 1, 8, 16)
                if keep is not None:
                    keep[f, z] = own
                value = fine_left(w, f, own, six, diag)
                sums[f] = value if k == 0 else sums[f] + value
            value = share[z + 1, 8:24, :]
            sums[3] = value if k == 0 else sums[3] + value
        for ch, value in sums.items():
            halves[ch, pair] = value

    loop(planes // 2, residual, 2)


def own_kernel(own, one, two, halves, to_right, to_left, edges, held, weights, diags):
    zero = jnp.zeros((32, 128), F32)
    for z in (0, 33):
        for ch in range(4):
            held[ch, z] = zero
        for ref in (one, two):
            for f in range(3):
                ref[f, z] = zero

    def plane(z):
        for ch in range(4):
            held[ch, z + 1, 8:24, :] = own[ch, z]

    loop(32, plane, 4)
    fine_sweeps(
        32, [(8, 16)] * 2, held, held.at[3], one, two, weights, diags, halves, 0.8, lambda ref: None, None
    )

    def some(low):
        for ch in range(4):
            to_right[ch, low], to_left[ch, low] = pack_planes(lambda z: own[ch, z], low, (16, 128))

    loop(4, some)

    def edge(z):
        for ch in range(4):
            edges[ch, z] = edge_columns(lambda at: own[ch, at], z, (16, 128))

    loop(16, edge, 2)


def rows_edge_kernel(own, rim, own_one, own_two, own_halves, two, coarse, edges, start, one, weights, diags, halves, pooled):
    gx = lax.axis_index("gx")
    zero = jnp.zeros((24, 128), F32)
    for z in (0, 33):
        for ch in range(4):
            start[ch, z] = zero
        for ref in (one, two):
            for f in range(3):
                ref[f, z] = zero

    def fill(z):
        for ch in range(4):
            start[ch, z + 1, 0:8, :] = own[ch, z, 8:16, :]
            start[ch, z + 1, 8:16, :] = rim[ch, z]
            start[ch, z + 1, 16:24, :] = own[ch, z, 0:8, :]
        for f in range(3):
            for ref, source in ((one, own_one), (two, own_two)):
                ref[f, z + 1, 0:8, :] = source[f, z + 1, 16:24, :]
                ref[f, z + 1, 16:24, :] = source[f, z + 1, 8:16, :]

    loop(32, fill, 4)
    upper = iota((8, 128), 0) < 4

    def both(ref, lead, step, shift=0):
        high = ref[(*lead, pl.ds(8 - step + shift, 8), slice(None))]
        low = ref[(*lead, pl.ds(8 + step + shift, 8), slice(None))]
        return jnp.where(upper, high, low)

    def six_both(ref, f, z, step):
        value = both(ref, (f, z), step)
        return value, (
            both(ref, (f, z), step, -1),
            both(ref, (f, z), step, 1),
            roll(value, 1),
            roll(value, -1),
            both(ref, (f, z - 1), step),
            both(ref, (f, z + 1), step),
        )

    def put(ref, f, z, step, value):
        ref[f, z, pl.ds(8 - step, 4), :] = value[0:4]
        ref[f, z, pl.ds(12 + step, 4), :] = value[4:8]

    row = iota((16, 128), 0) + 5
    low, high = jnp.where(gx > 0, 1, 0), jnp.where(gx < NX - 1, 1, 0)
    inside = jnp.where((row >= 8) & (row < 12), high, jnp.where((row >= 12) & (row < 16), low, 1))
    omega = 0.8 * inside.astype(F32)

    def weigh_all(z):
        value, six = six_of(start, (3,), z + 1, 5, 16)
        w, diag = fine_weights(value, six, omega)
        diags[z, 5:21, :] = diag
        for i in range(6):
            weights[i, z, 5:21, :] = w[i]

    loop(32, weigh_all, 4)

    for step, source, target in ((1, start, one), (2, one, two)):

        def sweep(z):
            w = [both(weights, (i, z), step) for i in range(6)]
            for f in range(3):
                value, six = six_both(source, f, z + 1, step)
                put(target, f, z + 1, step, fine_sweep(w, f, value, six))

        loop(32, sweep, 4)

    sub = iota((8, 128), 0)

    def residual(pair):
        sums = {}
        for k in range(2):
            z = 2 * pair + k
            w = [both(weights, (i, z), 3) for i in range(6)]
            diag = both(diags, (z,), 3)
            for f in range(3):
                value, six = six_both(two, f, z + 1, 3)
                value = fine_left(w, f, value, six, diag)
                sums[f] = value if k == 0 else sums[f] + value
        for f in range(3):
            halves[f, pair, 0:8, :] = jnp.where(sub < 3, roll(sums[f], 3, 0), own_halves[f, pair, 0:8, :])
            halves[f, pair, 8:16, :] = jnp.where(sub >= 5, roll(sums[f], 5, 0), own_halves[f, pair, 8:16, :])
        halves[3, pair] = own_halves[3, pair]

    loop(16, residual, 2)
    pool = jnp.where(iota((128, 128), 0) // 2 == iota((128, 128), 1), 0.125, 0.0)
    pooled[...] = dot(halves[...].reshape(1024, 128), pool)
    for ch in range(4):
        even = pooled[pl.ds(256 * ch, 128, stride=2), :]
        odd = pooled[pl.ds(256 * ch + 1, 128, stride=2), :]
        coarse[ch] = (even + odd).reshape(16, 8, 128)

    def edge(z):
        for ch in range(4):
            edges[ch, z] = edge_columns(lambda at: rim[ch, at], z, (8, 128))

    loop(16, edge, 2)


def rim_kernel(
    edges, edges_rim, owned, near, far, field, coarse, packed,
    start, share, one, two, weights, diags, halves, pooled,
):
    gx, gy = lax.axis_index("gx"), lax.axis_index("gy")
    lane = iota((24, 128), 1)
    part = lane % 64
    is_after = (part >= 7) & (part < 22)
    is_before = (part >= 42) & (part < 57)
    first_core = lax.rem(gy, 2) == 0

    def unpack(low):
        for ch in range(4):
            target = start.at[ch] if ch < 3 else share
            from_right = jnp.where(first_core, near[ch, low], far[ch, low])
            from_left = jnp.where(first_core, far[ch, low], near[ch, low])
            for h in range(4):
                z = 4 * h + low
                after_y = roll(from_right, 7 - 16 * (h + 1))
                before_y = roll(from_left, 41 - 16 * h)
                own = jnp.concatenate([edges[ch, z], edges_rim[ch, z]], axis=0)
                value = jnp.where(is_after, after_y, jnp.where(is_before, before_y, own))
                target[z + 1, 8:24, :] = value[0:16]
                target[z + 1, 0:8, :] = value[16:24]
                target[z + 1, 24:32, :] = value[16:24]

    loop(4, unpack)

    half_of = iota((32, 128), 1)

    def wrap_one(ref):
        ref[0] = jnp.where(half_of >= 64, roll(ref[16], 64), 0.0)
        ref[17] = jnp.where(half_of < 64, roll(ref[1], 64), 0.0)

    def wrap(ref):
        for f in range(3):
            wrap_one(ref.at[f])

    wrap_one(share)
    wrap(start)
    row = iota((24, 128), 0) + 6
    low, high = jnp.where(gx > 0, 1, 0), jnp.where(gx < NX - 1, 1, 0)
    inside_x = jnp.where(row < 8, low, jnp.where(row >= 24, high, 1))
    inside_y = jnp.where(
        part < 32,
        jnp.where((part < 7) | (gy < NY - 1), 1, 0),
        jnp.where((part >= 57) | (gy > 0), 1, 0),
    )
    omega = 0.8 * (inside_x * inside_y).astype(F32)
    fine_sweeps(
        16, [(6, 24), (7, 24)], start, share, one, two, weights, diags, halves, omega, wrap, field
    )

    source, target = iota((128, 128), 0), iota((128, 128), 1)
    spot = source % 64
    column = jnp.where(spot < 32, 121 + spot, 128 + spot - 57)
    to = jnp.where(spot < 32, column // 2, (column // 2 + 64) % 128)
    from_rim = (iota((64, 128), 1) < 2) | (iota((64, 128), 1) >= 62)
    mixed = halves[...].reshape(512, 128)
    for half in range(2):
        pool = jnp.where((to == target) & (source // 64 == half), 0.125, 0.0)
        pooled[...] = dot(mixed, pool)
        for ch in range(4):
            even = pooled[pl.ds(128 * ch, 64, stride=2), :]
            odd = pooled[pl.ds(128 * ch + 1, 64, stride=2), :]
            at = pl.ds(8 * half, 8)
            rest = owned[ch, at].reshape(64, 128)
            coarse[ch, at] = jnp.where(from_rim, even + odd, rest).reshape(8, 8, 128)

    lane = iota((8, 128), 1)
    for ch in range(4):
        for group in range(2):
            tiles = [None] * 5
            for k in range(8):
                moved = roll(coarse[ch, 8 * group + k], 8 + 80 * k)
                tile, off = divmod(80 * k, 128)
                tiles[tile] = moved if off == 0 else jnp.where(lane >= off, moved, tiles[tile])
                if off + 80 > 128:
                    tiles[tile + 1] = moved
            for tile in range(5):
                packed[ch, group, tile] = tiles[tile]


def base_kernel(two, rim, e_one, e_two, base, wide, spread):
    copy = jnp.where(iota((128, 128), 0) == iota((128, 128), 1) // 2, 1.0, 0.0)
    value = dot(e_two[...].reshape(192, 128), copy)
    for block in range(24):
        rows = value[8 * block : 8 * block + 4, :]
        wide[pl.ds(8 * block, 4, stride=2), :] = rows
        wide[pl.ds(8 * block + 1, 4, stride=2), :] = rows
    value = e_one[...].reshape(24, 2, 8, 128) + wide[...].reshape(24, 1, 8, 128)
    value = dot(value.reshape(384, 128), copy)
    flat = spread.reshape(768, 128)
    for block in range(48):
        rows = value[8 * block : 8 * block + 8, :]
        flat[pl.ds(16 * block, 8, stride=2), :] = rows
        flat[pl.ds(16 * block + 1, 8, stride=2), :] = rows
    lane = iota((16, 128), 1)

    def pair(k):
        for f in range(3):
            for z in (2 * k, 2 * k + 1):
                value = rim[f, z]
                for half in range(2):
                    low = roll(value, -57 - 64 * half)
                    high = roll(value, 121 - 64 * half)
                    at = z + 16 * half
                    own = jnp.concatenate([two[f, at + 1, 16:24, :], two[f, at + 1, 0:8, :]], axis=0)
                    own = jnp.where(lane < 3, low, jnp.where(lane >= 125, high, own))
                    base[f, at] = own + spread[f, k + 8 * half]

    loop(8, pair, 1)


def resist(share):
    return recip(1.0 - 0.9 * share)


def level_weights(own, six, omega):
    faces = [2.0 * recip(own + other) for other in six]
    diag = (faces[0] + faces[1]) + (faces[2] + faces[3]) + (faces[4] + faces[5])
    gain = omega * recip(diag)
    return gain, [gain * w for w in faces], diag


def middle_kernel(
    mine, near, far, sent, e_one, e_two,
    share, rest, rhs, first, second, weights, diags, halves, pooled,
    rest2, first2, second2, rhs2, share2, weights2, diags2,
):
    gx, gy = lax.axis_index("gx"), lax.axis_index("gy")
    low_x, high_x = jnp.where(gx > 0, 1, 0), jnp.where(gx < NX - 1, 1, 0)
    low_y, high_y = jnp.where(gy > 0, 1, 0), jnp.where(gy < NY - 1, 1, 0)

    for f in range(3):
        for ref in (first, second):
            ref[f, 0] = jnp.zeros((32, 128), F32)
            ref[f, 17] = jnp.zeros((32, 128), F32)
    for z in (0, 17):
        rest[z] = jnp.ones((32, 128), F32)
    lane = iota((8, 128), 1)
    even = lax.rem(gx, 2) == 0
    near_row, far_row = jnp.where(even, 16, 0), jnp.where(even, 0, 16)
    starts = (pl.multiple_of(near_row, 8), pl.multiple_of(far_row, 8), 8)

    def fill(group):
        for k in range(8):
            z = 8 * group + k
            tile, off = divmod(80 * k, 128)
            for ch in range(4):
                parts = []
                for ref in (near, far):
                    value = ref[ch, group, tile]
                    if off + 80 > 128:
                        value = jnp.where(lane >= off, value, ref[ch, group, tile + 1])
                    parts.append(roll(value, -8 - 80 * k))
                parts.append(mine[ch, z])
                for at, value in zip(starts, parts):
                    if ch < 3:
                        rhs[ch, z, pl.ds(at, 8), :] = value
                    else:
                        share[z, pl.ds(at, 8), :] = value
                        rest[z + 1, pl.ds(at, 8), :] = resist(value)
            rest[z + 1, 24:32, :] = jnp.ones((8, 128), F32)

    loop(2, fill)

    row, lane = iota((24, 128), 0) + 1, iota((24, 128), 1)
    in_x = jnp.where(row < 8, low_x, jnp.where(row >= 16, high_x, 1))
    in_y = jnp.where(lane < 64, 1, jnp.where(lane < 96, high_y, low_y))
    omega = 0.8 * (in_x * in_y).astype(F32)

    def start(z):
        own, six = six_of(rest, (), z + 1, 1, 24)
        gain, w, diag = level_weights(own, six, omega)
        for i in range(6):
            weights[i, z, 1:25, :] = w[i]
        diags[z, 1:25, :] = (1.25 * 0.25) * diag
        for f in range(3):
            first[f, z + 1, 1:25, :] = (4.0 * gain) * rhs[f, z, 1:25, :]

    loop(16, start, 2)

    def sweep(z):
        w = [weights[i, z, 3:27, :] for i in range(6)]
        for f in range(3):
            own, six = six_of(first, (f,), z + 1, 3, 24)
            second[f, z + 1, 3:27, :] = 1.2 * own + weigh(w, six)

    loop(16, sweep, 4)

    def left(pair):
        sums = {}
        for k in range(2):
            z = 2 * pair + k
            w = [weights[i, z, 4:20, :] for i in range(6)]
            diag = diags[z, 4:20, :]
            for f in range(3):
                own, six = six_of(second, (f,), z + 1, 4, 16)
                change = (first[f, z + 1, 4:20, :] - 0.8 * own) + weigh(w, six)
                value = change * diag
                sums[f] = value if k == 0 else sums[f] + value
                e_one[f, z] = second[f, z + 1, 8:16, :]
        for f in range(3):
            halves[f, pair, 0:16, :] = sums[f]
            halves[f, pair, 16:24, :] = jnp.zeros((8, 128), F32)
        halves[3, pair] = share[2 * pair] + share[2 * pair + 1]

    loop(8, left, 2)

    source, target = iota((128, 128), 0), iota((128, 128), 1)
    pool = jnp.where(source // 2 + jnp.where(source >= 96, 64, 0) == target, 0.125, 0.0)
    pooled[...] = dot(halves[...].reshape(4 * 8 * 24, 128), pool)
    for z in (0, 9):
        rest2[z] = jnp.ones((24, 128), F32)
        for f in range(3):
            first2[f, z] = jnp.zeros((24, 128), F32)
            second2[f, z] = jnp.zeros((24, 128), F32)
    for z in range(8):
        for f in range(3):
            base = (f * 8 + z) * 24
            rhs2[f, z] = pooled[pl.ds(base, 8, stride=2), :] + pooled[pl.ds(base + 1, 8, stride=2), :]
        base = (3 * 8 + z) * 24
        value = pooled[pl.ds(base + 2, 8, stride=2), :] + pooled[pl.ds(base + 3, 8, stride=2), :]
        rest2[z + 1, 0:8, :] = resist(value)
        value = pooled[pl.ds(base + 8, 8, stride=2), :] + pooled[pl.ds(base + 9, 8, stride=2), :]
        rest2[z + 1, 3:11, :] = resist(value)
        share2[z] = value

    row, lane = iota((8, 128), 0) + 1, iota((8, 128), 1)
    in_x = jnp.where(row < 3, low_x, jnp.where(row >= 7, high_x, 1))
    in_y = jnp.where(lane < 32, 1, jnp.where(lane < 96, high_y, low_y))
    omega2 = 0.8 * (in_x * in_y).astype(F32)

    def start2(z):
        own, six = six_of(rest2, (), z + 1, 1, 8)
        gain, w, diag = level_weights(own, six, omega2)
        for i in range(6):
            weights2[i, z, 1:9, :] = w[i]
        diags2[z, 1:9, :] = (1.25 * 0.0625) * diag
        for f in range(3):
            first2[f, z + 1, 1:9, :] = (16.0 * gain) * rhs2[f, z]

    loop(8, start2, 8)

    def sweep2(z):
        w = [weights2[i, z, 2:10, :] for i in range(6)]
        for f in range(3):
            own, six = six_of(first2, (f,), z + 1, 2, 8)
            second2[f, z + 1, 2:10, :] = 1.2 * own + weigh(w, six)

    loop(8, sweep2, 8)

    own_row = iota((8, 128), 0) < 4
    parts = []
    for pair in range(4):
        sums = {}
        for k in range(2):
            z = 2 * pair + k
            w = [weights2[i, z, 3:11, :] for i in range(6)]
            diag = diags2[z, 3:11, :]
            for f in range(3):
                own, six = six_of(second2, (f,), z + 1, 3, 8)
                e_two[f, z] = own
                change = (first2[f, z + 1, 3:11, :] - 0.8 * own) + weigh(w, six)
                value = jnp.where(own_row, change * diag, 0.0)
                sums[f] = value if k == 0 else sums[f] + value
            value = jnp.where(own_row, share2[z], 0.0)
            sums[3] = value if k == 0 else sums[3] + value
        parts.append(sums)

    pool = jnp.where((source < 32) & (source // 2 == target % 16), 0.125, 0.0)
    rows = jnp.concatenate([parts[pair][ch] for ch in range(4) for pair in range(4)], axis=0)
    spread = dot(rows, pool)
    at, to = iota((32, 128), 0), iota((32, 128), 1)
    keep = (at // 8 == to // 32) & ((at % 8) // 2 == (to // 16) % 2)
    result = jnp.concatenate(
        [
            jnp.sum(jnp.where(keep, spread[32 * ch : 32 * ch + 32], 0.0), axis=0, keepdims=True)
            for ch in range(4)
        ],
        axis=0,
    )
    for copy in range(CHIPS):
        sent[copy] = result


def swap_blocks(x):
    sub, group = iota((8, 128), 0), iota((8, 128), 1) // 16
    for bit in (4, 2, 1):
        up = roll(roll(x, -bit, 0), 16 * bit)
        down = up if bit == 4 else roll(roll(x, bit, 0), -16 * bit)
        sub_set, group_set = (sub & bit) != 0, (group & bit) != 0
        x = jnp.where(sub_set == group_set, x, jnp.where(sub_set, down, up))
    return x


def top_kernel(
    mine, other, base, out,
    natural, first, second, four, weights, diags, lefts, final, sems,
):
    gx, gy = lax.axis_index("gx"), lax.axis_index("gy")
    first_core = lax.rem(gy, 2) == 0
    lane, sub = iota((16, 128), 1), iota((16, 128), 0)
    cells = [(z, x, half) for z in range(4) for x in range(2) for half in range(2)]

    def lay(g):
        for ch in range(4):
            rows = pl.ds(32 * g + ch, 8, stride=4)
            pair = mine[rows, :], other[rows, :]
            natural[ch, 0, pl.ds(pl.multiple_of(8 * g, 8), 8), :] = swap_blocks(
                jnp.where(first_core, pair[0], pair[1])
            )
            natural[ch, 1, pl.ds(pl.multiple_of(8 * g, 8), 8), :] = swap_blocks(
                jnp.where(first_core, pair[1], pair[0])
            )

    loop(16, lay, 4)
    flat = natural.reshape(1024, 128)

    def plane(ch, z, x, half):
        return flat[pl.ds((ch * 2 + half) * 128 + z * 2 + x, 16, stride=8), :]

    def neighbours(at, z, x, half, outside):
        own, other = at(z, x, half), at(z, 1 - x, half)
        beside = at(z, x, 1 - half)
        shifted = roll(other, 1 if x == 0 else -1, 0)
        low, high = (shifted, other) if x == 0 else (other, shifted)
        left, right = roll(own, 1), roll(own, -1)
        left = jnp.where(lane % 16 == 0, roll(beside, 1 if half == 0 else -15), left)
        right = jnp.where(lane % 16 == 15, roll(beside, 15 if half == 0 else -1), right)
        down = at(z - 1, x, half) if z > 0 else outside
        up = at(z + 1, x, half) if z < 3 else outside
        return own, [low, high, left, right, down, up]

    def edge_masks(x, half):
        return [
            sub > 0 if x == 0 else None,
            sub < 15 if x == 1 else None,
            lane > 0 if half == 0 else None,
            lane < 127 if half == 1 else None,
            None,
            None,
        ]

    def key(z, x, half):
        return (z * 2 + x) * 2 + half

    shares = {c: plane(3, *c) for c in cells}
    rests = {c: resist(shares[c]) for c in cells}
    ones, zeros = jnp.ones((16, 128), F32), jnp.zeros((16, 128), F32)
    for z, x, half in cells:
        own, six = neighbours(lambda *c: rests[c], z, x, half, ones)
        masks = edge_masks(x, half)
        six = [s if m is None else jnp.where(m, s, 1.0) for s, m in zip(six, masks)]
        gain, w, diag = level_weights(own, six, 0.8)
        at = key(z, x, half)
        for i in range(6):
            weights[i, at] = w[i] if masks[i] is None else jnp.where(masks[i], w[i], 0.0)
        diags[at] = (1.25 * 0.25**3) * diag
        for f in range(3):
            first[f, at] = (64.0 * gain) * plane(f, z, x, half)

    for z, x, half in cells:
        at = key(z, x, half)
        w = [weights[i, at] for i in range(6)]
        for f in range(3):
            own, six = neighbours(lambda *c: first[f, key(*c)], z, x, half, zeros)
            second[half, f, z * 2 + x] = 1.2 * own + weigh(w, six)

    for z4 in range(2):
        for half in range(2):
            sums = [None] * 4
            for z in (2 * z4, 2 * z4 + 1):
                for x in range(2):
                    at = key(z, x, half)
                    w = [weights[i, at] for i in range(6)]
                    diag = diags[at]
                    for f in range(3):
                        own, six = neighbours(
                            lambda c, d, e: second[e, f, c * 2 + d], z, x, half, zeros
                        )
                        value = ((first[f, at] - 0.8 * own) + weigh(w, six)) * diag
                        sums[f] = value if sums[f] is None else sums[f] + value
                    share = shares[z, x, half]
                    sums[3] = share if sums[3] is None else sums[3] + share
            for ch in range(4):
                lefts[ch, z4, :, 128 * half : 128 * half + 128] = sums[ch]

    source = iota((256, 128), 0)
    column = ((source % 128) // 16) * 16 + (source // 128) * 8 + (source % 16) // 2
    pool = jnp.where(column == iota((256, 128), 1), 0.125, 0.0)
    level = dot(lefts[...].reshape(128, 256), pool)

    def coarsest(ch, z):
        return level[(ch * 2 + z) * 16 : (ch * 2 + z) * 16 + 16, :]

    masks = [sub > 0, sub < 15, lane > 0, lane < 127]
    resists = [resist(coarsest(3, z)) for z in range(2)]
    gains, ws, ds = [], [], []
    for z in range(2):
        own, other = resists[z], resists[1 - z]
        six = [roll(own, 1, 0), roll(own, -1, 0), roll(own, 1), roll(own, -1)]
        six = [jnp.where(m, s, 1.0) for m, s in zip(masks, six)] + [other, ones]
        gain, w, diag = level_weights(own, six, 0.8)
        gains.append(gain)
        ds.append(diag)
        ws.append([jnp.where(m, v, 0.0) for m, v in zip(masks, w)] + [w[4]])
    whole = jnp.sum(ds[0] + ds[1], keepdims=True)

    def around(values, z):
        own, other = values[z], values[1 - z]
        return weigh(ws[z], (roll(own, 1, 0), roll(own, -1, 0), roll(own, 1), roll(own, -1), other))

    begin = [[256.0 * gains[z] * coarsest(f, z) for z in range(2)] for f in range(3)]
    values = begin
    for step in range(5):
        values = [
            [(0.2 * values[f][z] + begin[f][z]) + around(values[f], z) for z in range(2)] for f in range(3)
        ]
    for f in range(3):
        change = [(begin[f][z] - 0.8 * values[f][z]) + around(values[f], z) for z in range(2)]
        total = jnp.sum(1.25 * (change[0] * ds[0] + change[1] * ds[1]), keepdims=True)
        for z in range(2):
            four[2 * f + z] = values[f][z] + total / whole

    copy = jnp.where(iota((128, 128), 0) == iota((128, 128), 1) // 2, 1.0, 0.0)
    rows = four.reshape(96, 128)[pl.ds(gx, 6, stride=16), :]
    rows = jnp.concatenate([jnp.broadcast_to(rows[i : i + 1], (4, 128)) for i in range(6)], axis=0)
    three = dot(turn(rows, -8 * gy), copy)
    flat = second.reshape(768, 128)
    halves = [flat[pl.ds(gx + 384 * half, 24, stride=16), :] for half in range(2)]
    three = three + turn(jnp.where(first_core, halves[0], halves[1]), -16 * lax.div(gy, 2))

    copy = jnp.where(iota((128, 128), 0) == iota((128, 128), 1) // 8, 1.0, 0.0)
    three = dot(three, copy)
    copies = []
    for f in range(3):
        for z in range(4):
            for x in range(2):
                at = f * 8 + z * 2 + x
                value = jnp.broadcast_to(three[at : at + 1], (8, 128))
                for k in range(8 * z, 8 * z + 8):
                    final[f, k, 8 * x : 8 * x + 8, :] = base[f, k, 8 * x : 8 * x + 8, :] + value
            if z % 2 == 1:
                part = (f, pl.ds(8 * z - 8, 16))
                copy = pltpu.make_async_copy(final.at[part], out.at[part], sems.at[len(copies)])
                copy.start()
                copies.append(copy)
    for copy in copies:
        copy.wait()


def local(labels, guess):
    swap_near = [(i, i ^ 1) for i in range(NY)]
    swap_far = [(i, j) for k in range(1, NY - 1, 2) for i, j in ((k, k + 1), (k + 1, k))]
    to_near, to_far, own = call(
        rows_kernel,
        [(12, 32, 128)] * 2 + [(4, 32, 16, 128)],
        [pltpu.VMEM((32, 16, 128), jnp.int32), pltpu.SemaphoreType.DMA((4,))],
        in_specs=[ANY, ANY],
    )(pltpu.with_memory_space_constraint(guess, pltpu.HBM), pltpu.with_memory_space_constraint(labels, pltpu.HBM))
    from_near = lax.ppermute(to_near, "gx", swap_near)
    from_far = lax.ppermute(to_far, "gx", swap_far)
    own_one, own_two, halves, to_right, to_left, edges = call(
        own_kernel,
        [(3, 34, 32, 128)] * 2 + [(4, 16, 16, 128)] + [(4, 4, 16, 128)] * 2 + [(4, 16, 16, 128)],
        [(4, 34, 32, 128), (6, 32, 32, 128), (32, 32, 128)],
        flops=20_000_000,
    )(own)
    to_near, to_far, rim_rows = call(pack_kernel, [(4, 4, 24, 128)] * 2 + [(4, 32, 8, 128)], [])(
        to_right, to_left, from_near, from_far
    )
    from_far = lax.ppermute(to_far, "gy", swap_far)
    from_near = lax.ppermute(to_near, "gy", swap_near)
    two, part, edges_rim = call(
        rows_edge_kernel,
        [(3, 34, 24, 128), (4, 16, 8, 128), (4, 16, 8, 128)],
        [(4, 34, 24, 128), (3, 34, 24, 128), (6, 32, 24, 128), (32, 24, 128)]
        + [(4, 16, 16, 128), (1024, 128)],
        flops=10_000_000,
    )(own, rim_rows, own_one, own_two, halves)
    rim, coarse, packed = call(
        rim_kernel,
        [(3, 16, 16, 128), (4, 16, 8, 128), (4, 2, 5, 8, 128)],
        [(3, 18, 32, 128), (18, 32, 128)]
        + [(3, 18, 32, 128)] * 2
        + [(6, 16, 32, 128), (16, 32, 128)]
        + [(4, 8, 16, 128), (512, 128)],
        flops=10_000_000,
    )(edges, edges_rim, part, from_near, from_far)
    from_near = lax.ppermute(packed, "gx", swap_near)
    from_far = lax.ppermute(packed, "gx", swap_far)
    sent, e_one, e_two = call(
        middle_kernel,
        [(CHIPS, 4, 128), (3, 16, 8, 128), (3, 8, 8, 128)],
        [(16, 24, 128), (18, 32, 128), (3, 16, 32, 128), (3, 18, 32, 128), (3, 18, 32, 128)]
        + [(6, 16, 32, 128), (16, 32, 128), (4, 8, 24, 128), (768, 128)]
        + [(10, 24, 128), (3, 10, 24, 128), (3, 10, 24, 128), (3, 8, 8, 128), (8, 8, 128)]
        + [(6, 8, 16, 128), (8, 16, 128)],
    )(coarse, from_near, from_far)
    groups = [[i for i in range(NX * NY) if i % 2 == core] for core in range(2)]
    mine = lax.all_to_all(
        sent, ("gx", "gy"), split_axis=0, concat_axis=0, axis_index_groups=groups, tiled=True
    )
    (base,) = call(base_kernel, [(3, 32, 16, 128)], [(192, 128), (3, 16, 16, 128)])(two, rim, e_one, e_two)
    other = lax.ppermute(mine, "gy", swap_near)
    (out,) = call(
        top_kernel,
        [(3, 32, 16, 128)],
        [(4, 2, 128, 128), (3, 16, 16, 128), (2, 3, 8, 16, 128), (6, 16, 128), (6, 16, 16, 128)]
        + [(16, 16, 128), (4, 2, 16, 256), (3, 32, 16, 128), pltpu.SemaphoreType.DMA((6,))],
        out_specs=[ANY],
    )(mine.reshape(512, 128), other.reshape(512, 128), base)
    return out


def solution(mesh):
    return jax.shard_map(
        local,
        mesh=mesh,
        in_specs=(P(None, "gx", "gy"), P(None, None, "gx", "gy")),
        out_specs=P(None, None, "gx", "gy"),
        check_vma=False,
    )
```

```python
import jax
import jax.numpy as jnp
from jax import lax
from jax.experimental import pallas as pl
from jax.experimental.pallas import tpu as pltpu
from jax.sharding import PartitionSpec as P


F32 = jnp.float32
NX, NY, CHIPS = 16, 16, 128
BETWEEN = 2.0 * 0.1 / 1.1
ANY = pl.BlockSpec(memory_space=pltpu.HBM)


def dot(a, b):
    return jnp.dot(a, b, precision=lax.Precision.HIGHEST, preferred_element_type=F32)


def iota(shape, dim):
    return lax.broadcasted_iota(jnp.int32, shape, dim)


def roll(x, shift, axis=1):
    shift = shift % x.shape[axis]
    return x if shift == 0 else pltpu.roll(x, shift, axis)


def turn(x, shift):
    return pltpu.roll(x, lax.rem(shift + 256, 128), 1)


def recip(x):
    guess = pl.reciprocal(x, approx=True)
    return guess * (2.0 - x * guess)


def call(kernel, outs, scratch, flops=1_000_000, **kw):
    return pl.pallas_call(
        kernel,
        out_shape=[jax.ShapeDtypeStruct(s, F32) for s in outs],
        scratch_shapes=[pltpu.VMEM(s, F32) if isinstance(s, tuple) else s for s in scratch],
        compiler_params=pltpu.CompilerParams(vmem_limit_bytes=32 * 1024 * 1024),
        cost_estimate=pl.CostEstimate(flops=flops, bytes_accessed=4_000_000, transcendentals=0),
        **kw,
    )


def loop(count, body, unroll=1):
    def step(i, carry):
        body(i)
        return carry

    lax.fori_loop(0, count, step, 0, unroll=unroll)


def weigh(weights, values):
    parts = [w * v for w, v in zip(weights, values)]
    while len(parts) > 1:
        parts = [sum(parts[i : i + 2][1:], parts[i]) for i in range(0, len(parts), 2)]
    return parts[0]


def rows_kernel(guess, labels, near, far, own, phase, sems):
    even = lax.rem(lax.axis_index("gx"), 2) == 0
    near_row, far_row = jnp.where(even, 13, 0), jnp.where(even, 0, 13)
    copies = [pltpu.make_async_copy(labels, phase, sems.at[3])]
    for f in range(3):
        copies.append(pltpu.make_async_copy(guess.at[f], own.at[f], sems.at[f]))
    for copy in copies:
        copy.start()
    copies[0].wait()
    own[3] = jnp.where(phase[...] == 1, 0.0, 1.0).astype(F32)
    flat = own.reshape(4 * 32 * 16, 128)
    for ch in (3, 0, 1, 2):
        if ch < 3:
            copies[ch + 1].wait()
        for row in range(3):
            near[3 * ch + row] = flat[pl.ds(512 * ch + near_row + row, 32, stride=16), :]
            far[3 * ch + row] = flat[pl.ds(512 * ch + far_row + row, 32, stride=16), :]


def pack_kernel(to_right, to_left, x_near, x_far, near, far, rim):
    first_core = lax.rem(lax.axis_index("gy"), 2) == 0
    even = lax.rem(lax.axis_index("gx"), 2) == 0
    near_row, far_row = jnp.where(even, 0, 5), jnp.where(even, 5, 0)
    flat = rim.reshape(4 * 32 * 8, 128)
    for ch in range(4):
        for row in range(3):
            flat[pl.ds(256 * ch + near_row + row, 32, stride=8), :] = x_near[3 * ch + row]
            flat[pl.ds(256 * ch + far_row + row, 32, stride=8), :] = x_far[3 * ch + row]

    def some(low):
        for ch in range(4):
            right, left = pack_planes(lambda z: rim[ch, z], low, (8, 128))
            for at, right, left in (
                (slice(0, 16), to_right[ch, low], to_left[ch, low]),
                (slice(16, 24), right, left),
            ):
                near[ch, low, at, :] = jnp.where(first_core, right, left)
                far[ch, low, at, :] = jnp.where(first_core, left, right)

    loop(4, some)


def pack_planes(plane, low, shape):
    group = iota(shape, 1) // 16
    right = left = jnp.zeros(shape, F32)
    for h in range(8):
        moved = roll(plane(4 * h + low), 16 * h + 16)
        right = jnp.where(group == h, moved, right)
        left = jnp.where(group == (h + 1) % 8, moved, left)
    return right, left


def edge_columns(plane, z, shape):
    lane = iota(shape, 1)
    value = jnp.zeros(shape, F32)
    for half in range(2):
        source = plane(z + 16 * half)
        base = 64 * half
        value = jnp.where((lane >= base) & (lane < base + 7), roll(source, base + 7), value)
        value = jnp.where((lane >= base + 57) & (lane < base + 64), roll(source, base + 57), value)
    return value


def six_of(ref, lead, z, first, count):
    own = ref[(*lead, z, pl.ds(first, count), slice(None))]
    return own, (
        ref[(*lead, z, pl.ds(first - 1, count), slice(None))],
        ref[(*lead, z, pl.ds(first + 1, count), slice(None))],
        roll(own, 1),
        roll(own, -1),
        ref[(*lead, z - 1, pl.ds(first, count), slice(None))],
        ref[(*lead, z + 1, pl.ds(first, count), slice(None))],
    )


def block_of(ref, lead, z, planes, first, count):
    rows = pl.ds(first, count)
    own = [ref[(*lead, z + k, rows, slice(None))] for k in range(-1, planes + 1)]
    result = []
    for k in range(planes):
        value = own[k + 1]
        six = (
            ref[(*lead, z + k, pl.ds(first - 1, count), slice(None))],
            ref[(*lead, z + k, pl.ds(first + 1, count), slice(None))],
            roll(value, 1),
            roll(value, -1),
            own[k],
            own[k + 2],
        )
        result.append((value, six))
    return result


def face(total):
    return jnp.where(total < 0.5, 1.0, jnp.where(total < 1.5, BETWEEN, 0.1))


def fine_weights(own, six, omega):
    faces = [face(own + other) for other in six]
    diag = (faces[0] + faces[1]) + (faces[2] + faces[3]) + (faces[4] + faces[5])
    gain = omega * recip(diag)
    return [gain * value for value in faces], 1.25 * diag


def fine_sweep(w, f, own, six):
    return (0.2 * own + (w[2 * f + 1] - w[2 * f])) + weigh(w, six)


def fine_left(w, f, own, six, diag):
    return (((w[2 * f + 1] - w[2 * f]) - 0.8 * own) + weigh(w, six)) * diag


def fine_sweeps(planes, windows, start, share, one, two, weights, diags, halves, omega, wrap, keep):
    first, count = windows[0]

    def first_sweep(step):
        z = 4 * step
        w = []
        for k, (own, six) in enumerate(block_of(share, (), z + 1, 4, first, count)):
            now, diag = fine_weights(own, six, omega)
            diags[z + k, pl.ds(first, count), :] = diag
            for i in range(6):
                weights[i, z + k, pl.ds(first, count), :] = now[i]
            w.append(now)
        for f in range(3):
            for k, (own, six) in enumerate(block_of(start, (f,), z + 1, 4, first, count)):
                one[f, z + k + 1, pl.ds(first, count), :] = fine_sweep(w[k], f, own, six)

    loop(planes // 4, first_sweep)
    wrap(one)
    second, count2 = windows[1]

    def second_sweep(step):
        z = 4 * step
        w = [[weights[i, z + k, pl.ds(second, count2), :] for i in range(6)] for k in range(4)]
        for f in range(3):
            for k, (own, six) in enumerate(block_of(one, (f,), z + 1, 4, second, count2)):
                two[f, z + k + 1, pl.ds(second, count2), :] = fine_sweep(w[k], f, own, six)

    loop(planes // 4, second_sweep)
    wrap(two)

    def residual(step):
        z = 4 * step
        w = [[weights[i, z + k, 8:24, :] for i in range(6)] for k in range(4)]
        diag = [diags[z + k, 8:24, :] for k in range(4)]
        for f in range(3):
            values = []
            for k, (own, six) in enumerate(block_of(two, (f,), z + 1, 4, 8, 16)):
                if keep is not None:
                    keep[f, z + k] = own
                values.append(fine_left(w[k], f, own, six, diag[k]))
            for pair in range(2):
                halves[f, 2 * step + pair] = values[2 * pair] + values[2 * pair + 1]
        for pair in range(2):
            at = z + 2 * pair + 1
            halves[3, 2 * step + pair] = share[at, 8:24, :] + share[at + 1, 8:24, :]

    loop(planes // 4, residual)


def own_kernel(own, one, two, halves, to_right, to_left, edges, held, weights, diags):
    zero = jnp.zeros((32, 128), F32)
    for z in (0, 33):
        for ch in range(4):
            held[ch, z] = zero
        for ref in (one, two):
            for f in range(3):
                ref[f, z] = zero

    def plane(z):
        for ch in range(4):
            held[ch, z + 1, 8:24, :] = own[ch, z]

    loop(32, plane, 4)
    fine_sweeps(
        32, [(8, 16)] * 2, held, held.at[3], one, two, weights, diags, halves, 0.8, lambda ref: None, None
    )

    def some(low):
        for ch in range(4):
            to_right[ch, low], to_left[ch, low] = pack_planes(lambda z: own[ch, z], low, (16, 128))

    loop(4, some)

    def edge(z):
        for ch in range(4):
            edges[ch, z] = edge_columns(lambda at: own[ch, at], z, (16, 128))

    loop(16, edge, 2)


def rows_edge_kernel(own, rim, own_one, own_two, own_halves, two, packed, edges, start, one, weights, diags, halves, pooled):
    gx = lax.axis_index("gx")
    zero = jnp.zeros((24, 128), F32)
    for z in (0, 33):
        for ch in range(4):
            start[ch, z] = zero
        for ref in (one, two):
            for f in range(3):
                ref[f, z] = zero

    def fill(z):
        for ch in range(4):
            start[ch, z + 1, 0:8, :] = own[ch, z, 8:16, :]
            start[ch, z + 1, 8:16, :] = rim[ch, z]
            start[ch, z + 1, 16:24, :] = own[ch, z, 0:8, :]
        for f in range(3):
            for ref, source in ((one, own_one), (two, own_two)):
                ref[f, z + 1, 0:8, :] = source[f, z + 1, 16:24, :]
                ref[f, z + 1, 16:24, :] = source[f, z + 1, 8:16, :]

    loop(32, fill, 4)
    upper = iota((8, 128), 0) < 4

    def both(ref, lead, step, shift=0):
        high = ref[(*lead, pl.ds(8 - step + shift, 8), slice(None))]
        low = ref[(*lead, pl.ds(8 + step + shift, 8), slice(None))]
        return jnp.where(upper, high, low)

    def block_both(ref, f, z, step):
        own = [both(ref, (f, z + k), step) for k in range(-1, 5)]
        result = []
        for k in range(4):
            value = own[k + 1]
            low, high = both(ref, (f, z + k), step, -1), both(ref, (f, z + k), step, 1)
            result.append((value, (low, high, roll(value, 1), roll(value, -1), own[k], own[k + 2])))
        return result

    def put(ref, f, z, step, value):
        ref[f, z, pl.ds(8 - step, 4), :] = value[0:4]
        ref[f, z, pl.ds(12 + step, 4), :] = value[4:8]

    row = iota((16, 128), 0) + 5
    low, high = jnp.where(gx > 0, 1, 0), jnp.where(gx < NX - 1, 1, 0)
    inside = jnp.where((row >= 8) & (row < 12), high, jnp.where((row >= 12) & (row < 16), low, 1))
    omega = 0.8 * inside.astype(F32)

    def weigh_all(step):
        z = 4 * step
        for k, (value, six) in enumerate(block_of(start, (3,), z + 1, 4, 5, 16)):
            w, diag = fine_weights(value, six, omega)
            diags[z + k, 5:21, :] = diag
            for i in range(6):
                weights[i, z + k, 5:21, :] = w[i]

    loop(8, weigh_all)

    for step, source, target in ((1, start, one), (2, one, two)):

        def sweep(block):
            z = 4 * block
            w = [[both(weights, (i, z + k), step) for i in range(6)] for k in range(4)]
            for f in range(3):
                for k, (value, six) in enumerate(block_both(source, f, z + 1, step)):
                    put(target, f, z + k + 1, step, fine_sweep(w[k], f, value, six))

        loop(8, sweep)

    sub = iota((8, 128), 0)

    def residual(block):
        z = 4 * block
        w = [[both(weights, (i, z + k), 3) for i in range(6)] for k in range(4)]
        diag = [both(diags, (z + k,), 3) for k in range(4)]
        for f in range(3):
            values = []
            for k, (value, six) in enumerate(block_both(two, f, z + 1, 3)):
                values.append(fine_left(w[k], f, value, six, diag[k]))
            for k in range(2):
                pair = 2 * block + k
                value = values[2 * k] + values[2 * k + 1]
                halves[f, pair, 0:8, :] = jnp.where(sub < 3, roll(value, 3, 0), own_halves[f, pair, 0:8, :])
                halves[f, pair, 8:16, :] = jnp.where(sub >= 5, roll(value, 5, 0), own_halves[f, pair, 8:16, :])
        for k in range(2):
            halves[3, 2 * block + k] = own_halves[3, 2 * block + k]

    loop(8, residual)
    source, target = iota((128, 128), 0), iota((128, 128), 1)
    value = None
    for half in range(2):
        pool = jnp.where(source // 2 + 64 * half == target, 0.125, 0.0)
        part = dot(halves[:, 8 * half : 8 * half + 8].reshape(512, 128), pool)
        value = part if value is None else value + part
    pooled[...] = value
    packed[...] = (pooled[pl.ds(0, 256, stride=2), :] + pooled[pl.ds(1, 256, stride=2), :]).reshape(4, 8, 8, 128)

    def edge(z):
        for ch in range(4):
            edges[ch, z] = edge_columns(lambda at: rim[ch, at], z, (8, 128))

    loop(16, edge, 2)


def rim_kernel(
    edges, edges_rim, near, far, field, packed,
    start, share, one, two, weights, diags, halves, pooled,
):
    gx, gy = lax.axis_index("gx"), lax.axis_index("gy")
    lane = iota((24, 128), 1)
    part = lane % 64
    is_after = (part >= 7) & (part < 22)
    is_before = (part >= 42) & (part < 57)
    first_core = lax.rem(gy, 2) == 0

    def unpack(low):
        for ch in range(4):
            target = start.at[ch] if ch < 3 else share
            from_right = jnp.where(first_core, near[ch, low], far[ch, low])
            from_left = jnp.where(first_core, far[ch, low], near[ch, low])
            for h in range(4):
                z = 4 * h + low
                after_y = roll(from_right, 7 - 16 * (h + 1))
                before_y = roll(from_left, 41 - 16 * h)
                own = jnp.concatenate([edges[ch, z], edges_rim[ch, z]], axis=0)
                value = jnp.where(is_after, after_y, jnp.where(is_before, before_y, own))
                target[z + 1, 8:24, :] = value[0:16]
                target[z + 1, 0:8, :] = value[16:24]
                target[z + 1, 24:32, :] = value[16:24]

    loop(4, unpack)

    half_of = iota((32, 128), 1)

    def wrap_one(ref):
        ref[0] = jnp.where(half_of >= 64, roll(ref[16], 64), 0.0)
        ref[17] = jnp.where(half_of < 64, roll(ref[1], 64), 0.0)

    def wrap(ref):
        for f in range(3):
            wrap_one(ref.at[f])

    wrap_one(share)
    wrap(start)
    row = iota((24, 128), 0) + 6
    low, high = jnp.where(gx > 0, 1, 0), jnp.where(gx < NX - 1, 1, 0)
    inside_x = jnp.where(row < 8, low, jnp.where(row >= 24, high, 1))
    inside_y = jnp.where(
        part < 32,
        jnp.where((part < 7) | (gy < NY - 1), 1, 0),
        jnp.where((part >= 57) | (gy > 0), 1, 0),
    )
    omega = 0.8 * (inside_x * inside_y).astype(F32)
    fine_sweeps(
        16, [(6, 24), (7, 24)], start, share, one, two, weights, diags, halves, omega, wrap, field
    )

    source, target = iota((128, 128), 0), iota((128, 128), 1)
    spot = source % 64
    column = jnp.where(spot < 32, 121 + spot, 71 + spot) // 2
    to = jnp.where(spot < 32, column - 62, column - 48)
    keep = ((spot < 32) & (to >= 0) & (to < 9)) | ((spot >= 32) & (to >= 9) & (to < 18))
    mixed = halves[...].reshape(4, 4, 2, 16, 128)
    value = None
    for odd in range(2):
        pool = jnp.where(keep & (to + 64 * odd + 32 * (source // 64) == target), 0.125, 0.0)
        part = dot(mixed[:, :, odd].reshape(256, 128), pool)
        value = part if value is None else value + part
    pooled[...] = value
    packed[...] = (pooled[pl.ds(0, 128, stride=2), :] + pooled[pl.ds(1, 128, stride=2), :]).reshape(4, 4, 8, 128)


def base_kernel(two, rim, e_one, e_two, base, wide, spread):
    copy = jnp.where(iota((128, 128), 0) == iota((128, 128), 1) // 2, 1.0, 0.0)
    value = dot(e_two[...].reshape(192, 128), copy)
    for block in range(24):
        rows = value[8 * block : 8 * block + 4, :]
        wide[pl.ds(8 * block, 4, stride=2), :] = rows
        wide[pl.ds(8 * block + 1, 4, stride=2), :] = rows
    value = e_one[...].reshape(24, 2, 8, 128) + wide[...].reshape(24, 1, 8, 128)
    value = dot(value.reshape(384, 128), copy)
    flat = spread.reshape(768, 128)
    for block in range(48):
        rows = value[8 * block : 8 * block + 8, :]
        flat[pl.ds(16 * block, 8, stride=2), :] = rows
        flat[pl.ds(16 * block + 1, 8, stride=2), :] = rows
    lane = iota((16, 128), 1)

    def pair(k):
        for f in range(3):
            for z in (2 * k, 2 * k + 1):
                value = rim[f, z]
                for half in range(2):
                    low = roll(value, -57 - 64 * half)
                    high = roll(value, 121 - 64 * half)
                    at = z + 16 * half
                    own = jnp.concatenate([two[f, at + 1, 16:24, :], two[f, at + 1, 0:8, :]], axis=0)
                    own = jnp.where(lane < 3, low, jnp.where(lane >= 125, high, own))
                    base[f, at] = own + spread[f, k + 8 * half]

    loop(8, pair, 1)


def resist(share):
    return recip(1.0 - 0.9 * share)


def level_weights(own, six, omega):
    faces = [2.0 * recip(own + other) for other in six]
    diag = (faces[0] + faces[1]) + (faces[2] + faces[3]) + (faces[4] + faces[5])
    gain = omega * recip(diag)
    return gain, [gain * w for w in faces], diag


def middle_kernel(
    main, main_near, main_far, rim, rim_near, rim_far, sent, e_one, e_two,
    share, rest, rhs, first, second, weights, diags, halves, pooled,
    rest2, first2, second2, rhs2, share2, weights2,
):
    gx, gy = lax.axis_index("gx"), lax.axis_index("gy")
    low_x, high_x = jnp.where(gx > 0, 1, 0), jnp.where(gx < NX - 1, 1, 0)
    low_y, high_y = jnp.where(gy > 0, 1, 0), jnp.where(gy < NY - 1, 1, 0)

    for f in range(3):
        for ref in (first, second):
            ref[f, 0] = jnp.zeros((32, 128), F32)
            ref[f, 17] = jnp.zeros((32, 128), F32)
    for z in (0, 17):
        rest[z] = jnp.ones((32, 128), F32)
    lane = iota((8, 128), 1)
    even = lax.rem(gx, 2) == 0
    near_row, far_row = jnp.where(even, 16, 0), jnp.where(even, 0, 16)
    starts = (pl.multiple_of(near_row, 8), pl.multiple_of(far_row, 8), 8)

    sources = zip(starts, ((main_near, rim_near), (main_far, rim_far), (main, rim)))
    sources = list(sources)

    def fill(q):
        for odd in range(2):
            for half in range(2):
                z = 2 * q + odd + 8 * half
                base = 64 * odd + 32 * half
                for at, (inner, outer) in sources:
                    for ch in range(4):
                        edge = outer[ch, q]
                        value = jnp.where(lane < 62, roll(inner[ch, 2 * q + odd], 64 * half), roll(edge, 62 - base))
                        value = jnp.where((lane >= 96) | (lane < 2), roll(edge, 112 - base), value)
                        if ch < 3:
                            rhs[ch, z, pl.ds(at, 8), :] = value
                        else:
                            share[z, pl.ds(at, 8), :] = value
                            rest[z + 1, pl.ds(at, 8), :] = resist(value)
                rest[z + 1, 24:32, :] = jnp.ones((8, 128), F32)

    loop(4, fill)

    row, lane = iota((24, 128), 0) + 1, iota((24, 128), 1)
    in_x = jnp.where(row < 8, low_x, jnp.where(row >= 16, high_x, 1))
    in_y = jnp.where(lane < 64, 1, jnp.where(lane < 96, high_y, low_y))
    omega = 0.8 * (in_x * in_y).astype(F32)

    def start(step):
        z = 4 * step
        for k, (own, six) in enumerate(block_of(rest, (), z + 1, 4, 1, 24)):
            gain, w, diag = level_weights(own, six, omega)
            for i in range(6):
                weights[i, z + k, 1:25, :] = w[i]
            diags[z + k, 1:25, :] = (1.25 * 0.25) * diag
            for f in range(3):
                first[f, z + k + 1, 1:25, :] = (4.0 * gain) * rhs[f, z + k, 1:25, :]

    loop(4, start)

    def sweep(step):
        z = 4 * step
        w = [[weights[i, z + k, 3:27, :] for i in range(6)] for k in range(4)]
        for f in range(3):
            for k, (own, six) in enumerate(block_of(first, (f,), z + 1, 4, 3, 24)):
                second[f, z + k + 1, 3:27, :] = 1.2 * own + weigh(w[k], six)

    loop(4, sweep)

    def left(step):
        z = 4 * step
        w = [[weights[i, z + k, 4:20, :] for i in range(6)] for k in range(4)]
        diag = [diags[z + k, 4:20, :] for k in range(4)]
        for f in range(3):
            values = []
            for k, (own, six) in enumerate(block_of(second, (f,), z + 1, 4, 4, 16)):
                change = (first[f, z + k + 1, 4:20, :] - 0.8 * own) + weigh(w[k], six)
                values.append(change * diag[k])
                e_one[f, z + k] = second[f, z + k + 1, 8:16, :]
            for k in range(2):
                halves[f, 2 * step + k, 0:16, :] = values[2 * k] + values[2 * k + 1]
                halves[f, 2 * step + k, 16:24, :] = jnp.zeros((8, 128), F32)
        for k in range(2):
            halves[3, 2 * step + k] = share[z + 2 * k] + share[z + 2 * k + 1]

    loop(4, left)

    source, target = iota((128, 128), 0), iota((128, 128), 1)
    pool = jnp.where(source // 2 + jnp.where(source >= 96, 64, 0) == target, 0.125, 0.0)
    pooled[...] = dot(halves[...].reshape(4 * 8 * 24, 128), pool)
    for z in (0, 9):
        rest2[z] = jnp.ones((24, 128), F32)
        for f in range(3):
            first2[f, z] = jnp.zeros((24, 128), F32)
            second2[f, z] = jnp.zeros((24, 128), F32)
    for z in range(8):
        for f in range(3):
            base = (f * 8 + z) * 24
            rhs2[f, z] = pooled[pl.ds(base, 8, stride=2), :] + pooled[pl.ds(base + 1, 8, stride=2), :]
        base = (3 * 8 + z) * 24
        value = pooled[pl.ds(base + 2, 8, stride=2), :] + pooled[pl.ds(base + 3, 8, stride=2), :]
        rest2[z + 1, 0:8, :] = resist(value)
        value = pooled[pl.ds(base + 8, 8, stride=2), :] + pooled[pl.ds(base + 9, 8, stride=2), :]
        rest2[z + 1, 3:11, :] = resist(value)
        share2[z] = value

    row, lane = iota((8, 128), 0) + 1, iota((8, 128), 1)
    in_x = jnp.where(row < 3, low_x, jnp.where(row >= 7, high_x, 1))
    in_y = jnp.where(lane < 32, 1, jnp.where(lane < 96, high_y, low_y))
    omega2 = 0.8 * (in_x * in_y).astype(F32)

    for z, (own, six) in enumerate(block_of(rest2, (), 1, 8, 1, 8)):
        gain, w, diag = level_weights(own, six, omega2)
        for i in range(6):
            weights2[i, z, 1:9, :] = w[i]
        weights2[6, z, 1:9, :] = (1.25 * 0.0625) * diag
        for f in range(3):
            first2[f, z + 1, 1:9, :] = (16.0 * gain) * rhs2[f, z]
    w = [[weights2[i, z, 2:10, :] for i in range(6)] for z in range(8)]
    for f in range(3):
        for z, (own, six) in enumerate(block_of(first2, (f,), 1, 8, 2, 8)):
            second2[f, z + 1, 2:10, :] = 1.2 * own + weigh(w[z], six)
    w = [[weights2[i, z, 3:11, :] for i in range(7)] for z in range(8)]
    own_row = iota((8, 128), 0) < 4
    parts = [{} for pair in range(4)]
    for f in range(3):
        for z, (own, six) in enumerate(block_of(second2, (f,), 1, 8, 3, 8)):
            e_two[f, z] = own
            change = (first2[f, z + 1, 3:11, :] - 0.8 * own) + weigh(w[z], six)
            value = jnp.where(own_row, change * w[z][6], 0.0)
            sums = parts[z // 2]
            sums[f] = value if z % 2 == 0 else sums[f] + value
    for z in range(8):
        value = jnp.where(own_row, share2[z], 0.0)
        sums = parts[z // 2]
        sums[3] = value if z % 2 == 0 else sums[3] + value

    pool = jnp.where((source < 32) & (source // 2 == target % 16), 0.125, 0.0)
    rows = jnp.concatenate([parts[pair][ch] for ch in range(4) for pair in range(4)], axis=0)
    spread = dot(rows, pool)
    at, to = iota((32, 128), 0), iota((32, 128), 1)
    keep = (at // 8 == to // 32) & ((at % 8) // 2 == (to // 16) % 2)
    result = jnp.concatenate(
        [
            jnp.sum(jnp.where(keep, spread[32 * ch : 32 * ch + 32], 0.0), axis=0, keepdims=True)
            for ch in range(4)
        ],
        axis=0,
    )
    for copy in range(CHIPS):
        sent[copy] = result


def swap_blocks(x):
    sub, group = iota((8, 128), 0), iota((8, 128), 1) // 16
    for bit in (4, 2, 1):
        up = roll(roll(x, -bit, 0), 16 * bit)
        down = up if bit == 4 else roll(roll(x, bit, 0), -16 * bit)
        sub_set, group_set = (sub & bit) != 0, (group & bit) != 0
        x = jnp.where(sub_set == group_set, x, jnp.where(sub_set, down, up))
    return x


def top_kernel(
    mine, other, base, out,
    natural, first, second, four, weights, diags, lefts, final, sems,
):
    gx, gy = lax.axis_index("gx"), lax.axis_index("gy")
    first_core = lax.rem(gy, 2) == 0
    lane, sub = iota((16, 128), 1), iota((16, 128), 0)
    cells = [(z, x, half) for z in range(4) for x in range(2) for half in range(2)]

    def lay(g):
        for ch in range(4):
            rows = pl.ds(32 * g + ch, 8, stride=4)
            pair = mine[rows, :], other[rows, :]
            natural[ch, 0, pl.ds(pl.multiple_of(8 * g, 8), 8), :] = swap_blocks(
                jnp.where(first_core, pair[0], pair[1])
            )
            natural[ch, 1, pl.ds(pl.multiple_of(8 * g, 8), 8), :] = swap_blocks(
                jnp.where(first_core, pair[1], pair[0])
            )

    loop(16, lay, 4)
    flat = natural.reshape(1024, 128)

    def plane(ch, z, x, half):
        return flat[pl.ds((ch * 2 + half) * 128 + z * 2 + x, 16, stride=8), :]

    def neighbours(at, z, x, half, outside):
        own, other = at(z, x, half), at(z, 1 - x, half)
        beside = at(z, x, 1 - half)
        shifted = roll(other, 1 if x == 0 else -1, 0)
        low, high = (shifted, other) if x == 0 else (other, shifted)
        left, right = roll(own, 1), roll(own, -1)
        left = jnp.where(lane % 16 == 0, roll(beside, 1 if half == 0 else -15), left)
        right = jnp.where(lane % 16 == 15, roll(beside, 15 if half == 0 else -1), right)
        down = at(z - 1, x, half) if z > 0 else outside
        up = at(z + 1, x, half) if z < 3 else outside
        return own, [low, high, left, right, down, up]

    def edge_masks(x, half):
        return [
            sub > 0 if x == 0 else None,
            sub < 15 if x == 1 else None,
            lane > 0 if half == 0 else None,
            lane < 127 if half == 1 else None,
            None,
            None,
        ]

    def key(z, x, half):
        return (z * 2 + x) * 2 + half

    shares = {c: plane(3, *c) for c in cells}
    rests = {c: resist(shares[c]) for c in cells}
    ones, zeros = jnp.ones((16, 128), F32), jnp.zeros((16, 128), F32)
    for z, x, half in cells:
        own, six = neighbours(lambda *c: rests[c], z, x, half, ones)
        masks = edge_masks(x, half)
        six = [s if m is None else jnp.where(m, s, 1.0) for s, m in zip(six, masks)]
        gain, w, diag = level_weights(own, six, 0.8)
        at = key(z, x, half)
        for i in range(6):
            weights[i, at] = w[i] if masks[i] is None else jnp.where(masks[i], w[i], 0.0)
        diags[at] = (1.25 * 0.25**3) * diag
        for f in range(3):
            first[f, at] = (64.0 * gain) * plane(f, z, x, half)

    for z, x, half in cells:
        at = key(z, x, half)
        w = [weights[i, at] for i in range(6)]
        for f in range(3):
            own, six = neighbours(lambda *c: first[f, key(*c)], z, x, half, zeros)
            second[half, f, z * 2 + x] = 1.2 * own + weigh(w, six)

    for z4 in range(2):
        for half in range(2):
            sums = [None] * 4
            for z in (2 * z4, 2 * z4 + 1):
                for x in range(2):
                    at = key(z, x, half)
                    w = [weights[i, at] for i in range(6)]
                    diag = diags[at]
                    for f in range(3):
                        own, six = neighbours(
                            lambda c, d, e: second[e, f, c * 2 + d], z, x, half, zeros
                        )
                        value = ((first[f, at] - 0.8 * own) + weigh(w, six)) * diag
                        sums[f] = value if sums[f] is None else sums[f] + value
                    share = shares[z, x, half]
                    sums[3] = share if sums[3] is None else sums[3] + share
            for ch in range(4):
                lefts[ch, z4, :, 128 * half : 128 * half + 128] = sums[ch]

    source = iota((256, 128), 0)
    column = ((source % 128) // 16) * 16 + (source // 128) * 8 + (source % 16) // 2
    pool = jnp.where(column == iota((256, 128), 1), 0.125, 0.0)
    level = dot(lefts[...].reshape(128, 256), pool)

    def coarsest(ch, z):
        return level[(ch * 2 + z) * 16 : (ch * 2 + z) * 16 + 16, :]

    masks = [sub > 0, sub < 15, lane > 0, lane < 127]
    resists = [resist(coarsest(3, z)) for z in range(2)]
    gains, ws, ds = [], [], []
    for z in range(2):
        own, other = resists[z], resists[1 - z]
        six = [roll(own, 1, 0), roll(own, -1, 0), roll(own, 1), roll(own, -1)]
        six = [jnp.where(m, s, 1.0) for m, s in zip(masks, six)] + [other, ones]
        gain, w, diag = level_weights(own, six, 0.8)
        gains.append(gain)
        ds.append(diag)
        ws.append([jnp.where(m, v, 0.0) for m, v in zip(masks, w)] + [w[4]])
    whole = jnp.sum(ds[0] + ds[1], keepdims=True)

    def around(values, z):
        own, other = values[z], values[1 - z]
        return weigh(ws[z], (roll(own, 1, 0), roll(own, -1, 0), roll(own, 1), roll(own, -1), other))

    begin = [[256.0 * gains[z] * coarsest(f, z) for z in range(2)] for f in range(3)]
    values = begin
    for step in range(5):
        values = [
            [(0.2 * values[f][z] + begin[f][z]) + around(values[f], z) for z in range(2)] for f in range(3)
        ]
    for f in range(3):
        change = [(begin[f][z] - 0.8 * values[f][z]) + around(values[f], z) for z in range(2)]
        total = jnp.sum(1.25 * (change[0] * ds[0] + change[1] * ds[1]), keepdims=True)
        for z in range(2):
            four[2 * f + z] = values[f][z] + total / whole

    copy = jnp.where(iota((128, 128), 0) == iota((128, 128), 1) // 2, 1.0, 0.0)
    rows = four.reshape(96, 128)[pl.ds(gx, 6, stride=16), :]
    rows = jnp.concatenate([jnp.broadcast_to(rows[i : i + 1], (4, 128)) for i in range(6)], axis=0)
    three = dot(turn(rows, -8 * gy), copy)
    flat = second.reshape(768, 128)
    halves = [flat[pl.ds(gx + 384 * half, 24, stride=16), :] for half in range(2)]
    three = three + turn(jnp.where(first_core, halves[0], halves[1]), -16 * lax.div(gy, 2))

    copy = jnp.where(iota((128, 128), 0) == iota((128, 128), 1) // 8, 1.0, 0.0)
    three = dot(three, copy)
    copies = []
    for f in range(3):
        for z in range(4):
            for x in range(2):
                at = f * 8 + z * 2 + x
                value = jnp.broadcast_to(three[at : at + 1], (8, 128))
                for k in range(8 * z, 8 * z + 8):
                    final[f, k, 8 * x : 8 * x + 8, :] = base[f, k, 8 * x : 8 * x + 8, :] + value
            if z % 2 == 1:
                part = (f, pl.ds(8 * z - 8, 16))
                copy = pltpu.make_async_copy(final.at[part], out.at[part], sems.at[len(copies)])
                copy.start()
                copies.append(copy)
    for copy in copies:
        copy.wait()


def local(labels, guess):
    swap_near = [(i, i ^ 1) for i in range(NY)]
    swap_far = [(i, j) for k in range(1, NY - 1, 2) for i, j in ((k, k + 1), (k + 1, k))]
    to_near, to_far, own = call(
        rows_kernel,
        [(12, 32, 128)] * 2 + [(4, 32, 16, 128)],
        [pltpu.VMEM((32, 16, 128), jnp.int32), pltpu.SemaphoreType.DMA((4,))],
        in_specs=[ANY, ANY],
    )(pltpu.with_memory_space_constraint(guess, pltpu.HBM), pltpu.with_memory_space_constraint(labels, pltpu.HBM))
    from_near = lax.ppermute(to_near, "gx", swap_near)
    from_far = lax.ppermute(to_far, "gx", swap_far)
    own_one, own_two, halves, to_right, to_left, edges = call(
        own_kernel,
        [(3, 34, 32, 128)] * 2 + [(4, 16, 16, 128)] + [(4, 4, 16, 128)] * 2 + [(4, 16, 16, 128)],
        [(4, 34, 32, 128), (6, 32, 32, 128), (32, 32, 128)],
        flops=20_000_000,
    )(own)
    to_near, to_far, rim_rows = call(pack_kernel, [(4, 4, 24, 128)] * 2 + [(4, 32, 8, 128)], [])(
        to_right, to_left, from_near, from_far
    )
    from_far = lax.ppermute(to_far, "gy", swap_far)
    from_near = lax.ppermute(to_near, "gy", swap_near)
    two, main, edges_rim = call(
        rows_edge_kernel,
        [(3, 34, 24, 128), (4, 8, 8, 128), (4, 16, 8, 128)],
        [(4, 34, 24, 128), (3, 34, 24, 128), (6, 32, 24, 128), (32, 24, 128)]
        + [(4, 16, 16, 128), (512, 128)],
        flops=10_000_000,
    )(own, rim_rows, own_one, own_two, halves)
    main_near = lax.ppermute(main, "gx", swap_near)
    main_far = lax.ppermute(main, "gx", swap_far)
    rim, rim_one = call(
        rim_kernel,
        [(3, 16, 16, 128), (4, 4, 8, 128)],
        [(3, 18, 32, 128), (18, 32, 128)]
        + [(3, 18, 32, 128)] * 2
        + [(6, 16, 32, 128), (16, 32, 128)]
        + [(4, 8, 16, 128), (256, 128)],
        flops=10_000_000,
    )(edges, edges_rim, from_near, from_far)
    rim_near = lax.ppermute(rim_one, "gx", swap_near)
    rim_far = lax.ppermute(rim_one, "gx", swap_far)
    sent, e_one, e_two = call(
        middle_kernel,
        [(CHIPS, 4, 128), (3, 16, 8, 128), (3, 8, 8, 128)],
        [(16, 24, 128), (18, 32, 128), (3, 16, 32, 128), (3, 18, 32, 128), (3, 18, 32, 128)]
        + [(6, 16, 32, 128), (16, 32, 128), (4, 8, 24, 128), (768, 128)]
        + [(10, 24, 128), (3, 10, 24, 128), (3, 10, 24, 128), (3, 8, 8, 128), (8, 8, 128)]
        + [(7, 8, 16, 128)],
    )(main, main_near, main_far, rim_one, rim_near, rim_far)
    groups = [[i for i in range(NX * NY) if i % 2 == core] for core in range(2)]
    mine = lax.all_to_all(
        sent, ("gx", "gy"), split_axis=0, concat_axis=0, axis_index_groups=groups, tiled=True
    )
    (base,) = call(base_kernel, [(3, 32, 16, 128)], [(192, 128), (3, 16, 16, 128)])(two, rim, e_one, e_two)
    other = lax.ppermute(mine, "gy", swap_near)
    (out,) = call(
        top_kernel,
        [(3, 32, 16, 128)],
        [(4, 2, 128, 128), (3, 16, 16, 128), (2, 3, 8, 16, 128), (6, 16, 128), (6, 16, 16, 128)]
        + [(16, 16, 128), (4, 2, 16, 256), (3, 32, 16, 128), pltpu.SemaphoreType.DMA((6,))],
        out_specs=[ANY],
    )(mine.reshape(512, 128), other.reshape(512, 128), base)
    return out


def solution(mesh):
    return jax.shard_map(
        local,
        mesh=mesh,
        in_specs=(P(None, "gx", "gy"), P(None, None, "gx", "gy")),
        out_specs=P(None, None, "gx", "gy"),
        check_vma=False,
    )
```

```python
import jax
import jax.numpy as jnp
from jax import lax
from jax.experimental import pallas as pl
from jax.experimental.pallas import tpu as pltpu
from jax.sharding import PartitionSpec as P


F32 = jnp.float32
NX, NY, CHIPS = 16, 16, 128
BETWEEN = 2.0 * 0.1 / 1.1
ANY = pl.BlockSpec(memory_space=pltpu.HBM)


def dot(a, b):
    return jnp.dot(a, b, precision=lax.Precision.HIGHEST, preferred_element_type=F32)


def iota(shape, dim):
    return lax.broadcasted_iota(jnp.int32, shape, dim)


def roll(x, shift, axis=1):
    shift = shift % x.shape[axis]
    return x if shift == 0 else pltpu.roll(x, shift, axis)


def turn(x, shift):
    return pltpu.roll(x, lax.rem(shift + 256, 128), 1)


def recip(x):
    guess = pl.reciprocal(x, approx=True)
    return guess * (2.0 - x * guess)


def inner(index):
    return (index > 0) & (index < 15)


def call(kernel, outs, scratch, flops=1_000_000, **kw):
    return pl.pallas_call(
        kernel,
        out_shape=[jax.ShapeDtypeStruct(s, F32) for s in outs],
        scratch_shapes=[pltpu.VMEM(s, F32) if isinstance(s, tuple) else s for s in scratch],
        compiler_params=pltpu.CompilerParams(vmem_limit_bytes=32 * 1024 * 1024),
        cost_estimate=pl.CostEstimate(flops=flops, bytes_accessed=4_000_000, transcendentals=0),
        **kw,
    )


def loop(count, body, unroll=1):
    def step(i, carry):
        body(i)
        return carry

    lax.fori_loop(0, count, step, 0, unroll=unroll)


def weigh(weights, values):
    parts = [w * v for w, v in zip(weights, values)]
    while len(parts) > 1:
        parts = [sum(parts[i : i + 2][1:], parts[i]) for i in range(0, len(parts), 2)]
    return parts[0]


def rows_kernel(guess, labels, near, far, own, phase, sems):
    even = lax.rem(lax.axis_index("gx"), 2) == 0
    near_row, far_row = jnp.where(even, 13, 0), jnp.where(even, 0, 13)
    copies = [pltpu.make_async_copy(labels, phase, sems.at[3])]
    for f in range(3):
        copies.append(pltpu.make_async_copy(guess.at[f], own.at[f], sems.at[f]))
    for copy in copies:
        copy.start()
    copies[0].wait()
    own[3] = jnp.where(phase[...] == 1, 0.0, 1.0).astype(F32)
    flat = own.reshape(4 * 32 * 16, 128)
    for ch in (3, 0, 1, 2):
        if ch < 3:
            copies[ch + 1].wait()
        for row in range(3):
            near[3 * ch + row] = flat[pl.ds(512 * ch + near_row + row, 32, stride=16), :]
            far[3 * ch + row] = flat[pl.ds(512 * ch + far_row + row, 32, stride=16), :]


def pack_kernel(to_right, to_left, x_near, x_far, near, far, rim):
    first_core = lax.rem(lax.axis_index("gy"), 2) == 0
    even = lax.rem(lax.axis_index("gx"), 2) == 0
    near_row, far_row = jnp.where(even, 0, 5), jnp.where(even, 5, 0)
    has_far = inner(lax.axis_index("gx"))
    flat = rim.reshape(4 * 32 * 8, 128)
    for ch in range(4):
        for row in range(3):
            flat[pl.ds(256 * ch + near_row + row, 32, stride=8), :] = x_near[3 * ch + row]
            flat[pl.ds(256 * ch + far_row + row, 32, stride=8), :] = jnp.where(has_far, x_far[3 * ch + row], 0.0)

    def some(low):
        for ch in range(4):
            right, left = pack_planes(lambda z: rim[ch, z], low, (8, 128))
            for at, right, left in (
                (slice(0, 16), to_right[ch, low], to_left[ch, low]),
                (slice(16, 24), right, left),
            ):
                near[ch, low, at, :] = jnp.where(first_core, right, left)
                far[ch, low, at, :] = jnp.where(first_core, left, right)

    loop(4, some)


def pack_planes(plane, low, shape):
    group = iota(shape, 1) // 16
    right = left = jnp.zeros(shape, F32)
    for h in range(8):
        moved = roll(plane(4 * h + low), 16 * h + 16)
        right = jnp.where(group == h, moved, right)
        left = jnp.where(group == (h + 1) % 8, moved, left)
    return right, left


def edge_columns(plane, z, shape):
    lane = iota(shape, 1)
    value = jnp.zeros(shape, F32)
    for half in range(2):
        source = plane(z + 16 * half)
        base = 64 * half
        value = jnp.where((lane >= base) & (lane < base + 7), roll(source, base + 7), value)
        value = jnp.where((lane >= base + 57) & (lane < base + 64), roll(source, base + 57), value)
    return value


def six_of(ref, lead, z, first, count):
    own = ref[(*lead, z, pl.ds(first, count), slice(None))]
    return own, (
        ref[(*lead, z, pl.ds(first - 1, count), slice(None))],
        ref[(*lead, z, pl.ds(first + 1, count), slice(None))],
        roll(own, 1),
        roll(own, -1),
        ref[(*lead, z - 1, pl.ds(first, count), slice(None))],
        ref[(*lead, z + 1, pl.ds(first, count), slice(None))],
    )


def block_of(ref, lead, z, planes, first, count):
    rows = pl.ds(first, count)
    own = [ref[(*lead, z + k, rows, slice(None))] for k in range(-1, planes + 1)]
    result = []
    for k in range(planes):
        value = own[k + 1]
        six = (
            ref[(*lead, z + k, pl.ds(first - 1, count), slice(None))],
            ref[(*lead, z + k, pl.ds(first + 1, count), slice(None))],
            roll(value, 1),
            roll(value, -1),
            own[k],
            own[k + 2],
        )
        result.append((value, six))
    return result


def face(total):
    return jnp.where(total < 0.5, 1.0, jnp.where(total < 1.5, BETWEEN, 0.1))


def fine_weights(own, six, omega):
    faces = [face(own + other) for other in six]
    diag = (faces[0] + faces[1]) + (faces[2] + faces[3]) + (faces[4] + faces[5])
    gain = omega * recip(diag)
    return [gain * value for value in faces], 1.25 * diag


def fine_sweep(w, f, own, six):
    return (0.2 * own + (w[2 * f + 1] - w[2 * f])) + weigh(w, six)


def fine_left(w, f, own, six, diag):
    return (((w[2 * f + 1] - w[2 * f]) - 0.8 * own) + weigh(w, six)) * diag


def fine_sweeps(planes, windows, start, share, one, two, weights, diags, halves, omega, wrap, keep):
    first, count = windows[0]

    def first_sweep(step):
        z = 4 * step
        w = []
        for k, (own, six) in enumerate(block_of(share, (), z + 1, 4, first, count)):
            now, diag = fine_weights(own, six, omega)
            diags[z + k, pl.ds(first, count), :] = diag
            for i in range(6):
                weights[i, z + k, pl.ds(first, count), :] = now[i]
            w.append(now)
        for f in range(3):
            for k, (own, six) in enumerate(block_of(start, (f,), z + 1, 4, first, count)):
                one[f, z + k + 1, pl.ds(first, count), :] = fine_sweep(w[k], f, own, six)

    loop(planes // 4, first_sweep)
    wrap(one)
    second, count2 = windows[1]

    def second_sweep(step):
        z = 4 * step
        w = [[weights[i, z + k, pl.ds(second, count2), :] for i in range(6)] for k in range(4)]
        for f in range(3):
            for k, (own, six) in enumerate(block_of(one, (f,), z + 1, 4, second, count2)):
                two[f, z + k + 1, pl.ds(second, count2), :] = fine_sweep(w[k], f, own, six)

    loop(planes // 4, second_sweep)
    wrap(two)

    def residual(step):
        z = 4 * step
        w = [[weights[i, z + k, 8:24, :] for i in range(6)] for k in range(4)]
        diag = [diags[z + k, 8:24, :] for k in range(4)]
        for f in range(3):
            values = []
            for k, (own, six) in enumerate(block_of(two, (f,), z + 1, 4, 8, 16)):
                if keep is not None:
                    keep[f, z + k] = own
                values.append(fine_left(w[k], f, own, six, diag[k]))
            for pair in range(2):
                halves[f, 2 * step + pair] = values[2 * pair] + values[2 * pair + 1]
        for pair in range(2):
            at = z + 2 * pair + 1
            halves[3, 2 * step + pair] = share[at, 8:24, :] + share[at + 1, 8:24, :]

    loop(planes // 4, residual)


def own_kernel(own, one, two, halves, to_right, to_left, edges, held, weights, diags):
    zero = jnp.zeros((32, 128), F32)
    for z in (0, 33):
        for ch in range(4):
            held[ch, z] = zero
        for ref in (one, two):
            for f in range(3):
                ref[f, z] = zero

    def plane(z):
        for ch in range(4):
            held[ch, z + 1, 8:24, :] = own[ch, z]

    loop(32, plane, 4)
    fine_sweeps(
        32, [(8, 16)] * 2, held, held.at[3], one, two, weights, diags, halves, 0.8, lambda ref: None, None
    )

    def some(low):
        for ch in range(4):
            to_right[ch, low], to_left[ch, low] = pack_planes(lambda z: own[ch, z], low, (16, 128))

    loop(4, some)

    def edge(z):
        for ch in range(4):
            edges[ch, z] = edge_columns(lambda at: own[ch, at], z, (16, 128))

    loop(16, edge, 2)


def rows_edge_kernel(own, rim, own_one, own_two, own_halves, two, packed, edges, start, one, weights, diags, halves, pooled):
    gx = lax.axis_index("gx")
    zero = jnp.zeros((24, 128), F32)
    for z in (0, 33):
        for ch in range(4):
            start[ch, z] = zero
        for ref in (one, two):
            for f in range(3):
                ref[f, z] = zero

    def fill(z):
        for ch in range(4):
            start[ch, z + 1, 0:8, :] = own[ch, z, 8:16, :]
            start[ch, z + 1, 8:16, :] = rim[ch, z]
            start[ch, z + 1, 16:24, :] = own[ch, z, 0:8, :]
        for f in range(3):
            for ref, source in ((one, own_one), (two, own_two)):
                ref[f, z + 1, 0:8, :] = source[f, z + 1, 16:24, :]
                ref[f, z + 1, 16:24, :] = source[f, z + 1, 8:16, :]

    loop(32, fill, 4)
    upper = iota((8, 128), 0) < 4

    def both(ref, lead, step, shift=0):
        high = ref[(*lead, pl.ds(8 - step + shift, 8), slice(None))]
        low = ref[(*lead, pl.ds(8 + step + shift, 8), slice(None))]
        return jnp.where(upper, high, low)

    def block_both(ref, f, z, step):
        own = [both(ref, (f, z + k), step) for k in range(-1, 5)]
        result = []
        for k in range(4):
            value = own[k + 1]
            low, high = both(ref, (f, z + k), step, -1), both(ref, (f, z + k), step, 1)
            result.append((value, (low, high, roll(value, 1), roll(value, -1), own[k], own[k + 2])))
        return result

    def put(ref, f, z, step, value):
        ref[f, z, pl.ds(8 - step, 4), :] = value[0:4]
        ref[f, z, pl.ds(12 + step, 4), :] = value[4:8]

    row = iota((16, 128), 0) + 5
    low, high = jnp.where(gx > 0, 1, 0), jnp.where(gx < NX - 1, 1, 0)
    inside = jnp.where((row >= 8) & (row < 12), high, jnp.where((row >= 12) & (row < 16), low, 1))
    omega = 0.8 * inside.astype(F32)

    def weigh_all(step):
        z = 4 * step
        for k, (value, six) in enumerate(block_of(start, (3,), z + 1, 4, 5, 16)):
            w, diag = fine_weights(value, six, omega)
            diags[z + k, 5:21, :] = diag
            for i in range(6):
                weights[i, z + k, 5:21, :] = w[i]

    loop(8, weigh_all)

    for step, source, target in ((1, start, one), (2, one, two)):

        def sweep(block):
            z = 4 * block
            w = [[both(weights, (i, z + k), step) for i in range(6)] for k in range(4)]
            for f in range(3):
                for k, (value, six) in enumerate(block_both(source, f, z + 1, step)):
                    put(target, f, z + k + 1, step, fine_sweep(w[k], f, value, six))

        loop(8, sweep)

    sub = iota((8, 128), 0)

    def residual(block):
        z = 4 * block
        w = [[both(weights, (i, z + k), 3) for i in range(6)] for k in range(4)]
        diag = [both(diags, (z + k,), 3) for k in range(4)]
        for f in range(3):
            values = []
            for k, (value, six) in enumerate(block_both(two, f, z + 1, 3)):
                values.append(fine_left(w[k], f, value, six, diag[k]))
            for k in range(2):
                pair = 2 * block + k
                value = values[2 * k] + values[2 * k + 1]
                halves[f, pair, 0:8, :] = jnp.where(sub < 3, roll(value, 3, 0), own_halves[f, pair, 0:8, :])
                halves[f, pair, 8:16, :] = jnp.where(sub >= 5, roll(value, 5, 0), own_halves[f, pair, 8:16, :])
        for k in range(2):
            halves[3, 2 * block + k] = own_halves[3, 2 * block + k]

    loop(8, residual)
    source, target = iota((128, 128), 0), iota((128, 128), 1)
    value = None
    for half in range(2):
        pool = jnp.where(source // 2 + 64 * half == target, 0.125, 0.0)
        part = dot(halves[:, 8 * half : 8 * half + 8].reshape(512, 128), pool)
        value = part if value is None else value + part
    pooled[...] = value
    packed[...] = (pooled[pl.ds(0, 256, stride=2), :] + pooled[pl.ds(1, 256, stride=2), :]).reshape(4, 8, 8, 128)

    def edge(z):
        for ch in range(4):
            edges[ch, z] = edge_columns(lambda at: rim[ch, at], z, (8, 128))

    loop(16, edge, 2)


def rim_kernel(
    edges, edges_rim, near, far, field, packed,
    start, share, one, two, weights, diags, halves, pooled,
):
    gx, gy = lax.axis_index("gx"), lax.axis_index("gy")
    lane = iota((24, 128), 1)
    part = lane % 64
    is_after = (part >= 7) & (part < 22)
    is_before = (part >= 42) & (part < 57)
    first_core = lax.rem(gy, 2) == 0

    def unpack(low):
        for ch in range(4):
            target = start.at[ch] if ch < 3 else share
            from_near, from_far = near[ch, low], jnp.where(inner(gy), far[ch, low], 0.0)
            from_right = jnp.where(first_core, from_near, from_far)
            from_left = jnp.where(first_core, from_far, from_near)
            for h in range(4):
                z = 4 * h + low
                after_y = roll(from_right, 7 - 16 * (h + 1))
                before_y = roll(from_left, 41 - 16 * h)
                own = jnp.concatenate([edges[ch, z], edges_rim[ch, z]], axis=0)
                value = jnp.where(is_after, after_y, jnp.where(is_before, before_y, own))
                target[z + 1, 8:24, :] = value[0:16]
                target[z + 1, 0:8, :] = value[16:24]
                target[z + 1, 24:32, :] = value[16:24]

    loop(4, unpack)

    half_of = iota((32, 128), 1)

    def wrap_one(ref):
        ref[0] = jnp.where(half_of >= 64, roll(ref[16], 64), 0.0)
        ref[17] = jnp.where(half_of < 64, roll(ref[1], 64), 0.0)

    def wrap(ref):
        for f in range(3):
            wrap_one(ref.at[f])

    wrap_one(share)
    wrap(start)
    row = iota((24, 128), 0) + 6
    low, high = jnp.where(gx > 0, 1, 0), jnp.where(gx < NX - 1, 1, 0)
    inside_x = jnp.where(row < 8, low, jnp.where(row >= 24, high, 1))
    inside_y = jnp.where(
        part < 32,
        jnp.where((part < 7) | (gy < NY - 1), 1, 0),
        jnp.where((part >= 57) | (gy > 0), 1, 0),
    )
    omega = 0.8 * (inside_x * inside_y).astype(F32)
    fine_sweeps(
        16, [(6, 24), (7, 24)], start, share, one, two, weights, diags, halves, omega, wrap, field
    )

    source, target = iota((128, 128), 0), iota((128, 128), 1)
    spot = source % 64
    column = jnp.where(spot < 32, 121 + spot, 71 + spot) // 2
    to = jnp.where(spot < 32, column - 62, column - 48)
    keep = ((spot < 32) & (to >= 0) & (to < 9)) | ((spot >= 32) & (to >= 9) & (to < 18))
    mixed = halves[...].reshape(4, 4, 2, 16, 128)
    value = None
    for odd in range(2):
        pool = jnp.where(keep & (to + 64 * odd + 32 * (source // 64) == target), 0.125, 0.0)
        part = dot(mixed[:, :, odd].reshape(256, 128), pool)
        value = part if value is None else value + part
    pooled[...] = value
    packed[...] = (pooled[pl.ds(0, 128, stride=2), :] + pooled[pl.ds(1, 128, stride=2), :]).reshape(4, 4, 8, 128)


def base_kernel(two, rim, e_one, e_two, base, wide, spread):
    copy = jnp.where(iota((128, 128), 0) == iota((128, 128), 1) // 2, 1.0, 0.0)
    value = dot(e_two[...].reshape(192, 128), copy)
    for block in range(24):
        rows = value[8 * block : 8 * block + 4, :]
        wide[pl.ds(8 * block, 4, stride=2), :] = rows
        wide[pl.ds(8 * block + 1, 4, stride=2), :] = rows
    value = e_one[...].reshape(24, 2, 8, 128) + wide[...].reshape(24, 1, 8, 128)
    value = dot(value.reshape(384, 128), copy)
    flat = spread.reshape(768, 128)
    for block in range(48):
        rows = value[8 * block : 8 * block + 8, :]
        flat[pl.ds(16 * block, 8, stride=2), :] = rows
        flat[pl.ds(16 * block + 1, 8, stride=2), :] = rows
    lane = iota((16, 128), 1)

    def pair(k):
        for f in range(3):
            for z in (2 * k, 2 * k + 1):
                value = rim[f, z]
                for half in range(2):
                    low = roll(value, -57 - 64 * half)
                    high = roll(value, 121 - 64 * half)
                    at = z + 16 * half
                    own = jnp.concatenate([two[f, at + 1, 16:24, :], two[f, at + 1, 0:8, :]], axis=0)
                    own = jnp.where(lane < 3, low, jnp.where(lane >= 125, high, own))
                    base[f, at] = own + spread[f, k + 8 * half]

    loop(8, pair, 1)


def resist(share):
    return recip(1.0 - 0.9 * share)


def level_weights(own, six, omega):
    faces = [2.0 * recip(own + other) for other in six]
    diag = (faces[0] + faces[1]) + (faces[2] + faces[3]) + (faces[4] + faces[5])
    gain = omega * recip(diag)
    return gain, [gain * w for w in faces], diag


def middle_kernel(
    main, main_near, main_far, rim, rim_near, rim_far, sent, e_one, e_two,
    share, rest, rhs, first, second, weights, diags, halves, pooled,
    rest2, first2, second2, rhs2, share2, weights2,
):
    gx, gy = lax.axis_index("gx"), lax.axis_index("gy")
    low_x, high_x = jnp.where(gx > 0, 1, 0), jnp.where(gx < NX - 1, 1, 0)
    low_y, high_y = jnp.where(gy > 0, 1, 0), jnp.where(gy < NY - 1, 1, 0)

    for f in range(3):
        for ref in (first, second):
            ref[f, 0] = jnp.zeros((32, 128), F32)
            ref[f, 17] = jnp.zeros((32, 128), F32)
    for z in (0, 17):
        rest[z] = jnp.ones((32, 128), F32)
    lane = iota((8, 128), 1)
    even = lax.rem(gx, 2) == 0
    near_row, far_row = jnp.where(even, 16, 0), jnp.where(even, 0, 16)
    starts = (pl.multiple_of(near_row, 8), pl.multiple_of(far_row, 8), 8)

    sources = zip(starts, ((main_near, rim_near), (main_far, rim_far), (main, rim)))
    sources = list(sources)
    has_far = inner(gx)

    def fill(q):
        for odd in range(2):
            for half in range(2):
                z = 2 * q + odd + 8 * half
                base = 64 * odd + 32 * half
                for at, (middle, outer) in sources:
                    for ch in range(4):
                        edge, body = outer[ch, q], middle[ch, 2 * q + odd]
                        if outer is rim_far:
                            edge, body = jnp.where(has_far, edge, 0.0), jnp.where(has_far, body, 0.0)
                        value = jnp.where(lane < 62, roll(body, 64 * half), roll(edge, 62 - base))
                        value = jnp.where((lane >= 96) | (lane < 2), roll(edge, 112 - base), value)
                        if ch < 3:
                            rhs[ch, z, pl.ds(at, 8), :] = value
                        else:
                            share[z, pl.ds(at, 8), :] = value
                            rest[z + 1, pl.ds(at, 8), :] = resist(value)
                rest[z + 1, 24:32, :] = jnp.ones((8, 128), F32)

    loop(4, fill)

    row, lane = iota((24, 128), 0) + 1, iota((24, 128), 1)
    in_x = jnp.where(row < 8, low_x, jnp.where(row >= 16, high_x, 1))
    in_y = jnp.where(lane < 64, 1, jnp.where(lane < 96, high_y, low_y))
    omega = 0.8 * (in_x * in_y).astype(F32)

    def start(step):
        z = 4 * step
        for k, (own, six) in enumerate(block_of(rest, (), z + 1, 4, 1, 24)):
            gain, w, diag = level_weights(own, six, omega)
            for i in range(6):
                weights[i, z + k, 1:25, :] = w[i]
            diags[z + k, 1:25, :] = (1.25 * 0.25) * diag
            for f in range(3):
                first[f, z + k + 1, 1:25, :] = (4.0 * gain) * rhs[f, z + k, 1:25, :]

    loop(4, start)

    def sweep(step):
        z = 4 * step
        w = [[weights[i, z + k, 3:27, :] for i in range(6)] for k in range(4)]
        for f in range(3):
            for k, (own, six) in enumerate(block_of(first, (f,), z + 1, 4, 3, 24)):
                second[f, z + k + 1, 3:27, :] = 1.2 * own + weigh(w[k], six)

    loop(4, sweep)

    def left(step):
        z = 4 * step
        w = [[weights[i, z + k, 4:20, :] for i in range(6)] for k in range(4)]
        diag = [diags[z + k, 4:20, :] for k in range(4)]
        for f in range(3):
            values = []
            for k, (own, six) in enumerate(block_of(second, (f,), z + 1, 4, 4, 16)):
                change = (first[f, z + k + 1, 4:20, :] - 0.8 * own) + weigh(w[k], six)
                values.append(change * diag[k])
                e_one[f, z + k] = second[f, z + k + 1, 8:16, :]
            for k in range(2):
                halves[f, 2 * step + k, 0:16, :] = values[2 * k] + values[2 * k + 1]
                halves[f, 2 * step + k, 16:24, :] = jnp.zeros((8, 128), F32)
        for k in range(2):
            halves[3, 2 * step + k] = share[z + 2 * k] + share[z + 2 * k + 1]

    loop(4, left)

    source, target = iota((128, 128), 0), iota((128, 128), 1)
    pool = jnp.where(source // 2 + jnp.where(source >= 96, 64, 0) == target, 0.125, 0.0)
    pooled[...] = dot(halves[...].reshape(4 * 8 * 24, 128), pool)
    for z in (0, 9):
        rest2[z] = jnp.ones((24, 128), F32)
        for f in range(3):
            first2[f, z] = jnp.zeros((24, 128), F32)
            second2[f, z] = jnp.zeros((24, 128), F32)
    for z in range(8):
        for f in range(3):
            base = (f * 8 + z) * 24
            rhs2[f, z] = pooled[pl.ds(base, 8, stride=2), :] + pooled[pl.ds(base + 1, 8, stride=2), :]
        base = (3 * 8 + z) * 24
        value = pooled[pl.ds(base + 2, 8, stride=2), :] + pooled[pl.ds(base + 3, 8, stride=2), :]
        rest2[z + 1, 0:8, :] = resist(value)
        value = pooled[pl.ds(base + 8, 8, stride=2), :] + pooled[pl.ds(base + 9, 8, stride=2), :]
        rest2[z + 1, 3:11, :] = resist(value)
        share2[z] = value

    row, lane = iota((8, 128), 0) + 1, iota((8, 128), 1)
    in_x = jnp.where(row < 3, low_x, jnp.where(row >= 7, high_x, 1))
    in_y = jnp.where(lane < 32, 1, jnp.where(lane < 96, high_y, low_y))
    omega2 = 0.8 * (in_x * in_y).astype(F32)

    for z, (own, six) in enumerate(block_of(rest2, (), 1, 8, 1, 8)):
        gain, w, diag = level_weights(own, six, omega2)
        for i in range(6):
            weights2[i, z, 1:9, :] = w[i]
        weights2[6, z, 1:9, :] = (1.25 * 0.0625) * diag
        for f in range(3):
            first2[f, z + 1, 1:9, :] = (16.0 * gain) * rhs2[f, z]
    w = [[weights2[i, z, 2:10, :] for i in range(6)] for z in range(8)]
    for f in range(3):
        for z, (own, six) in enumerate(block_of(first2, (f,), 1, 8, 2, 8)):
            second2[f, z + 1, 2:10, :] = 1.2 * own + weigh(w[z], six)
    w = [[weights2[i, z, 3:11, :] for i in range(7)] for z in range(8)]
    own_row = iota((8, 128), 0) < 4
    parts = [{} for pair in range(4)]
    for f in range(3):
        for z, (own, six) in enumerate(block_of(second2, (f,), 1, 8, 3, 8)):
            e_two[f, z] = own
            change = (first2[f, z + 1, 3:11, :] - 0.8 * own) + weigh(w[z], six)
            value = jnp.where(own_row, change * w[z][6], 0.0)
            sums = parts[z // 2]
            sums[f] = value if z % 2 == 0 else sums[f] + value
    for z in range(8):
        value = jnp.where(own_row, share2[z], 0.0)
        sums = parts[z // 2]
        sums[3] = value if z % 2 == 0 else sums[3] + value

    pool = jnp.where((source < 32) & (source // 2 == target % 16), 0.125, 0.0)
    rows = jnp.concatenate([parts[pair][ch] for ch in range(4) for pair in range(4)], axis=0)
    spread = dot(rows, pool)
    at, to = iota((32, 128), 0), iota((32, 128), 1)
    keep = (at // 8 == to // 32) & ((at % 8) // 2 == (to // 16) % 2)
    result = jnp.concatenate(
        [
            jnp.sum(jnp.where(keep, spread[32 * ch : 32 * ch + 32], 0.0), axis=0, keepdims=True)
            for ch in range(4)
        ],
        axis=0,
    )
    for copy in range(CHIPS):
        sent[copy] = result


def swap_blocks(x):
    sub, group = iota((8, 128), 0), iota((8, 128), 1) // 16
    for bit in (4, 2, 1):
        up = roll(roll(x, -bit, 0), 16 * bit)
        down = up if bit == 4 else roll(roll(x, bit, 0), -16 * bit)
        sub_set, group_set = (sub & bit) != 0, (group & bit) != 0
        x = jnp.where(sub_set == group_set, x, jnp.where(sub_set, down, up))
    return x


def top_kernel(
    mine, other, base, out,
    natural, first, second, four, weights, diags, lefts, final, sems,
):
    gx, gy = lax.axis_index("gx"), lax.axis_index("gy")
    first_core = lax.rem(gy, 2) == 0
    lane, sub = iota((16, 128), 1), iota((16, 128), 0)
    cells = [(z, x, half) for z in range(4) for x in range(2) for half in range(2)]

    def lay(g):
        for ch in range(4):
            rows = pl.ds(32 * g + ch, 8, stride=4)
            pair = mine[rows, :], other[rows, :]
            natural[ch, 0, pl.ds(pl.multiple_of(8 * g, 8), 8), :] = swap_blocks(
                jnp.where(first_core, pair[0], pair[1])
            )
            natural[ch, 1, pl.ds(pl.multiple_of(8 * g, 8), 8), :] = swap_blocks(
                jnp.where(first_core, pair[1], pair[0])
            )

    loop(16, lay, 4)
    flat = natural.reshape(1024, 128)

    def plane(ch, z, x, half):
        return flat[pl.ds((ch * 2 + half) * 128 + z * 2 + x, 16, stride=8), :]

    def neighbours(at, z, x, half, outside):
        own, other = at(z, x, half), at(z, 1 - x, half)
        beside = at(z, x, 1 - half)
        shifted = roll(other, 1 if x == 0 else -1, 0)
        low, high = (shifted, other) if x == 0 else (other, shifted)
        left, right = roll(own, 1), roll(own, -1)
        left = jnp.where(lane % 16 == 0, roll(beside, 1 if half == 0 else -15), left)
        right = jnp.where(lane % 16 == 15, roll(beside, 15 if half == 0 else -1), right)
        down = at(z - 1, x, half) if z > 0 else outside
        up = at(z + 1, x, half) if z < 3 else outside
        return own, [low, high, left, right, down, up]

    def edge_masks(x, half):
        return [
            sub > 0 if x == 0 else None,
            sub < 15 if x == 1 else None,
            lane > 0 if half == 0 else None,
            lane < 127 if half == 1 else None,
            None,
            None,
        ]

    def key(z, x, half):
        return (z * 2 + x) * 2 + half

    shares = {c: plane(3, *c) for c in cells}
    rests = {c: resist(shares[c]) for c in cells}
    ones, zeros = jnp.ones((16, 128), F32), jnp.zeros((16, 128), F32)
    for z, x, half in cells:
        own, six = neighbours(lambda *c: rests[c], z, x, half, ones)
        masks = edge_masks(x, half)
        six = [s if m is None else jnp.where(m, s, 1.0) for s, m in zip(six, masks)]
        gain, w, diag = level_weights(own, six, 0.8)
        at = key(z, x, half)
        for i in range(6):
            weights[i, at] = w[i] if masks[i] is None else jnp.where(masks[i], w[i], 0.0)
        diags[at] = (1.25 * 0.25**3) * diag
        for f in range(3):
            first[f, at] = (64.0 * gain) * plane(f, z, x, half)

    for z, x, half in cells:
        at = key(z, x, half)
        w = [weights[i, at] for i in range(6)]
        for f in range(3):
            own, six = neighbours(lambda *c: first[f, key(*c)], z, x, half, zeros)
            second[half, f, z * 2 + x] = 1.2 * own + weigh(w, six)

    for z4 in range(2):
        for half in range(2):
            sums = [None] * 4
            for z in (2 * z4, 2 * z4 + 1):
                for x in range(2):
                    at = key(z, x, half)
                    w = [weights[i, at] for i in range(6)]
                    diag = diags[at]
                    for f in range(3):
                        own, six = neighbours(
                            lambda c, d, e: second[e, f, c * 2 + d], z, x, half, zeros
                        )
                        value = ((first[f, at] - 0.8 * own) + weigh(w, six)) * diag
                        sums[f] = value if sums[f] is None else sums[f] + value
                    share = shares[z, x, half]
                    sums[3] = share if sums[3] is None else sums[3] + share
            for ch in range(4):
                lefts[ch, z4, :, 128 * half : 128 * half + 128] = sums[ch]

    source = iota((256, 128), 0)
    column = ((source % 128) // 16) * 16 + (source // 128) * 8 + (source % 16) // 2
    pool = jnp.where(column == iota((256, 128), 1), 0.125, 0.0)
    level = dot(lefts[...].reshape(128, 256), pool)

    def coarsest(ch, z):
        return level[(ch * 2 + z) * 16 : (ch * 2 + z) * 16 + 16, :]

    masks = [sub > 0, sub < 15, lane > 0, lane < 127]
    resists = [resist(coarsest(3, z)) for z in range(2)]
    gains, ws, ds = [], [], []
    for z in range(2):
        own, other = resists[z], resists[1 - z]
        six = [roll(own, 1, 0), roll(own, -1, 0), roll(own, 1), roll(own, -1)]
        six = [jnp.where(m, s, 1.0) for m, s in zip(masks, six)] + [other, ones]
        gain, w, diag = level_weights(own, six, 0.8)
        gains.append(gain)
        ds.append(diag)
        ws.append([jnp.where(m, v, 0.0) for m, v in zip(masks, w)] + [w[4]])
    whole = jnp.sum(ds[0] + ds[1], keepdims=True)

    def around(values, z):
        own, other = values[z], values[1 - z]
        return weigh(ws[z], (roll(own, 1, 0), roll(own, -1, 0), roll(own, 1), roll(own, -1), other))

    begin = [[256.0 * gains[z] * coarsest(f, z) for z in range(2)] for f in range(3)]
    values = begin
    for step in range(5):
        values = [
            [(0.2 * values[f][z] + begin[f][z]) + around(values[f], z) for z in range(2)] for f in range(3)
        ]
    for f in range(3):
        change = [(begin[f][z] - 0.8 * values[f][z]) + around(values[f], z) for z in range(2)]
        total = jnp.sum(1.25 * (change[0] * ds[0] + change[1] * ds[1]), keepdims=True)
        for z in range(2):
            four[2 * f + z] = values[f][z] + total / whole

    copy = jnp.where(iota((128, 128), 0) == iota((128, 128), 1) // 2, 1.0, 0.0)
    rows = four.reshape(96, 128)[pl.ds(gx, 6, stride=16), :]
    rows = jnp.concatenate([jnp.broadcast_to(rows[i : i + 1], (4, 128)) for i in range(6)], axis=0)
    three = dot(turn(rows, -8 * gy), copy)
    flat = second.reshape(768, 128)
    halves = [flat[pl.ds(gx + 384 * half, 24, stride=16), :] for half in range(2)]
    three = three + turn(jnp.where(first_core, halves[0], halves[1]), -16 * lax.div(gy, 2))

    copy = jnp.where(iota((128, 128), 0) == iota((128, 128), 1) // 8, 1.0, 0.0)
    three = dot(three, copy)
    copies = []
    for f in range(3):
        for z in range(4):
            for x in range(2):
                at = f * 8 + z * 2 + x
                value = jnp.broadcast_to(three[at : at + 1], (8, 128))
                for k in range(8 * z, 8 * z + 8):
                    final[f, k, 8 * x : 8 * x + 8, :] = base[f, k, 8 * x : 8 * x + 8, :] + value
            if z % 2 == 1:
                part = (f, pl.ds(8 * z - 8, 16))
                copy = pltpu.make_async_copy(final.at[part], out.at[part], sems.at[len(copies)])
                copy.start()
                copies.append(copy)
    for copy in copies:
        copy.wait()


def local(labels, guess):
    swap_near = [(i, i ^ 1) for i in range(NY)]
    swap_far = [(i, (i + 1 if i % 2 else i - 1) % NY) for i in range(NY)]
    to_near, to_far, own = call(
        rows_kernel,
        [(12, 32, 128)] * 2 + [(4, 32, 16, 128)],
        [pltpu.VMEM((32, 16, 128), jnp.int32), pltpu.SemaphoreType.DMA((4,))],
        in_specs=[ANY, ANY],
    )(pltpu.with_memory_space_constraint(guess, pltpu.HBM), pltpu.with_memory_space_constraint(labels, pltpu.HBM))
    from_near = lax.ppermute(to_near, "gx", swap_near)
    from_far = lax.ppermute(to_far, "gx", swap_far)
    own_one, own_two, halves, to_right, to_left, edges = call(
        own_kernel,
        [(3, 34, 32, 128)] * 2 + [(4, 16, 16, 128)] + [(4, 4, 16, 128)] * 2 + [(4, 16, 16, 128)],
        [(4, 34, 32, 128), (6, 32, 32, 128), (32, 32, 128)],
        flops=20_000_000,
    )(own)
    to_near, to_far, rim_rows = call(pack_kernel, [(4, 4, 24, 128)] * 2 + [(4, 32, 8, 128)], [])(
        to_right, to_left, from_near, from_far
    )
    from_far = lax.ppermute(to_far, "gy", swap_far)
    from_near = lax.ppermute(to_near, "gy", swap_near)
    two, main, edges_rim = call(
        rows_edge_kernel,
        [(3, 34, 24, 128), (4, 8, 8, 128), (4, 16, 8, 128)],
        [(4, 34, 24, 128), (3, 34, 24, 128), (6, 32, 24, 128), (32, 24, 128)]
        + [(4, 16, 16, 128), (512, 128)],
        flops=10_000_000,
    )(own, rim_rows, own_one, own_two, halves)
    main_near = lax.ppermute(main, "gx", swap_near)
    main_far = lax.ppermute(main, "gx", swap_far)
    rim, rim_one = call(
        rim_kernel,
        [(3, 16, 16, 128), (4, 4, 8, 128)],
        [(3, 18, 32, 128), (18, 32, 128)]
        + [(3, 18, 32, 128)] * 2
        + [(6, 16, 32, 128), (16, 32, 128)]
        + [(4, 8, 16, 128), (256, 128)],
        flops=10_000_000,
    )(edges, edges_rim, from_near, from_far)
    rim_near = lax.ppermute(rim_one, "gx", swap_near)
    rim_far = lax.ppermute(rim_one, "gx", swap_far)
    sent, e_one, e_two = call(
        middle_kernel,
        [(CHIPS, 4, 128), (3, 16, 8, 128), (3, 8, 8, 128)],
        [(16, 24, 128), (18, 32, 128), (3, 16, 32, 128), (3, 18, 32, 128), (3, 18, 32, 128)]
        + [(6, 16, 32, 128), (16, 32, 128), (4, 8, 24, 128), (768, 128)]
        + [(10, 24, 128), (3, 10, 24, 128), (3, 10, 24, 128), (3, 8, 8, 128), (8, 8, 128)]
        + [(7, 8, 16, 128)],
    )(main, main_near, main_far, rim_one, rim_near, rim_far)
    groups = [[i for i in range(NX * NY) if i % 2 == core] for core in range(2)]
    mine = lax.all_to_all(
        sent, ("gx", "gy"), split_axis=0, concat_axis=0, axis_index_groups=groups, tiled=True
    )
    (base,) = call(base_kernel, [(3, 32, 16, 128)], [(192, 128), (3, 16, 16, 128)])(two, rim, e_one, e_two)
    other = lax.ppermute(mine, "gy", swap_near)
    (out,) = call(
        top_kernel,
        [(3, 32, 16, 128)],
        [(4, 2, 128, 128), (3, 16, 16, 128), (2, 3, 8, 16, 128), (6, 16, 128), (6, 16, 16, 128)]
        + [(16, 16, 128), (4, 2, 16, 256), (3, 32, 16, 128), pltpu.SemaphoreType.DMA((6,))],
        out_specs=[ANY],
    )(mine.reshape(512, 128), other.reshape(512, 128), base)
    return out


def solution(mesh):
    return jax.shard_map(
        local,
        mesh=mesh,
        in_specs=(P(None, "gx", "gy"), P(None, None, "gx", "gy")),
        out_specs=P(None, None, "gx", "gy"),
        check_vma=False,
    )
```

```python
import jax
import jax.numpy as jnp
from jax import lax
from jax.experimental import pallas as pl
from jax.experimental.pallas import tpu as pltpu
from jax.sharding import PartitionSpec as P


F32 = jnp.float32
NX, NY, CHIPS = 16, 16, 128
BETWEEN = 2.0 * 0.1 / 1.1
ANY = pl.BlockSpec(memory_space=pltpu.HBM)


def dot(a, b):
    return jnp.dot(a, b, precision=lax.Precision.HIGHEST, preferred_element_type=F32)


def iota(shape, dim):
    return lax.broadcasted_iota(jnp.int32, shape, dim)


def roll(x, shift, axis=1):
    shift = shift % x.shape[axis]
    return x if shift == 0 else pltpu.roll(x, shift, axis)


def turn(x, shift):
    return pltpu.roll(x, lax.rem(shift + 256, 128), 1)


def recip(x):
    guess = pl.reciprocal(x, approx=True)
    return guess * (2.0 - x * guess)


def inner(index):
    return (index > 0) & (index < 15)


def call(kernel, outs, scratch, flops=1_000_000, **kw):
    return pl.pallas_call(
        kernel,
        out_shape=[jax.ShapeDtypeStruct(s, F32) for s in outs],
        scratch_shapes=[pltpu.VMEM(s, F32) if isinstance(s, tuple) else s for s in scratch],
        compiler_params=pltpu.CompilerParams(vmem_limit_bytes=32 * 1024 * 1024),
        cost_estimate=pl.CostEstimate(flops=flops, bytes_accessed=4_000_000, transcendentals=0),
        **kw,
    )


def loop(count, body, unroll=1):
    def step(i, carry):
        body(i)
        return carry

    lax.fori_loop(0, count, step, 0, unroll=unroll)


def weigh(weights, values):
    parts = [w * v for w, v in zip(weights, values)]
    while len(parts) > 1:
        parts = [sum(parts[i : i + 2][1:], parts[i]) for i in range(0, len(parts), 2)]
    return parts[0]


def rows_kernel(guess, labels, near, far, own, phase, sems):
    even = lax.rem(lax.axis_index("gx"), 2) == 0
    near_row, far_row = jnp.where(even, 13, 0), jnp.where(even, 0, 13)
    copies = [pltpu.make_async_copy(labels, phase, sems.at[3])]
    for f in range(3):
        copies.append(pltpu.make_async_copy(guess.at[f], own.at[f], sems.at[f]))
    for copy in copies:
        copy.start()
    copies[0].wait()
    own[3] = jnp.where(phase[...] == 1, 0.0, 1.0).astype(F32)
    flat = own.reshape(4 * 32 * 16, 128)
    for ch in (3, 0, 1, 2):
        if ch < 3:
            copies[ch + 1].wait()
        for row in range(3):
            near[3 * ch + row] = flat[pl.ds(512 * ch + near_row + row, 32, stride=16), :]
            far[3 * ch + row] = flat[pl.ds(512 * ch + far_row + row, 32, stride=16), :]


def pack_kernel(to_right, to_left, x_near, x_far, near, far, rim):
    first_core = lax.rem(lax.axis_index("gy"), 2) == 0
    even = lax.rem(lax.axis_index("gx"), 2) == 0
    near_row, far_row = jnp.where(even, 0, 5), jnp.where(even, 5, 0)
    has_far = inner(lax.axis_index("gx"))
    flat = rim.reshape(4 * 32 * 8, 128)
    for ch in range(4):
        for row in range(3):
            flat[pl.ds(256 * ch + near_row + row, 32, stride=8), :] = x_near[3 * ch + row]
            flat[pl.ds(256 * ch + far_row + row, 32, stride=8), :] = jnp.where(has_far, x_far[3 * ch + row], 0.0)

    def some(low):
        for ch in range(4):
            right, left = pack_planes(lambda z: rim[ch, z], low, (8, 128))
            for at, right, left in (
                (slice(0, 16), to_right[ch, low], to_left[ch, low]),
                (slice(16, 24), right, left),
            ):
                near[ch, low, at, :] = jnp.where(first_core, right, left)
                far[ch, low, at, :] = jnp.where(first_core, left, right)

    loop(4, some)


def pack_planes(plane, low, shape):
    group = iota(shape, 1) // 16
    right = left = jnp.zeros(shape, F32)
    for h in range(8):
        moved = roll(plane(4 * h + low), 16 * h + 16)
        right = jnp.where(group == h, moved, right)
        left = jnp.where(group == (h + 1) % 8, moved, left)
    return right, left


def edge_columns(plane, z, shape):
    lane = iota(shape, 1)
    value = jnp.zeros(shape, F32)
    for half in range(2):
        source = plane(z + 16 * half)
        base = 64 * half
        value = jnp.where((lane >= base) & (lane < base + 7), roll(source, base + 7), value)
        value = jnp.where((lane >= base + 57) & (lane < base + 64), roll(source, base + 57), value)
    return value


def six_of(ref, lead, z, first, count):
    own = ref[(*lead, z, pl.ds(first, count), slice(None))]
    return own, (
        ref[(*lead, z, pl.ds(first - 1, count), slice(None))],
        ref[(*lead, z, pl.ds(first + 1, count), slice(None))],
        roll(own, 1),
        roll(own, -1),
        ref[(*lead, z - 1, pl.ds(first, count), slice(None))],
        ref[(*lead, z + 1, pl.ds(first, count), slice(None))],
    )


def block_of(ref, lead, z, planes, first, count):
    rows = pl.ds(first, count)
    own = [ref[(*lead, z + k, rows, slice(None))] for k in range(-1, planes + 1)]
    result = []
    for k in range(planes):
        value = own[k + 1]
        six = (
            ref[(*lead, z + k, pl.ds(first - 1, count), slice(None))],
            ref[(*lead, z + k, pl.ds(first + 1, count), slice(None))],
            roll(value, 1),
            roll(value, -1),
            own[k],
            own[k + 2],
        )
        result.append((value, six))
    return result


def face(total):
    return jnp.where(total < 0.5, 1.0, jnp.where(total < 1.5, BETWEEN, 0.1))


def fine_weights(own, six, omega):
    faces = [face(own + other) for other in six]
    diag = (faces[0] + faces[1]) + (faces[2] + faces[3]) + (faces[4] + faces[5])
    gain = omega * recip(diag)
    return [gain * value for value in faces], 1.25 * diag


def fine_sweep(w, f, own, six):
    return (0.2 * own + (w[2 * f + 1] - w[2 * f])) + weigh(w, six)


def fine_left(w, f, own, six, diag):
    return (((w[2 * f + 1] - w[2 * f]) - 0.8 * own) + weigh(w, six)) * diag


def fine_sweeps(planes, windows, start, share, one, two, weights, diags, halves, omega, wrap, keep):
    first, count = windows[0]

    def first_sweep(step):
        z = 4 * step
        w = []
        for k, (own, six) in enumerate(block_of(share, (), z + 1, 4, first, count)):
            now, diag = fine_weights(own, six, omega)
            diags[z + k, pl.ds(first, count), :] = diag
            for i in range(6):
                weights[i, z + k, pl.ds(first, count), :] = now[i]
            w.append(now)
        for f in range(3):
            for k, (own, six) in enumerate(block_of(start, (f,), z + 1, 4, first, count)):
                one[f, z + k + 1, pl.ds(first, count), :] = fine_sweep(w[k], f, own, six)

    loop(planes // 4, first_sweep)
    wrap(one)
    second, count2 = windows[1]

    def second_sweep(step):
        z = 4 * step
        w = [[weights[i, z + k, pl.ds(second, count2), :] for i in range(6)] for k in range(4)]
        for f in range(3):
            for k, (own, six) in enumerate(block_of(one, (f,), z + 1, 4, second, count2)):
                two[f, z + k + 1, pl.ds(second, count2), :] = fine_sweep(w[k], f, own, six)

    loop(planes // 4, second_sweep)
    wrap(two)

    def residual(step):
        z = 4 * step
        w = [[weights[i, z + k, 8:24, :] for i in range(6)] for k in range(4)]
        diag = [diags[z + k, 8:24, :] for k in range(4)]
        for f in range(3):
            values = []
            for k, (own, six) in enumerate(block_of(two, (f,), z + 1, 4, 8, 16)):
                if keep is not None:
                    keep[f, z + k] = own
                values.append(fine_left(w[k], f, own, six, diag[k]))
            for pair in range(2):
                halves[f, 2 * step + pair] = values[2 * pair] + values[2 * pair + 1]
        for pair in range(2):
            at = z + 2 * pair + 1
            halves[3, 2 * step + pair] = share[at, 8:24, :] + share[at + 1, 8:24, :]

    loop(planes // 4, residual)


def own_kernel(own, one, two, halves, to_right, to_left, edges, held, weights, diags):
    zero = jnp.zeros((32, 128), F32)
    for z in (0, 33):
        for ch in range(4):
            held[ch, z] = zero
        for ref in (one, two):
            for f in range(3):
                ref[f, z] = zero

    def plane(z):
        for ch in range(4):
            held[ch, z + 1, 8:24, :] = own[ch, z]

    loop(32, plane, 4)
    fine_sweeps(
        32, [(8, 16)] * 2, held, held.at[3], one, two, weights, diags, halves, 0.8, lambda ref: None, None
    )

    def some(low):
        for ch in range(4):
            to_right[ch, low], to_left[ch, low] = pack_planes(lambda z: own[ch, z], low, (16, 128))

    loop(4, some)

    def edge(z):
        for ch in range(4):
            edges[ch, z] = edge_columns(lambda at: own[ch, at], z, (16, 128))

    loop(16, edge, 2)


def rows_edge_kernel(own, rim, own_one, own_two, own_halves, two, packed, edges, start, one, weights, diags, halves, pooled):
    gx = lax.axis_index("gx")
    zero = jnp.zeros((24, 128), F32)
    for z in (0, 33):
        for ch in range(4):
            start[ch, z] = zero
        for ref in (one, two):
            for f in range(3):
                ref[f, z] = zero

    def fill(z):
        for ch in range(4):
            start[ch, z + 1, 0:8, :] = own[ch, z, 8:16, :]
            start[ch, z + 1, 8:16, :] = rim[ch, z]
            start[ch, z + 1, 16:24, :] = own[ch, z, 0:8, :]
        for f in range(3):
            for ref, source in ((one, own_one), (two, own_two)):
                ref[f, z + 1, 0:8, :] = source[f, z + 1, 16:24, :]
                ref[f, z + 1, 16:24, :] = source[f, z + 1, 8:16, :]

    loop(32, fill, 4)
    upper = iota((8, 128), 0) < 4

    def both(ref, lead, step, shift=0):
        high = ref[(*lead, pl.ds(8 - step + shift, 8), slice(None))]
        low = ref[(*lead, pl.ds(8 + step + shift, 8), slice(None))]
        return jnp.where(upper, high, low)

    def block_both(ref, f, z, step):
        own = [both(ref, (f, z + k), step) for k in range(-1, 5)]
        result = []
        for k in range(4):
            value = own[k + 1]
            low, high = both(ref, (f, z + k), step, -1), both(ref, (f, z + k), step, 1)
            result.append((value, (low, high, roll(value, 1), roll(value, -1), own[k], own[k + 2])))
        return result

    def put(ref, f, z, step, value):
        ref[f, z, pl.ds(8 - step, 4), :] = value[0:4]
        ref[f, z, pl.ds(12 + step, 4), :] = value[4:8]

    row = iota((16, 128), 0) + 5
    low, high = jnp.where(gx > 0, 1, 0), jnp.where(gx < NX - 1, 1, 0)
    inside = jnp.where((row >= 8) & (row < 12), high, jnp.where((row >= 12) & (row < 16), low, 1))
    omega = 0.8 * inside.astype(F32)

    def weigh_all(step):
        z = 4 * step
        for k, (value, six) in enumerate(block_of(start, (3,), z + 1, 4, 5, 16)):
            w, diag = fine_weights(value, six, omega)
            diags[z + k, 5:21, :] = diag
            for i in range(6):
                weights[i, z + k, 5:21, :] = w[i]

    loop(8, weigh_all)

    for step, source, target in ((1, start, one), (2, one, two)):

        def sweep(block):
            z = 4 * block
            w = [[both(weights, (i, z + k), step) for i in range(6)] for k in range(4)]
            for f in range(3):
                for k, (value, six) in enumerate(block_both(source, f, z + 1, step)):
                    put(target, f, z + k + 1, step, fine_sweep(w[k], f, value, six))

        loop(8, sweep)

    sub = iota((8, 128), 0)

    def residual(block):
        z = 4 * block
        w = [[both(weights, (i, z + k), 3) for i in range(6)] for k in range(4)]
        diag = [both(diags, (z + k,), 3) for k in range(4)]
        for f in range(3):
            values = []
            for k, (value, six) in enumerate(block_both(two, f, z + 1, 3)):
                values.append(fine_left(w[k], f, value, six, diag[k]))
            for k in range(2):
                pair = 2 * block + k
                value = values[2 * k] + values[2 * k + 1]
                halves[f, pair, 0:8, :] = jnp.where(sub < 3, roll(value, 3, 0), own_halves[f, pair, 0:8, :])
                halves[f, pair, 8:16, :] = jnp.where(sub >= 5, roll(value, 5, 0), own_halves[f, pair, 8:16, :])
        for k in range(2):
            halves[3, 2 * block + k] = own_halves[3, 2 * block + k]

    loop(8, residual)
    source, target = iota((128, 128), 0), iota((128, 128), 1)
    value = None
    for half in range(2):
        pool = jnp.where(source // 2 + 64 * half == target, 0.125, 0.0)
        part = dot(halves[:, 8 * half : 8 * half + 8].reshape(512, 128), pool)
        value = part if value is None else value + part
    pooled[...] = value
    packed[...] = (pooled[pl.ds(0, 256, stride=2), :] + pooled[pl.ds(1, 256, stride=2), :]).reshape(4, 8, 8, 128)

    def edge(z):
        for ch in range(4):
            edges[ch, z] = edge_columns(lambda at: rim[ch, at], z, (8, 128))

    loop(16, edge, 2)


def rim_kernel(
    edges, edges_rim, near, far, field, packed,
    start, share, one, two, weights, diags, halves, pooled,
):
    gx, gy = lax.axis_index("gx"), lax.axis_index("gy")
    lane = iota((24, 128), 1)
    part = lane % 64
    is_after = (part >= 7) & (part < 22)
    is_before = (part >= 42) & (part < 57)
    first_core = lax.rem(gy, 2) == 0

    def unpack(low):
        for ch in range(4):
            target = start.at[ch] if ch < 3 else share
            from_near, from_far = near[ch, low], jnp.where(inner(gy), far[ch, low], 0.0)
            from_right = jnp.where(first_core, from_near, from_far)
            from_left = jnp.where(first_core, from_far, from_near)
            for h in range(4):
                z = 4 * h + low
                after_y = roll(from_right, 7 - 16 * (h + 1))
                before_y = roll(from_left, 41 - 16 * h)
                own = jnp.concatenate([edges[ch, z], edges_rim[ch, z]], axis=0)
                value = jnp.where(is_after, after_y, jnp.where(is_before, before_y, own))
                target[z + 1, 8:24, :] = value[0:16]
                target[z + 1, 0:8, :] = value[16:24]
                target[z + 1, 24:32, :] = value[16:24]

    loop(4, unpack)

    half_of = iota((32, 128), 1)

    def wrap_one(ref):
        ref[0] = jnp.where(half_of >= 64, roll(ref[16], 64), 0.0)
        ref[17] = jnp.where(half_of < 64, roll(ref[1], 64), 0.0)

    def wrap(ref):
        for f in range(3):
            wrap_one(ref.at[f])

    wrap_one(share)
    wrap(start)
    row = iota((24, 128), 0) + 6
    low, high = jnp.where(gx > 0, 1, 0), jnp.where(gx < NX - 1, 1, 0)
    inside_x = jnp.where(row < 8, low, jnp.where(row >= 24, high, 1))
    inside_y = jnp.where(
        part < 32,
        jnp.where((part < 7) | (gy < NY - 1), 1, 0),
        jnp.where((part >= 57) | (gy > 0), 1, 0),
    )
    omega = 0.8 * (inside_x * inside_y).astype(F32)
    fine_sweeps(
        16, [(6, 24), (7, 24)], start, share, one, two, weights, diags, halves, omega, wrap, field
    )

    source, target = iota((128, 128), 0), iota((128, 128), 1)
    spot = source % 64
    column = jnp.where(spot < 32, 121 + spot, 71 + spot) // 2
    to = jnp.where(spot < 32, column - 62, column - 48)
    keep = ((spot < 32) & (to >= 0) & (to < 9)) | ((spot >= 32) & (to >= 9) & (to < 18))
    mixed = halves[...].reshape(4, 4, 2, 16, 128)
    value = None
    for odd in range(2):
        pool = jnp.where(keep & (to + 64 * odd + 32 * (source // 64) == target), 0.125, 0.0)
        part = dot(mixed[:, :, odd].reshape(256, 128), pool)
        value = part if value is None else value + part
    pooled[...] = value
    packed[...] = (pooled[pl.ds(0, 128, stride=2), :] + pooled[pl.ds(1, 128, stride=2), :]).reshape(4, 4, 8, 128)


def base_kernel(two, rim, e_one, e_two, base, wide, spread):
    copy = jnp.where(iota((128, 128), 0) == iota((128, 128), 1) // 2, 1.0, 0.0)
    value = dot(e_two[...].reshape(192, 128), copy)
    for block in range(24):
        rows = value[8 * block : 8 * block + 4, :]
        wide[pl.ds(8 * block, 4, stride=2), :] = rows
        wide[pl.ds(8 * block + 1, 4, stride=2), :] = rows
    value = e_one[...].reshape(24, 2, 8, 128) + wide[...].reshape(24, 1, 8, 128)
    value = dot(value.reshape(384, 128), copy)
    flat = spread.reshape(768, 128)
    for block in range(48):
        rows = value[8 * block : 8 * block + 8, :]
        flat[pl.ds(16 * block, 8, stride=2), :] = rows
        flat[pl.ds(16 * block + 1, 8, stride=2), :] = rows
    lane = iota((16, 128), 1)

    def pair(k):
        for f in range(3):
            for z in (2 * k, 2 * k + 1):
                value = rim[f, z]
                for half in range(2):
                    low = roll(value, -57 - 64 * half)
                    high = roll(value, 121 - 64 * half)
                    at = z + 16 * half
                    own = jnp.concatenate([two[f, at + 1, 16:24, :], two[f, at + 1, 0:8, :]], axis=0)
                    own = jnp.where(lane < 3, low, jnp.where(lane >= 125, high, own))
                    base[f, at] = own + spread[f, k + 8 * half]

    loop(8, pair, 1)


def resist(share):
    return recip(1.0 - 0.9 * share)


def level_weights(own, six, omega):
    faces = [2.0 * recip(own + other) for other in six]
    diag = (faces[0] + faces[1]) + (faces[2] + faces[3]) + (faces[4] + faces[5])
    gain = omega * recip(diag)
    return gain, [gain * w for w in faces], diag


def middle_kernel(
    main, main_near, main_far, rim, rim_near, rim_far, sent, e_one, e_two,
    share, rest, rhs, first, second, weights, diags, halves, pooled,
    rest2, first2, second2, rhs2, share2, weights2,
):
    gx, gy = lax.axis_index("gx"), lax.axis_index("gy")
    low_x, high_x = jnp.where(gx > 0, 1, 0), jnp.where(gx < NX - 1, 1, 0)
    low_y, high_y = jnp.where(gy > 0, 1, 0), jnp.where(gy < NY - 1, 1, 0)

    for f in range(3):
        for ref in (first, second):
            ref[f, 0] = jnp.zeros((32, 128), F32)
            ref[f, 17] = jnp.zeros((32, 128), F32)
    for z in (0, 17):
        rest[z] = jnp.ones((32, 128), F32)
    lane = iota((8, 128), 1)
    even = lax.rem(gx, 2) == 0
    near_row, far_row = jnp.where(even, 16, 0), jnp.where(even, 0, 16)
    starts = (pl.multiple_of(near_row, 8), pl.multiple_of(far_row, 8), 8)

    sources = zip(starts, ((main_near, rim_near), (main_far, rim_far), (main, rim)))
    sources = list(sources)
    has_far = inner(gx)

    def fill(q):
        for odd in range(2):
            for half in range(2):
                z = 2 * q + odd + 8 * half
                base = 64 * odd + 32 * half
                for at, (middle, outer) in sources:
                    for ch in range(4):
                        edge, body = outer[ch, q], middle[ch, 2 * q + odd]
                        if outer is rim_far:
                            edge, body = jnp.where(has_far, edge, 0.0), jnp.where(has_far, body, 0.0)
                        value = jnp.where(lane < 62, roll(body, 64 * half), roll(edge, 62 - base))
                        value = jnp.where((lane >= 96) | (lane < 2), roll(edge, 112 - base), value)
                        if ch < 3:
                            rhs[ch, z, pl.ds(at, 8), :] = value
                        else:
                            share[z, pl.ds(at, 8), :] = value
                            rest[z + 1, pl.ds(at, 8), :] = resist(value)
                rest[z + 1, 24:32, :] = jnp.ones((8, 128), F32)

    loop(4, fill)

    row, lane = iota((24, 128), 0) + 1, iota((24, 128), 1)
    in_x = jnp.where(row < 8, low_x, jnp.where(row >= 16, high_x, 1))
    in_y = jnp.where(lane < 64, 1, jnp.where(lane < 96, high_y, low_y))
    omega = 0.8 * (in_x * in_y).astype(F32)

    def start(step):
        z = 4 * step
        for k, (own, six) in enumerate(block_of(rest, (), z + 1, 4, 1, 24)):
            gain, w, diag = level_weights(own, six, omega)
            for i in range(6):
                weights[i, z + k, 1:25, :] = w[i]
            diags[z + k, 1:25, :] = (1.25 * 0.25) * diag
            for f in range(3):
                first[f, z + k + 1, 1:25, :] = (4.0 * gain) * rhs[f, z + k, 1:25, :]

    loop(4, start)

    def sweep(step):
        z = 4 * step
        w = [[weights[i, z + k, 3:27, :] for i in range(6)] for k in range(4)]
        for f in range(3):
            for k, (own, six) in enumerate(block_of(first, (f,), z + 1, 4, 3, 24)):
                second[f, z + k + 1, 3:27, :] = 1.2 * own + weigh(w[k], six)

    loop(4, sweep)

    def left(step):
        z = 4 * step
        w = [[weights[i, z + k, 4:20, :] for i in range(6)] for k in range(4)]
        diag = [diags[z + k, 4:20, :] for k in range(4)]
        for f in range(3):
            values = []
            for k, (own, six) in enumerate(block_of(second, (f,), z + 1, 4, 4, 16)):
                change = (first[f, z + k + 1, 4:20, :] - 0.8 * own) + weigh(w[k], six)
                values.append(change * diag[k])
                e_one[f, z + k] = second[f, z + k + 1, 8:16, :]
            for k in range(2):
                halves[f, 2 * step + k, 0:16, :] = values[2 * k] + values[2 * k + 1]
                halves[f, 2 * step + k, 16:24, :] = jnp.zeros((8, 128), F32)
        for k in range(2):
            halves[3, 2 * step + k] = share[z + 2 * k] + share[z + 2 * k + 1]

    loop(4, left)

    source, target = iota((128, 128), 0), iota((128, 128), 1)
    pool = jnp.where(source // 2 + jnp.where(source >= 96, 64, 0) == target, 0.125, 0.0)
    pooled[...] = dot(halves[...].reshape(4 * 8 * 24, 128), pool)
    for z in (0, 9):
        rest2[z] = jnp.ones((24, 128), F32)
        for f in range(3):
            first2[f, z] = jnp.zeros((24, 128), F32)
            second2[f, z] = jnp.zeros((24, 128), F32)
    for z in range(8):
        for f in range(3):
            base = (f * 8 + z) * 24
            rhs2[f, z] = pooled[pl.ds(base, 8, stride=2), :] + pooled[pl.ds(base + 1, 8, stride=2), :]
        base = (3 * 8 + z) * 24
        value = pooled[pl.ds(base + 2, 8, stride=2), :] + pooled[pl.ds(base + 3, 8, stride=2), :]
        rest2[z + 1, 0:8, :] = resist(value)
        value = pooled[pl.ds(base + 8, 8, stride=2), :] + pooled[pl.ds(base + 9, 8, stride=2), :]
        rest2[z + 1, 3:11, :] = resist(value)
        share2[z] = value

    row, lane = iota((8, 128), 0) + 1, iota((8, 128), 1)
    in_x = jnp.where(row < 3, low_x, jnp.where(row >= 7, high_x, 1))
    in_y = jnp.where(lane < 32, 1, jnp.where(lane < 96, high_y, low_y))
    omega2 = 0.8 * (in_x * in_y).astype(F32)

    for z, (own, six) in enumerate(block_of(rest2, (), 1, 8, 1, 8)):
        gain, w, diag = level_weights(own, six, omega2)
        for i in range(6):
            weights2[i, z, 1:9, :] = w[i]
        weights2[6, z, 1:9, :] = (1.25 * 0.0625) * diag
        for f in range(3):
            first2[f, z + 1, 1:9, :] = (16.0 * gain) * rhs2[f, z]
    w = [[weights2[i, z, 2:10, :] for i in range(6)] for z in range(8)]
    for f in range(3):
        for z, (own, six) in enumerate(block_of(first2, (f,), 1, 8, 2, 8)):
            second2[f, z + 1, 2:10, :] = 1.2 * own + weigh(w[z], six)
    w = [[weights2[i, z, 3:11, :] for i in range(7)] for z in range(8)]
    own_row = iota((8, 128), 0) < 4
    parts = [{} for pair in range(4)]
    for f in range(3):
        for z, (own, six) in enumerate(block_of(second2, (f,), 1, 8, 3, 8)):
            e_two[f, z] = own
            change = (first2[f, z + 1, 3:11, :] - 0.8 * own) + weigh(w[z], six)
            value = jnp.where(own_row, change * w[z][6], 0.0)
            sums = parts[z // 2]
            sums[f] = value if z % 2 == 0 else sums[f] + value
    for z in range(8):
        value = jnp.where(own_row, share2[z], 0.0)
        sums = parts[z // 2]
        sums[3] = value if z % 2 == 0 else sums[3] + value

    pool = jnp.where((source < 32) & (source // 2 == target % 16), 0.125, 0.0)
    rows = jnp.concatenate([parts[pair][ch] for ch in range(4) for pair in range(4)], axis=0)
    spread = dot(rows, pool)
    at, to = iota((32, 128), 0), iota((32, 128), 1)
    keep = (at // 8 == to // 32) & ((at % 8) // 2 == (to // 16) % 2)
    result = jnp.concatenate(
        [
            jnp.sum(jnp.where(keep, spread[32 * ch : 32 * ch + 32], 0.0), axis=0, keepdims=True)
            for ch in range(4)
        ],
        axis=0,
    )
    for copy in range(CHIPS):
        sent[copy] = result


def swap_blocks(x):
    sub, group = iota((8, 128), 0), iota((8, 128), 1) // 16
    for bit in (4, 2, 1):
        up = roll(roll(x, -bit, 0), 16 * bit)
        down = up if bit == 4 else roll(roll(x, bit, 0), -16 * bit)
        sub_set, group_set = (sub & bit) != 0, (group & bit) != 0
        x = jnp.where(sub_set == group_set, x, jnp.where(sub_set, down, up))
    return x


def top_kernel(
    mine, other, base, out,
    natural, first, second, four, weights, diags, lefts, final, sems,
):
    gx, gy = lax.axis_index("gx"), lax.axis_index("gy")
    first_core = lax.rem(gy, 2) == 0
    lane, sub = iota((16, 128), 1), iota((16, 128), 0)
    cells = [(z, x, half) for z in range(4) for x in range(2) for half in range(2)]

    def lay(g):
        for ch in range(4):
            rows = pl.ds(32 * g + ch, 8, stride=4)
            pair = mine[rows, :], other[rows, :]
            natural[ch, 0, pl.ds(pl.multiple_of(8 * g, 8), 8), :] = swap_blocks(
                jnp.where(first_core, pair[0], pair[1])
            )
            natural[ch, 1, pl.ds(pl.multiple_of(8 * g, 8), 8), :] = swap_blocks(
                jnp.where(first_core, pair[1], pair[0])
            )

    loop(16, lay, 4)
    flat = natural.reshape(1024, 128)

    def plane(ch, z, x, half):
        return flat[pl.ds((ch * 2 + half) * 128 + z * 2 + x, 16, stride=8), :]

    def neighbours(at, z, x, half, outside):
        own, other = at(z, x, half), at(z, 1 - x, half)
        beside = at(z, x, 1 - half)
        shifted = roll(other, 1 if x == 0 else -1, 0)
        low, high = (shifted, other) if x == 0 else (other, shifted)
        left, right = roll(own, 1), roll(own, -1)
        left = jnp.where(lane % 16 == 0, roll(beside, 1 if half == 0 else -15), left)
        right = jnp.where(lane % 16 == 15, roll(beside, 15 if half == 0 else -1), right)
        down = at(z - 1, x, half) if z > 0 else outside
        up = at(z + 1, x, half) if z < 3 else outside
        return own, [low, high, left, right, down, up]

    def edge_masks(x, half):
        return [
            sub > 0 if x == 0 else None,
            sub < 15 if x == 1 else None,
            lane > 0 if half == 0 else None,
            lane < 127 if half == 1 else None,
            None,
            None,
        ]

    def key(z, x, half):
        return (z * 2 + x) * 2 + half

    shares = {c: plane(3, *c) for c in cells}
    rests = {c: resist(shares[c]) for c in cells}
    ones, zeros = jnp.ones((16, 128), F32), jnp.zeros((16, 128), F32)
    for z, x, half in cells:
        own, six = neighbours(lambda *c: rests[c], z, x, half, ones)
        masks = edge_masks(x, half)
        six = [s if m is None else jnp.where(m, s, 1.0) for s, m in zip(six, masks)]
        gain, w, diag = level_weights(own, six, 0.8)
        at = key(z, x, half)
        for i in range(6):
            weights[i, at] = w[i] if masks[i] is None else jnp.where(masks[i], w[i], 0.0)
        diags[at] = (1.25 * 0.25**3) * diag
        for f in range(3):
            first[f, at] = (64.0 * gain) * plane(f, z, x, half)

    for z, x, half in cells:
        at = key(z, x, half)
        w = [weights[i, at] for i in range(6)]
        for f in range(3):
            own, six = neighbours(lambda *c: first[f, key(*c)], z, x, half, zeros)
            second[half, f, z * 2 + x] = 1.2 * own + weigh(w, six)

    for z4 in range(2):
        for half in range(2):
            sums = [None] * 4
            for z in (2 * z4, 2 * z4 + 1):
                for x in range(2):
                    at = key(z, x, half)
                    w = [weights[i, at] for i in range(6)]
                    diag = diags[at]
                    for f in range(3):
                        own, six = neighbours(
                            lambda c, d, e: second[e, f, c * 2 + d], z, x, half, zeros
                        )
                        value = ((first[f, at] - 0.8 * own) + weigh(w, six)) * diag
                        sums[f] = value if sums[f] is None else sums[f] + value
                    share = shares[z, x, half]
                    sums[3] = share if sums[3] is None else sums[3] + share
            for ch in range(4):
                lefts[ch, z4, :, 128 * half : 128 * half + 128] = sums[ch]

    source = iota((256, 128), 0)
    column = ((source % 128) // 16) * 16 + (source // 128) * 8 + (source % 16) // 2
    pool = jnp.where(column == iota((256, 128), 1), 0.125, 0.0)
    level = dot(lefts[...].reshape(128, 256), pool)

    def coarsest(ch, z):
        return level[(ch * 2 + z) * 16 : (ch * 2 + z) * 16 + 16, :]

    masks = [sub > 0, sub < 15, lane > 0, lane < 127]
    resists = [resist(coarsest(3, z)) for z in range(2)]
    gains, ws, ds = [], [], []
    for z in range(2):
        own, other = resists[z], resists[1 - z]
        six = [roll(own, 1, 0), roll(own, -1, 0), roll(own, 1), roll(own, -1)]
        six = [jnp.where(m, s, 1.0) for m, s in zip(masks, six)] + [other, ones]
        gain, w, diag = level_weights(own, six, 0.8)
        gains.append(gain)
        ds.append(diag)
        ws.append([jnp.where(m, v, 0.0) for m, v in zip(masks, w)] + [w[4]])
    whole = jnp.sum(ds[0] + ds[1], keepdims=True)

    def around(values, z):
        own, other = values[z], values[1 - z]
        return weigh(ws[z], (roll(own, 1, 0), roll(own, -1, 0), roll(own, 1), roll(own, -1), other))

    begin = [[256.0 * gains[z] * coarsest(f, z) for z in range(2)] for f in range(3)]
    values = begin
    for step in range(5):
        values = [
            [(0.2 * values[f][z] + begin[f][z]) + around(values[f], z) for z in range(2)] for f in range(3)
        ]
    for f in range(3):
        change = [(begin[f][z] - 0.8 * values[f][z]) + around(values[f], z) for z in range(2)]
        total = jnp.sum(1.25 * (change[0] * ds[0] + change[1] * ds[1]), keepdims=True)
        for z in range(2):
            four[2 * f + z] = values[f][z] + total / whole

    copy = jnp.where(iota((128, 128), 0) == iota((128, 128), 1) // 2, 1.0, 0.0)
    rows = four.reshape(96, 128)[pl.ds(gx, 6, stride=16), :]
    rows = jnp.concatenate([jnp.broadcast_to(rows[i : i + 1], (4, 128)) for i in range(6)], axis=0)
    three = dot(turn(rows, -8 * gy), copy)
    flat = second.reshape(768, 128)
    halves = [flat[pl.ds(gx + 384 * half, 24, stride=16), :] for half in range(2)]
    three = three + turn(jnp.where(first_core, halves[0], halves[1]), -16 * lax.div(gy, 2))

    copy = jnp.where(iota((128, 128), 0) == iota((128, 128), 1) // 8, 1.0, 0.0)
    three = dot(three, copy)
    copies = []
    for f in range(3):
        for z in range(4):
            for x in range(2):
                at = f * 8 + z * 2 + x
                value = jnp.broadcast_to(three[at : at + 1], (8, 128))
                for k in range(8 * z, 8 * z + 8):
                    final[f, k, 8 * x : 8 * x + 8, :] = base[f, k, 8 * x : 8 * x + 8, :] + value
            if z % 2 == 1:
                part = (f, pl.ds(8 * z - 8, 16))
                copy = pltpu.make_async_copy(final.at[part], out.at[part], sems.at[len(copies)])
                copy.start()
                copies.append(copy)
    for copy in copies:
        copy.wait()


def local(labels, guess):
    swap_near = [(i, i ^ 1) for i in range(NY)]
    far_x, far_y = [], []
    for x in range(NX):
        for y in range(NY):
            across_x, across_y = x + 1 if x % 2 else x - 1, y + 1 if y % 2 else y - 1
            to = (across_x, y) if 0 <= across_x < NX else (x, y ^ 1)
            far_x.append((x * NY + y, to[0] * NY + to[1]))
            to = (x, across_y) if 0 <= across_y < NY else (x ^ 1, y)
            far_y.append((x * NY + y, to[0] * NY + to[1]))
    both = ("gx", "gy")
    to_near, to_far, own = call(
        rows_kernel,
        [(12, 32, 128)] * 2 + [(4, 32, 16, 128)],
        [pltpu.VMEM((32, 16, 128), jnp.int32), pltpu.SemaphoreType.DMA((4,))],
        in_specs=[ANY, ANY],
    )(pltpu.with_memory_space_constraint(guess, pltpu.HBM), pltpu.with_memory_space_constraint(labels, pltpu.HBM))
    from_near = lax.ppermute(to_near, "gx", swap_near)
    from_far = lax.ppermute(to_far, both, far_x)
    own_one, own_two, halves, to_right, to_left, edges = call(
        own_kernel,
        [(3, 34, 32, 128)] * 2 + [(4, 16, 16, 128)] + [(4, 4, 16, 128)] * 2 + [(4, 16, 16, 128)],
        [(4, 34, 32, 128), (6, 32, 32, 128), (32, 32, 128)],
        flops=20_000_000,
    )(own)
    to_near, to_far, rim_rows = call(pack_kernel, [(4, 4, 24, 128)] * 2 + [(4, 32, 8, 128)], [])(
        to_right, to_left, from_near, from_far
    )
    from_far = lax.ppermute(to_far, both, far_y)
    from_near = lax.ppermute(to_near, "gy", swap_near)
    two, main, edges_rim = call(
        rows_edge_kernel,
        [(3, 34, 24, 128), (4, 8, 8, 128), (4, 16, 8, 128)],
        [(4, 34, 24, 128), (3, 34, 24, 128), (6, 32, 24, 128), (32, 24, 128)]
        + [(4, 16, 16, 128), (512, 128)],
        flops=10_000_000,
    )(own, rim_rows, own_one, own_two, halves)
    main_near = lax.ppermute(main, "gx", swap_near)
    main_far = lax.ppermute(main, both, far_x)
    rim, rim_one = call(
        rim_kernel,
        [(3, 16, 16, 128), (4, 4, 8, 128)],
        [(3, 18, 32, 128), (18, 32, 128)]
        + [(3, 18, 32, 128)] * 2
        + [(6, 16, 32, 128), (16, 32, 128)]
        + [(4, 8, 16, 128), (256, 128)],
        flops=10_000_000,
    )(edges, edges_rim, from_near, from_far)
    rim_near = lax.ppermute(rim_one, "gx", swap_near)
    rim_far = lax.ppermute(rim_one, both, far_x)
    sent, e_one, e_two = call(
        middle_kernel,
        [(CHIPS, 4, 128), (3, 16, 8, 128), (3, 8, 8, 128)],
        [(16, 24, 128), (18, 32, 128), (3, 16, 32, 128), (3, 18, 32, 128), (3, 18, 32, 128)]
        + [(6, 16, 32, 128), (16, 32, 128), (4, 8, 24, 128), (768, 128)]
        + [(10, 24, 128), (3, 10, 24, 128), (3, 10, 24, 128), (3, 8, 8, 128), (8, 8, 128)]
        + [(7, 8, 16, 128)],
    )(main, main_near, main_far, rim_one, rim_near, rim_far)
    groups = [[i for i in range(NX * NY) if i % 2 == core] for core in range(2)]
    mine = lax.all_to_all(
        sent, ("gx", "gy"), split_axis=0, concat_axis=0, axis_index_groups=groups, tiled=True
    )
    (base,) = call(base_kernel, [(3, 32, 16, 128)], [(192, 128), (3, 16, 16, 128)])(two, rim, e_one, e_two)
    other = lax.ppermute(mine, "gy", swap_near)
    (out,) = call(
        top_kernel,
        [(3, 32, 16, 128)],
        [(4, 2, 128, 128), (3, 16, 16, 128), (2, 3, 8, 16, 128), (6, 16, 128), (6, 16, 16, 128)]
        + [(16, 16, 128), (4, 2, 16, 256), (3, 32, 16, 128), pltpu.SemaphoreType.DMA((6,))],
        out_specs=[ANY],
    )(mine.reshape(512, 128), other.reshape(512, 128), base)
    return out


def solution(mesh):
    return jax.shard_map(
        local,
        mesh=mesh,
        in_specs=(P(None, "gx", "gy"), P(None, None, "gx", "gy")),
        out_specs=P(None, None, "gx", "gy"),
        check_vma=False,
    )
```

```python
import jax
import jax.numpy as jnp
from jax import lax
from jax.experimental import pallas as pl
from jax.experimental.pallas import tpu as pltpu
from jax.sharding import PartitionSpec as P


F32 = jnp.float32
NX, NY, CHIPS = 16, 16, 128
BETWEEN = 2.0 * 0.1 / 1.1
ANY = pl.BlockSpec(memory_space=pltpu.HBM)


def dot(a, b):
    return jnp.dot(a, b, precision=lax.Precision.HIGHEST, preferred_element_type=F32)


def iota(shape, dim):
    return lax.broadcasted_iota(jnp.int32, shape, dim)


def roll(x, shift, axis=1):
    shift = shift % x.shape[axis]
    return x if shift == 0 else pltpu.roll(x, shift, axis)


def turn(x, shift):
    return pltpu.roll(x, lax.rem(shift + 256, 128), 1)


def recip(x):
    guess = pl.reciprocal(x, approx=True)
    return guess * (2.0 - x * guess)


def inner(index):
    return (index > 0) & (index < 15)


def span(start, count):
    if start % 8 == 0:
        return pl.ds(start, count)
    return pl.ds(jnp.maximum(lax.axis_index("gx") - NX, 0) + start, count)


def call(kernel, outs, scratch, flops=1_000_000, **kw):
    return pl.pallas_call(
        kernel,
        out_shape=[jax.ShapeDtypeStruct(s, F32) for s in outs],
        scratch_shapes=[pltpu.VMEM(s, F32) if isinstance(s, tuple) else s for s in scratch],
        compiler_params=pltpu.CompilerParams(vmem_limit_bytes=32 * 1024 * 1024),
        cost_estimate=pl.CostEstimate(flops=flops, bytes_accessed=4_000_000, transcendentals=0),
        **kw,
    )


def loop(count, body, unroll=1):
    def step(i, carry):
        body(i)
        return carry

    lax.fori_loop(0, count, step, 0, unroll=unroll)


def weigh(weights, values):
    parts = [w * v for w, v in zip(weights, values)]
    while len(parts) > 1:
        parts = [sum(parts[i : i + 2][1:], parts[i]) for i in range(0, len(parts), 2)]
    return parts[0]


def rows_kernel(guess, labels, near, far, own, phase, sems):
    even = lax.rem(lax.axis_index("gx"), 2) == 0
    near_row, far_row = jnp.where(even, 13, 0), jnp.where(even, 0, 13)
    copies = [pltpu.make_async_copy(labels, phase, sems.at[3])]
    for f in range(3):
        copies.append(pltpu.make_async_copy(guess.at[f], own.at[f], sems.at[f]))
    for copy in copies:
        copy.start()
    copies[0].wait()
    own[3] = jnp.where(phase[...] == 1, 0.0, 1.0).astype(F32)
    flat = own.reshape(4 * 32 * 16, 128)
    for ch in (3, 0, 1, 2):
        if ch < 3:
            copies[ch + 1].wait()
        for row in range(3):
            near[3 * ch + row] = flat[pl.ds(512 * ch + near_row + row, 32, stride=16), :]
            far[3 * ch + row] = flat[pl.ds(512 * ch + far_row + row, 32, stride=16), :]


def pack_kernel(to_right, to_left, x_near, x_far, near, far, rim):
    first_core = lax.rem(lax.axis_index("gy"), 2) == 0
    even = lax.rem(lax.axis_index("gx"), 2) == 0
    near_row, far_row = jnp.where(even, 0, 5), jnp.where(even, 5, 0)
    has_far = inner(lax.axis_index("gx"))
    flat = rim.reshape(4 * 32 * 8, 128)
    for ch in range(4):
        for row in range(3):
            flat[pl.ds(256 * ch + near_row + row, 32, stride=8), :] = x_near[3 * ch + row]
            flat[pl.ds(256 * ch + far_row + row, 32, stride=8), :] = jnp.where(has_far, x_far[3 * ch + row], 0.0)

    def some(low):
        for ch in range(4):
            right, left = pack_planes(lambda z: rim[ch, z], low, (8, 128))
            for at, right, left in (
                (slice(0, 16), to_right[ch, low], to_left[ch, low]),
                (slice(16, 24), right, left),
            ):
                near[ch, low, at, :] = jnp.where(first_core, right, left)
                far[ch, low, at, :] = jnp.where(first_core, left, right)

    loop(4, some)


def pack_planes(plane, low, shape):
    group = iota(shape, 1) // 16
    right = left = jnp.zeros(shape, F32)
    for h in range(8):
        moved = roll(plane(4 * h + low), 16 * h + 16)
        right = jnp.where(group == h, moved, right)
        left = jnp.where(group == (h + 1) % 8, moved, left)
    return right, left


def edge_columns(plane, z, shape):
    lane = iota(shape, 1)
    value = jnp.zeros(shape, F32)
    for half in range(2):
        source = plane(z + 16 * half)
        base = 64 * half
        value = jnp.where((lane >= base) & (lane < base + 7), roll(source, base + 7), value)
        value = jnp.where((lane >= base + 57) & (lane < base + 64), roll(source, base + 57), value)
    return value


def six_of(ref, lead, z, first, count):
    own = ref[(*lead, z, pl.ds(first, count), slice(None))]
    return own, (
        ref[(*lead, z, pl.ds(first - 1, count), slice(None))],
        ref[(*lead, z, pl.ds(first + 1, count), slice(None))],
        roll(own, 1),
        roll(own, -1),
        ref[(*lead, z - 1, pl.ds(first, count), slice(None))],
        ref[(*lead, z + 1, pl.ds(first, count), slice(None))],
    )


def block_of(ref, lead, z, planes, first, count):
    rows = span(first, count)
    own = [ref[(*lead, z + k, rows, slice(None))] for k in range(-1, planes + 1)]
    result = []
    for k in range(planes):
        value = own[k + 1]
        six = (
            ref[(*lead, z + k, span(first - 1, count), slice(None))],
            ref[(*lead, z + k, span(first + 1, count), slice(None))],
            roll(value, 1),
            roll(value, -1),
            own[k],
            own[k + 2],
        )
        result.append((value, six))
    return result


def face(total):
    return jnp.where(total < 0.5, 1.0, jnp.where(total < 1.5, BETWEEN, 0.1))


def fine_weights(own, six, omega):
    faces = [face(own + other) for other in six]
    diag = (faces[0] + faces[1]) + (faces[2] + faces[3]) + (faces[4] + faces[5])
    gain = omega * recip(diag)
    return [gain * value for value in faces], 1.25 * diag


def fine_sweep(w, f, own, six):
    return (0.2 * own + (w[2 * f + 1] - w[2 * f])) + weigh(w, six)


def fine_left(w, f, own, six, diag):
    return (((w[2 * f + 1] - w[2 * f]) - 0.8 * own) + weigh(w, six)) * diag


def fine_sweeps(planes, windows, start, share, one, two, weights, diags, halves, omega, wrap, keep):
    first, count = windows[0]

    def first_sweep(step):
        z = 4 * step
        w = []
        for k, (own, six) in enumerate(block_of(share, (), z + 1, 4, first, count)):
            now, diag = fine_weights(own, six, omega)
            diags[z + k, span(first, count), :] = diag
            for i in range(6):
                weights[i, z + k, span(first, count), :] = now[i]
            w.append(now)
        for f in range(3):
            for k, (own, six) in enumerate(block_of(start, (f,), z + 1, 4, first, count)):
                one[f, z + k + 1, span(first, count), :] = fine_sweep(w[k], f, own, six)

    loop(planes // 4, first_sweep)
    wrap(one)
    second, count2 = windows[1]

    def second_sweep(step):
        z = 4 * step
        w = [[weights[i, z + k, span(second, count2), :] for i in range(6)] for k in range(4)]
        for f in range(3):
            for k, (own, six) in enumerate(block_of(one, (f,), z + 1, 4, second, count2)):
                two[f, z + k + 1, span(second, count2), :] = fine_sweep(w[k], f, own, six)

    loop(planes // 4, second_sweep)
    wrap(two)

    def residual(step):
        z = 4 * step
        w = [[weights[i, z + k, 8:24, :] for i in range(6)] for k in range(4)]
        diag = [diags[z + k, 8:24, :] for k in range(4)]
        for f in range(3):
            values = []
            for k, (own, six) in enumerate(block_of(two, (f,), z + 1, 4, 8, 16)):
                if keep is not None:
                    keep[f, z + k] = own
                values.append(fine_left(w[k], f, own, six, diag[k]))
            for pair in range(2):
                halves[f, 2 * step + pair] = values[2 * pair] + values[2 * pair + 1]
        for pair in range(2):
            at = z + 2 * pair + 1
            halves[3, 2 * step + pair] = share[at, 8:24, :] + share[at + 1, 8:24, :]

    loop(planes // 4, residual)


def own_kernel(own, one, two, halves, to_right, to_left, edges, held, weights, diags):
    zero = jnp.zeros((32, 128), F32)
    for z in (0, 33):
        for ch in range(4):
            held[ch, z] = zero
        for ref in (one, two):
            for f in range(3):
                ref[f, z] = zero

    def plane(z):
        for ch in range(4):
            held[ch, z + 1, 8:24, :] = own[ch, z]

    loop(32, plane, 4)
    fine_sweeps(
        32, [(8, 16)] * 2, held, held.at[3], one, two, weights, diags, halves, 0.8, lambda ref: None, None
    )

    def some(low):
        for ch in range(4):
            to_right[ch, low], to_left[ch, low] = pack_planes(lambda z: own[ch, z], low, (16, 128))

    loop(4, some)

    def edge(z):
        for ch in range(4):
            edges[ch, z] = edge_columns(lambda at: own[ch, at], z, (16, 128))

    loop(16, edge, 2)


def rows_edge_kernel(own, rim, own_one, own_two, own_halves, two, packed, edges, start, one, weights, diags, halves, pooled):
    gx = lax.axis_index("gx")
    zero = jnp.zeros((24, 128), F32)
    for z in (0, 33):
        for ch in range(4):
            start[ch, z] = zero
        for ref in (one, two):
            for f in range(3):
                ref[f, z] = zero

    def fill(z):
        for ch in range(4):
            start[ch, z + 1, 0:8, :] = own[ch, z, 8:16, :]
            start[ch, z + 1, 8:16, :] = rim[ch, z]
            start[ch, z + 1, 16:24, :] = own[ch, z, 0:8, :]
        for f in range(3):
            for ref, source in ((one, own_one), (two, own_two)):
                ref[f, z + 1, 0:8, :] = source[f, z + 1, 16:24, :]
                ref[f, z + 1, 16:24, :] = source[f, z + 1, 8:16, :]

    loop(32, fill, 4)
    upper = iota((8, 128), 0) < 4

    def both(ref, lead, step, shift=0):
        high = ref[(*lead, span(8 - step + shift, 8), slice(None))]
        low = ref[(*lead, span(8 + step + shift, 8), slice(None))]
        return jnp.where(upper, high, low)

    def block_both(ref, f, z, step):
        own = [both(ref, (f, z + k), step) for k in range(-1, 5)]
        result = []
        for k in range(4):
            value = own[k + 1]
            low, high = both(ref, (f, z + k), step, -1), both(ref, (f, z + k), step, 1)
            result.append((value, (low, high, roll(value, 1), roll(value, -1), own[k], own[k + 2])))
        return result

    def put(ref, f, z, step, value):
        ref[f, z, pl.ds(8 - step, 4), :] = value[0:4]
        ref[f, z, pl.ds(12 + step, 4), :] = value[4:8]

    row = iota((16, 128), 0) + 5
    low, high = jnp.where(gx > 0, 1, 0), jnp.where(gx < NX - 1, 1, 0)
    inside = jnp.where((row >= 8) & (row < 12), high, jnp.where((row >= 12) & (row < 16), low, 1))
    omega = 0.8 * inside.astype(F32)

    def weigh_all(step):
        z = 4 * step
        for k, (value, six) in enumerate(block_of(start, (3,), z + 1, 4, 5, 16)):
            w, diag = fine_weights(value, six, omega)
            diags[z + k, span(5, 16), :] = diag
            for i in range(6):
                weights[i, z + k, span(5, 16), :] = w[i]

    loop(8, weigh_all)

    for step, source, target in ((1, start, one), (2, one, two)):

        def sweep(block):
            z = 4 * block
            w = [[both(weights, (i, z + k), step) for i in range(6)] for k in range(4)]
            for f in range(3):
                for k, (value, six) in enumerate(block_both(source, f, z + 1, step)):
                    put(target, f, z + k + 1, step, fine_sweep(w[k], f, value, six))

        loop(8, sweep)

    sub = iota((8, 128), 0)

    def residual(block):
        z = 4 * block
        w = [[both(weights, (i, z + k), 3) for i in range(6)] for k in range(4)]
        diag = [both(diags, (z + k,), 3) for k in range(4)]
        for f in range(3):
            values = []
            for k, (value, six) in enumerate(block_both(two, f, z + 1, 3)):
                values.append(fine_left(w[k], f, value, six, diag[k]))
            for k in range(2):
                pair = 2 * block + k
                value = values[2 * k] + values[2 * k + 1]
                halves[f, pair, 0:8, :] = jnp.where(sub < 3, roll(value, 3, 0), own_halves[f, pair, 0:8, :])
                halves[f, pair, 8:16, :] = jnp.where(sub >= 5, roll(value, 5, 0), own_halves[f, pair, 8:16, :])
        for k in range(2):
            halves[3, 2 * block + k] = own_halves[3, 2 * block + k]

    loop(8, residual)
    source, target = iota((128, 128), 0), iota((128, 128), 1)
    value = None
    for half in range(2):
        pool = jnp.where(source // 2 + 64 * half == target, 0.125, 0.0)
        part = dot(halves[:, 8 * half : 8 * half + 8].reshape(512, 128), pool)
        value = part if value is None else value + part
    pooled[...] = value
    packed[...] = (pooled[pl.ds(0, 256, stride=2), :] + pooled[pl.ds(1, 256, stride=2), :]).reshape(4, 8, 8, 128)

    def edge(z):
        for ch in range(4):
            edges[ch, z] = edge_columns(lambda at: rim[ch, at], z, (8, 128))

    loop(16, edge, 2)


def rim_kernel(
    edges, edges_rim, near, far, field, packed,
    start, share, one, two, weights, diags, halves, pooled,
):
    gx, gy = lax.axis_index("gx"), lax.axis_index("gy")
    lane = iota((24, 128), 1)
    part = lane % 64
    is_after = (part >= 7) & (part < 22)
    is_before = (part >= 42) & (part < 57)
    first_core = lax.rem(gy, 2) == 0

    def unpack(low):
        for ch in range(4):
            target = start.at[ch] if ch < 3 else share
            from_near, from_far = near[ch, low], jnp.where(inner(gy), far[ch, low], 0.0)
            from_right = jnp.where(first_core, from_near, from_far)
            from_left = jnp.where(first_core, from_far, from_near)
            for h in range(4):
                z = 4 * h + low
                after_y = roll(from_right, 7 - 16 * (h + 1))
                before_y = roll(from_left, 41 - 16 * h)
                own = jnp.concatenate([edges[ch, z], edges_rim[ch, z]], axis=0)
                value = jnp.where(is_after, after_y, jnp.where(is_before, before_y, own))
                target[z + 1, 8:24, :] = value[0:16]
                target[z + 1, 0:8, :] = value[16:24]
                target[z + 1, 24:32, :] = value[16:24]

    loop(4, unpack)

    half_of = iota((32, 128), 1)

    def wrap_one(ref):
        ref[0] = jnp.where(half_of >= 64, roll(ref[16], 64), 0.0)
        ref[17] = jnp.where(half_of < 64, roll(ref[1], 64), 0.0)

    def wrap(ref):
        for f in range(3):
            wrap_one(ref.at[f])

    wrap_one(share)
    wrap(start)
    row = iota((24, 128), 0) + 6
    low, high = jnp.where(gx > 0, 1, 0), jnp.where(gx < NX - 1, 1, 0)
    inside_x = jnp.where(row < 8, low, jnp.where(row >= 24, high, 1))
    inside_y = jnp.where(
        part < 32,
        jnp.where((part < 7) | (gy < NY - 1), 1, 0),
        jnp.where((part >= 57) | (gy > 0), 1, 0),
    )
    omega = 0.8 * (inside_x * inside_y).astype(F32)
    fine_sweeps(
        16, [(6, 24), (7, 24)], start, share, one, two, weights, diags, halves, omega, wrap, field
    )

    source, target = iota((128, 128), 0), iota((128, 128), 1)
    spot = source % 64
    column = jnp.where(spot < 32, 121 + spot, 71 + spot) // 2
    to = jnp.where(spot < 32, column - 62, column - 48)
    keep = ((spot < 32) & (to >= 0) & (to < 9)) | ((spot >= 32) & (to >= 9) & (to < 18))
    mixed = halves[...].reshape(4, 4, 2, 16, 128)
    value = None
    for odd in range(2):
        pool = jnp.where(keep & (to + 64 * odd + 32 * (source // 64) == target), 0.125, 0.0)
        part = dot(mixed[:, :, odd].reshape(256, 128), pool)
        value = part if value is None else value + part
    pooled[...] = value
    packed[...] = (pooled[pl.ds(0, 128, stride=2), :] + pooled[pl.ds(1, 128, stride=2), :]).reshape(4, 4, 8, 128)


def base_kernel(two, rim, e_one, e_two, base, wide, spread):
    copy = jnp.where(iota((128, 128), 0) == iota((128, 128), 1) // 2, 1.0, 0.0)
    value = dot(e_two[...].reshape(192, 128), copy)
    for block in range(24):
        rows = value[8 * block : 8 * block + 4, :]
        wide[pl.ds(8 * block, 4, stride=2), :] = rows
        wide[pl.ds(8 * block + 1, 4, stride=2), :] = rows
    value = e_one[...].reshape(24, 2, 8, 128) + wide[...].reshape(24, 1, 8, 128)
    value = dot(value.reshape(384, 128), copy)
    flat = spread.reshape(768, 128)
    for block in range(48):
        rows = value[8 * block : 8 * block + 8, :]
        flat[pl.ds(16 * block, 8, stride=2), :] = rows
        flat[pl.ds(16 * block + 1, 8, stride=2), :] = rows
    lane = iota((16, 128), 1)

    def pair(k):
        for f in range(3):
            for z in (2 * k, 2 * k + 1):
                value = rim[f, z]
                for half in range(2):
                    low = roll(value, -57 - 64 * half)
                    high = roll(value, 121 - 64 * half)
                    at = z + 16 * half
                    own = jnp.concatenate([two[f, at + 1, 16:24, :], two[f, at + 1, 0:8, :]], axis=0)
                    own = jnp.where(lane < 3, low, jnp.where(lane >= 125, high, own))
                    base[f, at] = own + spread[f, k + 8 * half]

    loop(8, pair, 1)


def resist(share):
    return recip(1.0 - 0.9 * share)


def level_weights(own, six, omega):
    faces = [2.0 * recip(own + other) for other in six]
    diag = (faces[0] + faces[1]) + (faces[2] + faces[3]) + (faces[4] + faces[5])
    gain = omega * recip(diag)
    return gain, [gain * w for w in faces], diag


def middle_kernel(
    main, main_near, main_far, rim, rim_near, rim_far, sent, e_one, e_two,
    share, rest, rhs, first, second, weights, diags, halves, pooled,
    rest2, first2, second2, rhs2, share2, weights2,
):
    gx, gy = lax.axis_index("gx"), lax.axis_index("gy")
    low_x, high_x = jnp.where(gx > 0, 1, 0), jnp.where(gx < NX - 1, 1, 0)
    low_y, high_y = jnp.where(gy > 0, 1, 0), jnp.where(gy < NY - 1, 1, 0)

    for f in range(3):
        for ref in (first, second):
            ref[f, 0] = jnp.zeros((32, 128), F32)
            ref[f, 17] = jnp.zeros((32, 128), F32)
    for z in (0, 17):
        rest[z] = jnp.ones((32, 128), F32)
    lane = iota((8, 128), 1)
    even = lax.rem(gx, 2) == 0
    near_row, far_row = jnp.where(even, 16, 0), jnp.where(even, 0, 16)
    starts = (pl.multiple_of(near_row, 8), pl.multiple_of(far_row, 8), 8)

    sources = zip(starts, ((main_near, rim_near), (main_far, rim_far), (main, rim)))
    sources = list(sources)
    has_far = inner(gx)

    def fill(q):
        for odd in range(2):
            for half in range(2):
                z = 2 * q + odd + 8 * half
                base = 64 * odd + 32 * half
                for at, (middle, outer) in sources:
                    for ch in range(4):
                        edge, body = outer[ch, q], middle[ch, 2 * q + odd]
                        if outer is rim_far:
                            edge, body = jnp.where(has_far, edge, 0.0), jnp.where(has_far, body, 0.0)
                        value = jnp.where(lane < 62, roll(body, 64 * half), roll(edge, 62 - base))
                        value = jnp.where((lane >= 96) | (lane < 2), roll(edge, 112 - base), value)
                        if ch < 3:
                            rhs[ch, z, pl.ds(at, 8), :] = value
                        else:
                            share[z, pl.ds(at, 8), :] = value
                            rest[z + 1, pl.ds(at, 8), :] = resist(value)
                rest[z + 1, 24:32, :] = jnp.ones((8, 128), F32)

    loop(4, fill)

    row, lane = iota((24, 128), 0) + 1, iota((24, 128), 1)
    in_x = jnp.where(row < 8, low_x, jnp.where(row >= 16, high_x, 1))
    in_y = jnp.where(lane < 64, 1, jnp.where(lane < 96, high_y, low_y))
    omega = 0.8 * (in_x * in_y).astype(F32)

    def start(step):
        z = 4 * step
        for k, (own, six) in enumerate(block_of(rest, (), z + 1, 4, 1, 24)):
            gain, w, diag = level_weights(own, six, omega)
            for i in range(6):
                weights[i, z + k, span(1, 24), :] = w[i]
            diags[z + k, span(1, 24), :] = (1.25 * 0.25) * diag
            for f in range(3):
                first[f, z + k + 1, span(1, 24), :] = (4.0 * gain) * rhs[f, z + k, span(1, 24), :]

    loop(4, start)

    def sweep(step):
        z = 4 * step
        w = [[weights[i, z + k, span(3, 24), :] for i in range(6)] for k in range(4)]
        for f in range(3):
            for k, (own, six) in enumerate(block_of(first, (f,), z + 1, 4, 3, 24)):
                second[f, z + k + 1, span(3, 24), :] = 1.2 * own + weigh(w[k], six)

    loop(4, sweep)

    def left(step):
        z = 4 * step
        w = [[weights[i, z + k, span(4, 16), :] for i in range(6)] for k in range(4)]
        diag = [diags[z + k, span(4, 16), :] for k in range(4)]
        for f in range(3):
            values = []
            for k, (own, six) in enumerate(block_of(second, (f,), z + 1, 4, 4, 16)):
                change = (first[f, z + k + 1, span(4, 16), :] - 0.8 * own) + weigh(w[k], six)
                values.append(change * diag[k])
                e_one[f, z + k] = second[f, z + k + 1, 8:16, :]
            for k in range(2):
                halves[f, 2 * step + k, 0:16, :] = values[2 * k] + values[2 * k + 1]
                halves[f, 2 * step + k, 16:24, :] = jnp.zeros((8, 128), F32)
        for k in range(2):
            halves[3, 2 * step + k] = share[z + 2 * k] + share[z + 2 * k + 1]

    loop(4, left)

    source, target = iota((128, 128), 0), iota((128, 128), 1)
    pool = jnp.where(source // 2 + jnp.where(source >= 96, 64, 0) == target, 0.125, 0.0)
    pooled[...] = dot(halves[...].reshape(4 * 8 * 24, 128), pool)
    for z in (0, 9):
        rest2[z] = jnp.ones((24, 128), F32)
        for f in range(3):
            first2[f, z] = jnp.zeros((24, 128), F32)
            second2[f, z] = jnp.zeros((24, 128), F32)
    for z in range(8):
        for f in range(3):
            base = (f * 8 + z) * 24
            rhs2[f, z] = pooled[pl.ds(base, 8, stride=2), :] + pooled[pl.ds(base + 1, 8, stride=2), :]
        base = (3 * 8 + z) * 24
        value = pooled[pl.ds(base + 2, 8, stride=2), :] + pooled[pl.ds(base + 3, 8, stride=2), :]
        rest2[z + 1, 0:8, :] = resist(value)
        value = pooled[pl.ds(base + 8, 8, stride=2), :] + pooled[pl.ds(base + 9, 8, stride=2), :]
        rest2[z + 1, 3:11, :] = resist(value)
        share2[z] = value

    row, lane = iota((8, 128), 0) + 1, iota((8, 128), 1)
    in_x = jnp.where(row < 3, low_x, jnp.where(row >= 7, high_x, 1))
    in_y = jnp.where(lane < 32, 1, jnp.where(lane < 96, high_y, low_y))
    omega2 = 0.8 * (in_x * in_y).astype(F32)

    for z, (own, six) in enumerate(block_of(rest2, (), 1, 8, 1, 8)):
        gain, w, diag = level_weights(own, six, omega2)
        for i in range(6):
            weights2[i, z, span(1, 8), :] = w[i]
        weights2[6, z, span(1, 8), :] = (1.25 * 0.0625) * diag
        for f in range(3):
            first2[f, z + 1, span(1, 8), :] = (16.0 * gain) * rhs2[f, z]
    w = [[weights2[i, z, span(2, 8), :] for i in range(6)] for z in range(8)]
    for f in range(3):
        for z, (own, six) in enumerate(block_of(first2, (f,), 1, 8, 2, 8)):
            second2[f, z + 1, span(2, 8), :] = 1.2 * own + weigh(w[z], six)
    w = [[weights2[i, z, span(3, 8), :] for i in range(7)] for z in range(8)]
    own_row = iota((8, 128), 0) < 4
    parts = [{} for pair in range(4)]
    for f in range(3):
        for z, (own, six) in enumerate(block_of(second2, (f,), 1, 8, 3, 8)):
            e_two[f, z] = own
            change = (first2[f, z + 1, span(3, 8), :] - 0.8 * own) + weigh(w[z], six)
            value = jnp.where(own_row, change * w[z][6], 0.0)
            sums = parts[z // 2]
            sums[f] = value if z % 2 == 0 else sums[f] + value
    for z in range(8):
        value = jnp.where(own_row, share2[z], 0.0)
        sums = parts[z // 2]
        sums[3] = value if z % 2 == 0 else sums[3] + value

    pool = jnp.where((source < 32) & (source // 2 == target % 16), 0.125, 0.0)
    rows = jnp.concatenate([parts[pair][ch] for ch in range(4) for pair in range(4)], axis=0)
    spread = dot(rows, pool)
    at, to = iota((32, 128), 0), iota((32, 128), 1)
    keep = (at // 8 == to // 32) & ((at % 8) // 2 == (to // 16) % 2)
    result = jnp.concatenate(
        [
            jnp.sum(jnp.where(keep, spread[32 * ch : 32 * ch + 32], 0.0), axis=0, keepdims=True)
            for ch in range(4)
        ],
        axis=0,
    )
    for copy in range(CHIPS):
        sent[copy] = result


def swap_blocks(x):
    sub, group = iota((8, 128), 0), iota((8, 128), 1) // 16
    for bit in (4, 2, 1):
        up = roll(roll(x, -bit, 0), 16 * bit)
        down = up if bit == 4 else roll(roll(x, bit, 0), -16 * bit)
        sub_set, group_set = (sub & bit) != 0, (group & bit) != 0
        x = jnp.where(sub_set == group_set, x, jnp.where(sub_set, down, up))
    return x


def top_kernel(
    mine, other, base, out,
    natural, first, second, four, weights, diags, lefts, final, sems,
):
    gx, gy = lax.axis_index("gx"), lax.axis_index("gy")
    first_core = lax.rem(gy, 2) == 0
    lane, sub = iota((16, 128), 1), iota((16, 128), 0)
    cells = [(z, x, half) for z in range(4) for x in range(2) for half in range(2)]

    def lay(g):
        for ch in range(4):
            rows = pl.ds(32 * g + ch, 8, stride=4)
            pair = mine[rows, :], other[rows, :]
            natural[ch, 0, pl.ds(pl.multiple_of(8 * g, 8), 8), :] = swap_blocks(
                jnp.where(first_core, pair[0], pair[1])
            )
            natural[ch, 1, pl.ds(pl.multiple_of(8 * g, 8), 8), :] = swap_blocks(
                jnp.where(first_core, pair[1], pair[0])
            )

    loop(16, lay, 4)
    flat = natural.reshape(1024, 128)

    def plane(ch, z, x, half):
        return flat[pl.ds((ch * 2 + half) * 128 + z * 2 + x, 16, stride=8), :]

    def neighbours(at, z, x, half, outside):
        own, other = at(z, x, half), at(z, 1 - x, half)
        beside = at(z, x, 1 - half)
        shifted = roll(other, 1 if x == 0 else -1, 0)
        low, high = (shifted, other) if x == 0 else (other, shifted)
        left, right = roll(own, 1), roll(own, -1)
        left = jnp.where(lane % 16 == 0, roll(beside, 1 if half == 0 else -15), left)
        right = jnp.where(lane % 16 == 15, roll(beside, 15 if half == 0 else -1), right)
        down = at(z - 1, x, half) if z > 0 else outside
        up = at(z + 1, x, half) if z < 3 else outside
        return own, [low, high, left, right, down, up]

    def edge_masks(x, half):
        return [
            sub > 0 if x == 0 else None,
            sub < 15 if x == 1 else None,
            lane > 0 if half == 0 else None,
            lane < 127 if half == 1 else None,
            None,
            None,
        ]

    def key(z, x, half):
        return (z * 2 + x) * 2 + half

    shares = {c: plane(3, *c) for c in cells}
    rests = {c: resist(shares[c]) for c in cells}
    ones, zeros = jnp.ones((16, 128), F32), jnp.zeros((16, 128), F32)
    for z, x, half in cells:
        own, six = neighbours(lambda *c: rests[c], z, x, half, ones)
        masks = edge_masks(x, half)
        six = [s if m is None else jnp.where(m, s, 1.0) for s, m in zip(six, masks)]
        gain, w, diag = level_weights(own, six, 0.8)
        at = key(z, x, half)
        for i in range(6):
            weights[i, at] = w[i] if masks[i] is None else jnp.where(masks[i], w[i], 0.0)
        diags[at] = (1.25 * 0.25**3) * diag
        for f in range(3):
            first[f, at] = (64.0 * gain) * plane(f, z, x, half)

    for z, x, half in cells:
        at = key(z, x, half)
        w = [weights[i, at] for i in range(6)]
        for f in range(3):
            own, six = neighbours(lambda *c: first[f, key(*c)], z, x, half, zeros)
            second[half, f, z * 2 + x] = 1.2 * own + weigh(w, six)

    for z4 in range(2):
        for half in range(2):
            sums = [None] * 4
            for z in (2 * z4, 2 * z4 + 1):
                for x in range(2):
                    at = key(z, x, half)
                    w = [weights[i, at] for i in range(6)]
                    diag = diags[at]
                    for f in range(3):
                        own, six = neighbours(
                            lambda c, d, e: second[e, f, c * 2 + d], z, x, half, zeros
                        )
                        value = ((first[f, at] - 0.8 * own) + weigh(w, six)) * diag
                        sums[f] = value if sums[f] is None else sums[f] + value
                    share = shares[z, x, half]
                    sums[3] = share if sums[3] is None else sums[3] + share
            for ch in range(4):
                lefts[ch, z4, :, 128 * half : 128 * half + 128] = sums[ch]

    source = iota((256, 128), 0)
    column = ((source % 128) // 16) * 16 + (source // 128) * 8 + (source % 16) // 2
    pool = jnp.where(column == iota((256, 128), 1), 0.125, 0.0)
    level = dot(lefts[...].reshape(128, 256), pool)

    def coarsest(ch, z):
        return level[(ch * 2 + z) * 16 : (ch * 2 + z) * 16 + 16, :]

    masks = [sub > 0, sub < 15, lane > 0, lane < 127]
    resists = [resist(coarsest(3, z)) for z in range(2)]
    gains, ws, ds = [], [], []
    for z in range(2):
        own, other = resists[z], resists[1 - z]
        six = [roll(own, 1, 0), roll(own, -1, 0), roll(own, 1), roll(own, -1)]
        six = [jnp.where(m, s, 1.0) for m, s in zip(masks, six)] + [other, ones]
        gain, w, diag = level_weights(own, six, 0.8)
        gains.append(gain)
        ds.append(diag)
        ws.append([jnp.where(m, v, 0.0) for m, v in zip(masks, w)] + [w[4]])
    whole = jnp.sum(ds[0] + ds[1], keepdims=True)

    def around(values, z):
        own, other = values[z], values[1 - z]
        return weigh(ws[z], (roll(own, 1, 0), roll(own, -1, 0), roll(own, 1), roll(own, -1), other))

    begin = [[256.0 * gains[z] * coarsest(f, z) for z in range(2)] for f in range(3)]
    values = begin
    for step in range(5):
        values = [
            [(0.2 * values[f][z] + begin[f][z]) + around(values[f], z) for z in range(2)] for f in range(3)
        ]
    for f in range(3):
        change = [(begin[f][z] - 0.8 * values[f][z]) + around(values[f], z) for z in range(2)]
        total = jnp.sum(1.25 * (change[0] * ds[0] + change[1] * ds[1]), keepdims=True)
        for z in range(2):
            four[2 * f + z] = values[f][z] + total / whole

    copy = jnp.where(iota((128, 128), 0) == iota((128, 128), 1) // 2, 1.0, 0.0)
    rows = four.reshape(96, 128)[pl.ds(gx, 6, stride=16), :]
    rows = jnp.concatenate([jnp.broadcast_to(rows[i : i + 1], (4, 128)) for i in range(6)], axis=0)
    three = dot(turn(rows, -8 * gy), copy)
    flat = second.reshape(768, 128)
    halves = [flat[pl.ds(gx + 384 * half, 24, stride=16), :] for half in range(2)]
    three = three + turn(jnp.where(first_core, halves[0], halves[1]), -16 * lax.div(gy, 2))

    copy = jnp.where(iota((128, 128), 0) == iota((128, 128), 1) // 8, 1.0, 0.0)
    three = dot(three, copy)
    copies = []
    for f in range(3):
        for z in range(4):
            for x in range(2):
                at = f * 8 + z * 2 + x
                value = jnp.broadcast_to(three[at : at + 1], (8, 128))
                for k in range(8 * z, 8 * z + 8):
                    final[f, k, 8 * x : 8 * x + 8, :] = base[f, k, 8 * x : 8 * x + 8, :] + value
            if z % 2 == 1:
                part = (f, pl.ds(8 * z - 8, 16))
                copy = pltpu.make_async_copy(final.at[part], out.at[part], sems.at[len(copies)])
                copy.start()
                copies.append(copy)
    for copy in copies:
        copy.wait()


def local(labels, guess):
    swap_near = [(i, i ^ 1) for i in range(NY)]
    far_x, far_y = [], []
    for x in range(NX):
        for y in range(NY):
            across_x, across_y = x + 1 if x % 2 else x - 1, y + 1 if y % 2 else y - 1
            to = (across_x, y) if 0 <= across_x < NX else (x, y ^ 1)
            far_x.append((x * NY + y, to[0] * NY + to[1]))
            to = (x, across_y) if 0 <= across_y < NY else (x ^ 1, y)
            far_y.append((x * NY + y, to[0] * NY + to[1]))
    both = ("gx", "gy")
    to_near, to_far, own = call(
        rows_kernel,
        [(12, 32, 128)] * 2 + [(4, 32, 16, 128)],
        [pltpu.VMEM((32, 16, 128), jnp.int32), pltpu.SemaphoreType.DMA((4,))],
        in_specs=[ANY, ANY],
    )(pltpu.with_memory_space_constraint(guess, pltpu.HBM), pltpu.with_memory_space_constraint(labels, pltpu.HBM))
    from_near = lax.ppermute(to_near, "gx", swap_near)
    from_far = lax.ppermute(to_far, both, far_x)
    own_one, own_two, halves, to_right, to_left, edges = call(
        own_kernel,
        [(3, 34, 32, 128)] * 2 + [(4, 16, 16, 128)] + [(4, 4, 16, 128)] * 2 + [(4, 16, 16, 128)],
        [(4, 34, 32, 128), (6, 32, 32, 128), (32, 32, 128)],
        flops=20_000_000,
    )(own)
    to_near, to_far, rim_rows = call(pack_kernel, [(4, 4, 24, 128)] * 2 + [(4, 32, 8, 128)], [])(
        to_right, to_left, from_near, from_far
    )
    from_far = lax.ppermute(to_far, both, far_y)
    from_near = lax.ppermute(to_near, "gy", swap_near)
    two, main, edges_rim = call(
        rows_edge_kernel,
        [(3, 34, 24, 128), (4, 8, 8, 128), (4, 16, 8, 128)],
        [(4, 34, 24, 128), (3, 34, 24, 128), (6, 32, 24, 128), (32, 24, 128)]
        + [(4, 16, 16, 128), (512, 128)],
        flops=10_000_000,
    )(own, rim_rows, own_one, own_two, halves)
    main_near = lax.ppermute(main, "gx", swap_near)
    main_far = lax.ppermute(main, both, far_x)
    rim, rim_one = call(
        rim_kernel,
        [(3, 16, 16, 128), (4, 4, 8, 128)],
        [(3, 18, 32, 128), (18, 32, 128)]
        + [(3, 18, 32, 128)] * 2
        + [(6, 16, 32, 128), (16, 32, 128)]
        + [(4, 8, 16, 128), (256, 128)],
        flops=10_000_000,
    )(edges, edges_rim, from_near, from_far)
    rim_near = lax.ppermute(rim_one, "gx", swap_near)
    rim_far = lax.ppermute(rim_one, both, far_x)
    sent, e_one, e_two = call(
        middle_kernel,
        [(CHIPS, 4, 128), (3, 16, 8, 128), (3, 8, 8, 128)],
        [(16, 24, 128), (18, 32, 128), (3, 16, 32, 128), (3, 18, 32, 128), (3, 18, 32, 128)]
        + [(6, 16, 32, 128), (16, 32, 128), (4, 8, 24, 128), (768, 128)]
        + [(10, 24, 128), (3, 10, 24, 128), (3, 10, 24, 128), (3, 8, 8, 128), (8, 8, 128)]
        + [(7, 8, 16, 128)],
    )(main, main_near, main_far, rim_one, rim_near, rim_far)
    groups = [[i for i in range(NX * NY) if i % 2 == core] for core in range(2)]
    mine = lax.all_to_all(
        sent, ("gx", "gy"), split_axis=0, concat_axis=0, axis_index_groups=groups, tiled=True
    )
    (base,) = call(base_kernel, [(3, 32, 16, 128)], [(192, 128), (3, 16, 16, 128)])(two, rim, e_one, e_two)
    other = lax.ppermute(mine, "gy", swap_near)
    (out,) = call(
        top_kernel,
        [(3, 32, 16, 128)],
        [(4, 2, 128, 128), (3, 16, 16, 128), (2, 3, 8, 16, 128), (6, 16, 128), (6, 16, 16, 128)]
        + [(16, 16, 128), (4, 2, 16, 256), (3, 32, 16, 128), pltpu.SemaphoreType.DMA((6,))],
        out_specs=[ANY],
    )(mine.reshape(512, 128), other.reshape(512, 128), base)
    return out


def solution(mesh):
    return jax.shard_map(
        local,
        mesh=mesh,
        in_specs=(P(None, "gx", "gy"), P(None, None, "gx", "gy")),
        out_specs=P(None, None, "gx", "gy"),
        check_vma=False,
    )
```

```python
import jax
import jax.numpy as jnp
from jax import lax
from jax.experimental import pallas as pl
from jax.experimental.pallas import tpu as pltpu
from jax.sharding import PartitionSpec as P


F32 = jnp.float32
NX, NY, CHIPS = 16, 16, 128
BETWEEN = 2.0 * 0.1 / 1.1
ANY = pl.BlockSpec(memory_space=pltpu.HBM)


def dot(a, b):
    return jnp.dot(a, b, precision=lax.Precision.HIGHEST, preferred_element_type=F32)


def dot_exact(a, b):
    high = a.astype(jnp.bfloat16)
    low = (a - high.astype(F32)).astype(jnp.bfloat16)
    b = b.astype(jnp.bfloat16)
    return jnp.dot(
        jnp.concatenate([high, low], axis=1), jnp.concatenate([b, b], axis=0), preferred_element_type=F32
    )


def iota(shape, dim):
    return lax.broadcasted_iota(jnp.int32, shape, dim)


def roll(x, shift, axis=1):
    shift = shift % x.shape[axis]
    return x if shift == 0 else pltpu.roll(x, shift, axis)


def turn(x, shift):
    return pltpu.roll(x, lax.rem(shift + 256, 128), 1)


def recip(x):
    guess = pl.reciprocal(x, approx=True)
    return guess * (2.0 - x * guess)


def inner(index):
    return (index > 0) & (index < 15)


def call(kernel, outs, scratch, flops=1_000_000, **kw):
    return pl.pallas_call(
        kernel,
        out_shape=[jax.ShapeDtypeStruct(s, F32) for s in outs],
        scratch_shapes=[pltpu.VMEM(s, F32) if isinstance(s, tuple) else s for s in scratch],
        compiler_params=pltpu.CompilerParams(vmem_limit_bytes=32 * 1024 * 1024),
        cost_estimate=pl.CostEstimate(flops=flops, bytes_accessed=4_000_000, transcendentals=0),
        **kw,
    )


def loop(count, body, unroll=1):
    def step(i, carry):
        body(i)
        return carry

    lax.fori_loop(0, count, step, 0, unroll=unroll)


def weigh(weights, values):
    parts = [w * v for w, v in zip(weights, values)]
    while len(parts) > 1:
        parts = [sum(parts[i : i + 2][1:], parts[i]) for i in range(0, len(parts), 2)]
    return parts[0]


def rows_kernel(guess, labels, near, far, own, phase, sems):
    even = lax.rem(lax.axis_index("gx"), 2) == 0
    near_row, far_row = jnp.where(even, 13, 0), jnp.where(even, 0, 13)
    copies = [pltpu.make_async_copy(labels, phase, sems.at[3])]
    for f in range(3):
        copies.append(pltpu.make_async_copy(guess.at[f], own.at[f], sems.at[f]))
    for copy in copies:
        copy.start()
    copies[0].wait()
    own[3] = jnp.where(phase[...] == 1, 0.0, 1.0).astype(F32)
    flat = own.reshape(4 * 32 * 16, 128)
    for ch in (3, 0, 1, 2):
        if ch < 3:
            copies[ch + 1].wait()
        for row in range(3):
            near[3 * ch + row] = flat[pl.ds(512 * ch + near_row + row, 32, stride=16), :]
            far[3 * ch + row] = flat[pl.ds(512 * ch + far_row + row, 32, stride=16), :]


def pack_kernel(to_right, to_left, x_near, x_far, near, far, rim):
    first_core = lax.rem(lax.axis_index("gy"), 2) == 0
    even = lax.rem(lax.axis_index("gx"), 2) == 0
    near_row, far_row = jnp.where(even, 0, 5), jnp.where(even, 5, 0)
    has_far = inner(lax.axis_index("gx"))
    flat = rim.reshape(4 * 32 * 8, 128)
    for ch in range(4):
        for row in range(3):
            flat[pl.ds(256 * ch + near_row + row, 32, stride=8), :] = x_near[3 * ch + row]
            flat[pl.ds(256 * ch + far_row + row, 32, stride=8), :] = jnp.where(has_far, x_far[3 * ch + row], 0.0)

    def some(low):
        for ch in range(4):
            right, left = pack_planes(lambda z: rim[ch, z], low, (8, 128))
            for at, right, left in (
                (slice(0, 16), to_right[ch, low], to_left[ch, low]),
                (slice(16, 24), right, left),
            ):
                near[ch, low, at, :] = jnp.where(first_core, right, left)
                far[ch, low, at, :] = jnp.where(first_core, left, right)

    loop(4, some)


def pack_planes(plane, low, shape):
    group = iota(shape, 1) // 16
    right = left = jnp.zeros(shape, F32)
    for h in range(8):
        moved = roll(plane(4 * h + low), 16 * h + 16)
        right = jnp.where(group == h, moved, right)
        left = jnp.where(group == (h + 1) % 8, moved, left)
    return right, left


def edge_columns(plane, z, shape):
    lane = iota(shape, 1)
    value = jnp.zeros(shape, F32)
    for half in range(2):
        source = plane(z + 16 * half)
        base = 64 * half
        value = jnp.where((lane >= base) & (lane < base + 7), roll(source, base + 7), value)
        value = jnp.where((lane >= base + 57) & (lane < base + 64), roll(source, base + 57), value)
    return value


def six_of(ref, lead, z, first, count):
    own = ref[(*lead, z, pl.ds(first, count), slice(None))]
    return own, (
        ref[(*lead, z, pl.ds(first - 1, count), slice(None))],
        ref[(*lead, z, pl.ds(first + 1, count), slice(None))],
        roll(own, 1),
        roll(own, -1),
        ref[(*lead, z - 1, pl.ds(first, count), slice(None))],
        ref[(*lead, z + 1, pl.ds(first, count), slice(None))],
    )


def block_of(ref, lead, z, planes, first, count):
    rows = pl.ds(first, count)
    own = [ref[(*lead, z + k, rows, slice(None))] for k in range(-1, planes + 1)]
    result = []
    for k in range(planes):
        value = own[k + 1]
        six = (
            ref[(*lead, z + k, pl.ds(first - 1, count), slice(None))],
            ref[(*lead, z + k, pl.ds(first + 1, count), slice(None))],
            roll(value, 1),
            roll(value, -1),
            own[k],
            own[k + 2],
        )
        result.append((value, six))
    return result


def fine_weights(own, six, omega):
    base, slope = 1.0 + (BETWEEN - 1.0) * own, (BETWEEN - 1.0) + (1.1 - 2.0 * BETWEEN) * own
    total = (six[0] + six[1]) + (six[2] + six[3]) + (six[4] + six[5])
    diag = 6.0 * base + slope * total
    gain = omega * recip(diag)
    base, slope = gain * base, gain * slope
    return [base + slope * other for other in six], 1.25 * diag


def fine_sweep(w, f, own, six):
    return (0.2 * own + (w[2 * f + 1] - w[2 * f])) + weigh(w, six)


def fine_left(w, f, own, six, diag):
    return (((w[2 * f + 1] - w[2 * f]) - 0.8 * own) + weigh(w, six)) * diag


def fine_sweeps(planes, windows, start, share, one, two, weights, diags, halves, omega, wrap, keep):
    first, count = windows[0]

    def first_sweep(step):
        z = 4 * step
        w = []
        for k, (own, six) in enumerate(block_of(share, (), z + 1, 4, first, count)):
            now, diag = fine_weights(own, six, omega)
            diags[z + k, pl.ds(first, count), :] = diag
            for i in range(6):
                weights[i, z + k, pl.ds(first, count), :] = now[i]
            w.append(now)
        for f in range(3):
            for k, (own, six) in enumerate(block_of(start, (f,), z + 1, 4, first, count)):
                one[f, z + k + 1, pl.ds(first, count), :] = fine_sweep(w[k], f, own, six)

    loop(planes // 4, first_sweep)
    wrap(one)
    second, count2 = windows[1]

    def second_sweep(step):
        z = 4 * step
        w = [[weights[i, z + k, pl.ds(second, count2), :] for i in range(6)] for k in range(4)]
        for f in range(3):
            for k, (own, six) in enumerate(block_of(one, (f,), z + 1, 4, second, count2)):
                two[f, z + k + 1, pl.ds(second, count2), :] = fine_sweep(w[k], f, own, six)

    loop(planes // 4, second_sweep)
    wrap(two)

    def residual(step):
        z = 4 * step
        w = [[weights[i, z + k, 8:24, :] for i in range(6)] for k in range(4)]
        diag = [diags[z + k, 8:24, :] for k in range(4)]
        for f in range(3):
            values = []
            for k, (own, six) in enumerate(block_of(two, (f,), z + 1, 4, 8, 16)):
                if keep is not None:
                    keep[f, z + k] = own
                values.append(fine_left(w[k], f, own, six, diag[k]))
            for pair in range(2):
                halves[f, 2 * step + pair] = values[2 * pair] + values[2 * pair + 1]
        for pair in range(2):
            at = z + 2 * pair + 1
            halves[3, 2 * step + pair] = share[at, 8:24, :] + share[at + 1, 8:24, :]

    loop(planes // 4, residual)


def own_kernel(own, one, two, halves, to_right, to_left, edges, held, weights, diags):
    zero = jnp.zeros((32, 128), F32)
    for z in (0, 33):
        for ch in range(4):
            held[ch, z] = zero
        for ref in (one, two):
            for f in range(3):
                ref[f, z] = zero

    def plane(z):
        for ch in range(4):
            held[ch, z + 1, 8:24, :] = own[ch, z]

    loop(32, plane, 4)
    fine_sweeps(
        32, [(8, 16)] * 2, held, held.at[3], one, two, weights, diags, halves, 0.8, lambda ref: None, None
    )

    def some(low):
        for ch in range(4):
            to_right[ch, low], to_left[ch, low] = pack_planes(lambda z: own[ch, z], low, (16, 128))

    loop(4, some)

    def edge(z):
        for ch in range(4):
            edges[ch, z] = edge_columns(lambda at: own[ch, at], z, (16, 128))

    loop(16, edge, 2)


def rows_edge_kernel(own, rim, own_one, own_two, own_halves, two, packed, edges, start, one, weights, diags, halves, pooled):
    gx = lax.axis_index("gx")
    zero = jnp.zeros((24, 128), F32)
    for z in (0, 33):
        for ch in range(4):
            start[ch, z] = zero
        for ref in (one, two):
            for f in range(3):
                ref[f, z] = zero

    def fill(z):
        for ch in range(4):
            start[ch, z + 1, 0:8, :] = own[ch, z, 8:16, :]
            start[ch, z + 1, 8:16, :] = rim[ch, z]
            start[ch, z + 1, 16:24, :] = own[ch, z, 0:8, :]
        for f in range(3):
            for ref, source in ((one, own_one), (two, own_two)):
                ref[f, z + 1, 0:8, :] = source[f, z + 1, 16:24, :]
                ref[f, z + 1, 16:24, :] = source[f, z + 1, 8:16, :]

    loop(32, fill, 4)
    upper = iota((8, 128), 0) < 4

    def both(ref, lead, step, shift=0):
        high = ref[(*lead, pl.ds(8 - step + shift, 8), slice(None))]
        low = ref[(*lead, pl.ds(8 + step + shift, 8), slice(None))]
        return jnp.where(upper, high, low)

    def block_both(ref, f, z, step):
        own = [both(ref, (f, z + k), step) for k in range(-1, 5)]
        result = []
        for k in range(4):
            value = own[k + 1]
            low, high = both(ref, (f, z + k), step, -1), both(ref, (f, z + k), step, 1)
            result.append((value, (low, high, roll(value, 1), roll(value, -1), own[k], own[k + 2])))
        return result

    def put(ref, f, z, step, value):
        ref[f, z, pl.ds(8 - step, 4), :] = value[0:4]
        ref[f, z, pl.ds(12 + step, 4), :] = value[4:8]

    row = iota((16, 128), 0) + 5
    low, high = jnp.where(gx > 0, 1, 0), jnp.where(gx < NX - 1, 1, 0)
    inside = jnp.where((row >= 8) & (row < 12), high, jnp.where((row >= 12) & (row < 16), low, 1))
    omega = 0.8 * inside.astype(F32)

    def weigh_all(step):
        z = 4 * step
        for k, (value, six) in enumerate(block_of(start, (3,), z + 1, 4, 5, 16)):
            w, diag = fine_weights(value, six, omega)
            diags[z + k, 5:21, :] = diag
            for i in range(6):
                weights[i, z + k, 5:21, :] = w[i]

    loop(8, weigh_all)

    for step, source, target in ((1, start, one), (2, one, two)):

        def sweep(block):
            z = 4 * block
            w = [[both(weights, (i, z + k), step) for i in range(6)] for k in range(4)]
            for f in range(3):
                for k, (value, six) in enumerate(block_both(source, f, z + 1, step)):
                    put(target, f, z + k + 1, step, fine_sweep(w[k], f, value, six))

        loop(8, sweep)

    sub = iota((8, 128), 0)

    def residual(block):
        z = 4 * block
        w = [[both(weights, (i, z + k), 3) for i in range(6)] for k in range(4)]
        diag = [both(diags, (z + k,), 3) for k in range(4)]
        for f in range(3):
            values = []
            for k, (value, six) in enumerate(block_both(two, f, z + 1, 3)):
                values.append(fine_left(w[k], f, value, six, diag[k]))
            for k in range(2):
                pair = 2 * block + k
                value = values[2 * k] + values[2 * k + 1]
                halves[f, pair, 0:8, :] = jnp.where(sub < 3, roll(value, 3, 0), own_halves[f, pair, 0:8, :])
                halves[f, pair, 8:16, :] = jnp.where(sub >= 5, roll(value, 5, 0), own_halves[f, pair, 8:16, :])
        for k in range(2):
            halves[3, 2 * block + k] = own_halves[3, 2 * block + k]

    loop(8, residual)
    source, target = iota((128, 128), 0), iota((128, 128), 1)
    value = None
    for half in range(2):
        pool = jnp.where(source // 2 + 64 * half == target, 0.125, 0.0)
        part = dot_exact(halves[:, 8 * half : 8 * half + 8].reshape(512, 128), pool)
        value = part if value is None else value + part
    pooled[...] = value
    packed[...] = (pooled[pl.ds(0, 256, stride=2), :] + pooled[pl.ds(1, 256, stride=2), :]).reshape(4, 8, 8, 128)

    def edge(z):
        for ch in range(4):
            edges[ch, z] = edge_columns(lambda at: rim[ch, at], z, (8, 128))

    loop(16, edge, 2)


def rim_kernel(
    edges, edges_rim, near, far, field, packed,
    start, share, one, two, weights, diags, halves, pooled,
):
    gx, gy = lax.axis_index("gx"), lax.axis_index("gy")
    lane = iota((24, 128), 1)
    part = lane % 64
    is_after = (part >= 7) & (part < 22)
    is_before = (part >= 42) & (part < 57)
    first_core = lax.rem(gy, 2) == 0

    def unpack(low):
        for ch in range(4):
            target = start.at[ch] if ch < 3 else share
            from_near, from_far = near[ch, low], jnp.where(inner(gy), far[ch, low], 0.0)
            from_right = jnp.where(first_core, from_near, from_far)
            from_left = jnp.where(first_core, from_far, from_near)
            for h in range(4):
                z = 4 * h + low
                after_y = roll(from_right, 7 - 16 * (h + 1))
                before_y = roll(from_left, 41 - 16 * h)
                own = jnp.concatenate([edges[ch, z], edges_rim[ch, z]], axis=0)
                value = jnp.where(is_after, after_y, jnp.where(is_before, before_y, own))
                target[z + 1, 8:24, :] = value[0:16]
                target[z + 1, 0:8, :] = value[16:24]
                target[z + 1, 24:32, :] = value[16:24]

    loop(4, unpack)

    half_of = iota((32, 128), 1)

    def wrap_one(ref):
        ref[0] = jnp.where(half_of >= 64, roll(ref[16], 64), 0.0)
        ref[17] = jnp.where(half_of < 64, roll(ref[1], 64), 0.0)

    def wrap(ref):
        for f in range(3):
            wrap_one(ref.at[f])

    wrap_one(share)
    wrap(start)
    row = iota((24, 128), 0) + 6
    low, high = jnp.where(gx > 0, 1, 0), jnp.where(gx < NX - 1, 1, 0)
    inside_x = jnp.where(row < 8, low, jnp.where(row >= 24, high, 1))
    inside_y = jnp.where(
        part < 32,
        jnp.where((part < 7) | (gy < NY - 1), 1, 0),
        jnp.where((part >= 57) | (gy > 0), 1, 0),
    )
    omega = 0.8 * (inside_x * inside_y).astype(F32)
    fine_sweeps(
        16, [(6, 24), (7, 24)], start, share, one, two, weights, diags, halves, omega, wrap, field
    )

    source, target = iota((128, 128), 0), iota((128, 128), 1)
    spot = source % 64
    column = jnp.where(spot < 32, 121 + spot, 71 + spot) // 2
    to = jnp.where(spot < 32, column - 62, column - 48)
    keep = ((spot < 32) & (to >= 0) & (to < 9)) | ((spot >= 32) & (to >= 9) & (to < 18))
    mixed = halves[...].reshape(4, 4, 2, 16, 128)
    value = None
    for odd in range(2):
        pool = jnp.where(keep & (to + 64 * odd + 32 * (source // 64) == target), 0.125, 0.0)
        part = dot_exact(mixed[:, :, odd].reshape(256, 128), pool)
        value = part if value is None else value + part
    pooled[...] = value
    packed[...] = (pooled[pl.ds(0, 128, stride=2), :] + pooled[pl.ds(1, 128, stride=2), :]).reshape(4, 4, 8, 128)


def base_kernel(two, rim, e_one, e_two, base, wide, spread):
    copy = jnp.where(iota((128, 128), 0) == iota((128, 128), 1) // 2, 1.0, 0.0)
    value = dot_exact(e_two[...].reshape(192, 128), copy)
    for block in range(24):
        rows = value[8 * block : 8 * block + 4, :]
        wide[pl.ds(8 * block, 4, stride=2), :] = rows
        wide[pl.ds(8 * block + 1, 4, stride=2), :] = rows
    value = e_one[...].reshape(24, 2, 8, 128) + wide[...].reshape(24, 1, 8, 128)
    value = dot_exact(value.reshape(384, 128), copy)
    flat = spread.reshape(768, 128)
    for block in range(48):
        rows = value[8 * block : 8 * block + 8, :]
        flat[pl.ds(16 * block, 8, stride=2), :] = rows
        flat[pl.ds(16 * block + 1, 8, stride=2), :] = rows
    lane = iota((16, 128), 1)

    def pair(k):
        for f in range(3):
            for z in (2 * k, 2 * k + 1):
                value = rim[f, z]
                for half in range(2):
                    low = roll(value, -57 - 64 * half)
                    high = roll(value, 121 - 64 * half)
                    at = z + 16 * half
                    own = jnp.concatenate([two[f, at + 1, 16:24, :], two[f, at + 1, 0:8, :]], axis=0)
                    own = jnp.where(lane < 3, low, jnp.where(lane >= 125, high, own))
                    base[f, at] = own + spread[f, k + 8 * half]

    loop(8, pair, 1)


def resist(share):
    return recip(2.0 - 1.8 * share)


def level_weights(own, six, omega):
    faces = [recip(own + other) for other in six]
    diag = (faces[0] + faces[1]) + (faces[2] + faces[3]) + (faces[4] + faces[5])
    gain = omega * recip(diag)
    return gain, [gain * w for w in faces], diag


def middle_kernel(
    main, main_near, main_far, rim, rim_near, rim_far, sent, e_one, e_two,
    share, rest, rhs, first, second, weights, diags, halves, pooled,
    rest2, first2, second2, rhs2, share2, weights2,
):
    gx, gy = lax.axis_index("gx"), lax.axis_index("gy")
    low_x, high_x = jnp.where(gx > 0, 1, 0), jnp.where(gx < NX - 1, 1, 0)
    low_y, high_y = jnp.where(gy > 0, 1, 0), jnp.where(gy < NY - 1, 1, 0)

    for f in range(3):
        for ref in (first, second):
            ref[f, 0] = jnp.zeros((32, 128), F32)
            ref[f, 17] = jnp.zeros((32, 128), F32)
    for z in (0, 17):
        rest[z] = jnp.full((32, 128), 0.5, F32)
    lane = iota((8, 128), 1)
    even = lax.rem(gx, 2) == 0
    near_row, far_row = jnp.where(even, 16, 0), jnp.where(even, 0, 16)
    starts = (pl.multiple_of(near_row, 8), pl.multiple_of(far_row, 8), 8)

    sources = zip(starts, ((main_near, rim_near), (main_far, rim_far), (main, rim)))
    sources = list(sources)
    has_far = inner(gx)

    def fill(q):
        for odd in range(2):
            for half in range(2):
                z = 2 * q + odd + 8 * half
                base = 64 * odd + 32 * half
                for at, (middle, outer) in sources:
                    for ch in range(4):
                        edge, body = outer[ch, q], middle[ch, 2 * q + odd]
                        if outer is rim_far:
                            edge, body = jnp.where(has_far, edge, 0.0), jnp.where(has_far, body, 0.0)
                        value = jnp.where(lane < 62, roll(body, 64 * half), roll(edge, 62 - base))
                        value = jnp.where((lane >= 96) | (lane < 2), roll(edge, 112 - base), value)
                        if ch < 3:
                            rhs[ch, z, pl.ds(at, 8), :] = value
                        else:
                            share[z, pl.ds(at, 8), :] = value
                            rest[z + 1, pl.ds(at, 8), :] = resist(value)
                rest[z + 1, 24:32, :] = jnp.full((8, 128), 0.5, F32)

    loop(4, fill)

    row, lane = iota((24, 128), 0) + 1, iota((24, 128), 1)
    in_x = jnp.where(row < 8, low_x, jnp.where(row >= 16, high_x, 1))
    in_y = jnp.where(lane < 64, 1, jnp.where(lane < 96, high_y, low_y))
    omega = 0.8 * (in_x * in_y).astype(F32)

    def start(step):
        z = 4 * step
        for k, (own, six) in enumerate(block_of(rest, (), z + 1, 4, 1, 24)):
            gain, w, diag = level_weights(own, six, omega)
            for i in range(6):
                weights[i, z + k, 1:25, :] = w[i]
            diags[z + k, 1:25, :] = (1.25 * 0.25) * diag
            for f in range(3):
                first[f, z + k + 1, 1:25, :] = (4.0 * gain) * rhs[f, z + k, 1:25, :]

    loop(4, start)

    def sweep(step):
        z = 4 * step
        w = [[weights[i, z + k, 3:27, :] for i in range(6)] for k in range(4)]
        for f in range(3):
            for k, (own, six) in enumerate(block_of(first, (f,), z + 1, 4, 3, 24)):
                second[f, z + k + 1, 3:27, :] = 1.2 * own + weigh(w[k], six)

    loop(4, sweep)

    def left(step):
        z = 4 * step
        w = [[weights[i, z + k, 4:20, :] for i in range(6)] for k in range(4)]
        diag = [diags[z + k, 4:20, :] for k in range(4)]
        for f in range(3):
            values = []
            for k, (own, six) in enumerate(block_of(second, (f,), z + 1, 4, 4, 16)):
                change = (first[f, z + k + 1, 4:20, :] - 0.8 * own) + weigh(w[k], six)
                values.append(change * diag[k])
                e_one[f, z + k] = second[f, z + k + 1, 8:16, :]
            for k in range(2):
                halves[f, 2 * step + k, 0:16, :] = values[2 * k] + values[2 * k + 1]
                halves[f, 2 * step + k, 16:24, :] = jnp.zeros((8, 128), F32)
        for k in range(2):
            halves[3, 2 * step + k] = share[z + 2 * k] + share[z + 2 * k + 1]

    loop(4, left)

    source, target = iota((128, 128), 0), iota((128, 128), 1)
    pool = jnp.where(source // 2 + jnp.where(source >= 96, 64, 0) == target, 0.125, 0.0)
    pooled[...] = dot_exact(halves[...].reshape(4 * 8 * 24, 128), pool)
    for z in (0, 9):
        rest2[z] = jnp.full((24, 128), 0.5, F32)
        for f in range(3):
            first2[f, z] = jnp.zeros((24, 128), F32)
            second2[f, z] = jnp.zeros((24, 128), F32)
    for z in range(8):
        for f in range(3):
            base = (f * 8 + z) * 24
            rhs2[f, z] = pooled[pl.ds(base, 8, stride=2), :] + pooled[pl.ds(base + 1, 8, stride=2), :]
        base = (3 * 8 + z) * 24
        value = pooled[pl.ds(base + 2, 8, stride=2), :] + pooled[pl.ds(base + 3, 8, stride=2), :]
        rest2[z + 1, 0:8, :] = resist(value)
        value = pooled[pl.ds(base + 8, 8, stride=2), :] + pooled[pl.ds(base + 9, 8, stride=2), :]
        rest2[z + 1, 3:11, :] = resist(value)
        share2[z] = value

    row, lane = iota((8, 128), 0) + 1, iota((8, 128), 1)
    in_x = jnp.where(row < 3, low_x, jnp.where(row >= 7, high_x, 1))
    in_y = jnp.where(lane < 32, 1, jnp.where(lane < 96, high_y, low_y))
    omega2 = 0.8 * (in_x * in_y).astype(F32)

    for z, (own, six) in enumerate(block_of(rest2, (), 1, 8, 1, 8)):
        gain, w, diag = level_weights(own, six, omega2)
        for i in range(6):
            weights2[i, z, 1:9, :] = w[i]
        weights2[6, z, 1:9, :] = (1.25 * 0.0625) * diag
        for f in range(3):
            first2[f, z + 1, 1:9, :] = (16.0 * gain) * rhs2[f, z]
    w = [[weights2[i, z, 2:10, :] for i in range(6)] for z in range(8)]
    for f in range(3):
        for z, (own, six) in enumerate(block_of(first2, (f,), 1, 8, 2, 8)):
            second2[f, z + 1, 2:10, :] = 1.2 * own + weigh(w[z], six)
    w = [[weights2[i, z, 3:11, :] for i in range(7)] for z in range(8)]
    own_row = iota((8, 128), 0) < 4
    parts = [{} for pair in range(4)]
    for f in range(3):
        for z, (own, six) in enumerate(block_of(second2, (f,), 1, 8, 3, 8)):
            e_two[f, z] = own
            change = (first2[f, z + 1, 3:11, :] - 0.8 * own) + weigh(w[z], six)
            value = jnp.where(own_row, change * w[z][6], 0.0)
            sums = parts[z // 2]
            sums[f] = value if z % 2 == 0 else sums[f] + value
    for z in range(8):
        value = jnp.where(own_row, share2[z], 0.0)
        sums = parts[z // 2]
        sums[3] = value if z % 2 == 0 else sums[3] + value

    pool = jnp.where((source < 32) & (source // 2 == target % 16), 0.125, 0.0)
    rows = jnp.concatenate([parts[pair][ch] for ch in range(4) for pair in range(4)], axis=0)
    spread = dot(rows, pool)
    at, to = iota((32, 128), 0), iota((32, 128), 1)
    keep = (at // 8 == to // 32) & ((at % 8) // 2 == (to // 16) % 2)
    result = jnp.concatenate(
        [
            jnp.sum(jnp.where(keep, spread[32 * ch : 32 * ch + 32], 0.0), axis=0, keepdims=True)
            for ch in range(4)
        ],
        axis=0,
    )
    for copy in range(CHIPS):
        sent[copy] = result


def swap_blocks(x):
    sub, group = iota((8, 128), 0), iota((8, 128), 1) // 16
    for bit in (4, 2, 1):
        up = roll(roll(x, -bit, 0), 16 * bit)
        down = up if bit == 4 else roll(roll(x, bit, 0), -16 * bit)
        sub_set, group_set = (sub & bit) != 0, (group & bit) != 0
        x = jnp.where(sub_set == group_set, x, jnp.where(sub_set, down, up))
    return x


def top_kernel(
    mine, other, base, out,
    natural, first, second, four, weights, diags, lefts, final, sems,
):
    gx, gy = lax.axis_index("gx"), lax.axis_index("gy")
    first_core = lax.rem(gy, 2) == 0
    lane, sub = iota((16, 128), 1), iota((16, 128), 0)
    cells = [(z, x, half) for z in range(4) for x in range(2) for half in range(2)]

    def lay(g):
        for ch in range(4):
            rows = pl.ds(32 * g + ch, 8, stride=4)
            pair = mine[rows, :], other[rows, :]
            natural[ch, 0, pl.ds(pl.multiple_of(8 * g, 8), 8), :] = swap_blocks(
                jnp.where(first_core, pair[0], pair[1])
            )
            natural[ch, 1, pl.ds(pl.multiple_of(8 * g, 8), 8), :] = swap_blocks(
                jnp.where(first_core, pair[1], pair[0])
            )

    loop(16, lay, 4)
    flat = natural.reshape(1024, 128)

    def plane(ch, z, x, half):
        return flat[pl.ds((ch * 2 + half) * 128 + z * 2 + x, 16, stride=8), :]

    def neighbours(at, z, x, half, outside):
        own, other = at(z, x, half), at(z, 1 - x, half)
        beside = at(z, x, 1 - half)
        shifted = roll(other, 1 if x == 0 else -1, 0)
        low, high = (shifted, other) if x == 0 else (other, shifted)
        left, right = roll(own, 1), roll(own, -1)
        left = jnp.where(lane % 16 == 0, roll(beside, 1 if half == 0 else -15), left)
        right = jnp.where(lane % 16 == 15, roll(beside, 15 if half == 0 else -1), right)
        down = at(z - 1, x, half) if z > 0 else outside
        up = at(z + 1, x, half) if z < 3 else outside
        return own, [low, high, left, right, down, up]

    def edge_masks(x, half):
        return [
            sub > 0 if x == 0 else None,
            sub < 15 if x == 1 else None,
            lane > 0 if half == 0 else None,
            lane < 127 if half == 1 else None,
            None,
            None,
        ]

    def key(z, x, half):
        return (z * 2 + x) * 2 + half

    shares = {c: plane(3, *c) for c in cells}
    rests = {c: resist(shares[c]) for c in cells}
    outside, zeros = jnp.full((16, 128), 0.5, F32), jnp.zeros((16, 128), F32)
    for z, x, half in cells:
        own, six = neighbours(lambda *c: rests[c], z, x, half, outside)
        masks = edge_masks(x, half)
        six = [s if m is None else jnp.where(m, s, 0.5) for s, m in zip(six, masks)]
        gain, w, diag = level_weights(own, six, 0.8)
        at = key(z, x, half)
        for i in range(6):
            weights[i, at] = w[i] if masks[i] is None else jnp.where(masks[i], w[i], 0.0)
        diags[at] = (1.25 * 0.25**3) * diag
        for f in range(3):
            first[f, at] = (64.0 * gain) * plane(f, z, x, half)

    for z, x, half in cells:
        at = key(z, x, half)
        w = [weights[i, at] for i in range(6)]
        for f in range(3):
            own, six = neighbours(lambda *c: first[f, key(*c)], z, x, half, zeros)
            second[half, f, z * 2 + x] = 1.2 * own + weigh(w, six)

    for z4 in range(2):
        for half in range(2):
            sums = [None] * 4
            for z in (2 * z4, 2 * z4 + 1):
                for x in range(2):
                    at = key(z, x, half)
                    w = [weights[i, at] for i in range(6)]
                    diag = diags[at]
                    for f in range(3):
                        own, six = neighbours(
                            lambda c, d, e: second[e, f, c * 2 + d], z, x, half, zeros
                        )
                        value = ((first[f, at] - 0.8 * own) + weigh(w, six)) * diag
                        sums[f] = value if sums[f] is None else sums[f] + value
                    share = shares[z, x, half]
                    sums[3] = share if sums[3] is None else sums[3] + share
            for ch in range(4):
                lefts[ch, z4, :, 128 * half : 128 * half + 128] = sums[ch]

    source = iota((256, 128), 0)
    column = ((source % 128) // 16) * 16 + (source // 128) * 8 + (source % 16) // 2
    pool = jnp.where(column == iota((256, 128), 1), 0.125, 0.0)
    level = dot_exact(lefts[...].reshape(128, 256), pool)

    def coarsest(ch, z):
        return level[(ch * 2 + z) * 16 : (ch * 2 + z) * 16 + 16, :]

    masks = [sub > 0, sub < 15, lane > 0, lane < 127]
    resists = [resist(coarsest(3, z)) for z in range(2)]
    gains, ws, ds = [], [], []
    for z in range(2):
        own, other = resists[z], resists[1 - z]
        six = [roll(own, 1, 0), roll(own, -1, 0), roll(own, 1), roll(own, -1)]
        six = [jnp.where(m, s, 0.5) for m, s in zip(masks, six)] + [other, outside]
        gain, w, diag = level_weights(own, six, 0.8)
        gains.append(gain)
        ds.append(diag)
        ws.append([jnp.where(m, v, 0.0) for m, v in zip(masks, w)] + [w[4]])
    whole = jnp.sum(ds[0] + ds[1], keepdims=True)

    def around(values, z):
        own, other = values[z], values[1 - z]
        return weigh(ws[z], (roll(own, 1, 0), roll(own, -1, 0), roll(own, 1), roll(own, -1), other))

    begin = [[256.0 * gains[z] * coarsest(f, z) for z in range(2)] for f in range(3)]
    values = begin
    for step in range(5):
        values = [
            [(0.2 * values[f][z] + begin[f][z]) + around(values[f], z) for z in range(2)] for f in range(3)
        ]
    for f in range(3):
        change = [(begin[f][z] - 0.8 * values[f][z]) + around(values[f], z) for z in range(2)]
        total = jnp.sum(1.25 * (change[0] * ds[0] + change[1] * ds[1]), keepdims=True)
        for z in range(2):
            four[2 * f + z] = values[f][z] + total / whole

    copy = jnp.where(iota((128, 128), 0) == iota((128, 128), 1) // 2, 1.0, 0.0)
    rows = four.reshape(96, 128)[pl.ds(gx, 6, stride=16), :]
    rows = jnp.concatenate([jnp.broadcast_to(rows[i : i + 1], (4, 128)) for i in range(6)], axis=0)
    three = dot(turn(rows, -8 * gy), copy)
    flat = second.reshape(768, 128)
    halves = [flat[pl.ds(gx + 384 * half, 24, stride=16), :] for half in range(2)]
    three = three + turn(jnp.where(first_core, halves[0], halves[1]), -16 * lax.div(gy, 2))

    copy = jnp.where(iota((128, 128), 0) == iota((128, 128), 1) // 8, 1.0, 0.0)
    three = dot(three, copy)
    copies = []
    for f in range(3):
        for z in range(4):
            for x in range(2):
                at = f * 8 + z * 2 + x
                value = jnp.broadcast_to(three[at : at + 1], (8, 128))
                for k in range(8 * z, 8 * z + 8):
                    final[f, k, 8 * x : 8 * x + 8, :] = base[f, k, 8 * x : 8 * x + 8, :] + value
            if z % 2 == 1:
                part = (f, pl.ds(8 * z - 8, 16))
                copy = pltpu.make_async_copy(final.at[part], out.at[part], sems.at[len(copies)])
                copy.start()
                copies.append(copy)
    for copy in copies:
        copy.wait()


def local(labels, guess):
    swap_near = [(i, i ^ 1) for i in range(NY)]
    far_x, far_y = [], []
    for x in range(NX):
        for y in range(NY):
            across_x, across_y = x + 1 if x % 2 else x - 1, y + 1 if y % 2 else y - 1
            to = (across_x, y) if 0 <= across_x < NX else (x, y ^ 1)
            far_x.append((x * NY + y, to[0] * NY + to[1]))
            to = (x, across_y) if 0 <= across_y < NY else (x ^ 1, y)
            far_y.append((x * NY + y, to[0] * NY + to[1]))
    both = ("gx", "gy")
    to_near, to_far, own = call(
        rows_kernel,
        [(12, 32, 128)] * 2 + [(4, 32, 16, 128)],
        [pltpu.VMEM((32, 16, 128), jnp.int32), pltpu.SemaphoreType.DMA((4,))],
        in_specs=[ANY, ANY],
    )(pltpu.with_memory_space_constraint(guess, pltpu.HBM), pltpu.with_memory_space_constraint(labels, pltpu.HBM))
    from_near = lax.ppermute(to_near, "gx", swap_near)
    from_far = lax.ppermute(to_far, both, far_x)
    own_one, own_two, halves, to_right, to_left, edges = call(
        own_kernel,
        [(3, 34, 32, 128)] * 2 + [(4, 16, 16, 128)] + [(4, 4, 16, 128)] * 2 + [(4, 16, 16, 128)],
        [(4, 34, 32, 128), (6, 32, 32, 128), (32, 32, 128)],
        flops=20_000_000,
    )(own)
    to_near, to_far, rim_rows = call(pack_kernel, [(4, 4, 24, 128)] * 2 + [(4, 32, 8, 128)], [])(
        to_right, to_left, from_near, from_far
    )
    from_far = lax.ppermute(to_far, both, far_y)
    from_near = lax.ppermute(to_near, "gy", swap_near)
    two, main, edges_rim = call(
        rows_edge_kernel,
        [(3, 34, 24, 128), (4, 8, 8, 128), (4, 16, 8, 128)],
        [(4, 34, 24, 128), (3, 34, 24, 128), (6, 32, 24, 128), (32, 24, 128)]
        + [(4, 16, 16, 128), (512, 128)],
        flops=10_000_000,
    )(own, rim_rows, own_one, own_two, halves)
    main_near = lax.ppermute(main, "gx", swap_near)
    main_far = lax.ppermute(main, both, far_x)
    rim, rim_one = call(
        rim_kernel,
        [(3, 16, 16, 128), (4, 4, 8, 128)],
        [(3, 18, 32, 128), (18, 32, 128)]
        + [(3, 18, 32, 128)] * 2
        + [(6, 16, 32, 128), (16, 32, 128)]
        + [(4, 8, 16, 128), (256, 128)],
        flops=10_000_000,
    )(edges, edges_rim, from_near, from_far)
    rim_near = lax.ppermute(rim_one, "gx", swap_near)
    rim_far = lax.ppermute(rim_one, both, far_x)
    sent, e_one, e_two = call(
        middle_kernel,
        [(CHIPS, 4, 128), (3, 16, 8, 128), (3, 8, 8, 128)],
        [(16, 24, 128), (18, 32, 128), (3, 16, 32, 128), (3, 18, 32, 128), (3, 18, 32, 128)]
        + [(6, 16, 32, 128), (16, 32, 128), (4, 8, 24, 128), (768, 128)]
        + [(10, 24, 128), (3, 10, 24, 128), (3, 10, 24, 128), (3, 8, 8, 128), (8, 8, 128)]
        + [(7, 8, 16, 128)],
    )(main, main_near, main_far, rim_one, rim_near, rim_far)
    groups = [[i for i in range(NX * NY) if i % 2 == core] for core in range(2)]
    mine = lax.all_to_all(
        sent, ("gx", "gy"), split_axis=0, concat_axis=0, axis_index_groups=groups, tiled=True
    )
    (base,) = call(base_kernel, [(3, 32, 16, 128)], [(192, 128), (3, 16, 16, 128)])(two, rim, e_one, e_two)
    other = lax.ppermute(mine, "gy", swap_near)
    (out,) = call(
        top_kernel,
        [(3, 32, 16, 128)],
        [(4, 2, 128, 128), (3, 16, 16, 128), (2, 3, 8, 16, 128), (6, 16, 128), (6, 16, 16, 128)]
        + [(16, 16, 128), (4, 2, 16, 256), (3, 32, 16, 128), pltpu.SemaphoreType.DMA((6,))],
        out_specs=[ANY],
    )(mine.reshape(512, 128), other.reshape(512, 128), base)
    return out


def solution(mesh):
    return jax.shard_map(
        local,
        mesh=mesh,
        in_specs=(P(None, "gx", "gy"), P(None, None, "gx", "gy")),
        out_specs=P(None, None, "gx", "gy"),
        check_vma=False,
    )
```

```python
import jax
import jax.numpy as jnp
from jax import lax
from jax.experimental import pallas as pl
from jax.experimental.pallas import tpu as pltpu
from jax.sharding import PartitionSpec as P


F32 = jnp.float32
NX, NY, CHIPS = 16, 16, 128
STEP, WIDE = 8, 16
BETWEEN = 2.0 * 0.1 / 1.1
ANY = pl.BlockSpec(memory_space=pltpu.HBM)


def dot(a, b):
    return jnp.dot(a, b, precision=lax.Precision.HIGHEST, preferred_element_type=F32)


def dot_exact(a, b):
    high = a.astype(jnp.bfloat16)
    low = (a - high.astype(F32)).astype(jnp.bfloat16)
    b = b.astype(jnp.bfloat16)
    return jnp.dot(
        jnp.concatenate([high, low], axis=1), jnp.concatenate([b, b], axis=0), preferred_element_type=F32
    )


def iota(shape, dim):
    return lax.broadcasted_iota(jnp.int32, shape, dim)


def roll(x, shift, axis=1):
    shift = shift % x.shape[axis]
    return x if shift == 0 else pltpu.roll(x, shift, axis)


def turn(x, shift):
    return pltpu.roll(x, lax.rem(shift + 256, 128), 1)


def recip(x):
    guess = pl.reciprocal(x, approx=True)
    return guess * (2.0 - x * guess)


def inner(index):
    return (index > 0) & (index < 15)


def call(kernel, outs, scratch, flops=1_000_000, **kw):
    return pl.pallas_call(
        kernel,
        out_shape=[jax.ShapeDtypeStruct(s, F32) for s in outs],
        scratch_shapes=[pltpu.VMEM(s, F32) if isinstance(s, tuple) else s for s in scratch],
        compiler_params=pltpu.CompilerParams(vmem_limit_bytes=32 * 1024 * 1024),
        cost_estimate=pl.CostEstimate(flops=flops, bytes_accessed=4_000_000, transcendentals=0),
        **kw,
    )


def loop(count, body, unroll=1):
    def step(i, carry):
        body(i)
        return carry

    lax.fori_loop(0, count, step, 0, unroll=unroll)


def weigh(weights, values):
    parts = [w * v for w, v in zip(weights, values)]
    while len(parts) > 1:
        parts = [sum(parts[i : i + 2][1:], parts[i]) for i in range(0, len(parts), 2)]
    return parts[0]


def rows_kernel(guess, labels, near, far, own, phase, sems):
    even = lax.rem(lax.axis_index("gx"), 2) == 0
    near_row, far_row = jnp.where(even, 13, 0), jnp.where(even, 0, 13)
    copies = [pltpu.make_async_copy(labels, phase, sems.at[3])]
    for f in range(3):
        copies.append(pltpu.make_async_copy(guess.at[f], own.at[f], sems.at[f]))
    for copy in copies:
        copy.start()
    copies[0].wait()
    own[3] = jnp.where(phase[...] == 1, 0.0, 1.0).astype(F32)
    flat = own.reshape(4 * 32 * 16, 128)
    for ch in (3, 0, 1, 2):
        if ch < 3:
            copies[ch + 1].wait()
        for row in range(3):
            near[3 * ch + row] = flat[pl.ds(512 * ch + near_row + row, 32, stride=16), :]
            far[3 * ch + row] = flat[pl.ds(512 * ch + far_row + row, 32, stride=16), :]


def pack_kernel(to_right, to_left, x_near, x_far, near, far, rim):
    first_core = lax.rem(lax.axis_index("gy"), 2) == 0
    even = lax.rem(lax.axis_index("gx"), 2) == 0
    near_row, far_row = jnp.where(even, 0, 5), jnp.where(even, 5, 0)
    has_far = inner(lax.axis_index("gx"))
    flat = rim.reshape(4 * 32 * 8, 128)
    for ch in range(4):
        for row in range(3):
            flat[pl.ds(256 * ch + near_row + row, 32, stride=8), :] = x_near[3 * ch + row]
            flat[pl.ds(256 * ch + far_row + row, 32, stride=8), :] = jnp.where(has_far, x_far[3 * ch + row], 0.0)

    def some(low):
        for ch in range(4):
            right, left = pack_planes(lambda z: rim[ch, z], low, (8, 128))
            for at, right, left in (
                (slice(0, 16), to_right[ch, low], to_left[ch, low]),
                (slice(16, 24), right, left),
            ):
                near[ch, low, at, :] = jnp.where(first_core, right, left)
                far[ch, low, at, :] = jnp.where(first_core, left, right)

    loop(4, some, 4)


def pack_planes(plane, low, shape):
    group = iota(shape, 1) // 16
    right = left = jnp.zeros(shape, F32)
    for h in range(8):
        moved = roll(plane(4 * h + low), 16 * h + 16)
        right = jnp.where(group == h, moved, right)
        left = jnp.where(group == (h + 1) % 8, moved, left)
    return right, left


def edge_columns(plane, z, shape):
    lane = iota(shape, 1)
    value = jnp.zeros(shape, F32)
    for half in range(2):
        source = plane(z + 16 * half)
        base = 64 * half
        value = jnp.where((lane >= base) & (lane < base + 7), roll(source, base + 7), value)
        value = jnp.where((lane >= base + 57) & (lane < base + 64), roll(source, base + 57), value)
    return value


def six_of(ref, lead, z, first, count):
    own = ref[(*lead, z, pl.ds(first, count), slice(None))]
    return own, (
        ref[(*lead, z, pl.ds(first - 1, count), slice(None))],
        ref[(*lead, z, pl.ds(first + 1, count), slice(None))],
        roll(own, 1),
        roll(own, -1),
        ref[(*lead, z - 1, pl.ds(first, count), slice(None))],
        ref[(*lead, z + 1, pl.ds(first, count), slice(None))],
    )


def block_of(ref, lead, z, planes, first, count):
    rows = pl.ds(first, count)
    own = [ref[(*lead, z + k, rows, slice(None))] for k in range(-1, planes + 1)]
    result = []
    for k in range(planes):
        value = own[k + 1]
        six = (
            ref[(*lead, z + k, pl.ds(first - 1, count), slice(None))],
            ref[(*lead, z + k, pl.ds(first + 1, count), slice(None))],
            roll(value, 1),
            roll(value, -1),
            own[k],
            own[k + 2],
        )
        result.append((value, six))
    return result


def fine_weights(own, six, omega):
    base, slope = 1.0 + (BETWEEN - 1.0) * own, (BETWEEN - 1.0) + (1.1 - 2.0 * BETWEEN) * own
    total = (six[0] + six[1]) + (six[2] + six[3]) + (six[4] + six[5])
    diag = 6.0 * base + slope * total
    gain = omega * recip(diag)
    base, slope = gain * base, gain * slope
    return [base + slope * other for other in six], 1.25 * diag


def fine_sweep(w, f, own, six):
    return (0.2 * own + (w[2 * f + 1] - w[2 * f])) + weigh(w, six)


def fine_left(w, f, own, six, diag):
    return (((w[2 * f + 1] - w[2 * f]) - 0.8 * own) + weigh(w, six)) * diag


def fine_sweeps(planes, windows, start, share, one, two, weights, diags, halves, omega, wrap, keep):
    first, count = windows[0]

    def first_sweep(step):
        z = STEP * step
        w = []
        for k, (own, six) in enumerate(block_of(share, (), z + 1, STEP, first, count)):
            now, diag = fine_weights(own, six, omega)
            diags[z + k, pl.ds(first, count), :] = diag
            for i in range(6):
                weights[i, z + k, pl.ds(first, count), :] = now[i]
            w.append(now)
        for f in range(3):
            for k, (own, six) in enumerate(block_of(start, (f,), z + 1, STEP, first, count)):
                one[f, z + k + 1, pl.ds(first, count), :] = fine_sweep(w[k], f, own, six)

    loop(planes // STEP, first_sweep)
    wrap(one)
    second, count2 = windows[1]

    def second_sweep(step):
        z = STEP * step
        w = [[weights[i, z + k, pl.ds(second, count2), :] for i in range(6)] for k in range(STEP)]
        for f in range(3):
            for k, (own, six) in enumerate(block_of(one, (f,), z + 1, STEP, second, count2)):
                two[f, z + k + 1, pl.ds(second, count2), :] = fine_sweep(w[k], f, own, six)

    loop(planes // STEP, second_sweep)
    wrap(two)

    def residual(step):
        z = STEP * step
        w = [[weights[i, z + k, 8:24, :] for i in range(6)] for k in range(STEP)]
        diag = [diags[z + k, 8:24, :] for k in range(STEP)]
        for f in range(3):
            values = []
            for k, (own, six) in enumerate(block_of(two, (f,), z + 1, STEP, 8, 16)):
                if keep is not None:
                    keep[f, z + k] = own
                values.append(fine_left(w[k], f, own, six, diag[k]))
            for pair in range(STEP // 2):
                halves[f, STEP // 2 * step + pair] = values[2 * pair] + values[2 * pair + 1]
        for pair in range(STEP // 2):
            at = z + 2 * pair + 1
            halves[3, STEP // 2 * step + pair] = share[at, 8:24, :] + share[at + 1, 8:24, :]

    loop(planes // STEP, residual)


def own_kernel(own, one, two, halves, to_right, to_left, edges, held, weights, diags):
    zero = jnp.zeros((32, 128), F32)
    for z in (0, 33):
        for ch in range(4):
            held[ch, z] = zero
        for ref in (one, two):
            for f in range(3):
                ref[f, z] = zero

    def plane(z):
        for ch in range(4):
            held[ch, z + 1, 8:24, :] = own[ch, z]

    loop(32, plane, 8)
    fine_sweeps(
        32, [(8, 16)] * 2, held, held.at[3], one, two, weights, diags, halves, 0.8, lambda ref: None, None
    )

    def some(low):
        for ch in range(4):
            to_right[ch, low], to_left[ch, low] = pack_planes(lambda z: own[ch, z], low, (16, 128))

    loop(4, some, 2)

    def edge(z):
        for ch in range(4):
            edges[ch, z] = edge_columns(lambda at: own[ch, at], z, (16, 128))

    loop(16, edge, 8)


def rows_edge_kernel(own, rim, own_one, own_two, own_halves, two, packed, edges, start, one, weights, diags, halves, pooled):
    gx = lax.axis_index("gx")
    zero = jnp.zeros((24, 128), F32)
    for z in (0, 33):
        for ch in range(4):
            start[ch, z] = zero
        for ref in (one, two):
            for f in range(3):
                ref[f, z] = zero

    def fill(z):
        for ch in range(4):
            start[ch, z + 1, 0:8, :] = own[ch, z, 8:16, :]
            start[ch, z + 1, 8:16, :] = rim[ch, z]
            start[ch, z + 1, 16:24, :] = own[ch, z, 0:8, :]
        for f in range(3):
            for ref, source in ((one, own_one), (two, own_two)):
                ref[f, z + 1, 0:8, :] = source[f, z + 1, 16:24, :]
                ref[f, z + 1, 16:24, :] = source[f, z + 1, 8:16, :]

    loop(32, fill, 8)
    upper = iota((8, 128), 0) < 4

    def both(ref, lead, step, shift=0):
        high = ref[(*lead, pl.ds(8 - step + shift, 8), slice(None))]
        low = ref[(*lead, pl.ds(8 + step + shift, 8), slice(None))]
        return jnp.where(upper, high, low)

    def block_both(ref, f, z, step):
        own = [both(ref, (f, z + k), step) for k in range(-1, WIDE + 1)]
        result = []
        for k in range(WIDE):
            value = own[k + 1]
            low, high = both(ref, (f, z + k), step, -1), both(ref, (f, z + k), step, 1)
            result.append((value, (low, high, roll(value, 1), roll(value, -1), own[k], own[k + 2])))
        return result

    def put(ref, f, z, step, value):
        ref[f, z, pl.ds(8 - step, 4), :] = value[0:4]
        ref[f, z, pl.ds(12 + step, 4), :] = value[4:8]

    row = iota((16, 128), 0) + 5
    low, high = jnp.where(gx > 0, 1, 0), jnp.where(gx < NX - 1, 1, 0)
    inside = jnp.where((row >= 8) & (row < 12), high, jnp.where((row >= 12) & (row < 16), low, 1))
    omega = 0.8 * inside.astype(F32)

    def weigh_all(step):
        z = WIDE * step
        for k, (value, six) in enumerate(block_of(start, (3,), z + 1, WIDE, 5, 16)):
            w, diag = fine_weights(value, six, omega)
            diags[z + k, 5:21, :] = diag
            for i in range(6):
                weights[i, z + k, 5:21, :] = w[i]

    loop(32 // WIDE, weigh_all)

    for step, source, target in ((1, start, one), (2, one, two)):

        def sweep(block):
            z = WIDE * block
            w = [[both(weights, (i, z + k), step) for i in range(6)] for k in range(WIDE)]
            for f in range(3):
                for k, (value, six) in enumerate(block_both(source, f, z + 1, step)):
                    put(target, f, z + k + 1, step, fine_sweep(w[k], f, value, six))

        loop(32 // WIDE, sweep)

    sub = iota((8, 128), 0)

    def residual(block):
        z = WIDE * block
        w = [[both(weights, (i, z + k), 3) for i in range(6)] for k in range(WIDE)]
        diag = [both(diags, (z + k,), 3) for k in range(WIDE)]
        for f in range(3):
            values = []
            for k, (value, six) in enumerate(block_both(two, f, z + 1, 3)):
                values.append(fine_left(w[k], f, value, six, diag[k]))
            for k in range(WIDE // 2):
                pair = WIDE // 2 * block + k
                value = values[2 * k] + values[2 * k + 1]
                halves[f, pair, 0:8, :] = jnp.where(sub < 3, roll(value, 3, 0), own_halves[f, pair, 0:8, :])
                halves[f, pair, 8:16, :] = jnp.where(sub >= 5, roll(value, 5, 0), own_halves[f, pair, 8:16, :])
        for k in range(WIDE // 2):
            halves[3, WIDE // 2 * block + k] = own_halves[3, WIDE // 2 * block + k]

    loop(32 // WIDE, residual)
    source, target = iota((128, 128), 0), iota((128, 128), 1)
    value = None
    for half in range(2):
        pool = jnp.where(source // 2 + 64 * half == target, 0.125, 0.0)
        part = dot_exact(halves[:, 8 * half : 8 * half + 8].reshape(512, 128), pool)
        value = part if value is None else value + part
    pooled[...] = value
    packed[...] = (pooled[pl.ds(0, 256, stride=2), :] + pooled[pl.ds(1, 256, stride=2), :]).reshape(4, 8, 8, 128)

    def edge(z):
        for ch in range(4):
            edges[ch, z] = edge_columns(lambda at: rim[ch, at], z, (8, 128))

    loop(16, edge, 8)


def rim_kernel(
    edges, edges_rim, near, far, field, packed,
    start, share, one, two, weights, diags, halves, pooled,
):
    gx, gy = lax.axis_index("gx"), lax.axis_index("gy")
    lane = iota((24, 128), 1)
    part = lane % 64
    is_after = (part >= 7) & (part < 22)
    is_before = (part >= 42) & (part < 57)
    first_core = lax.rem(gy, 2) == 0

    def unpack(low):
        for ch in range(4):
            target = start.at[ch] if ch < 3 else share
            from_near, from_far = near[ch, low], jnp.where(inner(gy), far[ch, low], 0.0)
            from_right = jnp.where(first_core, from_near, from_far)
            from_left = jnp.where(first_core, from_far, from_near)
            for h in range(4):
                z = 4 * h + low
                after_y = roll(from_right, 7 - 16 * (h + 1))
                before_y = roll(from_left, 41 - 16 * h)
                own = jnp.concatenate([edges[ch, z], edges_rim[ch, z]], axis=0)
                value = jnp.where(is_after, after_y, jnp.where(is_before, before_y, own))
                target[z + 1, 8:24, :] = value[0:16]
                target[z + 1, 0:8, :] = value[16:24]
                target[z + 1, 24:32, :] = value[16:24]

    loop(4, unpack, 2)

    half_of = iota((32, 128), 1)

    def wrap_one(ref):
        ref[0] = jnp.where(half_of >= 64, roll(ref[16], 64), 0.0)
        ref[17] = jnp.where(half_of < 64, roll(ref[1], 64), 0.0)

    def wrap(ref):
        for f in range(3):
            wrap_one(ref.at[f])

    wrap_one(share)
    wrap(start)
    row = iota((24, 128), 0) + 6
    low, high = jnp.where(gx > 0, 1, 0), jnp.where(gx < NX - 1, 1, 0)
    inside_x = jnp.where(row < 8, low, jnp.where(row >= 24, high, 1))
    inside_y = jnp.where(
        part < 32,
        jnp.where((part < 7) | (gy < NY - 1), 1, 0),
        jnp.where((part >= 57) | (gy > 0), 1, 0),
    )
    omega = 0.8 * (inside_x * inside_y).astype(F32)
    fine_sweeps(
        16, [(6, 24), (7, 24)], start, share, one, two, weights, diags, halves, omega, wrap, field
    )

    source, target = iota((128, 128), 0), iota((128, 128), 1)
    spot = source % 64
    column = jnp.where(spot < 32, 121 + spot, 71 + spot) // 2
    to = jnp.where(spot < 32, column - 62, column - 48)
    keep = ((spot < 32) & (to >= 0) & (to < 9)) | ((spot >= 32) & (to >= 9) & (to < 18))
    mixed = halves[...].reshape(4, 4, 2, 16, 128)
    value = None
    for odd in range(2):
        pool = jnp.where(keep & (to + 64 * odd + 32 * (source // 64) == target), 0.125, 0.0)
        part = dot_exact(mixed[:, :, odd].reshape(256, 128), pool)
        value = part if value is None else value + part
    pooled[...] = value
    packed[...] = (pooled[pl.ds(0, 128, stride=2), :] + pooled[pl.ds(1, 128, stride=2), :]).reshape(4, 4, 8, 128)


def base_kernel(two, rim, e_one, e_two, base, wide, spread):
    copy = jnp.where(iota((128, 128), 0) == iota((128, 128), 1) // 2, 1.0, 0.0)
    value = dot_exact(e_two[...].reshape(192, 128), copy)
    for block in range(24):
        rows = value[8 * block : 8 * block + 4, :]
        wide[pl.ds(8 * block, 4, stride=2), :] = rows
        wide[pl.ds(8 * block + 1, 4, stride=2), :] = rows
    value = e_one[...].reshape(24, 2, 8, 128) + wide[...].reshape(24, 1, 8, 128)
    value = dot_exact(value.reshape(384, 128), copy)
    flat = spread.reshape(768, 128)
    for block in range(48):
        rows = value[8 * block : 8 * block + 8, :]
        flat[pl.ds(16 * block, 8, stride=2), :] = rows
        flat[pl.ds(16 * block + 1, 8, stride=2), :] = rows
    lane = iota((16, 128), 1)

    def pair(k):
        for f in range(3):
            for z in (2 * k, 2 * k + 1):
                value = rim[f, z]
                for half in range(2):
                    low = roll(value, -57 - 64 * half)
                    high = roll(value, 121 - 64 * half)
                    at = z + 16 * half
                    own = jnp.concatenate([two[f, at + 1, 16:24, :], two[f, at + 1, 0:8, :]], axis=0)
                    own = jnp.where(lane < 3, low, jnp.where(lane >= 125, high, own))
                    base[f, at] = own + spread[f, k + 8 * half]

    loop(8, pair, 4)


def resist(share):
    return recip(2.0 - 1.8 * share)


def level_weights(own, six, omega):
    faces = [recip(own + other) for other in six]
    diag = (faces[0] + faces[1]) + (faces[2] + faces[3]) + (faces[4] + faces[5])
    gain = omega * recip(diag)
    return gain, [gain * w for w in faces], diag


def middle_kernel(
    main, main_near, main_far, rim, rim_near, rim_far, sent, e_one, e_two,
    share, rest, rhs, first, second, weights, diags, halves, pooled,
    rest2, first2, second2, rhs2, share2, weights2,
):
    gx, gy = lax.axis_index("gx"), lax.axis_index("gy")
    low_x, high_x = jnp.where(gx > 0, 1, 0), jnp.where(gx < NX - 1, 1, 0)
    low_y, high_y = jnp.where(gy > 0, 1, 0), jnp.where(gy < NY - 1, 1, 0)

    for f in range(3):
        for ref in (first, second):
            ref[f, 0] = jnp.zeros((32, 128), F32)
            ref[f, 17] = jnp.zeros((32, 128), F32)
    for z in (0, 17):
        rest[z] = jnp.full((32, 128), 0.5, F32)
    lane = iota((8, 128), 1)
    even = lax.rem(gx, 2) == 0
    near_row, far_row = jnp.where(even, 16, 0), jnp.where(even, 0, 16)
    starts = (pl.multiple_of(near_row, 8), pl.multiple_of(far_row, 8), 8)

    sources = zip(starts, ((main_near, rim_near), (main_far, rim_far), (main, rim)))
    sources = list(sources)
    has_far = inner(gx)

    def fill(q):
        for odd in range(2):
            for half in range(2):
                z = 2 * q + odd + 8 * half
                base = 64 * odd + 32 * half
                for at, (middle, outer) in sources:
                    for ch in range(4):
                        edge, body = outer[ch, q], middle[ch, 2 * q + odd]
                        if outer is rim_far:
                            edge, body = jnp.where(has_far, edge, 0.0), jnp.where(has_far, body, 0.0)
                        value = jnp.where(lane < 62, roll(body, 64 * half), roll(edge, 62 - base))
                        value = jnp.where((lane >= 96) | (lane < 2), roll(edge, 112 - base), value)
                        if ch < 3:
                            rhs[ch, z, pl.ds(at, 8), :] = value
                        else:
                            share[z, pl.ds(at, 8), :] = value
                            rest[z + 1, pl.ds(at, 8), :] = resist(value)
                rest[z + 1, 24:32, :] = jnp.full((8, 128), 0.5, F32)

    loop(4, fill)

    row, lane = iota((24, 128), 0) + 1, iota((24, 128), 1)
    in_x = jnp.where(row < 8, low_x, jnp.where(row >= 16, high_x, 1))
    in_y = jnp.where(lane < 64, 1, jnp.where(lane < 96, high_y, low_y))
    omega = 0.8 * (in_x * in_y).astype(F32)

    def start(step):
        z = STEP * step
        for k, (own, six) in enumerate(block_of(rest, (), z + 1, STEP, 1, 24)):
            gain, w, diag = level_weights(own, six, omega)
            for i in range(6):
                weights[i, z + k, 1:25, :] = w[i]
            diags[z + k, 1:25, :] = (1.25 * 0.25) * diag
            for f in range(3):
                first[f, z + k + 1, 1:25, :] = (4.0 * gain) * rhs[f, z + k, 1:25, :]

    loop(16 // STEP, start)

    def sweep(step):
        z = STEP * step
        w = [[weights[i, z + k, 3:27, :] for i in range(6)] for k in range(STEP)]
        for f in range(3):
            for k, (own, six) in enumerate(block_of(first, (f,), z + 1, STEP, 3, 24)):
                second[f, z + k + 1, 3:27, :] = 1.2 * own + weigh(w[k], six)

    loop(16 // STEP, sweep)

    def left(step):
        z = STEP * step
        w = [[weights[i, z + k, 4:20, :] for i in range(6)] for k in range(STEP)]
        diag = [diags[z + k, 4:20, :] for k in range(STEP)]
        for f in range(3):
            values = []
            for k, (own, six) in enumerate(block_of(second, (f,), z + 1, STEP, 4, 16)):
                change = (first[f, z + k + 1, 4:20, :] - 0.8 * own) + weigh(w[k], six)
                values.append(change * diag[k])
                e_one[f, z + k] = second[f, z + k + 1, 8:16, :]
            for k in range(STEP // 2):
                halves[f, STEP // 2 * step + k, 0:16, :] = values[2 * k] + values[2 * k + 1]
                halves[f, STEP // 2 * step + k, 16:24, :] = jnp.zeros((8, 128), F32)
        for k in range(STEP // 2):
            halves[3, STEP // 2 * step + k] = share[z + 2 * k] + share[z + 2 * k + 1]

    loop(16 // STEP, left)

    source, target = iota((128, 128), 0), iota((128, 128), 1)
    pool = jnp.where(source // 2 + jnp.where(source >= 96, 64, 0) == target, 0.125, 0.0)
    pooled[...] = dot_exact(halves[...].reshape(4 * 8 * 24, 128), pool)
    for z in (0, 9):
        rest2[z] = jnp.full((24, 128), 0.5, F32)
        for f in range(3):
            first2[f, z] = jnp.zeros((24, 128), F32)
            second2[f, z] = jnp.zeros((24, 128), F32)
    for z in range(8):
        for f in range(3):
            base = (f * 8 + z) * 24
            rhs2[f, z] = pooled[pl.ds(base, 8, stride=2), :] + pooled[pl.ds(base + 1, 8, stride=2), :]
        base = (3 * 8 + z) * 24
        value = pooled[pl.ds(base + 2, 8, stride=2), :] + pooled[pl.ds(base + 3, 8, stride=2), :]
        rest2[z + 1, 0:8, :] = resist(value)
        value = pooled[pl.ds(base + 8, 8, stride=2), :] + pooled[pl.ds(base + 9, 8, stride=2), :]
        rest2[z + 1, 3:11, :] = resist(value)
        share2[z] = value

    row, lane = iota((8, 128), 0) + 1, iota((8, 128), 1)
    in_x = jnp.where(row < 3, low_x, jnp.where(row >= 7, high_x, 1))
    in_y = jnp.where(lane < 32, 1, jnp.where(lane < 96, high_y, low_y))
    omega2 = 0.8 * (in_x * in_y).astype(F32)

    for z, (own, six) in enumerate(block_of(rest2, (), 1, 8, 1, 8)):
        gain, w, diag = level_weights(own, six, omega2)
        for i in range(6):
            weights2[i, z, 1:9, :] = w[i]
        weights2[6, z, 1:9, :] = (1.25 * 0.0625) * diag
        for f in range(3):
            first2[f, z + 1, 1:9, :] = (16.0 * gain) * rhs2[f, z]
    w = [[weights2[i, z, 2:10, :] for i in range(6)] for z in range(8)]
    for f in range(3):
        for z, (own, six) in enumerate(block_of(first2, (f,), 1, 8, 2, 8)):
            second2[f, z + 1, 2:10, :] = 1.2 * own + weigh(w[z], six)
    w = [[weights2[i, z, 3:11, :] for i in range(7)] for z in range(8)]
    own_row = iota((8, 128), 0) < 4
    parts = [{} for pair in range(4)]
    for f in range(3):
        for z, (own, six) in enumerate(block_of(second2, (f,), 1, 8, 3, 8)):
            e_two[f, z] = own
            change = (first2[f, z + 1, 3:11, :] - 0.8 * own) + weigh(w[z], six)
            value = jnp.where(own_row, change * w[z][6], 0.0)
            sums = parts[z // 2]
            sums[f] = value if z % 2 == 0 else sums[f] + value
    for z in range(8):
        value = jnp.where(own_row, share2[z], 0.0)
        sums = parts[z // 2]
        sums[3] = value if z % 2 == 0 else sums[3] + value

    pool = jnp.where((source < 32) & (source // 2 == target % 16), 0.125, 0.0)
    rows = jnp.concatenate([parts[pair][ch] for ch in range(4) for pair in range(4)], axis=0)
    spread = dot(rows, pool)
    at, to = iota((32, 128), 0), iota((32, 128), 1)
    keep = (at // 8 == to // 32) & ((at % 8) // 2 == (to // 16) % 2)
    result = jnp.concatenate(
        [
            jnp.sum(jnp.where(keep, spread[32 * ch : 32 * ch + 32], 0.0), axis=0, keepdims=True)
            for ch in range(4)
        ],
        axis=0,
    )
    for copy in range(CHIPS):
        sent[copy] = result


def swap_blocks(x):
    sub, group = iota((8, 128), 0), iota((8, 128), 1) // 16
    for bit in (4, 2, 1):
        up = roll(roll(x, -bit, 0), 16 * bit)
        down = up if bit == 4 else roll(roll(x, bit, 0), -16 * bit)
        sub_set, group_set = (sub & bit) != 0, (group & bit) != 0
        x = jnp.where(sub_set == group_set, x, jnp.where(sub_set, down, up))
    return x


def top_kernel(
    mine, other, base, out,
    natural, first, second, four, weights, diags, lefts, final, sems,
):
    gx, gy = lax.axis_index("gx"), lax.axis_index("gy")
    first_core = lax.rem(gy, 2) == 0
    lane, sub = iota((16, 128), 1), iota((16, 128), 0)
    cells = [(z, x, half) for z in range(4) for x in range(2) for half in range(2)]

    def lay(g):
        for ch in range(4):
            rows = pl.ds(32 * g + ch, 8, stride=4)
            pair = mine[rows, :], other[rows, :]
            natural[ch, 0, pl.ds(pl.multiple_of(8 * g, 8), 8), :] = swap_blocks(
                jnp.where(first_core, pair[0], pair[1])
            )
            natural[ch, 1, pl.ds(pl.multiple_of(8 * g, 8), 8), :] = swap_blocks(
                jnp.where(first_core, pair[1], pair[0])
            )

    loop(16, lay, 4)
    flat = natural.reshape(1024, 128)

    def plane(ch, z, x, half):
        return flat[pl.ds((ch * 2 + half) * 128 + z * 2 + x, 16, stride=8), :]

    def neighbours(at, z, x, half, outside):
        own, other = at(z, x, half), at(z, 1 - x, half)
        beside = at(z, x, 1 - half)
        shifted = roll(other, 1 if x == 0 else -1, 0)
        low, high = (shifted, other) if x == 0 else (other, shifted)
        left, right = roll(own, 1), roll(own, -1)
        left = jnp.where(lane % 16 == 0, roll(beside, 1 if half == 0 else -15), left)
        right = jnp.where(lane % 16 == 15, roll(beside, 15 if half == 0 else -1), right)
        down = at(z - 1, x, half) if z > 0 else outside
        up = at(z + 1, x, half) if z < 3 else outside
        return own, [low, high, left, right, down, up]

    def edge_masks(x, half):
        return [
            sub > 0 if x == 0 else None,
            sub < 15 if x == 1 else None,
            lane > 0 if half == 0 else None,
            lane < 127 if half == 1 else None,
            None,
            None,
        ]

    def key(z, x, half):
        return (z * 2 + x) * 2 + half

    shares = {c: plane(3, *c) for c in cells}
    rests = {c: resist(shares[c]) for c in cells}
    outside, zeros = jnp.full((16, 128), 0.5, F32), jnp.zeros((16, 128), F32)
    for z, x, half in cells:
        own, six = neighbours(lambda *c: rests[c], z, x, half, outside)
        masks = edge_masks(x, half)
        six = [s if m is None else jnp.where(m, s, 0.5) for s, m in zip(six, masks)]
        gain, w, diag = level_weights(own, six, 0.8)
        at = key(z, x, half)
        for i in range(6):
            weights[i, at] = w[i] if masks[i] is None else jnp.where(masks[i], w[i], 0.0)
        diags[at] = (1.25 * 0.25**3) * diag
        for f in range(3):
            first[f, at] = (64.0 * gain) * plane(f, z, x, half)

    for z, x, half in cells:
        at = key(z, x, half)
        w = [weights[i, at] for i in range(6)]
        for f in range(3):
            own, six = neighbours(lambda *c: first[f, key(*c)], z, x, half, zeros)
            second[half, f, z * 2 + x] = 1.2 * own + weigh(w, six)

    for z4 in range(2):
        for half in range(2):
            sums = [None] * 4
            for z in (2 * z4, 2 * z4 + 1):
                for x in range(2):
                    at = key(z, x, half)
                    w = [weights[i, at] for i in range(6)]
                    diag = diags[at]
                    for f in range(3):
                        own, six = neighbours(
                            lambda c, d, e: second[e, f, c * 2 + d], z, x, half, zeros
                        )
                        value = ((first[f, at] - 0.8 * own) + weigh(w, six)) * diag
                        sums[f] = value if sums[f] is None else sums[f] + value
                    share = shares[z, x, half]
                    sums[3] = share if sums[3] is None else sums[3] + share
            for ch in range(4):
                lefts[ch, z4, :, 128 * half : 128 * half + 128] = sums[ch]

    source = iota((256, 128), 0)
    column = ((source % 128) // 16) * 16 + (source // 128) * 8 + (source % 16) // 2
    pool = jnp.where(column == iota((256, 128), 1), 0.125, 0.0)
    level = dot_exact(lefts[...].reshape(128, 256), pool)

    def coarsest(ch, z):
        return level[(ch * 2 + z) * 16 : (ch * 2 + z) * 16 + 16, :]

    masks = [sub > 0, sub < 15, lane > 0, lane < 127]
    resists = [resist(coarsest(3, z)) for z in range(2)]
    gains, ws, ds = [], [], []
    for z in range(2):
        own, other = resists[z], resists[1 - z]
        six = [roll(own, 1, 0), roll(own, -1, 0), roll(own, 1), roll(own, -1)]
        six = [jnp.where(m, s, 0.5) for m, s in zip(masks, six)] + [other, outside]
        gain, w, diag = level_weights(own, six, 0.8)
        gains.append(gain)
        ds.append(diag)
        ws.append([jnp.where(m, v, 0.0) for m, v in zip(masks, w)] + [w[4]])
    whole = jnp.sum(ds[0] + ds[1], keepdims=True)

    def around(values, z):
        own, other = values[z], values[1 - z]
        return weigh(ws[z], (roll(own, 1, 0), roll(own, -1, 0), roll(own, 1), roll(own, -1), other))

    begin = [[256.0 * gains[z] * coarsest(f, z) for z in range(2)] for f in range(3)]
    values = begin
    for step in range(5):
        values = [
            [(0.2 * values[f][z] + begin[f][z]) + around(values[f], z) for z in range(2)] for f in range(3)
        ]
    for f in range(3):
        change = [(begin[f][z] - 0.8 * values[f][z]) + around(values[f], z) for z in range(2)]
        total = jnp.sum(1.25 * (change[0] * ds[0] + change[1] * ds[1]), keepdims=True)
        for z in range(2):
            four[2 * f + z] = values[f][z] + total / whole

    copy = jnp.where(iota((128, 128), 0) == iota((128, 128), 1) // 2, 1.0, 0.0)
    rows = four.reshape(96, 128)[pl.ds(gx, 6, stride=16), :]
    rows = jnp.concatenate([jnp.broadcast_to(rows[i : i + 1], (4, 128)) for i in range(6)], axis=0)
    three = dot(turn(rows, -8 * gy), copy)
    flat = second.reshape(768, 128)
    halves = [flat[pl.ds(gx + 384 * half, 24, stride=16), :] for half in range(2)]
    three = three + turn(jnp.where(first_core, halves[0], halves[1]), -16 * lax.div(gy, 2))

    copy = jnp.where(iota((128, 128), 0) == iota((128, 128), 1) // 8, 1.0, 0.0)
    three = dot(three, copy)
    copies = []
    for f in range(3):
        for z in range(4):
            for x in range(2):
                at = f * 8 + z * 2 + x
                value = jnp.broadcast_to(three[at : at + 1], (8, 128))
                for k in range(8 * z, 8 * z + 8):
                    final[f, k, 8 * x : 8 * x + 8, :] = base[f, k, 8 * x : 8 * x + 8, :] + value
            if z % 2 == 1:
                part = (f, pl.ds(8 * z - 8, 16))
                copy = pltpu.make_async_copy(final.at[part], out.at[part], sems.at[len(copies)])
                copy.start()
                copies.append(copy)
    for copy in copies:
        copy.wait()


def local(labels, guess):
    swap_near = [(i, i ^ 1) for i in range(NY)]
    far_x, far_y = [], []
    for x in range(NX):
        for y in range(NY):
            across_x, across_y = x + 1 if x % 2 else x - 1, y + 1 if y % 2 else y - 1
            to = (across_x, y) if 0 <= across_x < NX else (x, y ^ 1)
            far_x.append((x * NY + y, to[0] * NY + to[1]))
            to = (x, across_y) if 0 <= across_y < NY else (x ^ 1, y)
            far_y.append((x * NY + y, to[0] * NY + to[1]))
    both = ("gx", "gy")
    to_near, to_far, own = call(
        rows_kernel,
        [(12, 32, 128)] * 2 + [(4, 32, 16, 128)],
        [pltpu.VMEM((32, 16, 128), jnp.int32), pltpu.SemaphoreType.DMA((4,))],
        in_specs=[ANY, ANY],
    )(pltpu.with_memory_space_constraint(guess, pltpu.HBM), pltpu.with_memory_space_constraint(labels, pltpu.HBM))
    from_near = lax.ppermute(to_near, "gx", swap_near)
    from_far = lax.ppermute(to_far, both, far_x)
    own_one, own_two, halves, to_right, to_left, edges = call(
        own_kernel,
        [(3, 34, 32, 128)] * 2 + [(4, 16, 16, 128)] + [(4, 4, 16, 128)] * 2 + [(4, 16, 16, 128)],
        [(4, 34, 32, 128), (6, 32, 32, 128), (32, 32, 128)],
        flops=20_000_000,
    )(own)
    to_near, to_far, rim_rows = call(pack_kernel, [(4, 4, 24, 128)] * 2 + [(4, 32, 8, 128)], [])(
        to_right, to_left, from_near, from_far
    )
    from_far = lax.ppermute(to_far, both, far_y)
    from_near = lax.ppermute(to_near, "gy", swap_near)
    two, main, edges_rim = call(
        rows_edge_kernel,
        [(3, 34, 24, 128), (4, 8, 8, 128), (4, 16, 8, 128)],
        [(4, 34, 24, 128), (3, 34, 24, 128), (6, 32, 24, 128), (32, 24, 128)]
        + [(4, 16, 16, 128), (512, 128)],
        flops=10_000_000,
    )(own, rim_rows, own_one, own_two, halves)
    main_near = lax.ppermute(main, "gx", swap_near)
    main_far = lax.ppermute(main, both, far_x)
    rim, rim_one = call(
        rim_kernel,
        [(3, 16, 16, 128), (4, 4, 8, 128)],
        [(3, 18, 32, 128), (18, 32, 128)]
        + [(3, 18, 32, 128)] * 2
        + [(6, 16, 32, 128), (16, 32, 128)]
        + [(4, 8, 16, 128), (256, 128)],
        flops=10_000_000,
    )(edges, edges_rim, from_near, from_far)
    rim_near = lax.ppermute(rim_one, "gx", swap_near)
    rim_far = lax.ppermute(rim_one, both, far_x)
    sent, e_one, e_two = call(
        middle_kernel,
        [(CHIPS, 4, 128), (3, 16, 8, 128), (3, 8, 8, 128)],
        [(16, 24, 128), (18, 32, 128), (3, 16, 32, 128), (3, 18, 32, 128), (3, 18, 32, 128)]
        + [(6, 16, 32, 128), (16, 32, 128), (4, 8, 24, 128), (768, 128)]
        + [(10, 24, 128), (3, 10, 24, 128), (3, 10, 24, 128), (3, 8, 8, 128), (8, 8, 128)]
        + [(7, 8, 16, 128)],
    )(main, main_near, main_far, rim_one, rim_near, rim_far)
    groups = [[i for i in range(NX * NY) if i % 2 == core] for core in range(2)]
    mine = lax.all_to_all(
        sent, ("gx", "gy"), split_axis=0, concat_axis=0, axis_index_groups=groups, tiled=True
    )
    (base,) = call(base_kernel, [(3, 32, 16, 128)], [(192, 128), (3, 16, 16, 128)])(two, rim, e_one, e_two)
    other = lax.ppermute(mine, "gy", swap_near)
    (out,) = call(
        top_kernel,
        [(3, 32, 16, 128)],
        [(4, 2, 128, 128), (3, 16, 16, 128), (2, 3, 8, 16, 128), (6, 16, 128), (6, 16, 16, 128)]
        + [(16, 16, 128), (4, 2, 16, 256), (3, 32, 16, 128), pltpu.SemaphoreType.DMA((6,))],
        out_specs=[ANY],
    )(mine.reshape(512, 128), other.reshape(512, 128), base)
    return out


def solution(mesh):
    return jax.shard_map(
        local,
        mesh=mesh,
        in_specs=(P(None, "gx", "gy"), P(None, None, "gx", "gy")),
        out_specs=P(None, None, "gx", "gy"),
        check_vma=False,
    )
```

```python
import jax
import jax.numpy as jnp
from jax import lax
from jax.experimental import pallas as pl
from jax.experimental.pallas import tpu as pltpu
from jax.sharding import PartitionSpec as P


F32 = jnp.float32
NX, NY, CHIPS = 16, 16, 128
STEP, WIDE = 16, 32
BETWEEN = 2.0 * 0.1 / 1.1
ANY = pl.BlockSpec(memory_space=pltpu.HBM)


def dot(a, b):
    return jnp.dot(a, b, precision=lax.Precision.HIGHEST, preferred_element_type=F32)


def dot_exact(a, b):
    high = a.astype(jnp.bfloat16)
    low = (a - high.astype(F32)).astype(jnp.bfloat16)
    b = b.astype(jnp.bfloat16)
    return jnp.dot(
        jnp.concatenate([high, low], axis=1), jnp.concatenate([b, b], axis=0), preferred_element_type=F32
    )


def iota(shape, dim):
    return lax.broadcasted_iota(jnp.int32, shape, dim)


def roll(x, shift, axis=1):
    shift = shift % x.shape[axis]
    return x if shift == 0 else pltpu.roll(x, shift, axis)


def turn(x, shift):
    return pltpu.roll(x, lax.rem(shift + 256, 128), 1)


def recip(x):
    guess = pl.reciprocal(x, approx=True)
    return guess * (2.0 - x * guess)


def inner(index):
    return (index > 0) & (index < 15)


def call(kernel, outs, scratch, flops=1_000_000, **kw):
    return pl.pallas_call(
        kernel,
        out_shape=[jax.ShapeDtypeStruct(s, F32) for s in outs],
        scratch_shapes=[pltpu.VMEM(s, F32) if isinstance(s, tuple) else s for s in scratch],
        compiler_params=pltpu.CompilerParams(vmem_limit_bytes=32 * 1024 * 1024),
        cost_estimate=pl.CostEstimate(flops=flops, bytes_accessed=4_000_000, transcendentals=0),
        **kw,
    )


def loop(count, body, unroll=1):
    def step(i, carry):
        body(i)
        return carry

    lax.fori_loop(0, count, step, 0, unroll=unroll)


def weigh(weights, values):
    parts = [w * v for w, v in zip(weights, values)]
    while len(parts) > 1:
        parts = [sum(parts[i : i + 2][1:], parts[i]) for i in range(0, len(parts), 2)]
    return parts[0]


def rows_kernel(guess, labels, near, far, own, phase, sems):
    even = lax.rem(lax.axis_index("gx"), 2) == 0
    near_row, far_row = jnp.where(even, 13, 0), jnp.where(even, 0, 13)
    copies = [pltpu.make_async_copy(labels, phase, sems.at[3])]
    for f in range(3):
        copies.append(pltpu.make_async_copy(guess.at[f], own.at[f], sems.at[f]))
    for copy in copies:
        copy.start()
    copies[0].wait()
    own[3] = jnp.where(phase[...] == 1, 0.0, 1.0).astype(F32)
    flat = own.reshape(4 * 32 * 16, 128)
    for ch in (3, 0, 1, 2):
        if ch < 3:
            copies[ch + 1].wait()
        for row in range(3):
            near[3 * ch + row] = flat[pl.ds(512 * ch + near_row + row, 32, stride=16), :]
            far[3 * ch + row] = flat[pl.ds(512 * ch + far_row + row, 32, stride=16), :]


def pack_kernel(to_right, to_left, x_near, x_far, near, far, rim):
    first_core = lax.rem(lax.axis_index("gy"), 2) == 0
    even = lax.rem(lax.axis_index("gx"), 2) == 0
    near_row, far_row = jnp.where(even, 0, 5), jnp.where(even, 5, 0)
    has_far = inner(lax.axis_index("gx"))
    flat = rim.reshape(4 * 32 * 8, 128)
    for ch in range(4):
        for row in range(3):
            flat[pl.ds(256 * ch + near_row + row, 32, stride=8), :] = x_near[3 * ch + row]
            flat[pl.ds(256 * ch + far_row + row, 32, stride=8), :] = jnp.where(has_far, x_far[3 * ch + row], 0.0)

    def some(low):
        for ch in range(4):
            right, left = pack_planes(lambda z: rim[ch, z], low, (8, 128))
            for at, right, left in (
                (slice(0, 16), to_right[ch, low], to_left[ch, low]),
                (slice(16, 24), right, left),
            ):
                near[ch, low, at, :] = jnp.where(first_core, right, left)
                far[ch, low, at, :] = jnp.where(first_core, left, right)

    loop(4, some, 4)


def pack_planes(plane, low, shape):
    group = iota(shape, 1) // 16
    right = left = jnp.zeros(shape, F32)
    for h in range(8):
        moved = roll(plane(4 * h + low), 16 * h + 16)
        right = jnp.where(group == h, moved, right)
        left = jnp.where(group == (h + 1) % 8, moved, left)
    return right, left


def edge_columns(plane, z, shape):
    lane = iota(shape, 1)
    value = jnp.zeros(shape, F32)
    for half in range(2):
        source = plane(z + 16 * half)
        base = 64 * half
        value = jnp.where((lane >= base) & (lane < base + 7), roll(source, base + 7), value)
        value = jnp.where((lane >= base + 57) & (lane < base + 64), roll(source, base + 57), value)
    return value


def six_of(ref, lead, z, first, count):
    own = ref[(*lead, z, pl.ds(first, count), slice(None))]
    return own, (
        ref[(*lead, z, pl.ds(first - 1, count), slice(None))],
        ref[(*lead, z, pl.ds(first + 1, count), slice(None))],
        roll(own, 1),
        roll(own, -1),
        ref[(*lead, z - 1, pl.ds(first, count), slice(None))],
        ref[(*lead, z + 1, pl.ds(first, count), slice(None))],
    )


def block_of(ref, lead, z, planes, first, count):
    rows = pl.ds(first, count)
    own = [ref[(*lead, z + k, rows, slice(None))] for k in range(-1, planes + 1)]
    result = []
    for k in range(planes):
        value = own[k + 1]
        six = (
            ref[(*lead, z + k, pl.ds(first - 1, count), slice(None))],
            ref[(*lead, z + k, pl.ds(first + 1, count), slice(None))],
            roll(value, 1),
            roll(value, -1),
            own[k],
            own[k + 2],
        )
        result.append((value, six))
    return result


def fine_weights(own, six, omega):
    base, slope = 1.0 + (BETWEEN - 1.0) * own, (BETWEEN - 1.0) + (1.1 - 2.0 * BETWEEN) * own
    total = (six[0] + six[1]) + (six[2] + six[3]) + (six[4] + six[5])
    diag = 6.0 * base + slope * total
    gain = omega * recip(diag)
    base, slope = gain * base, gain * slope
    return [base + slope * other for other in six], 1.25 * diag


def fine_sweep(w, f, own, six):
    return (0.2 * own + (w[2 * f + 1] - w[2 * f])) + weigh(w, six)


def fine_left(w, f, own, six, diag):
    return (((w[2 * f + 1] - w[2 * f]) - 0.8 * own) + weigh(w, six)) * diag


def fine_sweeps(planes, windows, start, share, one, two, weights, diags, halves, omega, wrap, keep, size):
    first, count = windows[0]

    def first_sweep(step):
        z = size * step
        w = []
        for k, (own, six) in enumerate(block_of(share, (), z + 1, size, first, count)):
            now, diag = fine_weights(own, six, omega)
            diags[z + k, pl.ds(first, count), :] = diag
            for i in range(6):
                weights[i, z + k, pl.ds(first, count), :] = now[i]
            w.append(now)
        for f in range(3):
            for k, (own, six) in enumerate(block_of(start, (f,), z + 1, size, first, count)):
                one[f, z + k + 1, pl.ds(first, count), :] = fine_sweep(w[k], f, own, six)

    loop(planes // size, first_sweep)
    wrap(one)
    second, count2 = windows[1]

    def second_sweep(step):
        z = size * step
        w = [[weights[i, z + k, pl.ds(second, count2), :] for i in range(6)] for k in range(size)]
        for f in range(3):
            for k, (own, six) in enumerate(block_of(one, (f,), z + 1, size, second, count2)):
                two[f, z + k + 1, pl.ds(second, count2), :] = fine_sweep(w[k], f, own, six)

    loop(planes // size, second_sweep)
    wrap(two)

    def residual(step):
        z = size * step
        w = [[weights[i, z + k, 8:24, :] for i in range(6)] for k in range(size)]
        diag = [diags[z + k, 8:24, :] for k in range(size)]
        for f in range(3):
            values = []
            for k, (own, six) in enumerate(block_of(two, (f,), z + 1, size, 8, 16)):
                if keep is not None:
                    keep[f, z + k] = own
                values.append(fine_left(w[k], f, own, six, diag[k]))
            for pair in range(size // 2):
                halves[f, size // 2 * step + pair] = values[2 * pair] + values[2 * pair + 1]
        for pair in range(size // 2):
            at = z + 2 * pair + 1
            halves[3, size // 2 * step + pair] = share[at, 8:24, :] + share[at + 1, 8:24, :]

    loop(planes // size, residual)


def own_kernel(own, one, two, halves, to_right, to_left, edges, held, weights, diags):
    zero = jnp.zeros((32, 128), F32)
    for z in (0, 33):
        for ch in range(4):
            held[ch, z] = zero
        for ref in (one, two):
            for f in range(3):
                ref[f, z] = zero

    def plane(z):
        for ch in range(4):
            held[ch, z + 1, 8:24, :] = own[ch, z]

    loop(32, plane, 8)
    fine_sweeps(
        32, [(8, 16)] * 2, held, held.at[3], one, two, weights, diags, halves, 0.8, lambda ref: None, None, 8
    )

    def some(low):
        for ch in range(4):
            to_right[ch, low], to_left[ch, low] = pack_planes(lambda z: own[ch, z], low, (16, 128))

    loop(4, some, 2)

    def edge(z):
        for ch in range(4):
            edges[ch, z] = edge_columns(lambda at: own[ch, at], z, (16, 128))

    loop(16, edge, 8)


def rows_edge_kernel(own, rim, own_one, own_two, own_halves, two, coarse, edges, start, one, weights, diags, halves, pooled):
    gx = lax.axis_index("gx")
    zero = jnp.zeros((24, 128), F32)
    for z in (0, 33):
        for ch in range(4):
            start[ch, z] = zero
        for ref in (one, two):
            for f in range(3):
                ref[f, z] = zero

    def fill(z):
        for ch in range(4):
            start[ch, z + 1, 0:8, :] = own[ch, z, 8:16, :]
            start[ch, z + 1, 8:16, :] = rim[ch, z]
            start[ch, z + 1, 16:24, :] = own[ch, z, 0:8, :]
        for f in range(3):
            for ref, source in ((one, own_one), (two, own_two)):
                ref[f, z + 1, 0:8, :] = source[f, z + 1, 16:24, :]
                ref[f, z + 1, 16:24, :] = source[f, z + 1, 8:16, :]

    loop(32, fill, 8)
    upper = iota((8, 128), 0) < 4

    def both(ref, lead, step, shift=0):
        high = ref[(*lead, pl.ds(8 - step + shift, 8), slice(None))]
        low = ref[(*lead, pl.ds(8 + step + shift, 8), slice(None))]
        return jnp.where(upper, high, low)

    def block_both(ref, f, z, step):
        own = [both(ref, (f, z + k), step) for k in range(-1, WIDE + 1)]
        result = []
        for k in range(WIDE):
            value = own[k + 1]
            low, high = both(ref, (f, z + k), step, -1), both(ref, (f, z + k), step, 1)
            result.append((value, (low, high, roll(value, 1), roll(value, -1), own[k], own[k + 2])))
        return result

    def put(ref, f, z, step, value):
        ref[f, z, pl.ds(8 - step, 4), :] = value[0:4]
        ref[f, z, pl.ds(12 + step, 4), :] = value[4:8]

    row = iota((16, 128), 0) + 5
    low, high = jnp.where(gx > 0, 1, 0), jnp.where(gx < NX - 1, 1, 0)
    inside = jnp.where((row >= 8) & (row < 12), high, jnp.where((row >= 12) & (row < 16), low, 1))
    omega = 0.8 * inside.astype(F32)

    def weigh_all(step):
        z = WIDE * step
        for k, (value, six) in enumerate(block_of(start, (3,), z + 1, WIDE, 5, 16)):
            w, diag = fine_weights(value, six, omega)
            diags[z + k, 5:21, :] = diag
            for i in range(6):
                weights[i, z + k, 5:21, :] = w[i]

    loop(32 // WIDE, weigh_all)

    for step, source, target in ((1, start, one), (2, one, two)):

        def sweep(block):
            z = WIDE * block
            w = [[both(weights, (i, z + k), step) for i in range(6)] for k in range(WIDE)]
            for f in range(3):
                for k, (value, six) in enumerate(block_both(source, f, z + 1, step)):
                    put(target, f, z + k + 1, step, fine_sweep(w[k], f, value, six))

        loop(32 // WIDE, sweep)

    sub = iota((8, 128), 0)

    def residual(block):
        z = WIDE * block
        w = [[both(weights, (i, z + k), 3) for i in range(6)] for k in range(WIDE)]
        diag = [both(diags, (z + k,), 3) for k in range(WIDE)]
        for f in range(3):
            values = []
            for k, (value, six) in enumerate(block_both(two, f, z + 1, 3)):
                values.append(fine_left(w[k], f, value, six, diag[k]))
            for k in range(WIDE // 2):
                pair = WIDE // 2 * block + k
                value = values[2 * k] + values[2 * k + 1]
                halves[f, pair, 0:8, :] = jnp.where(sub < 3, roll(value, 3, 0), own_halves[f, pair, 0:8, :])
                halves[f, pair, 8:16, :] = jnp.where(sub >= 5, roll(value, 5, 0), own_halves[f, pair, 8:16, :])
        for k in range(WIDE // 2):
            halves[3, WIDE // 2 * block + k] = own_halves[3, WIDE // 2 * block + k]

    loop(32 // WIDE, residual)
    pool = jnp.where(iota((128, 128), 0) // 2 == iota((128, 128), 1), 0.125, 0.0)
    pooled[...] = dot_exact(halves[...].reshape(1024, 128), pool)
    coarse[...] = (pooled[pl.ds(0, 512, stride=2), :] + pooled[pl.ds(1, 512, stride=2), :]).reshape(4, 16, 8, 128)

    def edge(z):
        for ch in range(4):
            edges[ch, z] = edge_columns(lambda at: rim[ch, at], z, (8, 128))

    loop(16, edge, 8)


def rim_kernel(
    edges, edges_rim, owned, near, far, field, coarse, packed,
    start, share, one, two, weights, diags, halves, pooled,
):
    gx, gy = lax.axis_index("gx"), lax.axis_index("gy")
    lane = iota((24, 128), 1)
    part = lane % 64
    is_after = (part >= 7) & (part < 22)
    is_before = (part >= 42) & (part < 57)
    first_core = lax.rem(gy, 2) == 0

    def unpack(low):
        for ch in range(4):
            target = start.at[ch] if ch < 3 else share
            from_near, from_far = near[ch, low], jnp.where(inner(gy), far[ch, low], 0.0)
            from_right = jnp.where(first_core, from_near, from_far)
            from_left = jnp.where(first_core, from_far, from_near)
            for h in range(4):
                z = 4 * h + low
                after_y = roll(from_right, 7 - 16 * (h + 1))
                before_y = roll(from_left, 41 - 16 * h)
                own = jnp.concatenate([edges[ch, z], edges_rim[ch, z]], axis=0)
                value = jnp.where(is_after, after_y, jnp.where(is_before, before_y, own))
                target[z + 1, 8:24, :] = value[0:16]
                target[z + 1, 0:8, :] = value[16:24]
                target[z + 1, 24:32, :] = value[16:24]

    loop(4, unpack, 2)

    half_of = iota((32, 128), 1)

    def wrap_one(ref):
        ref[0] = jnp.where(half_of >= 64, roll(ref[16], 64), 0.0)
        ref[17] = jnp.where(half_of < 64, roll(ref[1], 64), 0.0)

    def wrap(ref):
        for f in range(3):
            wrap_one(ref.at[f])

    wrap_one(share)
    wrap(start)
    row = iota((24, 128), 0) + 6
    low, high = jnp.where(gx > 0, 1, 0), jnp.where(gx < NX - 1, 1, 0)
    inside_x = jnp.where(row < 8, low, jnp.where(row >= 24, high, 1))
    inside_y = jnp.where(
        part < 32,
        jnp.where((part < 7) | (gy < NY - 1), 1, 0),
        jnp.where((part >= 57) | (gy > 0), 1, 0),
    )
    omega = 0.8 * (inside_x * inside_y).astype(F32)
    fine_sweeps(
        16, [(6, 24), (7, 24)], start, share, one, two, weights, diags, halves, omega, wrap, field, STEP
    )

    source, target = iota((128, 128), 0), iota((128, 128), 1)
    spot = source % 64
    column = jnp.where(spot < 32, 121 + spot, 128 + spot - 57)
    to = jnp.where(spot < 32, column // 2, (column // 2 + 64) % 128)
    from_rim = (iota((64, 128), 1) < 2) | (iota((64, 128), 1) >= 62)
    mixed = halves[...].reshape(512, 128)
    for half in range(2):
        pool = jnp.where((to == target) & (source // 64 == half), 0.125, 0.0)
        pooled[...] = dot_exact(mixed, pool)
        for ch in range(4):
            even = pooled[pl.ds(128 * ch, 64, stride=2), :]
            odd = pooled[pl.ds(128 * ch + 1, 64, stride=2), :]
            at = pl.ds(8 * half, 8)
            rest = owned[ch, at].reshape(64, 128)
            coarse[ch, at] = jnp.where(from_rim, even + odd, rest).reshape(8, 8, 128)

    lane = iota((8, 128), 1)
    for ch in range(4):
        for group in range(2):
            tiles = [None] * 5
            for k in range(8):
                moved = roll(coarse[ch, 8 * group + k], 8 + 80 * k)
                tile, off = divmod(80 * k, 128)
                tiles[tile] = moved if off == 0 else jnp.where(lane >= off, moved, tiles[tile])
                if off + 80 > 128:
                    tiles[tile + 1] = moved
            for tile in range(5):
                packed[ch, group, tile] = tiles[tile]


def base_kernel(two, rim, e_one, e_two, base, wide, spread):
    copy = jnp.where(iota((128, 128), 0) == iota((128, 128), 1) // 2, 1.0, 0.0)
    value = dot_exact(e_two[...].reshape(192, 128), copy)
    for block in range(24):
        rows = value[8 * block : 8 * block + 4, :]
        wide[pl.ds(8 * block, 4, stride=2), :] = rows
        wide[pl.ds(8 * block + 1, 4, stride=2), :] = rows
    value = e_one[...].reshape(24, 2, 8, 128) + wide[...].reshape(24, 1, 8, 128)
    value = dot_exact(value.reshape(384, 128), copy)
    flat = spread.reshape(768, 128)
    for block in range(48):
        rows = value[8 * block : 8 * block + 8, :]
        flat[pl.ds(16 * block, 8, stride=2), :] = rows
        flat[pl.ds(16 * block + 1, 8, stride=2), :] = rows
    lane = iota((16, 128), 1)

    def pair(k):
        for f in range(3):
            for z in (2 * k, 2 * k + 1):
                value = rim[f, z]
                for half in range(2):
                    low = roll(value, -57 - 64 * half)
                    high = roll(value, 121 - 64 * half)
                    at = z + 16 * half
                    own = jnp.concatenate([two[f, at + 1, 16:24, :], two[f, at + 1, 0:8, :]], axis=0)
                    own = jnp.where(lane < 3, low, jnp.where(lane >= 125, high, own))
                    base[f, at] = own + spread[f, k + 8 * half]

    loop(8, pair, 4)


def resist(share):
    return recip(2.0 - 1.8 * share)


def level_weights(own, six, omega):
    faces = [recip(own + other) for other in six]
    diag = (faces[0] + faces[1]) + (faces[2] + faces[3]) + (faces[4] + faces[5])
    gain = omega * recip(diag)
    return gain, [gain * w for w in faces], diag


def middle_kernel(
    mine, near, far, sent, e_one, e_two,
    share, rest, rhs, first, second, weights, diags, halves, pooled,
    rest2, first2, second2, rhs2, share2, weights2,
):
    gx, gy = lax.axis_index("gx"), lax.axis_index("gy")
    low_x, high_x = jnp.where(gx > 0, 1, 0), jnp.where(gx < NX - 1, 1, 0)
    low_y, high_y = jnp.where(gy > 0, 1, 0), jnp.where(gy < NY - 1, 1, 0)

    for f in range(3):
        for ref in (first, second):
            ref[f, 0] = jnp.zeros((32, 128), F32)
            ref[f, 17] = jnp.zeros((32, 128), F32)
    for z in (0, 17):
        rest[z] = jnp.full((32, 128), 0.5, F32)
    lane = iota((8, 128), 1)
    even = lax.rem(gx, 2) == 0
    near_row, far_row = jnp.where(even, 16, 0), jnp.where(even, 0, 16)
    starts = (pl.multiple_of(near_row, 8), pl.multiple_of(far_row, 8), 8)

    has_far = inner(gx)

    def fill(group):
        for k in range(8):
            z = 8 * group + k
            tile, off = divmod(80 * k, 128)
            for ch in range(4):
                parts = []
                for ref in (near, far):
                    value = ref[ch, group, tile]
                    if off + 80 > 128:
                        value = jnp.where(lane >= off, value, ref[ch, group, tile + 1])
                    value = value if ref is near else jnp.where(has_far, value, 0.0)
                    parts.append(roll(value, -8 - 80 * k))
                parts.append(mine[ch, z])
                for at, value in zip(starts, parts):
                    if ch < 3:
                        rhs[ch, z, pl.ds(at, 8), :] = value
                    else:
                        share[z, pl.ds(at, 8), :] = value
                        rest[z + 1, pl.ds(at, 8), :] = resist(value)
            rest[z + 1, 24:32, :] = jnp.full((8, 128), 0.5, F32)

    loop(2, fill, 2)

    row, lane = iota((24, 128), 0) + 1, iota((24, 128), 1)
    in_x = jnp.where(row < 8, low_x, jnp.where(row >= 16, high_x, 1))
    in_y = jnp.where(lane < 64, 1, jnp.where(lane < 96, high_y, low_y))
    omega = 0.8 * (in_x * in_y).astype(F32)

    def start(step):
        z = STEP * step
        for k, (own, six) in enumerate(block_of(rest, (), z + 1, STEP, 1, 24)):
            gain, w, diag = level_weights(own, six, omega)
            for i in range(6):
                weights[i, z + k, 1:25, :] = w[i]
            diags[z + k, 1:25, :] = (1.25 * 0.25) * diag
            for f in range(3):
                first[f, z + k + 1, 1:25, :] = (4.0 * gain) * rhs[f, z + k, 1:25, :]

    loop(16 // STEP, start)

    def sweep(step):
        z = STEP * step
        w = [[weights[i, z + k, 3:27, :] for i in range(6)] for k in range(STEP)]
        for f in range(3):
            for k, (own, six) in enumerate(block_of(first, (f,), z + 1, STEP, 3, 24)):
                second[f, z + k + 1, 3:27, :] = 1.2 * own + weigh(w[k], six)

    loop(16 // STEP, sweep)

    def left(step):
        z = STEP * step
        w = [[weights[i, z + k, 4:20, :] for i in range(6)] for k in range(STEP)]
        diag = [diags[z + k, 4:20, :] for k in range(STEP)]
        for f in range(3):
            values = []
            for k, (own, six) in enumerate(block_of(second, (f,), z + 1, STEP, 4, 16)):
                change = (first[f, z + k + 1, 4:20, :] - 0.8 * own) + weigh(w[k], six)
                values.append(change * diag[k])
                e_one[f, z + k] = second[f, z + k + 1, 8:16, :]
            for k in range(STEP // 2):
                halves[f, STEP // 2 * step + k, 0:16, :] = values[2 * k] + values[2 * k + 1]
                halves[f, STEP // 2 * step + k, 16:24, :] = jnp.zeros((8, 128), F32)
        for k in range(STEP // 2):
            halves[3, STEP // 2 * step + k] = share[z + 2 * k] + share[z + 2 * k + 1]

    loop(16 // STEP, left)

    source, target = iota((128, 128), 0), iota((128, 128), 1)
    pool = jnp.where(source // 2 + jnp.where(source >= 96, 64, 0) == target, 0.125, 0.0)
    pooled[...] = dot_exact(halves[...].reshape(4 * 8 * 24, 128), pool)
    for z in (0, 9):
        rest2[z] = jnp.full((24, 128), 0.5, F32)
        for f in range(3):
            first2[f, z] = jnp.zeros((24, 128), F32)
            second2[f, z] = jnp.zeros((24, 128), F32)
    for z in range(8):
        for f in range(3):
            base = (f * 8 + z) * 24
            rhs2[f, z] = pooled[pl.ds(base, 8, stride=2), :] + pooled[pl.ds(base + 1, 8, stride=2), :]
        base = (3 * 8 + z) * 24
        value = pooled[pl.ds(base + 2, 8, stride=2), :] + pooled[pl.ds(base + 3, 8, stride=2), :]
        rest2[z + 1, 0:8, :] = resist(value)
        value = pooled[pl.ds(base + 8, 8, stride=2), :] + pooled[pl.ds(base + 9, 8, stride=2), :]
        rest2[z + 1, 3:11, :] = resist(value)
        share2[z] = value

    row, lane = iota((8, 128), 0) + 1, iota((8, 128), 1)
    in_x = jnp.where(row < 3, low_x, jnp.where(row >= 7, high_x, 1))
    in_y = jnp.where(lane < 32, 1, jnp.where(lane < 96, high_y, low_y))
    omega2 = 0.8 * (in_x * in_y).astype(F32)

    for z, (own, six) in enumerate(block_of(rest2, (), 1, 8, 1, 8)):
        gain, w, diag = level_weights(own, six, omega2)
        for i in range(6):
            weights2[i, z, 1:9, :] = w[i]
        weights2[6, z, 1:9, :] = (1.25 * 0.0625) * diag
        for f in range(3):
            first2[f, z + 1, 1:9, :] = (16.0 * gain) * rhs2[f, z]
    w = [[weights2[i, z, 2:10, :] for i in range(6)] for z in range(8)]
    for f in range(3):
        for z, (own, six) in enumerate(block_of(first2, (f,), 1, 8, 2, 8)):
            second2[f, z + 1, 2:10, :] = 1.2 * own + weigh(w[z], six)
    w = [[weights2[i, z, 3:11, :] for i in range(7)] for z in range(8)]
    own_row = iota((8, 128), 0) < 4
    parts = [{} for pair in range(4)]
    for f in range(3):
        for z, (own, six) in enumerate(block_of(second2, (f,), 1, 8, 3, 8)):
            e_two[f, z] = own
            change = (first2[f, z + 1, 3:11, :] - 0.8 * own) + weigh(w[z], six)
            value = jnp.where(own_row, change * w[z][6], 0.0)
            sums = parts[z // 2]
            sums[f] = value if z % 2 == 0 else sums[f] + value
    for z in range(8):
        value = jnp.where(own_row, share2[z], 0.0)
        sums = parts[z // 2]
        sums[3] = value if z % 2 == 0 else sums[3] + value

    pool = jnp.where((source < 32) & (source // 2 == target % 16), 0.125, 0.0)
    rows = jnp.concatenate([parts[pair][ch] for ch in range(4) for pair in range(4)], axis=0)
    spread = dot(rows, pool)
    at, to = iota((32, 128), 0), iota((32, 128), 1)
    keep = (at // 8 == to // 32) & ((at % 8) // 2 == (to // 16) % 2)
    result = jnp.concatenate(
        [
            jnp.sum(jnp.where(keep, spread[32 * ch : 32 * ch + 32], 0.0), axis=0, keepdims=True)
            for ch in range(4)
        ],
        axis=0,
    )
    for copy in range(CHIPS):
        sent[copy] = result


def swap_blocks(x):
    sub, group = iota((8, 128), 0), iota((8, 128), 1) // 16
    for bit in (4, 2, 1):
        up = roll(roll(x, -bit, 0), 16 * bit)
        down = up if bit == 4 else roll(roll(x, bit, 0), -16 * bit)
        sub_set, group_set = (sub & bit) != 0, (group & bit) != 0
        x = jnp.where(sub_set == group_set, x, jnp.where(sub_set, down, up))
    return x


def top_kernel(
    mine, other, base, out,
    natural, first, second, four, weights, diags, lefts, final, sems,
):
    gx, gy = lax.axis_index("gx"), lax.axis_index("gy")
    first_core = lax.rem(gy, 2) == 0
    lane, sub = iota((16, 128), 1), iota((16, 128), 0)
    cells = [(z, x, half) for z in range(4) for x in range(2) for half in range(2)]

    def lay(g):
        for ch in range(4):
            rows = pl.ds(32 * g + ch, 8, stride=4)
            pair = mine[rows, :], other[rows, :]
            natural[ch, 0, pl.ds(pl.multiple_of(8 * g, 8), 8), :] = swap_blocks(
                jnp.where(first_core, pair[0], pair[1])
            )
            natural[ch, 1, pl.ds(pl.multiple_of(8 * g, 8), 8), :] = swap_blocks(
                jnp.where(first_core, pair[1], pair[0])
            )

    loop(16, lay, 16)
    flat = natural.reshape(1024, 128)

    def plane(ch, z, x, half):
        return flat[pl.ds((ch * 2 + half) * 128 + z * 2 + x, 16, stride=8), :]

    def neighbours(at, z, x, half, outside):
        own, other = at(z, x, half), at(z, 1 - x, half)
        beside = at(z, x, 1 - half)
        shifted = roll(other, 1 if x == 0 else -1, 0)
        low, high = (shifted, other) if x == 0 else (other, shifted)
        left, right = roll(own, 1), roll(own, -1)
        left = jnp.where(lane % 16 == 0, roll(beside, 1 if half == 0 else -15), left)
        right = jnp.where(lane % 16 == 15, roll(beside, 15 if half == 0 else -1), right)
        down = at(z - 1, x, half) if z > 0 else outside
        up = at(z + 1, x, half) if z < 3 else outside
        return own, [low, high, left, right, down, up]

    def edge_masks(x, half):
        return [
            sub > 0 if x == 0 else None,
            sub < 15 if x == 1 else None,
            lane > 0 if half == 0 else None,
            lane < 127 if half == 1 else None,
            None,
            None,
        ]

    def key(z, x, half):
        return (z * 2 + x) * 2 + half

    shares = {c: plane(3, *c) for c in cells}
    rests = {c: resist(shares[c]) for c in cells}
    outside, zeros = jnp.full((16, 128), 0.5, F32), jnp.zeros((16, 128), F32)
    for z, x, half in cells:
        own, six = neighbours(lambda *c: rests[c], z, x, half, outside)
        masks = edge_masks(x, half)
        six = [s if m is None else jnp.where(m, s, 0.5) for s, m in zip(six, masks)]
        gain, w, diag = level_weights(own, six, 0.8)
        at = key(z, x, half)
        for i in range(6):
            weights[i, at] = w[i] if masks[i] is None else jnp.where(masks[i], w[i], 0.0)
        diags[at] = (1.25 * 0.25**3) * diag
        for f in range(3):
            first[f, at] = (64.0 * gain) * plane(f, z, x, half)

    for z, x, half in cells:
        at = key(z, x, half)
        w = [weights[i, at] for i in range(6)]
        for f in range(3):
            own, six = neighbours(lambda *c: first[f, key(*c)], z, x, half, zeros)
            second[half, f, z * 2 + x] = 1.2 * own + weigh(w, six)

    for z4 in range(2):
        for half in range(2):
            sums = [None] * 4
            for z in (2 * z4, 2 * z4 + 1):
                for x in range(2):
                    at = key(z, x, half)
                    w = [weights[i, at] for i in range(6)]
                    diag = diags[at]
                    for f in range(3):
                        own, six = neighbours(
                            lambda c, d, e: second[e, f, c * 2 + d], z, x, half, zeros
                        )
                        value = ((first[f, at] - 0.8 * own) + weigh(w, six)) * diag
                        sums[f] = value if sums[f] is None else sums[f] + value
                    share = shares[z, x, half]
                    sums[3] = share if sums[3] is None else sums[3] + share
            for ch in range(4):
                lefts[ch, z4, :, 128 * half : 128 * half + 128] = sums[ch]

    source = iota((256, 128), 0)
    column = ((source % 128) // 16) * 16 + (source // 128) * 8 + (source % 16) // 2
    pool = jnp.where(column == iota((256, 128), 1), 0.125, 0.0)
    level = dot_exact(lefts[...].reshape(128, 256), pool)

    def coarsest(ch, z):
        return level[(ch * 2 + z) * 16 : (ch * 2 + z) * 16 + 16, :]

    masks = [sub > 0, sub < 15, lane > 0, lane < 127]
    resists = [resist(coarsest(3, z)) for z in range(2)]
    gains, ws, ds = [], [], []
    for z in range(2):
        own, other = resists[z], resists[1 - z]
        six = [roll(own, 1, 0), roll(own, -1, 0), roll(own, 1), roll(own, -1)]
        six = [jnp.where(m, s, 0.5) for m, s in zip(masks, six)] + [other, outside]
        gain, w, diag = level_weights(own, six, 0.8)
        gains.append(gain)
        ds.append(diag)
        ws.append([jnp.where(m, v, 0.0) for m, v in zip(masks, w)] + [w[4]])
    whole = jnp.sum(ds[0] + ds[1], keepdims=True)

    def around(values, z):
        own, other = values[z], values[1 - z]
        return weigh(ws[z], (roll(own, 1, 0), roll(own, -1, 0), roll(own, 1), roll(own, -1), other))

    begin = [[256.0 * gains[z] * coarsest(f, z) for z in range(2)] for f in range(3)]
    values = begin
    for step in range(5):
        values = [
            [(0.2 * values[f][z] + begin[f][z]) + around(values[f], z) for z in range(2)] for f in range(3)
        ]
    for f in range(3):
        change = [(begin[f][z] - 0.8 * values[f][z]) + around(values[f], z) for z in range(2)]
        total = jnp.sum(1.25 * (change[0] * ds[0] + change[1] * ds[1]), keepdims=True)
        for z in range(2):
            four[2 * f + z] = values[f][z] + total / whole

    copy = jnp.where(iota((128, 128), 0) == iota((128, 128), 1) // 2, 1.0, 0.0)
    rows = four.reshape(96, 128)[pl.ds(gx, 6, stride=16), :]
    rows = jnp.concatenate([jnp.broadcast_to(rows[i : i + 1], (4, 128)) for i in range(6)], axis=0)
    three = dot(turn(rows, -8 * gy), copy)
    flat = second.reshape(768, 128)
    halves = [flat[pl.ds(gx + 384 * half, 24, stride=16), :] for half in range(2)]
    three = three + turn(jnp.where(first_core, halves[0], halves[1]), -16 * lax.div(gy, 2))

    copy = jnp.where(iota((128, 128), 0) == iota((128, 128), 1) // 8, 1.0, 0.0)
    three = dot(three, copy)
    copies = []
    for f in range(3):
        for z in range(4):
            for x in range(2):
                at = f * 8 + z * 2 + x
                value = jnp.broadcast_to(three[at : at + 1], (8, 128))
                for k in range(8 * z, 8 * z + 8):
                    final[f, k, 8 * x : 8 * x + 8, :] = base[f, k, 8 * x : 8 * x + 8, :] + value
            if z % 2 == 1:
                part = (f, pl.ds(8 * z - 8, 16))
                copy = pltpu.make_async_copy(final.at[part], out.at[part], sems.at[len(copies)])
                copy.start()
                copies.append(copy)
    for copy in copies:
        copy.wait()


def local(labels, guess):
    swap_near = [(i, i ^ 1) for i in range(NY)]
    far_x, far_y = [], []
    for x in range(NX):
        for y in range(NY):
            across_x, across_y = x + 1 if x % 2 else x - 1, y + 1 if y % 2 else y - 1
            to = (across_x, y) if 0 <= across_x < NX else (x, y ^ 1)
            far_x.append((x * NY + y, to[0] * NY + to[1]))
            to = (x, across_y) if 0 <= across_y < NY else (x ^ 1, y)
            far_y.append((x * NY + y, to[0] * NY + to[1]))
    both = ("gx", "gy")
    to_near, to_far, own = call(
        rows_kernel,
        [(12, 32, 128)] * 2 + [(4, 32, 16, 128)],
        [pltpu.VMEM((32, 16, 128), jnp.int32), pltpu.SemaphoreType.DMA((4,))],
        in_specs=[ANY, ANY],
    )(pltpu.with_memory_space_constraint(guess, pltpu.HBM), pltpu.with_memory_space_constraint(labels, pltpu.HBM))
    from_near = lax.ppermute(to_near, "gx", swap_near)
    from_far = lax.ppermute(to_far, both, far_x)
    own_one, own_two, halves, to_right, to_left, edges = call(
        own_kernel,
        [(3, 34, 32, 128)] * 2 + [(4, 16, 16, 128)] + [(4, 4, 16, 128)] * 2 + [(4, 16, 16, 128)],
        [(4, 34, 32, 128), (6, 32, 32, 128), (32, 32, 128)],
        flops=20_000_000,
    )(own)
    to_near, to_far, rim_rows = call(pack_kernel, [(4, 4, 24, 128)] * 2 + [(4, 32, 8, 128)], [])(
        to_right, to_left, from_near, from_far
    )
    from_far = lax.ppermute(to_far, both, far_y)
    from_near = lax.ppermute(to_near, "gy", swap_near)
    two, part, edges_rim = call(
        rows_edge_kernel,
        [(3, 34, 24, 128), (4, 16, 8, 128), (4, 16, 8, 128)],
        [(4, 34, 24, 128), (3, 34, 24, 128), (6, 32, 24, 128), (32, 24, 128)]
        + [(4, 16, 16, 128), (1024, 128)],
        flops=10_000_000,
    )(own, rim_rows, own_one, own_two, halves)
    rim, coarse, packed = call(
        rim_kernel,
        [(3, 16, 16, 128), (4, 16, 8, 128), (4, 2, 5, 8, 128)],
        [(3, 18, 32, 128), (18, 32, 128)]
        + [(3, 18, 32, 128)] * 2
        + [(6, 16, 32, 128), (16, 32, 128)]
        + [(4, 8, 16, 128), (512, 128)],
        flops=10_000_000,
    )(edges, edges_rim, part, from_near, from_far)
    from_near = lax.ppermute(packed, "gx", swap_near)
    from_far = lax.ppermute(packed, both, far_x)
    sent, e_one, e_two = call(
        middle_kernel,
        [(CHIPS, 4, 128), (3, 16, 8, 128), (3, 8, 8, 128)],
        [(16, 24, 128), (18, 32, 128), (3, 16, 32, 128), (3, 18, 32, 128), (3, 18, 32, 128)]
        + [(6, 16, 32, 128), (16, 32, 128), (4, 8, 24, 128), (768, 128)]
        + [(10, 24, 128), (3, 10, 24, 128), (3, 10, 24, 128), (3, 8, 8, 128), (8, 8, 128)]
        + [(7, 8, 16, 128)],
    )(coarse, from_near, from_far)
    groups = [[i for i in range(NX * NY) if i % 2 == core] for core in range(2)]
    mine = lax.all_to_all(
        sent, ("gx", "gy"), split_axis=0, concat_axis=0, axis_index_groups=groups, tiled=True
    )
    (base,) = call(base_kernel, [(3, 32, 16, 128)], [(192, 128), (3, 16, 16, 128)])(two, rim, e_one, e_two)
    other = lax.ppermute(mine, "gy", swap_near)
    (out,) = call(
        top_kernel,
        [(3, 32, 16, 128)],
        [(4, 2, 128, 128), (3, 16, 16, 128), (2, 3, 8, 16, 128), (6, 16, 128), (6, 16, 16, 128)]
        + [(16, 16, 128), (4, 2, 16, 256), (3, 32, 16, 128), pltpu.SemaphoreType.DMA((6,))],
        out_specs=[ANY],
    )(mine.reshape(512, 128), other.reshape(512, 128), base)
    return out


def solution(mesh):
    return jax.shard_map(
        local,
        mesh=mesh,
        in_specs=(P(None, "gx", "gy"), P(None, None, "gx", "gy")),
        out_specs=P(None, None, "gx", "gy"),
        check_vma=False,
    )
```

```python
import jax
import jax.numpy as jnp
from jax import lax
from jax.experimental import pallas as pl
from jax.experimental.pallas import tpu as pltpu
from jax.sharding import PartitionSpec as P


F32 = jnp.float32
NX, NY, CHIPS = 16, 16, 128
STEP, WIDE = 16, 32
BETWEEN = 2.0 * 0.1 / 1.1
ANY = pl.BlockSpec(memory_space=pltpu.HBM)


def dot(a, b):
    return jnp.dot(a, b, precision=lax.Precision.HIGHEST, preferred_element_type=F32)


def dot_exact(a, b):
    high = a.astype(jnp.bfloat16)
    low = (a - high.astype(F32)).astype(jnp.bfloat16)
    b = b.astype(jnp.bfloat16)
    return jnp.dot(
        jnp.concatenate([high, low], axis=1), jnp.concatenate([b, b], axis=0), preferred_element_type=F32
    )


def iota(shape, dim):
    return lax.broadcasted_iota(jnp.int32, shape, dim)


def roll(x, shift, axis=1):
    shift = shift % x.shape[axis]
    return x if shift == 0 else pltpu.roll(x, shift, axis)


def turn(x, shift):
    return pltpu.roll(x, lax.rem(shift + 256, 128), 1)


def recip(x):
    guess = pl.reciprocal(x, approx=True)
    return guess * (2.0 - x * guess)


def inner(index):
    return (index > 0) & (index < 15)


def call(kernel, outs, scratch, flops=1_000_000, **kw):
    return pl.pallas_call(
        kernel,
        out_shape=[jax.ShapeDtypeStruct(s, F32) for s in outs],
        scratch_shapes=[pltpu.VMEM(s, F32) if isinstance(s, tuple) else s for s in scratch],
        compiler_params=pltpu.CompilerParams(vmem_limit_bytes=32 * 1024 * 1024),
        cost_estimate=pl.CostEstimate(flops=flops, bytes_accessed=4_000_000, transcendentals=0),
        **kw,
    )


def loop(count, body, unroll=1):
    def step(i, carry):
        body(i)
        return carry

    lax.fori_loop(0, count, step, 0, unroll=unroll)


def weigh(weights, values):
    parts = [w * v for w, v in zip(weights, values)]
    while len(parts) > 1:
        parts = [sum(parts[i : i + 2][1:], parts[i]) for i in range(0, len(parts), 2)]
    return parts[0]


def rows_kernel(guess, labels, near, far, own, phase, sems):
    even = lax.rem(lax.axis_index("gx"), 2) == 0
    near_row, far_row = jnp.where(even, 13, 0), jnp.where(even, 0, 13)
    copies = [pltpu.make_async_copy(labels, phase, sems.at[3])]
    for f in range(3):
        copies.append(pltpu.make_async_copy(guess.at[f], own.at[f], sems.at[f]))
    for copy in copies:
        copy.start()
    copies[0].wait()
    own[3] = jnp.where(phase[...] == 1, 0.0, 1.0).astype(F32)
    flat = own.reshape(4 * 32 * 16, 128)
    for ch in (3, 0, 1, 2):
        if ch < 3:
            copies[ch + 1].wait()
        for row in range(3):
            near[3 * ch + row] = flat[pl.ds(512 * ch + near_row + row, 32, stride=16), :]
            far[3 * ch + row] = flat[pl.ds(512 * ch + far_row + row, 32, stride=16), :]


def pack_kernel(to_right, to_left, x_near, x_far, near, far, rim):
    first_core = lax.rem(lax.axis_index("gy"), 2) == 0
    even = lax.rem(lax.axis_index("gx"), 2) == 0
    near_row, far_row = jnp.where(even, 0, 5), jnp.where(even, 5, 0)
    has_far = inner(lax.axis_index("gx"))
    flat = rim.reshape(4 * 32 * 8, 128)
    for ch in range(4):
        for row in range(3):
            flat[pl.ds(256 * ch + near_row + row, 32, stride=8), :] = x_near[3 * ch + row]
            flat[pl.ds(256 * ch + far_row + row, 32, stride=8), :] = jnp.where(has_far, x_far[3 * ch + row], 0.0)

    def some(low):
        for ch in range(4):
            right, left = pack_planes(lambda z: rim[ch, z], low, (8, 128))
            for at, right, left in (
                (slice(0, 16), to_right[ch, low], to_left[ch, low]),
                (slice(16, 24), right, left),
            ):
                near[ch, low, at, :] = jnp.where(first_core, right, left)
                far[ch, low, at, :] = jnp.where(first_core, left, right)

    loop(4, some, 4)


def pack_planes(plane, low, shape):
    group = iota(shape, 1) // 16
    right = left = jnp.zeros(shape, F32)
    for h in range(8):
        moved = roll(plane(4 * h + low), 16 * h + 16)
        right = jnp.where(group == h, moved, right)
        left = jnp.where(group == (h + 1) % 8, moved, left)
    return right, left


def edge_columns(plane, z, shape):
    lane = iota(shape, 1)
    value = jnp.zeros(shape, F32)
    for half in range(2):
        source = plane(z + 16 * half)
        base = 64 * half
        value = jnp.where((lane >= base) & (lane < base + 7), roll(source, base + 7), value)
        value = jnp.where((lane >= base + 57) & (lane < base + 64), roll(source, base + 57), value)
    return value


def six_of(ref, lead, z, first, count):
    own = ref[(*lead, z, pl.ds(first, count), slice(None))]
    return own, (
        ref[(*lead, z, pl.ds(first - 1, count), slice(None))],
        ref[(*lead, z, pl.ds(first + 1, count), slice(None))],
        roll(own, 1),
        roll(own, -1),
        ref[(*lead, z - 1, pl.ds(first, count), slice(None))],
        ref[(*lead, z + 1, pl.ds(first, count), slice(None))],
    )


def block_of(ref, lead, z, planes, first, count):
    rows = pl.ds(first, count)
    own = [ref[(*lead, z + k, rows, slice(None))] for k in range(-1, planes + 1)]
    result = []
    for k in range(planes):
        value = own[k + 1]
        six = (
            ref[(*lead, z + k, pl.ds(first - 1, count), slice(None))],
            ref[(*lead, z + k, pl.ds(first + 1, count), slice(None))],
            roll(value, 1),
            roll(value, -1),
            own[k],
            own[k + 2],
        )
        result.append((value, six))
    return result


def fine_weights(own, six, omega):
    base, slope = 1.0 + (BETWEEN - 1.0) * own, (BETWEEN - 1.0) + (1.1 - 2.0 * BETWEEN) * own
    total = (six[0] + six[1]) + (six[2] + six[3]) + (six[4] + six[5])
    diag = 6.0 * base + slope * total
    gain = omega * recip(diag)
    base, slope = gain * base, gain * slope
    return [base + slope * other for other in six], 1.25 * diag


def fine_sweep(w, f, own, six):
    return (0.2 * own + (w[2 * f + 1] - w[2 * f])) + weigh(w, six)


def fine_left(w, f, own, six, diag):
    return (((w[2 * f + 1] - w[2 * f]) - 0.8 * own) + weigh(w, six)) * diag


def fine_sweeps(planes, windows, start, share, one, two, weights, diags, halves, omega, wrap, keep, size):
    first, count = windows[0]

    def first_sweep(step):
        z = size * step
        w = []
        for k, (own, six) in enumerate(block_of(share, (), z + 1, size, first, count)):
            now, diag = fine_weights(own, six, omega)
            diags[z + k, pl.ds(first, count), :] = diag
            for i in range(6):
                weights[i, z + k, pl.ds(first, count), :] = now[i]
            w.append(now)
        for f in range(3):
            for k, (own, six) in enumerate(block_of(start, (f,), z + 1, size, first, count)):
                one[f, z + k + 1, pl.ds(first, count), :] = fine_sweep(w[k], f, own, six)

    loop(planes // size, first_sweep)
    wrap(one)
    second, count2 = windows[1]

    def second_sweep(step):
        z = size * step
        w = [[weights[i, z + k, pl.ds(second, count2), :] for i in range(6)] for k in range(size)]
        for f in range(3):
            for k, (own, six) in enumerate(block_of(one, (f,), z + 1, size, second, count2)):
                two[f, z + k + 1, pl.ds(second, count2), :] = fine_sweep(w[k], f, own, six)

    loop(planes // size, second_sweep)
    wrap(two)

    def residual(step):
        z = size * step
        w = [[weights[i, z + k, 8:24, :] for i in range(6)] for k in range(size)]
        diag = [diags[z + k, 8:24, :] for k in range(size)]
        for f in range(3):
            values = []
            for k, (own, six) in enumerate(block_of(two, (f,), z + 1, size, 8, 16)):
                if keep is not None:
                    keep[f, z + k] = own
                values.append(fine_left(w[k], f, own, six, diag[k]))
            for pair in range(size // 2):
                halves[f, size // 2 * step + pair] = values[2 * pair] + values[2 * pair + 1]
        for pair in range(size // 2):
            at = z + 2 * pair + 1
            halves[3, size // 2 * step + pair] = share[at, 8:24, :] + share[at + 1, 8:24, :]

    loop(planes // size, residual)


def own_kernel(own, one, two, halves, to_right, to_left, edges, held, weights, diags):
    zero = jnp.zeros((32, 128), F32)
    for z in (0, 33):
        for ch in range(4):
            held[ch, z] = zero
        for ref in (one, two):
            for f in range(3):
                ref[f, z] = zero

    def plane(z):
        for ch in range(4):
            held[ch, z + 1, 8:24, :] = own[ch, z]

    loop(32, plane, 8)
    fine_sweeps(
        32, [(8, 16)] * 2, held, held.at[3], one, two, weights, diags, halves, 0.8, lambda ref: None, None, 8
    )

    def some(low):
        for ch in range(4):
            to_right[ch, low], to_left[ch, low] = pack_planes(lambda z: own[ch, z], low, (16, 128))

    loop(4, some, 2)

    def edge(z):
        for ch in range(4):
            edges[ch, z] = edge_columns(lambda at: own[ch, at], z, (16, 128))

    loop(16, edge, 8)


def rows_edge_kernel(own, rim, own_one, own_two, own_halves, two, packed, edges, start, one, weights, diags, halves, pooled):
    gx = lax.axis_index("gx")
    zero = jnp.zeros((24, 128), F32)
    for z in (0, 33):
        for ch in range(4):
            start[ch, z] = zero
        for ref in (one, two):
            for f in range(3):
                ref[f, z] = zero

    def fill(z):
        for ch in range(4):
            start[ch, z + 1, 0:8, :] = own[ch, z, 8:16, :]
            start[ch, z + 1, 8:16, :] = rim[ch, z]
            start[ch, z + 1, 16:24, :] = own[ch, z, 0:8, :]
        for f in range(3):
            for ref, source in ((one, own_one), (two, own_two)):
                ref[f, z + 1, 0:8, :] = source[f, z + 1, 16:24, :]
                ref[f, z + 1, 16:24, :] = source[f, z + 1, 8:16, :]

    loop(32, fill, 8)
    upper = iota((8, 128), 0) < 4

    def both(ref, lead, step, shift=0):
        high = ref[(*lead, pl.ds(8 - step + shift, 8), slice(None))]
        low = ref[(*lead, pl.ds(8 + step + shift, 8), slice(None))]
        return jnp.where(upper, high, low)

    def block_both(ref, f, z, step):
        own = [both(ref, (f, z + k), step) for k in range(-1, WIDE + 1)]
        result = []
        for k in range(WIDE):
            value = own[k + 1]
            low, high = both(ref, (f, z + k), step, -1), both(ref, (f, z + k), step, 1)
            result.append((value, (low, high, roll(value, 1), roll(value, -1), own[k], own[k + 2])))
        return result

    def put(ref, f, z, step, value):
        ref[f, z, pl.ds(8 - step, 4), :] = value[0:4]
        ref[f, z, pl.ds(12 + step, 4), :] = value[4:8]

    row = iota((16, 128), 0) + 5
    low, high = jnp.where(gx > 0, 1, 0), jnp.where(gx < NX - 1, 1, 0)
    inside = jnp.where((row >= 8) & (row < 12), high, jnp.where((row >= 12) & (row < 16), low, 1))
    omega = 0.8 * inside.astype(F32)

    def weigh_all(step):
        z = WIDE * step
        for k, (value, six) in enumerate(block_of(start, (3,), z + 1, WIDE, 5, 16)):
            w, diag = fine_weights(value, six, omega)
            diags[z + k, 5:21, :] = diag
            for i in range(6):
                weights[i, z + k, 5:21, :] = w[i]

    loop(32 // WIDE, weigh_all)

    for step, source, target in ((1, start, one), (2, one, two)):

        def sweep(block):
            z = WIDE * block
            w = [[both(weights, (i, z + k), step) for i in range(6)] for k in range(WIDE)]
            for f in range(3):
                for k, (value, six) in enumerate(block_both(source, f, z + 1, step)):
                    put(target, f, z + k + 1, step, fine_sweep(w[k], f, value, six))

        loop(32 // WIDE, sweep)

    sub = iota((8, 128), 0)

    def residual(block):
        z = WIDE * block
        w = [[both(weights, (i, z + k), 3) for i in range(6)] for k in range(WIDE)]
        diag = [both(diags, (z + k,), 3) for k in range(WIDE)]
        for f in range(3):
            values = []
            for k, (value, six) in enumerate(block_both(two, f, z + 1, 3)):
                values.append(fine_left(w[k], f, value, six, diag[k]))
            for k in range(WIDE // 2):
                pair = WIDE // 2 * block + k
                value = values[2 * k] + values[2 * k + 1]
                halves[f, pair, 0:8, :] = jnp.where(sub < 3, roll(value, 3, 0), own_halves[f, pair, 0:8, :])
                halves[f, pair, 8:16, :] = jnp.where(sub >= 5, roll(value, 5, 0), own_halves[f, pair, 8:16, :])
        for k in range(WIDE // 2):
            halves[3, WIDE // 2 * block + k] = own_halves[3, WIDE // 2 * block + k]

    loop(32 // WIDE, residual)
    source, target = iota((128, 128), 0), iota((128, 128), 1)
    value = None
    for half in range(2):
        pool = jnp.where(source // 2 + 64 * half == target, 0.125, 0.0)
        part = dot_exact(halves[:, 8 * half : 8 * half + 8].reshape(512, 128), pool)
        value = part if value is None else value + part
    pooled[...] = value
    packed[...] = (pooled[pl.ds(0, 256, stride=2), :] + pooled[pl.ds(1, 256, stride=2), :]).reshape(4, 8, 8, 128)

    def edge(z):
        for ch in range(4):
            edges[ch, z] = edge_columns(lambda at: rim[ch, at], z, (8, 128))

    loop(16, edge, 8)


def rim_kernel(
    edges, edges_rim, near, far, field, packed,
    start, share, one, two, weights, diags, halves, pooled,
):
    gx, gy = lax.axis_index("gx"), lax.axis_index("gy")
    lane = iota((24, 128), 1)
    part = lane % 64
    is_after = (part >= 7) & (part < 22)
    is_before = (part >= 42) & (part < 57)
    first_core = lax.rem(gy, 2) == 0

    def unpack(low):
        for ch in range(4):
            target = start.at[ch] if ch < 3 else share
            from_near, from_far = near[ch, low], jnp.where(inner(gy), far[ch, low], 0.0)
            from_right = jnp.where(first_core, from_near, from_far)
            from_left = jnp.where(first_core, from_far, from_near)
            for h in range(4):
                z = 4 * h + low
                after_y = roll(from_right, 7 - 16 * (h + 1))
                before_y = roll(from_left, 41 - 16 * h)
                own = jnp.concatenate([edges[ch, z], edges_rim[ch, z]], axis=0)
                value = jnp.where(is_after, after_y, jnp.where(is_before, before_y, own))
                target[z + 1, 8:24, :] = value[0:16]
                target[z + 1, 0:8, :] = value[16:24]
                target[z + 1, 24:32, :] = value[16:24]

    loop(4, unpack, 2)

    half_of = iota((32, 128), 1)

    def wrap_one(ref):
        ref[0] = jnp.where(half_of >= 64, roll(ref[16], 64), 0.0)
        ref[17] = jnp.where(half_of < 64, roll(ref[1], 64), 0.0)

    def wrap(ref):
        for f in range(3):
            wrap_one(ref.at[f])

    wrap_one(share)
    wrap(start)
    row = iota((24, 128), 0) + 6
    low, high = jnp.where(gx > 0, 1, 0), jnp.where(gx < NX - 1, 1, 0)
    inside_x = jnp.where(row < 8, low, jnp.where(row >= 24, high, 1))
    inside_y = jnp.where(
        part < 32,
        jnp.where((part < 7) | (gy < NY - 1), 1, 0),
        jnp.where((part >= 57) | (gy > 0), 1, 0),
    )
    omega = 0.8 * (inside_x * inside_y).astype(F32)
    fine_sweeps(
        16, [(6, 24), (7, 24)], start, share, one, two, weights, diags, halves, omega, wrap, field, STEP
    )

    source, target = iota((128, 128), 0), iota((128, 128), 1)
    spot = source % 64
    column = jnp.where(spot < 32, 121 + spot, 71 + spot) // 2
    to = jnp.where(spot < 32, column - 62, column - 48)
    keep = ((spot < 32) & (to >= 0) & (to < 9)) | ((spot >= 32) & (to >= 9) & (to < 18))
    mixed = halves[...].reshape(4, 4, 2, 16, 128)
    value = None
    for odd in range(2):
        pool = jnp.where(keep & (to + 64 * odd + 32 * (source // 64) == target), 0.125, 0.0)
        part = dot_exact(mixed[:, :, odd].reshape(256, 128), pool)
        value = part if value is None else value + part
    pooled[...] = value
    packed[...] = (pooled[pl.ds(0, 128, stride=2), :] + pooled[pl.ds(1, 128, stride=2), :]).reshape(4, 4, 8, 128)


def base_kernel(two, rim, e_one, e_two, base, wide, spread):
    copy = jnp.where(iota((128, 128), 0) == iota((128, 128), 1) // 2, 1.0, 0.0)
    value = dot_exact(e_two[...].reshape(192, 128), copy)
    for block in range(24):
        rows = value[8 * block : 8 * block + 4, :]
        wide[pl.ds(8 * block, 4, stride=2), :] = rows
        wide[pl.ds(8 * block + 1, 4, stride=2), :] = rows
    value = e_one[...].reshape(24, 2, 8, 128) + wide[...].reshape(24, 1, 8, 128)
    value = dot_exact(value.reshape(384, 128), copy)
    flat = spread.reshape(768, 128)
    for block in range(48):
        rows = value[8 * block : 8 * block + 8, :]
        flat[pl.ds(16 * block, 8, stride=2), :] = rows
        flat[pl.ds(16 * block + 1, 8, stride=2), :] = rows
    lane = iota((16, 128), 1)

    def pair(k):
        for f in range(3):
            for z in (2 * k, 2 * k + 1):
                value = rim[f, z]
                for half in range(2):
                    low = roll(value, -57 - 64 * half)
                    high = roll(value, 121 - 64 * half)
                    at = z + 16 * half
                    own = jnp.concatenate([two[f, at + 1, 16:24, :], two[f, at + 1, 0:8, :]], axis=0)
                    own = jnp.where(lane < 3, low, jnp.where(lane >= 125, high, own))
                    base[f, at] = own + spread[f, k + 8 * half]

    loop(8, pair, 4)


def resist(share):
    return recip(2.0 - 1.8 * share)


def level_weights(own, six, omega):
    faces = [recip(own + other) for other in six]
    diag = (faces[0] + faces[1]) + (faces[2] + faces[3]) + (faces[4] + faces[5])
    gain = omega * recip(diag)
    return gain, [gain * w for w in faces], diag


def middle_kernel(
    main, main_near, main_far, rim, rim_near, rim_far, sent, e_one, e_two,
    share, rest, rhs, first, second, weights, diags, halves, pooled,
    rest2, first2, second2, rhs2, share2, weights2,
):
    gx, gy = lax.axis_index("gx"), lax.axis_index("gy")
    low_x, high_x = jnp.where(gx > 0, 1, 0), jnp.where(gx < NX - 1, 1, 0)
    low_y, high_y = jnp.where(gy > 0, 1, 0), jnp.where(gy < NY - 1, 1, 0)

    for f in range(3):
        for ref in (first, second):
            ref[f, 0] = jnp.zeros((32, 128), F32)
            ref[f, 17] = jnp.zeros((32, 128), F32)
    for z in (0, 17):
        rest[z] = jnp.full((32, 128), 0.5, F32)
    lane = iota((8, 128), 1)
    even = lax.rem(gx, 2) == 0
    near_row, far_row = jnp.where(even, 16, 0), jnp.where(even, 0, 16)
    starts = (pl.multiple_of(near_row, 8), pl.multiple_of(far_row, 8), 8)

    sources = zip(starts, ((main_near, rim_near), (main_far, rim_far), (main, rim)))
    sources = list(sources)
    has_far = inner(gx)

    def fill(q):
        for odd in range(2):
            for half in range(2):
                z = 2 * q + odd + 8 * half
                base = 64 * odd + 32 * half
                for at, (middle, outer) in sources:
                    for ch in range(4):
                        edge, body = outer[ch, q], middle[ch, 2 * q + odd]
                        if outer is rim_far:
                            edge, body = jnp.where(has_far, edge, 0.0), jnp.where(has_far, body, 0.0)
                        value = jnp.where(lane < 62, roll(body, 64 * half), roll(edge, 62 - base))
                        value = jnp.where((lane >= 96) | (lane < 2), roll(edge, 112 - base), value)
                        if ch < 3:
                            rhs[ch, z, pl.ds(at, 8), :] = value
                        else:
                            share[z, pl.ds(at, 8), :] = value
                            rest[z + 1, pl.ds(at, 8), :] = resist(value)
                rest[z + 1, 24:32, :] = jnp.full((8, 128), 0.5, F32)

    loop(4, fill, 2)

    row, lane = iota((24, 128), 0) + 1, iota((24, 128), 1)
    in_x = jnp.where(row < 8, low_x, jnp.where(row >= 16, high_x, 1))
    in_y = jnp.where(lane < 64, 1, jnp.where(lane < 96, high_y, low_y))
    omega = 0.8 * (in_x * in_y).astype(F32)

    def start(step):
        z = STEP * step
        for k, (own, six) in enumerate(block_of(rest, (), z + 1, STEP, 1, 24)):
            gain, w, diag = level_weights(own, six, omega)
            for i in range(6):
                weights[i, z + k, 1:25, :] = w[i]
            diags[z + k, 1:25, :] = (1.25 * 0.25) * diag
            for f in range(3):
                first[f, z + k + 1, 1:25, :] = (4.0 * gain) * rhs[f, z + k, 1:25, :]

    loop(16 // STEP, start)

    def sweep(step):
        z = STEP * step
        w = [[weights[i, z + k, 3:27, :] for i in range(6)] for k in range(STEP)]
        for f in range(3):
            for k, (own, six) in enumerate(block_of(first, (f,), z + 1, STEP, 3, 24)):
                second[f, z + k + 1, 3:27, :] = 1.2 * own + weigh(w[k], six)

    loop(16 // STEP, sweep)

    def left(step):
        z = STEP * step
        w = [[weights[i, z + k, 4:20, :] for i in range(6)] for k in range(STEP)]
        diag = [diags[z + k, 4:20, :] for k in range(STEP)]
        for f in range(3):
            values = []
            for k, (own, six) in enumerate(block_of(second, (f,), z + 1, STEP, 4, 16)):
                change = (first[f, z + k + 1, 4:20, :] - 0.8 * own) + weigh(w[k], six)
                values.append(change * diag[k])
                e_one[f, z + k] = second[f, z + k + 1, 8:16, :]
            for k in range(STEP // 2):
                halves[f, STEP // 2 * step + k, 0:16, :] = values[2 * k] + values[2 * k + 1]
                halves[f, STEP // 2 * step + k, 16:24, :] = jnp.zeros((8, 128), F32)
        for k in range(STEP // 2):
            halves[3, STEP // 2 * step + k] = share[z + 2 * k] + share[z + 2 * k + 1]

    loop(16 // STEP, left)

    source, target = iota((128, 128), 0), iota((128, 128), 1)
    pool = jnp.where(source // 2 + jnp.where(source >= 96, 64, 0) == target, 0.125, 0.0)
    pooled[...] = dot_exact(halves[...].reshape(4 * 8 * 24, 128), pool)
    for z in (0, 9):
        rest2[z] = jnp.full((24, 128), 0.5, F32)
        for f in range(3):
            first2[f, z] = jnp.zeros((24, 128), F32)
            second2[f, z] = jnp.zeros((24, 128), F32)
    for z in range(8):
        for f in range(3):
            base = (f * 8 + z) * 24
            rhs2[f, z] = pooled[pl.ds(base, 8, stride=2), :] + pooled[pl.ds(base + 1, 8, stride=2), :]
        base = (3 * 8 + z) * 24
        value = pooled[pl.ds(base + 2, 8, stride=2), :] + pooled[pl.ds(base + 3, 8, stride=2), :]
        rest2[z + 1, 0:8, :] = resist(value)
        value = pooled[pl.ds(base + 8, 8, stride=2), :] + pooled[pl.ds(base + 9, 8, stride=2), :]
        rest2[z + 1, 3:11, :] = resist(value)
        share2[z] = value

    row, lane = iota((8, 128), 0) + 1, iota((8, 128), 1)
    in_x = jnp.where(row < 3, low_x, jnp.where(row >= 7, high_x, 1))
    in_y = jnp.where(lane < 32, 1, jnp.where(lane < 96, high_y, low_y))
    omega2 = 0.8 * (in_x * in_y).astype(F32)

    for z, (own, six) in enumerate(block_of(rest2, (), 1, 8, 1, 8)):
        gain, w, diag = level_weights(own, six, omega2)
        for i in range(6):
            weights2[i, z, 1:9, :] = w[i]
        weights2[6, z, 1:9, :] = (1.25 * 0.0625) * diag
        for f in range(3):
            first2[f, z + 1, 1:9, :] = (16.0 * gain) * rhs2[f, z]
    w = [[weights2[i, z, 2:10, :] for i in range(6)] for z in range(8)]
    for f in range(3):
        for z, (own, six) in enumerate(block_of(first2, (f,), 1, 8, 2, 8)):
            second2[f, z + 1, 2:10, :] = 1.2 * own + weigh(w[z], six)
    w = [[weights2[i, z, 3:11, :] for i in range(7)] for z in range(8)]
    own_row = iota((8, 128), 0) < 4
    parts = [{} for pair in range(4)]
    for f in range(3):
        for z, (own, six) in enumerate(block_of(second2, (f,), 1, 8, 3, 8)):
            e_two[f, z] = own
            change = (first2[f, z + 1, 3:11, :] - 0.8 * own) + weigh(w[z], six)
            value = jnp.where(own_row, change * w[z][6], 0.0)
            sums = parts[z // 2]
            sums[f] = value if z % 2 == 0 else sums[f] + value
    for z in range(8):
        value = jnp.where(own_row, share2[z], 0.0)
        sums = parts[z // 2]
        sums[3] = value if z % 2 == 0 else sums[3] + value

    pool = jnp.where((source < 32) & (source // 2 == target % 16), 0.125, 0.0)
    rows = jnp.concatenate([parts[pair][ch] for ch in range(4) for pair in range(4)], axis=0)
    spread = dot(rows, pool)
    at, to = iota((32, 128), 0), iota((32, 128), 1)
    keep = (at // 8 == to // 32) & ((at % 8) // 2 == (to // 16) % 2)
    result = jnp.concatenate(
        [
            jnp.sum(jnp.where(keep, spread[32 * ch : 32 * ch + 32], 0.0), axis=0, keepdims=True)
            for ch in range(4)
        ],
        axis=0,
    )
    for copy in range(CHIPS):
        sent[copy] = result


def swap_blocks(x):
    sub, group = iota((8, 128), 0), iota((8, 128), 1) // 16
    for bit in (4, 2, 1):
        up = roll(roll(x, -bit, 0), 16 * bit)
        down = up if bit == 4 else roll(roll(x, bit, 0), -16 * bit)
        sub_set, group_set = (sub & bit) != 0, (group & bit) != 0
        x = jnp.where(sub_set == group_set, x, jnp.where(sub_set, down, up))
    return x


def top_kernel(
    mine, other, base, out,
    natural, first, second, four, weights, diags, lefts, final, sems,
):
    gx, gy = lax.axis_index("gx"), lax.axis_index("gy")
    first_core = lax.rem(gy, 2) == 0
    lane, sub = iota((16, 128), 1), iota((16, 128), 0)
    cells = [(z, x, half) for z in range(4) for x in range(2) for half in range(2)]

    def lay(g):
        for ch in range(4):
            rows = pl.ds(32 * g + ch, 8, stride=4)
            pair = mine[rows, :], other[rows, :]
            natural[ch, 0, pl.ds(pl.multiple_of(8 * g, 8), 8), :] = swap_blocks(
                jnp.where(first_core, pair[0], pair[1])
            )
            natural[ch, 1, pl.ds(pl.multiple_of(8 * g, 8), 8), :] = swap_blocks(
                jnp.where(first_core, pair[1], pair[0])
            )

    loop(16, lay, 4)
    flat = natural.reshape(1024, 128)

    def plane(ch, z, x, half):
        return flat[pl.ds((ch * 2 + half) * 128 + z * 2 + x, 16, stride=8), :]

    def neighbours(at, z, x, half, outside):
        own, other = at(z, x, half), at(z, 1 - x, half)
        beside = at(z, x, 1 - half)
        shifted = roll(other, 1 if x == 0 else -1, 0)
        low, high = (shifted, other) if x == 0 else (other, shifted)
        left, right = roll(own, 1), roll(own, -1)
        left = jnp.where(lane % 16 == 0, roll(beside, 1 if half == 0 else -15), left)
        right = jnp.where(lane % 16 == 15, roll(beside, 15 if half == 0 else -1), right)
        down = at(z - 1, x, half) if z > 0 else outside
        up = at(z + 1, x, half) if z < 3 else outside
        return own, [low, high, left, right, down, up]

    def edge_masks(x, half):
        return [
            sub > 0 if x == 0 else None,
            sub < 15 if x == 1 else None,
            lane > 0 if half == 0 else None,
            lane < 127 if half == 1 else None,
            None,
            None,
        ]

    def key(z, x, half):
        return (z * 2 + x) * 2 + half

    shares = {c: plane(3, *c) for c in cells}
    rests = {c: resist(shares[c]) for c in cells}
    outside, zeros = jnp.full((16, 128), 0.5, F32), jnp.zeros((16, 128), F32)
    for z, x, half in cells:
        own, six = neighbours(lambda *c: rests[c], z, x, half, outside)
        masks = edge_masks(x, half)
        six = [s if m is None else jnp.where(m, s, 0.5) for s, m in zip(six, masks)]
        gain, w, diag = level_weights(own, six, 0.8)
        at = key(z, x, half)
        for i in range(6):
            weights[i, at] = w[i] if masks[i] is None else jnp.where(masks[i], w[i], 0.0)
        diags[at] = (1.25 * 0.25**3) * diag
        for f in range(3):
            first[f, at] = (64.0 * gain) * plane(f, z, x, half)

    for z, x, half in cells:
        at = key(z, x, half)
        w = [weights[i, at] for i in range(6)]
        for f in range(3):
            own, six = neighbours(lambda *c: first[f, key(*c)], z, x, half, zeros)
            second[half, f, z * 2 + x] = 1.2 * own + weigh(w, six)

    for z4 in range(2):
        for half in range(2):
            sums = [None] * 4
            for z in (2 * z4, 2 * z4 + 1):
                for x in range(2):
                    at = key(z, x, half)
                    w = [weights[i, at] for i in range(6)]
                    diag = diags[at]
                    for f in range(3):
                        own, six = neighbours(
                            lambda c, d, e: second[e, f, c * 2 + d], z, x, half, zeros
                        )
                        value = ((first[f, at] - 0.8 * own) + weigh(w, six)) * diag
                        sums[f] = value if sums[f] is None else sums[f] + value
                    share = shares[z, x, half]
                    sums[3] = share if sums[3] is None else sums[3] + share
            for ch in range(4):
                lefts[ch, z4, :, 128 * half : 128 * half + 128] = sums[ch]

    source = iota((256, 128), 0)
    column = ((source % 128) // 16) * 16 + (source // 128) * 8 + (source % 16) // 2
    pool = jnp.where(column == iota((256, 128), 1), 0.125, 0.0)
    level = dot_exact(lefts[...].reshape(128, 256), pool)

    def coarsest(ch, z):
        return level[(ch * 2 + z) * 16 : (ch * 2 + z) * 16 + 16, :]

    masks = [sub > 0, sub < 15, lane > 0, lane < 127]
    resists = [resist(coarsest(3, z)) for z in range(2)]
    gains, ws, ds = [], [], []
    for z in range(2):
        own, other = resists[z], resists[1 - z]
        six = [roll(own, 1, 0), roll(own, -1, 0), roll(own, 1), roll(own, -1)]
        six = [jnp.where(m, s, 0.5) for m, s in zip(masks, six)] + [other, outside]
        gain, w, diag = level_weights(own, six, 0.8)
        gains.append(gain)
        ds.append(diag)
        ws.append([jnp.where(m, v, 0.0) for m, v in zip(masks, w)] + [w[4]])
    whole = jnp.sum(ds[0] + ds[1], keepdims=True)

    def around(values, z):
        own, other = values[z], values[1 - z]
        return weigh(ws[z], (roll(own, 1, 0), roll(own, -1, 0), roll(own, 1), roll(own, -1), other))

    begin = [[256.0 * gains[z] * coarsest(f, z) for z in range(2)] for f in range(3)]
    values = begin
    for step in range(5):
        values = [
            [(0.2 * values[f][z] + begin[f][z]) + around(values[f], z) for z in range(2)] for f in range(3)
        ]
    for f in range(3):
        change = [(begin[f][z] - 0.8 * values[f][z]) + around(values[f], z) for z in range(2)]
        total = jnp.sum(1.25 * (change[0] * ds[0] + change[1] * ds[1]), keepdims=True)
        for z in range(2):
            four[2 * f + z] = values[f][z] + total / whole

    copy = jnp.where(iota((128, 128), 0) == iota((128, 128), 1) // 2, 1.0, 0.0)
    rows = four.reshape(96, 128)[pl.ds(gx, 6, stride=16), :]
    rows = jnp.concatenate([jnp.broadcast_to(rows[i : i + 1], (4, 128)) for i in range(6)], axis=0)
    three = dot(turn(rows, -8 * gy), copy)
    flat = second.reshape(768, 128)
    halves = [flat[pl.ds(gx + 384 * half, 24, stride=16), :] for half in range(2)]
    three = three + turn(jnp.where(first_core, halves[0], halves[1]), -16 * lax.div(gy, 2))

    copy = jnp.where(iota((128, 128), 0) == iota((128, 128), 1) // 8, 1.0, 0.0)
    three = dot(three, copy)
    copies = []
    for f in range(3):
        for z in range(4):
            for x in range(2):
                at = f * 8 + z * 2 + x
                value = jnp.broadcast_to(three[at : at + 1], (8, 128))
                for k in range(8 * z, 8 * z + 8):
                    final[f, k, 8 * x : 8 * x + 8, :] = base[f, k, 8 * x : 8 * x + 8, :] + value
            if z % 2 == 1:
                part = (f, pl.ds(8 * z - 8, 16))
                copy = pltpu.make_async_copy(final.at[part], out.at[part], sems.at[len(copies)])
                copy.start()
                copies.append(copy)
    for copy in copies:
        copy.wait()


def local(labels, guess):
    swap_near = [(i, i ^ 1) for i in range(NY)]
    far_x, far_y = [], []
    for x in range(NX):
        for y in range(NY):
            across_x, across_y = x + 1 if x % 2 else x - 1, y + 1 if y % 2 else y - 1
            to = (across_x, y) if 0 <= across_x < NX else (x, y ^ 1)
            far_x.append((x * NY + y, to[0] * NY + to[1]))
            to = (x, across_y) if 0 <= across_y < NY else (x ^ 1, y)
            far_y.append((x * NY + y, to[0] * NY + to[1]))
    both = ("gx", "gy")
    to_near, to_far, own = call(
        rows_kernel,
        [(12, 32, 128)] * 2 + [(4, 32, 16, 128)],
        [pltpu.VMEM((32, 16, 128), jnp.int32), pltpu.SemaphoreType.DMA((4,))],
        in_specs=[ANY, ANY],
    )(pltpu.with_memory_space_constraint(guess, pltpu.HBM), pltpu.with_memory_space_constraint(labels, pltpu.HBM))
    from_near = lax.ppermute(to_near, "gx", swap_near)
    from_far = lax.ppermute(to_far, both, far_x)
    own_one, own_two, halves, to_right, to_left, edges = call(
        own_kernel,
        [(3, 34, 32, 128)] * 2 + [(4, 16, 16, 128)] + [(4, 4, 16, 128)] * 2 + [(4, 16, 16, 128)],
        [(4, 34, 32, 128), (6, 32, 32, 128), (32, 32, 128)],
        flops=20_000_000,
    )(own)
    to_near, to_far, rim_rows = call(pack_kernel, [(4, 4, 24, 128)] * 2 + [(4, 32, 8, 128)], [])(
        to_right, to_left, from_near, from_far
    )
    from_far = lax.ppermute(to_far, both, far_y)
    from_near = lax.ppermute(to_near, "gy", swap_near)
    two, main, edges_rim = call(
        rows_edge_kernel,
        [(3, 34, 24, 128), (4, 8, 8, 128), (4, 16, 8, 128)],
        [(4, 34, 24, 128), (3, 34, 24, 128), (6, 32, 24, 128), (32, 24, 128)]
        + [(4, 16, 16, 128), (512, 128)],
        flops=10_000_000,
    )(own, rim_rows, own_one, own_two, halves)
    main_near = lax.ppermute(main, "gx", swap_near)
    main_far = lax.ppermute(main, both, far_x)
    rim, rim_one = call(
        rim_kernel,
        [(3, 16, 16, 128), (4, 4, 8, 128)],
        [(3, 18, 32, 128), (18, 32, 128)]
        + [(3, 18, 32, 128)] * 2
        + [(6, 16, 32, 128), (16, 32, 128)]
        + [(4, 8, 16, 128), (256, 128)],
        flops=10_000_000,
    )(edges, edges_rim, from_near, from_far)
    rim_near = lax.ppermute(rim_one, "gx", swap_near)
    rim_far = lax.ppermute(rim_one, both, far_x)
    sent, e_one, e_two = call(
        middle_kernel,
        [(CHIPS, 4, 128), (3, 16, 8, 128), (3, 8, 8, 128)],
        [(16, 24, 128), (18, 32, 128), (3, 16, 32, 128), (3, 18, 32, 128), (3, 18, 32, 128)]
        + [(6, 16, 32, 128), (16, 32, 128), (4, 8, 24, 128), (768, 128)]
        + [(10, 24, 128), (3, 10, 24, 128), (3, 10, 24, 128), (3, 8, 8, 128), (8, 8, 128)]
        + [(7, 8, 16, 128)],
    )(main, main_near, main_far, rim_one, rim_near, rim_far)
    groups = [[i for i in range(NX * NY) if i % 2 == core] for core in range(2)]
    mine = lax.all_to_all(
        sent, ("gx", "gy"), split_axis=0, concat_axis=0, axis_index_groups=groups, tiled=True
    )
    (base,) = call(base_kernel, [(3, 32, 16, 128)], [(192, 128), (3, 16, 16, 128)])(two, rim, e_one, e_two)
    other = lax.ppermute(mine, "gy", swap_near)
    (out,) = call(
        top_kernel,
        [(3, 32, 16, 128)],
        [(4, 2, 128, 128), (3, 16, 16, 128), (2, 3, 8, 16, 128), (6, 16, 128), (6, 16, 16, 128)]
        + [(16, 16, 128), (4, 2, 16, 256), (3, 32, 16, 128), pltpu.SemaphoreType.DMA((6,))],
        out_specs=[ANY],
    )(mine.reshape(512, 128), other.reshape(512, 128), base)
    return out


def solution(mesh):
    return jax.shard_map(
        local,
        mesh=mesh,
        in_specs=(P(None, "gx", "gy"), P(None, None, "gx", "gy")),
        out_specs=P(None, None, "gx", "gy"),
        check_vma=False,
    )
```

```python
import jax
import jax.numpy as jnp
from jax import lax
from jax.experimental import pallas as pl
from jax.experimental.pallas import tpu as pltpu
from jax.sharding import PartitionSpec as P


F32 = jnp.float32
NX, NY, CHIPS = 16, 16, 128
STEP, WIDE = 16, 32
BETWEEN = 2.0 * 0.1 / 1.1
ANY = pl.BlockSpec(memory_space=pltpu.HBM)


def dot(a, b):
    return jnp.dot(a, b, precision=lax.Precision.HIGHEST, preferred_element_type=F32)


def dot_exact(a, b):
    high = a.astype(jnp.bfloat16)
    low = (a - high.astype(F32)).astype(jnp.bfloat16)
    b = b.astype(jnp.bfloat16)
    return jnp.dot(
        jnp.concatenate([high, low], axis=1), jnp.concatenate([b, b], axis=0), preferred_element_type=F32
    )


def iota(shape, dim):
    return lax.broadcasted_iota(jnp.int32, shape, dim)


def roll(x, shift, axis=1):
    shift = shift % x.shape[axis]
    return x if shift == 0 else pltpu.roll(x, shift, axis)


def turn(x, shift):
    return pltpu.roll(x, lax.rem(shift + 256, 128), 1)


def recip(x):
    guess = pl.reciprocal(x, approx=True)
    return guess * (2.0 - x * guess)


def inner(index):
    return (index > 0) & (index < 15)


def call(kernel, outs, scratch, flops=1_000_000, **kw):
    return pl.pallas_call(
        kernel,
        out_shape=[jax.ShapeDtypeStruct(s, F32) for s in outs],
        scratch_shapes=[pltpu.VMEM(s, F32) if isinstance(s, tuple) else s for s in scratch],
        compiler_params=pltpu.CompilerParams(vmem_limit_bytes=32 * 1024 * 1024),
        cost_estimate=pl.CostEstimate(flops=flops, bytes_accessed=4_000_000, transcendentals=0),
        **kw,
    )


def loop(count, body, unroll=1):
    def step(i, carry):
        body(i)
        return carry

    lax.fori_loop(0, count, step, 0, unroll=unroll)


def weigh(weights, values):
    parts = [w * v for w, v in zip(weights, values)]
    while len(parts) > 1:
        parts = [sum(parts[i : i + 2][1:], parts[i]) for i in range(0, len(parts), 2)]
    return parts[0]


def rows_kernel(guess, labels, near, far, own, phase, sems):
    even = lax.rem(lax.axis_index("gx"), 2) == 0
    near_row, far_row = jnp.where(even, 13, 0), jnp.where(even, 0, 13)
    copies = [pltpu.make_async_copy(labels, phase, sems.at[3])]
    for f in range(3):
        copies.append(pltpu.make_async_copy(guess.at[f], own.at[f], sems.at[f]))
    for copy in copies:
        copy.start()
    copies[0].wait()
    own[3] = jnp.where(phase[...] == 1, 0.0, 1.0).astype(F32)
    flat = own.reshape(4 * 32 * 16, 128)
    for ch in (3, 0, 1, 2):
        if ch < 3:
            copies[ch + 1].wait()
        for row in range(3):
            near[3 * ch + row] = flat[pl.ds(512 * ch + near_row + row, 32, stride=16), :]
            far[3 * ch + row] = flat[pl.ds(512 * ch + far_row + row, 32, stride=16), :]


def pack_kernel(to_right, to_left, x_near, x_far, near, far, rim):
    first_core = lax.rem(lax.axis_index("gy"), 2) == 0
    even = lax.rem(lax.axis_index("gx"), 2) == 0
    near_row, far_row = jnp.where(even, 0, 5), jnp.where(even, 5, 0)
    has_far = inner(lax.axis_index("gx"))
    flat = rim.reshape(4 * 32 * 8, 128)
    for ch in range(4):
        for row in range(3):
            flat[pl.ds(256 * ch + near_row + row, 32, stride=8), :] = x_near[3 * ch + row]
            flat[pl.ds(256 * ch + far_row + row, 32, stride=8), :] = jnp.where(has_far, x_far[3 * ch + row], 0.0)

    def some(low):
        for ch in range(4):
            right, left = pack_planes(lambda z: rim[ch, z], low, (8, 128))
            for at, right, left in (
                (slice(0, 16), to_right[ch, low], to_left[ch, low]),
                (slice(16, 24), right, left),
            ):
                near[ch, low, at, :] = jnp.where(first_core, right, left)
                far[ch, low, at, :] = jnp.where(first_core, left, right)

    loop(4, some, 4)


def pack_planes(plane, low, shape):
    group = iota(shape, 1) // 16
    right = left = jnp.zeros(shape, F32)
    for h in range(8):
        moved = roll(plane(4 * h + low), 16 * h + 16)
        right = jnp.where(group == h, moved, right)
        left = jnp.where(group == (h + 1) % 8, moved, left)
    return right, left


def edge_columns(plane, z, shape):
    lane = iota(shape, 1)
    value = jnp.zeros(shape, F32)
    for half in range(2):
        source = plane(z + 16 * half)
        base = 64 * half
        value = jnp.where((lane >= base) & (lane < base + 7), roll(source, base + 7), value)
        value = jnp.where((lane >= base + 57) & (lane < base + 64), roll(source, base + 57), value)
    return value


def six_of(ref, lead, z, first, count):
    own = ref[(*lead, z, pl.ds(first, count), slice(None))]
    return own, (
        ref[(*lead, z, pl.ds(first - 1, count), slice(None))],
        ref[(*lead, z, pl.ds(first + 1, count), slice(None))],
        roll(own, 1),
        roll(own, -1),
        ref[(*lead, z - 1, pl.ds(first, count), slice(None))],
        ref[(*lead, z + 1, pl.ds(first, count), slice(None))],
    )


def block_of(ref, lead, z, planes, first, count):
    rows = pl.ds(first, count)
    own = [ref[(*lead, z + k, rows, slice(None))] for k in range(-1, planes + 1)]
    result = []
    for k in range(planes):
        value = own[k + 1]
        six = (
            ref[(*lead, z + k, pl.ds(first - 1, count), slice(None))],
            ref[(*lead, z + k, pl.ds(first + 1, count), slice(None))],
            roll(value, 1),
            roll(value, -1),
            own[k],
            own[k + 2],
        )
        result.append((value, six))
    return result


def fine_weights(own, six, omega):
    base, slope = 1.0 + (BETWEEN - 1.0) * own, (BETWEEN - 1.0) + (1.1 - 2.0 * BETWEEN) * own
    total = (six[0] + six[1]) + (six[2] + six[3]) + (six[4] + six[5])
    diag = 6.0 * base + slope * total
    gain = omega * recip(diag)
    base, slope = gain * base, gain * slope
    return [base + slope * other for other in six], 1.25 * diag


def fine_sweep(w, f, own, six):
    return (0.2 * own + (w[2 * f + 1] - w[2 * f])) + weigh(w, six)


def fine_left(w, f, own, six, diag):
    return (((w[2 * f + 1] - w[2 * f]) - 0.8 * own) + weigh(w, six)) * diag


def fine_sweeps(planes, windows, start, share, one, two, weights, diags, halves, omega, wrap, keep, size):
    first, count = windows[0]

    def first_sweep(step):
        z = size * step
        w = []
        for k, (own, six) in enumerate(block_of(share, (), z + 1, size, first, count)):
            now, diag = fine_weights(own, six, omega)
            diags[z + k, pl.ds(first, count), :] = diag
            for i in range(6):
                weights[i, z + k, pl.ds(first, count), :] = now[i]
            w.append(now)
        for f in range(3):
            for k, (own, six) in enumerate(block_of(start, (f,), z + 1, size, first, count)):
                one[f, z + k + 1, pl.ds(first, count), :] = fine_sweep(w[k], f, own, six)

    loop(planes // size, first_sweep)
    wrap(one)
    second, count2 = windows[1]

    def second_sweep(step):
        z = size * step
        w = [[weights[i, z + k, pl.ds(second, count2), :] for i in range(6)] for k in range(size)]
        for f in range(3):
            for k, (own, six) in enumerate(block_of(one, (f,), z + 1, size, second, count2)):
                two[f, z + k + 1, pl.ds(second, count2), :] = fine_sweep(w[k], f, own, six)

    loop(planes // size, second_sweep)
    wrap(two)

    def residual(step):
        z = size * step
        w = [[weights[i, z + k, 8:24, :] for i in range(6)] for k in range(size)]
        diag = [diags[z + k, 8:24, :] for k in range(size)]
        for f in range(3):
            values = []
            for k, (own, six) in enumerate(block_of(two, (f,), z + 1, size, 8, 16)):
                if keep is not None:
                    keep[f, z + k] = own
                values.append(fine_left(w[k], f, own, six, diag[k]))
            for pair in range(size // 2):
                halves[f, size // 2 * step + pair] = values[2 * pair] + values[2 * pair + 1]
        for pair in range(size // 2):
            at = z + 2 * pair + 1
            halves[3, size // 2 * step + pair] = share[at, 8:24, :] + share[at + 1, 8:24, :]

    loop(planes // size, residual)


def own_kernel(own, one, two, halves, to_right, to_left, edges, held, weights, diags):
    zero = jnp.zeros((32, 128), F32)
    for z in (0, 33):
        for ch in range(4):
            held[ch, z] = zero
        for ref in (one, two):
            for f in range(3):
                ref[f, z] = zero

    def plane(z):
        for ch in range(4):
            held[ch, z + 1, 8:24, :] = own[ch, z]

    loop(32, plane, 8)
    fine_sweeps(
        32, [(8, 16)] * 2, held, held.at[3], one, two, weights, diags, halves, 0.8, lambda ref: None, None, 8
    )

    def some(low):
        for ch in range(4):
            to_right[ch, low], to_left[ch, low] = pack_planes(lambda z: own[ch, z], low, (16, 128))

    loop(4, some, 2)

    def edge(z):
        for ch in range(4):
            edges[ch, z] = edge_columns(lambda at: own[ch, at], z, (16, 128))

    loop(16, edge, 8)


def rows_edge_kernel(own, rim, own_one, own_two, own_halves, two, packed, edges, start, one, weights, diags, halves, pooled):
    gx = lax.axis_index("gx")
    zero = jnp.zeros((24, 128), F32)
    for z in (0, 33):
        for ch in range(4):
            start[ch, z] = zero
        for ref in (one, two):
            for f in range(3):
                ref[f, z] = zero

    def fill(z):
        for ch in range(4):
            start[ch, z + 1, 0:8, :] = own[ch, z, 8:16, :]
            start[ch, z + 1, 8:16, :] = rim[ch, z]
            start[ch, z + 1, 16:24, :] = own[ch, z, 0:8, :]
        for f in range(3):
            for ref, source in ((one, own_one), (two, own_two)):
                ref[f, z + 1, 0:8, :] = source[f, z + 1, 16:24, :]
                ref[f, z + 1, 16:24, :] = source[f, z + 1, 8:16, :]

    loop(32, fill, 8)
    upper = iota((8, 128), 0) < 4

    def both(ref, lead, step, shift=0):
        high = ref[(*lead, pl.ds(8 - step + shift, 8), slice(None))]
        low = ref[(*lead, pl.ds(8 + step + shift, 8), slice(None))]
        return jnp.where(upper, high, low)

    def block_both(ref, f, z, step):
        own = [both(ref, (f, z + k), step) for k in range(-1, WIDE + 1)]
        result = []
        for k in range(WIDE):
            value = own[k + 1]
            low, high = both(ref, (f, z + k), step, -1), both(ref, (f, z + k), step, 1)
            result.append((value, (low, high, roll(value, 1), roll(value, -1), own[k], own[k + 2])))
        return result

    def put(ref, f, z, step, value):
        ref[f, z, pl.ds(8 - step, 4), :] = value[0:4]
        ref[f, z, pl.ds(12 + step, 4), :] = value[4:8]

    row = iota((16, 128), 0) + 5
    low, high = jnp.where(gx > 0, 1, 0), jnp.where(gx < NX - 1, 1, 0)
    inside = jnp.where((row >= 8) & (row < 12), high, jnp.where((row >= 12) & (row < 16), low, 1))
    omega = 0.8 * inside.astype(F32)

    def weigh_all(step):
        z = WIDE * step
        for k, (value, six) in enumerate(block_of(start, (3,), z + 1, WIDE, 5, 16)):
            w, diag = fine_weights(value, six, omega)
            diags[z + k, 5:21, :] = diag
            for i in range(6):
                weights[i, z + k, 5:21, :] = w[i]

    loop(32 // WIDE, weigh_all)

    for step, source, target in ((1, start, one), (2, one, two)):

        def sweep(block):
            z = WIDE * block
            w = [[both(weights, (i, z + k), step) for i in range(6)] for k in range(WIDE)]
            for f in range(3):
                for k, (value, six) in enumerate(block_both(source, f, z + 1, step)):
                    put(target, f, z + k + 1, step, fine_sweep(w[k], f, value, six))

        loop(32 // WIDE, sweep)

    sub = iota((8, 128), 0)

    def residual(block):
        z = WIDE * block
        w = [[both(weights, (i, z + k), 3) for i in range(6)] for k in range(WIDE)]
        diag = [both(diags, (z + k,), 3) for k in range(WIDE)]
        for f in range(3):
            values = []
            for k, (value, six) in enumerate(block_both(two, f, z + 1, 3)):
                values.append(fine_left(w[k], f, value, six, diag[k]))
            for k in range(WIDE // 2):
                pair = WIDE // 2 * block + k
                value = values[2 * k] + values[2 * k + 1]
                halves[f, pair, 0:8, :] = jnp.where(sub < 3, roll(value, 3, 0), own_halves[f, pair, 0:8, :])
                halves[f, pair, 8:16, :] = jnp.where(sub >= 5, roll(value, 5, 0), own_halves[f, pair, 8:16, :])
        for k in range(WIDE // 2):
            halves[3, WIDE // 2 * block + k] = own_halves[3, WIDE // 2 * block + k]

    loop(32 // WIDE, residual)
    source, target = iota((128, 128), 0), iota((128, 128), 1)
    value = None
    for half in range(2):
        pool = jnp.where(source // 2 + 64 * half == target, 0.125, 0.0)
        part = dot_exact(halves[:, 8 * half : 8 * half + 8].reshape(512, 128), pool)
        value = part if value is None else value + part
    pooled[...] = value
    packed[...] = (pooled[pl.ds(0, 256, stride=2), :] + pooled[pl.ds(1, 256, stride=2), :]).reshape(4, 8, 8, 128)

    def edge(z):
        for ch in range(4):
            edges[ch, z] = edge_columns(lambda at: rim[ch, at], z, (8, 128))

    loop(16, edge, 8)


def rim_kernel(
    edges, edges_rim, near, far, field, packed,
    start, share, one, two, weights, diags, halves, pooled,
):
    gx, gy = lax.axis_index("gx"), lax.axis_index("gy")
    lane = iota((24, 128), 1)
    part = lane % 64
    is_after = (part >= 7) & (part < 22)
    is_before = (part >= 42) & (part < 57)
    first_core = lax.rem(gy, 2) == 0

    def unpack(low):
        for ch in range(4):
            target = start.at[ch] if ch < 3 else share
            from_near, from_far = near[ch, low], jnp.where(inner(gy), far[ch, low], 0.0)
            from_right = jnp.where(first_core, from_near, from_far)
            from_left = jnp.where(first_core, from_far, from_near)
            for h in range(4):
                z = 4 * h + low
                after_y = roll(from_right, 7 - 16 * (h + 1))
                before_y = roll(from_left, 41 - 16 * h)
                own = jnp.concatenate([edges[ch, z], edges_rim[ch, z]], axis=0)
                value = jnp.where(is_after, after_y, jnp.where(is_before, before_y, own))
                target[z + 1, 8:24, :] = value[0:16]
                target[z + 1, 0:8, :] = value[16:24]
                target[z + 1, 24:32, :] = value[16:24]

    loop(4, unpack, 2)

    half_of = iota((32, 128), 1)

    def wrap_one(ref):
        ref[0] = jnp.where(half_of >= 64, roll(ref[16], 64), 0.0)
        ref[17] = jnp.where(half_of < 64, roll(ref[1], 64), 0.0)

    def wrap(ref):
        for f in range(3):
            wrap_one(ref.at[f])

    wrap_one(share)
    wrap(start)
    row = iota((24, 128), 0) + 6
    low, high = jnp.where(gx > 0, 1, 0), jnp.where(gx < NX - 1, 1, 0)
    inside_x = jnp.where(row < 8, low, jnp.where(row >= 24, high, 1))
    inside_y = jnp.where(
        part < 32,
        jnp.where((part < 7) | (gy < NY - 1), 1, 0),
        jnp.where((part >= 57) | (gy > 0), 1, 0),
    )
    omega = 0.8 * (inside_x * inside_y).astype(F32)
    fine_sweeps(
        16, [(6, 24), (7, 24)], start, share, one, two, weights, diags, halves, omega, wrap, field, STEP
    )

    source, target = iota((128, 128), 0), iota((128, 128), 1)
    spot = source % 64
    column = jnp.where(spot < 32, 121 + spot, 71 + spot) // 2
    to = jnp.where(spot < 32, column - 62, column - 48)
    keep = ((spot < 32) & (to >= 0) & (to < 9)) | ((spot >= 32) & (to >= 9) & (to < 18))
    mixed = halves[...].reshape(4, 4, 2, 16, 128)
    value = None
    for odd in range(2):
        pool = jnp.where(keep & (to + 64 * odd + 32 * (source // 64) == target), 0.125, 0.0)
        part = dot_exact(mixed[:, :, odd].reshape(256, 128), pool)
        value = part if value is None else value + part
    pooled[...] = value
    packed[...] = (pooled[pl.ds(0, 128, stride=2), :] + pooled[pl.ds(1, 128, stride=2), :]).reshape(4, 4, 8, 128)


def base_kernel(two, rim, e_one, e_two, base, wide, spread):
    copy = jnp.where(iota((128, 128), 0) == iota((128, 128), 1) // 2, 1.0, 0.0)
    value = dot_exact(e_two[...].reshape(192, 128), copy)
    for block in range(24):
        rows = value[8 * block : 8 * block + 4, :]
        wide[pl.ds(8 * block, 4, stride=2), :] = rows
        wide[pl.ds(8 * block + 1, 4, stride=2), :] = rows
    value = e_one[...].reshape(24, 2, 8, 128) + wide[...].reshape(24, 1, 8, 128)
    value = dot_exact(value.reshape(384, 128), copy)
    flat = spread.reshape(768, 128)
    for block in range(48):
        rows = value[8 * block : 8 * block + 8, :]
        flat[pl.ds(16 * block, 8, stride=2), :] = rows
        flat[pl.ds(16 * block + 1, 8, stride=2), :] = rows
    lane = iota((16, 128), 1)

    def pair(k):
        for f in range(3):
            for z in (2 * k, 2 * k + 1):
                value = rim[f, z]
                for half in range(2):
                    low = roll(value, -57 - 64 * half)
                    high = roll(value, 121 - 64 * half)
                    at = z + 16 * half
                    own = jnp.concatenate([two[f, at + 1, 16:24, :], two[f, at + 1, 0:8, :]], axis=0)
                    own = jnp.where(lane < 3, low, jnp.where(lane >= 125, high, own))
                    base[f, at] = own + spread[f, k + 8 * half]

    loop(8, pair, 4)


def resist(share):
    return recip(2.0 - 1.8 * share)


def level_weights(own, six, omega):
    faces = [recip(own + other) for other in six]
    diag = (faces[0] + faces[1]) + (faces[2] + faces[3]) + (faces[4] + faces[5])
    gain = omega * recip(diag)
    return gain, [gain * w for w in faces], diag


def middle_kernel(
    main, main_near, main_far, rim, rim_near, rim_far, sent, e_one, e_two,
    share, rest, rhs, first, second, weights, diags, halves, pooled,
    rest2, first2, second2, rhs2, share2, weights2, placed,
):
    gx, gy = lax.axis_index("gx"), lax.axis_index("gy")
    low_x, high_x = jnp.where(gx > 0, 1, 0), jnp.where(gx < NX - 1, 1, 0)
    low_y, high_y = jnp.where(gy > 0, 1, 0), jnp.where(gy < NY - 1, 1, 0)

    for f in range(3):
        for ref in (first, second):
            ref[f, 0] = jnp.zeros((32, 128), F32)
            ref[f, 17] = jnp.zeros((32, 128), F32)
    for z in (0, 17):
        rest[z] = jnp.full((32, 128), 0.5, F32)
    lane = iota((8, 128), 1)
    even = lax.rem(gx, 2) == 0
    near_row, far_row = jnp.where(even, 16, 0), jnp.where(even, 0, 16)
    starts = (pl.multiple_of(near_row, 8), pl.multiple_of(far_row, 8), 8)

    has_far = inner(gx)
    source, target = iota((128, 128), 0), iota((128, 128), 1)
    rims = [rim_near[...].reshape(128, 128), jnp.where(has_far, rim_far[...].reshape(128, 128), 0.0)]
    rims = jnp.concatenate(rims + [rim[...].reshape(128, 128)], axis=0)
    for odd in range(2):
        for half in range(2):
            spot = source - (64 * odd + 32 * half)
            to = jnp.where(spot < 9, 62 + spot, (112 + spot) % 128)
            put = jnp.where((spot >= 0) & (spot < 18) & (to == target), 1.0, 0.0)
            placed[odd, half] = dot_exact(rims, put).reshape(3, 4, 4, 8, 128)

    def fill(q):
        for odd in range(2):
            for half in range(2):
                z = 2 * q + odd + 8 * half
                for i, (at, middle) in enumerate(zip(starts, (main_near, main_far, main))):
                    for ch in range(4):
                        body = roll(middle[ch, 2 * q + odd], 64 * half)
                        if i == 1:
                            body = jnp.where(has_far, body, 0.0)
                        value = jnp.where((lane >= 2) & (lane < 62), body, placed[odd, half, i, ch, q])
                        if ch < 3:
                            rhs[ch, z, pl.ds(at, 8), :] = value
                        else:
                            share[z, pl.ds(at, 8), :] = value
                            rest[z + 1, pl.ds(at, 8), :] = resist(value)
                rest[z + 1, 24:32, :] = jnp.full((8, 128), 0.5, F32)

    loop(4, fill, 2)

    row, lane = iota((24, 128), 0) + 1, iota((24, 128), 1)
    in_x = jnp.where(row < 8, low_x, jnp.where(row >= 16, high_x, 1))
    in_y = jnp.where(lane < 64, 1, jnp.where(lane < 96, high_y, low_y))
    omega = 0.8 * (in_x * in_y).astype(F32)

    def start(step):
        z = STEP * step
        for k, (own, six) in enumerate(block_of(rest, (), z + 1, STEP, 1, 24)):
            gain, w, diag = level_weights(own, six, omega)
            for i in range(6):
                weights[i, z + k, 1:25, :] = w[i]
            diags[z + k, 1:25, :] = (1.25 * 0.25) * diag
            for f in range(3):
                first[f, z + k + 1, 1:25, :] = (4.0 * gain) * rhs[f, z + k, 1:25, :]

    loop(16 // STEP, start)

    def sweep(step):
        z = STEP * step
        w = [[weights[i, z + k, 3:27, :] for i in range(6)] for k in range(STEP)]
        for f in range(3):
            for k, (own, six) in enumerate(block_of(first, (f,), z + 1, STEP, 3, 24)):
                second[f, z + k + 1, 3:27, :] = 1.2 * own + weigh(w[k], six)

    loop(16 // STEP, sweep)

    def left(step):
        z = STEP * step
        w = [[weights[i, z + k, 4:20, :] for i in range(6)] for k in range(STEP)]
        diag = [diags[z + k, 4:20, :] for k in range(STEP)]
        for f in range(3):
            values = []
            for k, (own, six) in enumerate(block_of(second, (f,), z + 1, STEP, 4, 16)):
                change = (first[f, z + k + 1, 4:20, :] - 0.8 * own) + weigh(w[k], six)
                values.append(change * diag[k])
                e_one[f, z + k] = second[f, z + k + 1, 8:16, :]
            for k in range(STEP // 2):
                halves[f, STEP // 2 * step + k, 0:16, :] = values[2 * k] + values[2 * k + 1]
                halves[f, STEP // 2 * step + k, 16:24, :] = jnp.zeros((8, 128), F32)
        for k in range(STEP // 2):
            halves[3, STEP // 2 * step + k] = share[z + 2 * k] + share[z + 2 * k + 1]

    loop(16 // STEP, left)

    source, target = iota((128, 128), 0), iota((128, 128), 1)
    pool = jnp.where(source // 2 + jnp.where(source >= 96, 64, 0) == target, 0.125, 0.0)
    pooled[...] = dot_exact(halves[...].reshape(4 * 8 * 24, 128), pool)
    for z in (0, 9):
        rest2[z] = jnp.full((24, 128), 0.5, F32)
        for f in range(3):
            first2[f, z] = jnp.zeros((24, 128), F32)
            second2[f, z] = jnp.zeros((24, 128), F32)
    for z in range(8):
        for f in range(3):
            base = (f * 8 + z) * 24
            rhs2[f, z] = pooled[pl.ds(base, 8, stride=2), :] + pooled[pl.ds(base + 1, 8, stride=2), :]
        base = (3 * 8 + z) * 24
        value = pooled[pl.ds(base + 2, 8, stride=2), :] + pooled[pl.ds(base + 3, 8, stride=2), :]
        rest2[z + 1, 0:8, :] = resist(value)
        value = pooled[pl.ds(base + 8, 8, stride=2), :] + pooled[pl.ds(base + 9, 8, stride=2), :]
        rest2[z + 1, 3:11, :] = resist(value)
        share2[z] = value

    row, lane = iota((8, 128), 0) + 1, iota((8, 128), 1)
    in_x = jnp.where(row < 3, low_x, jnp.where(row >= 7, high_x, 1))
    in_y = jnp.where(lane < 32, 1, jnp.where(lane < 96, high_y, low_y))
    omega2 = 0.8 * (in_x * in_y).astype(F32)

    for z, (own, six) in enumerate(block_of(rest2, (), 1, 8, 1, 8)):
        gain, w, diag = level_weights(own, six, omega2)
        for i in range(6):
            weights2[i, z, 1:9, :] = w[i]
        weights2[6, z, 1:9, :] = (1.25 * 0.0625) * diag
        for f in range(3):
            first2[f, z + 1, 1:9, :] = (16.0 * gain) * rhs2[f, z]
    w = [[weights2[i, z, 2:10, :] for i in range(6)] for z in range(8)]
    for f in range(3):
        for z, (own, six) in enumerate(block_of(first2, (f,), 1, 8, 2, 8)):
            second2[f, z + 1, 2:10, :] = 1.2 * own + weigh(w[z], six)
    w = [[weights2[i, z, 3:11, :] for i in range(7)] for z in range(8)]
    own_row = iota((8, 128), 0) < 4
    parts = [{} for pair in range(4)]
    for f in range(3):
        for z, (own, six) in enumerate(block_of(second2, (f,), 1, 8, 3, 8)):
            e_two[f, z] = own
            change = (first2[f, z + 1, 3:11, :] - 0.8 * own) + weigh(w[z], six)
            value = jnp.where(own_row, change * w[z][6], 0.0)
            sums = parts[z // 2]
            sums[f] = value if z % 2 == 0 else sums[f] + value
    for z in range(8):
        value = jnp.where(own_row, share2[z], 0.0)
        sums = parts[z // 2]
        sums[3] = value if z % 2 == 0 else sums[3] + value

    pool = jnp.where((source < 32) & (source // 2 == target % 16), 0.125, 0.0)
    rows = jnp.concatenate([parts[pair][ch] for ch in range(4) for pair in range(4)], axis=0)
    spread = dot(rows, pool)
    at, to = iota((32, 128), 0), iota((32, 128), 1)
    keep = (at // 8 == to // 32) & ((at % 8) // 2 == (to // 16) % 2)
    result = jnp.concatenate(
        [
            jnp.sum(jnp.where(keep, spread[32 * ch : 32 * ch + 32], 0.0), axis=0, keepdims=True)
            for ch in range(4)
        ],
        axis=0,
    )
    for copy in range(CHIPS):
        sent[copy] = result


def swap_blocks(x):
    sub, group = iota((8, 128), 0), iota((8, 128), 1) // 16
    for bit in (4, 2, 1):
        up = roll(roll(x, -bit, 0), 16 * bit)
        down = up if bit == 4 else roll(roll(x, bit, 0), -16 * bit)
        sub_set, group_set = (sub & bit) != 0, (group & bit) != 0
        x = jnp.where(sub_set == group_set, x, jnp.where(sub_set, down, up))
    return x


def top_kernel(
    mine, other, base, out,
    natural, first, second, four, weights, diags, lefts, final, sems,
):
    gx, gy = lax.axis_index("gx"), lax.axis_index("gy")
    first_core = lax.rem(gy, 2) == 0
    lane, sub = iota((16, 128), 1), iota((16, 128), 0)
    cells = [(z, x, half) for z in range(4) for x in range(2) for half in range(2)]

    def lay(g):
        for ch in range(4):
            rows = pl.ds(32 * g + ch, 8, stride=4)
            pair = mine[rows, :], other[rows, :]
            natural[ch, 0, pl.ds(pl.multiple_of(8 * g, 8), 8), :] = swap_blocks(
                jnp.where(first_core, pair[0], pair[1])
            )
            natural[ch, 1, pl.ds(pl.multiple_of(8 * g, 8), 8), :] = swap_blocks(
                jnp.where(first_core, pair[1], pair[0])
            )

    loop(16, lay, 4)
    flat = natural.reshape(1024, 128)

    def plane(ch, z, x, half):
        return flat[pl.ds((ch * 2 + half) * 128 + z * 2 + x, 16, stride=8), :]

    def neighbours(at, z, x, half, outside):
        own, other = at(z, x, half), at(z, 1 - x, half)
        beside = at(z, x, 1 - half)
        shifted = roll(other, 1 if x == 0 else -1, 0)
        low, high = (shifted, other) if x == 0 else (other, shifted)
        left, right = roll(own, 1), roll(own, -1)
        left = jnp.where(lane % 16 == 0, roll(beside, 1 if half == 0 else -15), left)
        right = jnp.where(lane % 16 == 15, roll(beside, 15 if half == 0 else -1), right)
        down = at(z - 1, x, half) if z > 0 else outside
        up = at(z + 1, x, half) if z < 3 else outside
        return own, [low, high, left, right, down, up]

    def edge_masks(x, half):
        return [
            sub > 0 if x == 0 else None,
            sub < 15 if x == 1 else None,
            lane > 0 if half == 0 else None,
            lane < 127 if half == 1 else None,
            None,
            None,
        ]

    def key(z, x, half):
        return (z * 2 + x) * 2 + half

    shares = {c: plane(3, *c) for c in cells}
    rests = {c: resist(shares[c]) for c in cells}
    outside, zeros = jnp.full((16, 128), 0.5, F32), jnp.zeros((16, 128), F32)
    for z, x, half in cells:
        own, six = neighbours(lambda *c: rests[c], z, x, half, outside)
        masks = edge_masks(x, half)
        six = [s if m is None else jnp.where(m, s, 0.5) for s, m in zip(six, masks)]
        gain, w, diag = level_weights(own, six, 0.8)
        at = key(z, x, half)
        for i in range(6):
            weights[i, at] = w[i] if masks[i] is None else jnp.where(masks[i], w[i], 0.0)
        diags[at] = (1.25 * 0.25**3) * diag
        for f in range(3):
            first[f, at] = (64.0 * gain) * plane(f, z, x, half)

    for z, x, half in cells:
        at = key(z, x, half)
        w = [weights[i, at] for i in range(6)]
        for f in range(3):
            own, six = neighbours(lambda *c: first[f, key(*c)], z, x, half, zeros)
            second[half, f, z * 2 + x] = 1.2 * own + weigh(w, six)

    for z4 in range(2):
        for half in range(2):
            sums = [None] * 4
            for z in (2 * z4, 2 * z4 + 1):
                for x in range(2):
                    at = key(z, x, half)
                    w = [weights[i, at] for i in range(6)]
                    diag = diags[at]
                    for f in range(3):
                        own, six = neighbours(
                            lambda c, d, e: second[e, f, c * 2 + d], z, x, half, zeros
                        )
                        value = ((first[f, at] - 0.8 * own) + weigh(w, six)) * diag
                        sums[f] = value if sums[f] is None else sums[f] + value
                    share = shares[z, x, half]
                    sums[3] = share if sums[3] is None else sums[3] + share
            for ch in range(4):
                lefts[ch, z4, :, 128 * half : 128 * half + 128] = sums[ch]

    source = iota((256, 128), 0)
    column = ((source % 128) // 16) * 16 + (source // 128) * 8 + (source % 16) // 2
    pool = jnp.where(column == iota((256, 128), 1), 0.125, 0.0)
    level = dot_exact(lefts[...].reshape(128, 256), pool)

    def coarsest(ch, z):
        return level[(ch * 2 + z) * 16 : (ch * 2 + z) * 16 + 16, :]

    masks = [sub > 0, sub < 15, lane > 0, lane < 127]
    resists = [resist(coarsest(3, z)) for z in range(2)]
    gains, ws, ds = [], [], []
    for z in range(2):
        own, other = resists[z], resists[1 - z]
        six = [roll(own, 1, 0), roll(own, -1, 0), roll(own, 1), roll(own, -1)]
        six = [jnp.where(m, s, 0.5) for m, s in zip(masks, six)] + [other, outside]
        gain, w, diag = level_weights(own, six, 0.8)
        gains.append(gain)
        ds.append(diag)
        ws.append([jnp.where(m, v, 0.0) for m, v in zip(masks, w)] + [w[4]])
    whole = jnp.sum(ds[0] + ds[1], keepdims=True)

    def around(values, z):
        own, other = values[z], values[1 - z]
        return weigh(ws[z], (roll(own, 1, 0), roll(own, -1, 0), roll(own, 1), roll(own, -1), other))

    begin = [[256.0 * gains[z] * coarsest(f, z) for z in range(2)] for f in range(3)]
    values = begin
    for step in range(5):
        values = [
            [(0.2 * values[f][z] + begin[f][z]) + around(values[f], z) for z in range(2)] for f in range(3)
        ]
    shifts = []
    for f in range(3):
        change = [(begin[f][z] - 0.8 * values[f][z]) + around(values[f], z) for z in range(2)]
        shifts.append(jnp.sum(1.25 * (change[0] * ds[0] + change[1] * ds[1]), keepdims=True) / whole)
        for z in range(2):
            four[2 * f + z] = values[f][z]

    rows = four.reshape(96, 128)[pl.ds(gx, 6, stride=16), :]
    upper = jnp.concatenate([jnp.broadcast_to(rows[i : i + 1], (4, 128)) for i in range(6)], axis=0)
    flat = second.reshape(768, 128)
    halves = [flat[pl.ds(gx + 384 * half, 24, stride=16), :] for half in range(2)]
    three = turn(jnp.where(first_core, halves[0], halves[1]), -16 * lax.div(gy, 2))
    both = jnp.concatenate([turn(upper, -8 * gy), three], axis=1)
    both = jnp.concatenate([both, jnp.zeros((8, 256), F32)], axis=0)
    source, target = iota((256, 128), 0), iota((256, 128), 1)
    copy = jnp.where(source == jnp.where(source < 128, target // 16, 128 + target // 8), 1.0, 0.0)
    three = dot_exact(both, copy)

    copies = []
    for f in range(3):
        for z in range(4):
            for x in range(2):
                at = f * 8 + z * 2 + x
                value = jnp.broadcast_to(three[at : at + 1] + shifts[f], (8, 128))
                for k in range(8 * z, 8 * z + 8):
                    final[f, k, 8 * x : 8 * x + 8, :] = base[f, k, 8 * x : 8 * x + 8, :] + value
            if z % 2 == 1:
                part = (f, pl.ds(8 * z - 8, 16))
                copy = pltpu.make_async_copy(final.at[part], out.at[part], sems.at[len(copies)])
                copy.start()
                copies.append(copy)
    for copy in copies:
        copy.wait()


def local(labels, guess):
    swap_near = [(i, i ^ 1) for i in range(NY)]
    far_x, far_y = [], []
    for x in range(NX):
        for y in range(NY):
            across_x, across_y = x + 1 if x % 2 else x - 1, y + 1 if y % 2 else y - 1
            to = (across_x, y) if 0 <= across_x < NX else (x, y ^ 1)
            far_x.append((x * NY + y, to[0] * NY + to[1]))
            to = (x, across_y) if 0 <= across_y < NY else (x ^ 1, y)
            far_y.append((x * NY + y, to[0] * NY + to[1]))
    both = ("gx", "gy")
    to_near, to_far, own = call(
        rows_kernel,
        [(12, 32, 128)] * 2 + [(4, 32, 16, 128)],
        [pltpu.VMEM((32, 16, 128), jnp.int32), pltpu.SemaphoreType.DMA((4,))],
        in_specs=[ANY, ANY],
    )(pltpu.with_memory_space_constraint(guess, pltpu.HBM), pltpu.with_memory_space_constraint(labels, pltpu.HBM))
    from_near = lax.ppermute(to_near, "gx", swap_near)
    from_far = lax.ppermute(to_far, both, far_x)
    own_one, own_two, halves, to_right, to_left, edges = call(
        own_kernel,
        [(3, 34, 32, 128)] * 2 + [(4, 16, 16, 128)] + [(4, 4, 16, 128)] * 2 + [(4, 16, 16, 128)],
        [(4, 34, 32, 128), (6, 32, 32, 128), (32, 32, 128)],
        flops=20_000_000,
    )(own)
    to_near, to_far, rim_rows = call(pack_kernel, [(4, 4, 24, 128)] * 2 + [(4, 32, 8, 128)], [])(
        to_right, to_left, from_near, from_far
    )
    from_far = lax.ppermute(to_far, both, far_y)
    from_near = lax.ppermute(to_near, "gy", swap_near)
    two, main, edges_rim = call(
        rows_edge_kernel,
        [(3, 34, 24, 128), (4, 8, 8, 128), (4, 16, 8, 128)],
        [(4, 34, 24, 128), (3, 34, 24, 128), (6, 32, 24, 128), (32, 24, 128)]
        + [(4, 16, 16, 128), (512, 128)],
        flops=10_000_000,
    )(own, rim_rows, own_one, own_two, halves)
    main_near = lax.ppermute(main, "gx", swap_near)
    main_far = lax.ppermute(main, both, far_x)
    rim, rim_one = call(
        rim_kernel,
        [(3, 16, 16, 128), (4, 4, 8, 128)],
        [(3, 18, 32, 128), (18, 32, 128)]
        + [(3, 18, 32, 128)] * 2
        + [(6, 16, 32, 128), (16, 32, 128)]
        + [(4, 8, 16, 128), (256, 128)],
        flops=10_000_000,
    )(edges, edges_rim, from_near, from_far)
    rim_near = lax.ppermute(rim_one, "gx", swap_near)
    rim_far = lax.ppermute(rim_one, both, far_x)
    sent, e_one, e_two = call(
        middle_kernel,
        [(CHIPS, 4, 128), (3, 16, 8, 128), (3, 8, 8, 128)],
        [(16, 24, 128), (18, 32, 128), (3, 16, 32, 128), (3, 18, 32, 128), (3, 18, 32, 128)]
        + [(6, 16, 32, 128), (16, 32, 128), (4, 8, 24, 128), (768, 128)]
        + [(10, 24, 128), (3, 10, 24, 128), (3, 10, 24, 128), (3, 8, 8, 128), (8, 8, 128)]
        + [(7, 8, 16, 128), (2, 2, 3, 4, 4, 8, 128)],
    )(main, main_near, main_far, rim_one, rim_near, rim_far)
    groups = [[i for i in range(NX * NY) if i % 2 == core] for core in range(2)]
    mine = lax.all_to_all(
        sent, ("gx", "gy"), split_axis=0, concat_axis=0, axis_index_groups=groups, tiled=True
    )
    (base,) = call(base_kernel, [(3, 32, 16, 128)], [(192, 128), (3, 16, 16, 128)])(two, rim, e_one, e_two)
    other = lax.ppermute(mine, "gy", swap_near)
    (out,) = call(
        top_kernel,
        [(3, 32, 16, 128)],
        [(4, 2, 128, 128), (3, 16, 16, 128), (2, 3, 8, 16, 128), (6, 16, 128), (6, 16, 16, 128)]
        + [(16, 16, 128), (4, 2, 16, 256), (3, 32, 16, 128), pltpu.SemaphoreType.DMA((6,))],
        out_specs=[ANY],
    )(mine.reshape(512, 128), other.reshape(512, 128), base)
    return out


def solution(mesh):
    return jax.shard_map(
        local,
        mesh=mesh,
        in_specs=(P(None, "gx", "gy"), P(None, None, "gx", "gy")),
        out_specs=P(None, None, "gx", "gy"),
        check_vma=False,
    )
```

```python
import jax
import jax.numpy as jnp
from jax import lax
from jax.experimental import pallas as pl
from jax.experimental.pallas import tpu as pltpu
from jax.sharding import PartitionSpec as P


F32 = jnp.float32
NX, NY, CHIPS = 16, 16, 128
STEP, WIDE = 16, 32
BETWEEN = 2.0 * 0.1 / 1.1
ANY = pl.BlockSpec(memory_space=pltpu.HBM)


def dot_exact(a, b):
    high = a.astype(jnp.bfloat16)
    low = (a - high.astype(F32)).astype(jnp.bfloat16)
    b = b.astype(jnp.bfloat16)
    return jnp.dot(
        jnp.concatenate([high, low], axis=1), jnp.concatenate([b, b], axis=0), preferred_element_type=F32
    )


def iota(shape, dim):
    return lax.broadcasted_iota(jnp.int32, shape, dim)


def roll(x, shift, axis=1):
    shift = shift % x.shape[axis]
    return x if shift == 0 else pltpu.roll(x, shift, axis)


def turn(x, shift):
    return pltpu.roll(x, lax.rem(shift + 256, 128), 1)


def recip(x):
    guess = pl.reciprocal(x, approx=True)
    return guess * (2.0 - x * guess)


def inner(index):
    return (index > 0) & (index < 15)


def call(kernel, outs, scratch, flops=1_000_000, **kw):
    return pl.pallas_call(
        kernel,
        out_shape=[jax.ShapeDtypeStruct(s, F32) for s in outs],
        scratch_shapes=[pltpu.VMEM(s, F32) if isinstance(s, tuple) else s for s in scratch],
        compiler_params=pltpu.CompilerParams(vmem_limit_bytes=32 * 1024 * 1024),
        cost_estimate=pl.CostEstimate(flops=flops, bytes_accessed=4_000_000, transcendentals=0),
        **kw,
    )


def loop(count, body, unroll=1):
    def step(i, carry):
        body(i)
        return carry

    lax.fori_loop(0, count, step, 0, unroll=unroll)


def weigh(weights, values):
    parts = [w * v for w, v in zip(weights, values)]
    while len(parts) > 1:
        parts = [sum(parts[i : i + 2][1:], parts[i]) for i in range(0, len(parts), 2)]
    return parts[0]


def rows_kernel(guess, labels, near, far, own, phase, sems):
    even = lax.rem(lax.axis_index("gx"), 2) == 0
    near_row, far_row = jnp.where(even, 13, 0), jnp.where(even, 0, 13)
    copies = [pltpu.make_async_copy(labels, phase, sems.at[3])]
    for f in range(3):
        copies.append(pltpu.make_async_copy(guess.at[f], own.at[f], sems.at[f]))
    for copy in copies:
        copy.start()
    copies[0].wait()
    own[3] = jnp.where(phase[...] == 1, 0.0, 1.0).astype(F32)
    flat = own.reshape(4 * 32 * 16, 128)
    for ch in (3, 0, 1, 2):
        if ch < 3:
            copies[ch + 1].wait()
        for row in range(3):
            near[3 * ch + row] = flat[pl.ds(512 * ch + near_row + row, 32, stride=16), :]
            far[3 * ch + row] = flat[pl.ds(512 * ch + far_row + row, 32, stride=16), :]


def pack_kernel(to_right, to_left, x_near, x_far, near, far, rim):
    first_core = lax.rem(lax.axis_index("gy"), 2) == 0
    even = lax.rem(lax.axis_index("gx"), 2) == 0
    near_row, far_row = jnp.where(even, 0, 5), jnp.where(even, 5, 0)
    has_far = inner(lax.axis_index("gx"))
    flat = rim.reshape(4 * 32 * 8, 128)
    for ch in range(4):
        for row in range(3):
            flat[pl.ds(256 * ch + near_row + row, 32, stride=8), :] = x_near[3 * ch + row]
            flat[pl.ds(256 * ch + far_row + row, 32, stride=8), :] = jnp.where(has_far, x_far[3 * ch + row], 0.0)

    def some(low):
        for ch in range(4):
            right, left = pack_planes(lambda z: rim[ch, z], low, (8, 128))
            for at, right, left in (
                (slice(0, 16), to_right[ch, low], to_left[ch, low]),
                (slice(16, 24), right, left),
            ):
                near[ch, low, at, :] = jnp.where(first_core, right, left)
                far[ch, low, at, :] = jnp.where(first_core, left, right)

    loop(4, some, 4)


def pack_planes(plane, low, shape):
    group = iota(shape, 1) // 16
    right = left = jnp.zeros(shape, F32)
    for h in range(8):
        moved = roll(plane(4 * h + low), 16 * h + 16)
        right = jnp.where(group == h, moved, right)
        left = jnp.where(group == (h + 1) % 8, moved, left)
    return right, left


def edge_columns(plane, z, shape):
    lane = iota(shape, 1)
    value = jnp.zeros(shape, F32)
    for half in range(2):
        source = plane(z + 16 * half)
        base = 64 * half
        value = jnp.where((lane >= base) & (lane < base + 7), roll(source, base + 7), value)
        value = jnp.where((lane >= base + 57) & (lane < base + 64), roll(source, base + 57), value)
    return value


def six_of(ref, lead, z, first, count):
    own = ref[(*lead, z, pl.ds(first, count), slice(None))]
    return own, (
        ref[(*lead, z, pl.ds(first - 1, count), slice(None))],
        ref[(*lead, z, pl.ds(first + 1, count), slice(None))],
        roll(own, 1),
        roll(own, -1),
        ref[(*lead, z - 1, pl.ds(first, count), slice(None))],
        ref[(*lead, z + 1, pl.ds(first, count), slice(None))],
    )


def block_of(ref, lead, z, planes, first, count):
    rows = pl.ds(first, count)
    own = [ref[(*lead, z + k, rows, slice(None))] for k in range(-1, planes + 1)]
    result = []
    for k in range(planes):
        value = own[k + 1]
        six = (
            ref[(*lead, z + k, pl.ds(first - 1, count), slice(None))],
            ref[(*lead, z + k, pl.ds(first + 1, count), slice(None))],
            roll(value, 1),
            roll(value, -1),
            own[k],
            own[k + 2],
        )
        result.append((value, six))
    return result


def fine_weights(own, six, omega):
    base, slope = 1.0 + (BETWEEN - 1.0) * own, (BETWEEN - 1.0) + (1.1 - 2.0 * BETWEEN) * own
    total = (six[0] + six[1]) + (six[2] + six[3]) + (six[4] + six[5])
    diag = 6.0 * base + slope * total
    gain = omega * recip(diag)
    base, slope = gain * base, gain * slope
    return [base + slope * other for other in six], 1.25 * diag


def fine_sweep(w, f, own, six):
    return (0.2 * own + (w[2 * f + 1] - w[2 * f])) + weigh(w, six)


def fine_left(w, f, own, six, diag):
    return (((w[2 * f + 1] - w[2 * f]) - 0.8 * own) + weigh(w, six)) * diag


def fine_sweeps(planes, windows, start, share, one, two, weights, diags, halves, omega, wrap, keep, size):
    first, count = windows[0]

    def first_sweep(step):
        z = size * step
        w = []
        for k, (own, six) in enumerate(block_of(share, (), z + 1, size, first, count)):
            now, diag = fine_weights(own, six, omega)
            diags[z + k, pl.ds(first, count), :] = diag
            for i in range(6):
                weights[i, z + k, pl.ds(first, count), :] = now[i]
            w.append(now)
        for f in range(3):
            for k, (own, six) in enumerate(block_of(start, (f,), z + 1, size, first, count)):
                one[f, z + k + 1, pl.ds(first, count), :] = fine_sweep(w[k], f, own, six)

    loop(planes // size, first_sweep)
    wrap(one)
    second, count2 = windows[1]

    def second_sweep(step):
        z = size * step
        w = [[weights[i, z + k, pl.ds(second, count2), :] for i in range(6)] for k in range(size)]
        for f in range(3):
            for k, (own, six) in enumerate(block_of(one, (f,), z + 1, size, second, count2)):
                two[f, z + k + 1, pl.ds(second, count2), :] = fine_sweep(w[k], f, own, six)

    loop(planes // size, second_sweep)
    wrap(two)

    def residual(step):
        z = size * step
        w = [[weights[i, z + k, 8:24, :] for i in range(6)] for k in range(size)]
        diag = [diags[z + k, 8:24, :] for k in range(size)]
        for f in range(3):
            values = []
            for k, (own, six) in enumerate(block_of(two, (f,), z + 1, size, 8, 16)):
                if keep is not None:
                    keep[f, z + k] = own
                values.append(fine_left(w[k], f, own, six, diag[k]))
            for pair in range(size // 2):
                halves[f, size // 2 * step + pair] = values[2 * pair] + values[2 * pair + 1]
        for pair in range(size // 2):
            at = z + 2 * pair + 1
            halves[3, size // 2 * step + pair] = share[at, 8:24, :] + share[at + 1, 8:24, :]

    loop(planes // size, residual)


def own_kernel(own, one, two, halves, to_right, to_left, edges, held, weights, diags):
    zero = jnp.zeros((32, 128), F32)
    for z in (0, 33):
        for ch in range(4):
            held[ch, z] = zero
        for ref in (one, two):
            for f in range(3):
                ref[f, z] = zero

    def plane(z):
        for ch in range(4):
            held[ch, z + 1, 8:24, :] = own[ch, z]

    loop(32, plane, 8)
    fine_sweeps(
        32, [(8, 16)] * 2, held, held.at[3], one, two, weights, diags, halves, 0.8, lambda ref: None, None, 8
    )

    def some(low):
        for ch in range(4):
            to_right[ch, low], to_left[ch, low] = pack_planes(lambda z: own[ch, z], low, (16, 128))

    loop(4, some, 2)

    def edge(z):
        for ch in range(4):
            edges[ch, z] = edge_columns(lambda at: own[ch, at], z, (16, 128))

    loop(16, edge, 8)


def rows_edge_kernel(own, rim, own_one, own_two, own_halves, two, packed, edges, start, one, weights, diags, halves, pooled):
    gx = lax.axis_index("gx")
    zero = jnp.zeros((24, 128), F32)
    for z in (0, 33):
        for ch in range(4):
            start[ch, z] = zero
        for ref in (one, two):
            for f in range(3):
                ref[f, z] = zero

    def fill(z):
        for ch in range(4):
            start[ch, z + 1, 0:8, :] = own[ch, z, 8:16, :]
            start[ch, z + 1, 8:16, :] = rim[ch, z]
            start[ch, z + 1, 16:24, :] = own[ch, z, 0:8, :]
        for f in range(3):
            for ref, source in ((one, own_one), (two, own_two)):
                ref[f, z + 1, 0:8, :] = source[f, z + 1, 16:24, :]
                ref[f, z + 1, 16:24, :] = source[f, z + 1, 8:16, :]

    loop(32, fill, 8)
    upper = iota((8, 128), 0) < 4

    def both(ref, lead, step, shift=0):
        high = ref[(*lead, pl.ds(8 - step + shift, 8), slice(None))]
        low = ref[(*lead, pl.ds(8 + step + shift, 8), slice(None))]
        return jnp.where(upper, high, low)

    def block_both(ref, f, z, step):
        own = [both(ref, (f, z + k), step) for k in range(-1, WIDE + 1)]
        result = []
        for k in range(WIDE):
            value = own[k + 1]
            low, high = both(ref, (f, z + k), step, -1), both(ref, (f, z + k), step, 1)
            result.append((value, (low, high, roll(value, 1), roll(value, -1), own[k], own[k + 2])))
        return result

    def put(ref, f, z, step, value):
        ref[f, z, pl.ds(8 - step, 4), :] = value[0:4]
        ref[f, z, pl.ds(12 + step, 4), :] = value[4:8]

    row = iota((16, 128), 0) + 5
    low, high = jnp.where(gx > 0, 1, 0), jnp.where(gx < NX - 1, 1, 0)
    inside = jnp.where((row >= 8) & (row < 12), high, jnp.where((row >= 12) & (row < 16), low, 1))
    omega = 0.8 * inside.astype(F32)

    def weigh_all(step):
        z = WIDE * step
        for k, (value, six) in enumerate(block_of(start, (3,), z + 1, WIDE, 5, 16)):
            w, diag = fine_weights(value, six, omega)
            diags[z + k, 5:21, :] = diag
            for i in range(6):
                weights[i, z + k, 5:21, :] = w[i]

    loop(32 // WIDE, weigh_all)

    for step, source, target in ((1, start, one), (2, one, two)):

        def sweep(block):
            z = WIDE * block
            w = [[both(weights, (i, z + k), step) for i in range(6)] for k in range(WIDE)]
            for f in range(3):
                for k, (value, six) in enumerate(block_both(source, f, z + 1, step)):
                    put(target, f, z + k + 1, step, fine_sweep(w[k], f, value, six))

        loop(32 // WIDE, sweep)

    sub = iota((8, 128), 0)

    def residual(block):
        z = WIDE * block
        w = [[both(weights, (i, z + k), 3) for i in range(6)] for k in range(WIDE)]
        diag = [both(diags, (z + k,), 3) for k in range(WIDE)]
        for f in range(3):
            values = []
            for k, (value, six) in enumerate(block_both(two, f, z + 1, 3)):
                values.append(fine_left(w[k], f, value, six, diag[k]))
            for k in range(WIDE // 2):
                pair = WIDE // 2 * block + k
                value = values[2 * k] + values[2 * k + 1]
                halves[f, pair, 0:8, :] = jnp.where(sub < 3, roll(value, 3, 0), own_halves[f, pair, 0:8, :])
                halves[f, pair, 8:16, :] = jnp.where(sub >= 5, roll(value, 5, 0), own_halves[f, pair, 8:16, :])
        for k in range(WIDE // 2):
            halves[3, WIDE // 2 * block + k] = own_halves[3, WIDE // 2 * block + k]

    loop(32 // WIDE, residual)
    source, target = iota((128, 128), 0), iota((128, 128), 1)
    value = None
    for half in range(2):
        pool = jnp.where(source // 2 + 64 * half == target, 0.125, 0.0)
        part = dot_exact(halves[:, 8 * half : 8 * half + 8].reshape(512, 128), pool)
        value = part if value is None else value + part
    pooled[...] = value
    packed[...] = (pooled[pl.ds(0, 256, stride=2), :] + pooled[pl.ds(1, 256, stride=2), :]).reshape(4, 8, 8, 128)

    def edge(z):
        for ch in range(4):
            edges[ch, z] = edge_columns(lambda at: rim[ch, at], z, (8, 128))

    loop(16, edge, 8)


def rim_kernel(
    edges, edges_rim, near, far, field, packed,
    start, share, one, two, weights, diags, halves, pooled,
):
    gx, gy = lax.axis_index("gx"), lax.axis_index("gy")
    lane = iota((24, 128), 1)
    part = lane % 64
    is_after = (part >= 7) & (part < 22)
    is_before = (part >= 42) & (part < 57)
    first_core = lax.rem(gy, 2) == 0

    def unpack(low):
        for ch in range(4):
            target = start.at[ch] if ch < 3 else share
            from_near, from_far = near[ch, low], jnp.where(inner(gy), far[ch, low], 0.0)
            from_right = jnp.where(first_core, from_near, from_far)
            from_left = jnp.where(first_core, from_far, from_near)
            for h in range(4):
                z = 4 * h + low
                after_y = roll(from_right, 7 - 16 * (h + 1))
                before_y = roll(from_left, 41 - 16 * h)
                own = jnp.concatenate([edges[ch, z], edges_rim[ch, z]], axis=0)
                value = jnp.where(is_after, after_y, jnp.where(is_before, before_y, own))
                target[z + 1, 8:24, :] = value[0:16]
                target[z + 1, 0:8, :] = value[16:24]
                target[z + 1, 24:32, :] = value[16:24]

    loop(4, unpack, 2)

    half_of = iota((32, 128), 1)

    def wrap_one(ref):
        ref[0] = jnp.where(half_of >= 64, roll(ref[16], 64), 0.0)
        ref[17] = jnp.where(half_of < 64, roll(ref[1], 64), 0.0)

    def wrap(ref):
        for f in range(3):
            wrap_one(ref.at[f])

    wrap_one(share)
    wrap(start)
    row = iota((24, 128), 0) + 6
    low, high = jnp.where(gx > 0, 1, 0), jnp.where(gx < NX - 1, 1, 0)
    inside_x = jnp.where(row < 8, low, jnp.where(row >= 24, high, 1))
    inside_y = jnp.where(
        part < 32,
        jnp.where((part < 7) | (gy < NY - 1), 1, 0),
        jnp.where((part >= 57) | (gy > 0), 1, 0),
    )
    omega = 0.8 * (inside_x * inside_y).astype(F32)
    fine_sweeps(
        16, [(6, 24), (7, 24)], start, share, one, two, weights, diags, halves, omega, wrap, field, STEP
    )

    source, target = iota((128, 128), 0), iota((128, 128), 1)
    spot = source % 64
    column = jnp.where(spot < 32, 121 + spot, 71 + spot) // 2
    to = jnp.where(spot < 32, column - 62, column - 48)
    keep = ((spot < 32) & (to >= 0) & (to < 9)) | ((spot >= 32) & (to >= 9) & (to < 18))
    mixed = halves[...].reshape(4, 4, 2, 16, 128)
    value = None
    for odd in range(2):
        pool = jnp.where(keep & (to + 64 * odd + 32 * (source // 64) == target), 0.125, 0.0)
        part = dot_exact(mixed[:, :, odd].reshape(256, 128), pool)
        value = part if value is None else value + part
    pooled[...] = value
    packed[...] = (pooled[pl.ds(0, 128, stride=2), :] + pooled[pl.ds(1, 128, stride=2), :]).reshape(4, 4, 8, 128)


def base_kernel(two, rim, e_one, e_two, base, wide, spread):
    copy = jnp.where(iota((128, 128), 0) == iota((128, 128), 1) // 2, 1.0, 0.0)
    value = dot_exact(e_two[...].reshape(192, 128), copy)
    for block in range(24):
        rows = value[8 * block : 8 * block + 4, :]
        wide[pl.ds(8 * block, 4, stride=2), :] = rows
        wide[pl.ds(8 * block + 1, 4, stride=2), :] = rows
    value = e_one[...].reshape(24, 2, 8, 128) + wide[...].reshape(24, 1, 8, 128)
    value = dot_exact(value.reshape(384, 128), copy)
    flat = spread.reshape(768, 128)
    for block in range(48):
        rows = value[8 * block : 8 * block + 8, :]
        flat[pl.ds(16 * block, 8, stride=2), :] = rows
        flat[pl.ds(16 * block + 1, 8, stride=2), :] = rows
    lane = iota((16, 128), 1)

    def pair(k):
        for f in range(3):
            for z in (2 * k, 2 * k + 1):
                value = rim[f, z]
                for half in range(2):
                    low = roll(value, -57 - 64 * half)
                    high = roll(value, 121 - 64 * half)
                    at = z + 16 * half
                    own = jnp.concatenate([two[f, at + 1, 16:24, :], two[f, at + 1, 0:8, :]], axis=0)
                    own = jnp.where(lane < 3, low, jnp.where(lane >= 125, high, own))
                    base[f, at] = own + spread[f, k + 8 * half]

    loop(8, pair, 4)


def resist(share):
    return recip(2.0 - 1.8 * share)


def level_weights(own, six, omega):
    faces = [recip(own + other) for other in six]
    diag = (faces[0] + faces[1]) + (faces[2] + faces[3]) + (faces[4] + faces[5])
    gain = omega * recip(diag)
    return gain, [gain * w for w in faces], diag


def middle_kernel(
    main, main_near, main_far, rim, rim_near, rim_far, sent, e_one, e_two,
    share, rest, rhs, first, second, weights, diags, halves, pooled,
    rest2, first2, second2, rhs2, share2, weights2,
):
    gx, gy = lax.axis_index("gx"), lax.axis_index("gy")
    low_x, high_x = jnp.where(gx > 0, 1, 0), jnp.where(gx < NX - 1, 1, 0)
    low_y, high_y = jnp.where(gy > 0, 1, 0), jnp.where(gy < NY - 1, 1, 0)

    for f in range(3):
        for ref in (first, second):
            ref[f, 0] = jnp.zeros((32, 128), F32)
            ref[f, 17] = jnp.zeros((32, 128), F32)
    for z in (0, 17):
        rest[z] = jnp.full((32, 128), 0.5, F32)
    lane = iota((8, 128), 1)
    even = lax.rem(gx, 2) == 0
    near_row, far_row = jnp.where(even, 16, 0), jnp.where(even, 0, 16)
    starts = (pl.multiple_of(near_row, 8), pl.multiple_of(far_row, 8), 8)

    sources = zip(starts, ((main_near, rim_near), (main_far, rim_far), (main, rim)))
    sources = list(sources)
    has_far = inner(gx)

    def fill(q):
        for odd in range(2):
            for half in range(2):
                z = 2 * q + odd + 8 * half
                base = 64 * odd + 32 * half
                for at, (middle, outer) in sources:
                    for ch in range(4):
                        edge, body = outer[ch, q], middle[ch, 2 * q + odd]
                        if outer is rim_far:
                            edge, body = jnp.where(has_far, edge, 0.0), jnp.where(has_far, body, 0.0)
                        value = jnp.where(lane < 62, roll(body, 64 * half), roll(edge, 62 - base))
                        value = jnp.where((lane >= 96) | (lane < 2), roll(edge, 112 - base), value)
                        if ch < 3:
                            rhs[ch, z, pl.ds(at, 8), :] = value
                        else:
                            share[z, pl.ds(at, 8), :] = value
                            rest[z + 1, pl.ds(at, 8), :] = resist(value)
                rest[z + 1, 24:32, :] = jnp.full((8, 128), 0.5, F32)

    loop(4, fill, 2)

    row, lane = iota((24, 128), 0) + 1, iota((24, 128), 1)
    in_x = jnp.where(row < 8, low_x, jnp.where(row >= 16, high_x, 1))
    in_y = jnp.where(lane < 64, 1, jnp.where(lane < 96, high_y, low_y))
    omega = 0.8 * (in_x * in_y).astype(F32)

    def start(step):
        z = STEP * step
        for k, (own, six) in enumerate(block_of(rest, (), z + 1, STEP, 1, 24)):
            gain, w, diag = level_weights(own, six, omega)
            for i in range(6):
                weights[i, z + k, 1:25, :] = w[i]
            diags[z + k, 1:25, :] = (1.25 * 0.25) * diag
            for f in range(3):
                first[f, z + k + 1, 1:25, :] = (4.0 * gain) * rhs[f, z + k, 1:25, :]

    loop(16 // STEP, start)

    def sweep(step):
        z = STEP * step
        w = [[weights[i, z + k, 3:27, :] for i in range(6)] for k in range(STEP)]
        for f in range(3):
            for k, (own, six) in enumerate(block_of(first, (f,), z + 1, STEP, 3, 24)):
                second[f, z + k + 1, 3:27, :] = 1.2 * own + weigh(w[k], six)

    loop(16 // STEP, sweep)

    def left(step):
        z = STEP * step
        w = [[weights[i, z + k, 4:20, :] for i in range(6)] for k in range(STEP)]
        diag = [diags[z + k, 4:20, :] for k in range(STEP)]
        for f in range(3):
            values = []
            for k, (own, six) in enumerate(block_of(second, (f,), z + 1, STEP, 4, 16)):
                change = (first[f, z + k + 1, 4:20, :] - 0.8 * own) + weigh(w[k], six)
                values.append(change * diag[k])
                e_one[f, z + k] = second[f, z + k + 1, 8:16, :]
            for k in range(STEP // 2):
                halves[f, STEP // 2 * step + k, 0:16, :] = values[2 * k] + values[2 * k + 1]
                halves[f, STEP // 2 * step + k, 16:24, :] = jnp.zeros((8, 128), F32)
        for k in range(STEP // 2):
            halves[3, STEP // 2 * step + k] = share[z + 2 * k] + share[z + 2 * k + 1]

    loop(16 // STEP, left)

    source, target = iota((128, 128), 0), iota((128, 128), 1)
    pool = jnp.where(source // 2 + jnp.where(source >= 96, 64, 0) == target, 0.125, 0.0)
    pooled[...] = dot_exact(halves[...].reshape(4 * 8 * 24, 128), pool)
    for z in (0, 9):
        rest2[z] = jnp.full((24, 128), 0.5, F32)
        for f in range(3):
            first2[f, z] = jnp.zeros((24, 128), F32)
            second2[f, z] = jnp.zeros((24, 128), F32)
    for z in range(8):
        for f in range(3):
            base = (f * 8 + z) * 24
            rhs2[f, z] = pooled[pl.ds(base, 8, stride=2), :] + pooled[pl.ds(base + 1, 8, stride=2), :]
        base = (3 * 8 + z) * 24
        value = pooled[pl.ds(base + 2, 8, stride=2), :] + pooled[pl.ds(base + 3, 8, stride=2), :]
        rest2[z + 1, 0:8, :] = resist(value)
        value = pooled[pl.ds(base + 8, 8, stride=2), :] + pooled[pl.ds(base + 9, 8, stride=2), :]
        rest2[z + 1, 3:11, :] = resist(value)
        share2[z] = value

    row, lane = iota((8, 128), 0) + 1, iota((8, 128), 1)
    in_x = jnp.where(row < 3, low_x, jnp.where(row >= 7, high_x, 1))
    in_y = jnp.where(lane < 32, 1, jnp.where(lane < 96, high_y, low_y))
    omega2 = 0.8 * (in_x * in_y).astype(F32)

    for z, (own, six) in enumerate(block_of(rest2, (), 1, 8, 1, 8)):
        gain, w, diag = level_weights(own, six, omega2)
        for i in range(6):
            weights2[i, z, 1:9, :] = w[i]
        weights2[6, z, 1:9, :] = (1.25 * 0.0625) * diag
        for f in range(3):
            first2[f, z + 1, 1:9, :] = (16.0 * gain) * rhs2[f, z]
    w = [[weights2[i, z, 2:10, :] for i in range(6)] for z in range(8)]
    for f in range(3):
        for z, (own, six) in enumerate(block_of(first2, (f,), 1, 8, 2, 8)):
            second2[f, z + 1, 2:10, :] = 1.2 * own + weigh(w[z], six)
    w = [[weights2[i, z, 3:11, :] for i in range(7)] for z in range(8)]
    own_row = iota((8, 128), 0) < 4
    parts = [{} for pair in range(4)]
    for f in range(3):
        for z, (own, six) in enumerate(block_of(second2, (f,), 1, 8, 3, 8)):
            e_two[f, z] = own
            change = (first2[f, z + 1, 3:11, :] - 0.8 * own) + weigh(w[z], six)
            value = jnp.where(own_row, change * w[z][6], 0.0)
            sums = parts[z // 2]
            sums[f] = value if z % 2 == 0 else sums[f] + value
    for z in range(8):
        value = jnp.where(own_row, share2[z], 0.0)
        sums = parts[z // 2]
        sums[3] = value if z % 2 == 0 else sums[3] + value

    pool = jnp.where((source < 32) & (source // 2 == target % 16), 0.125, 0.0)
    rows = jnp.concatenate([parts[pair][ch] for ch in range(4) for pair in range(4)], axis=0)
    spread = dot_exact(rows, pool)
    at, to = iota((32, 128), 0), iota((32, 128), 1)
    keep = (at // 8 == to // 32) & ((at % 8) // 2 == (to // 16) % 2)
    result = jnp.concatenate(
        [
            jnp.sum(jnp.where(keep, spread[32 * ch : 32 * ch + 32], 0.0), axis=0, keepdims=True)
            for ch in range(4)
        ],
        axis=0,
    )
    for copy in range(CHIPS):
        sent[copy] = result


def swap_blocks(x):
    sub, group = iota((8, 128), 0), iota((8, 128), 1) // 16
    for bit in (4, 2, 1):
        up = roll(roll(x, -bit, 0), 16 * bit)
        down = up if bit == 4 else roll(roll(x, bit, 0), -16 * bit)
        sub_set, group_set = (sub & bit) != 0, (group & bit) != 0
        x = jnp.where(sub_set == group_set, x, jnp.where(sub_set, down, up))
    return x


def lay_kernel(mine, laid):
    def lay(g):
        for ch in range(4):
            tile = swap_blocks(mine[pl.ds(32 * g + ch, 8, stride=4), :])
            laid[ch, pl.ds(pl.multiple_of(8 * g, 8), 8), :] = tile

    loop(16, lay, 4)


def top_kernel(
    mine, other, base, out,
    natural, first, second, four, weights, diags, lefts, final, sems,
):
    gx, gy = lax.axis_index("gx"), lax.axis_index("gy")
    first_core = lax.rem(gy, 2) == 0
    lane, sub = iota((16, 128), 1), iota((16, 128), 0)
    cells = [(z, x, half) for z in range(4) for x in range(2) for half in range(2)]

    parity = lax.rem(gy, 2)

    def lay(g):
        for ch in range(4):
            at = pl.ds(pl.multiple_of(8 * g, 8), 8)
            natural[ch, parity, at, :] = mine[ch, at, :]
            natural[ch, 1 - parity, at, :] = swap_blocks(other[pl.ds(32 * g + ch, 8, stride=4), :])

    loop(16, lay, 4)
    flat = natural.reshape(1024, 128)

    def plane(ch, z, x, half):
        return flat[pl.ds((ch * 2 + half) * 128 + z * 2 + x, 16, stride=8), :]

    def neighbours(at, z, x, half, outside):
        own, other = at(z, x, half), at(z, 1 - x, half)
        beside = at(z, x, 1 - half)
        shifted = roll(other, 1 if x == 0 else -1, 0)
        low, high = (shifted, other) if x == 0 else (other, shifted)
        left, right = roll(own, 1), roll(own, -1)
        left = jnp.where(lane % 16 == 0, roll(beside, 1 if half == 0 else -15), left)
        right = jnp.where(lane % 16 == 15, roll(beside, 15 if half == 0 else -1), right)
        down = at(z - 1, x, half) if z > 0 else outside
        up = at(z + 1, x, half) if z < 3 else outside
        return own, [low, high, left, right, down, up]

    def edge_masks(x, half):
        return [
            sub > 0 if x == 0 else None,
            sub < 15 if x == 1 else None,
            lane > 0 if half == 0 else None,
            lane < 127 if half == 1 else None,
            None,
            None,
        ]

    def key(z, x, half):
        return (z * 2 + x) * 2 + half

    shares = {c: plane(3, *c) for c in cells}
    rests = {c: resist(shares[c]) for c in cells}
    outside, zeros = jnp.full((16, 128), 0.5, F32), jnp.zeros((16, 128), F32)
    for z, x, half in cells:
        own, six = neighbours(lambda *c: rests[c], z, x, half, outside)
        masks = edge_masks(x, half)
        six = [s if m is None else jnp.where(m, s, 0.5) for s, m in zip(six, masks)]
        gain, w, diag = level_weights(own, six, 0.8)
        at = key(z, x, half)
        for i in range(6):
            weights[i, at] = w[i] if masks[i] is None else jnp.where(masks[i], w[i], 0.0)
        diags[at] = (1.25 * 0.25**3) * diag
        for f in range(3):
            first[f, at] = (64.0 * gain) * plane(f, z, x, half)

    for z, x, half in cells:
        at = key(z, x, half)
        w = [weights[i, at] for i in range(6)]
        for f in range(3):
            own, six = neighbours(lambda *c: first[f, key(*c)], z, x, half, zeros)
            second[half, f, z * 2 + x] = 1.2 * own + weigh(w, six)

    for z4 in range(2):
        for half in range(2):
            sums = [None] * 4
            for z in (2 * z4, 2 * z4 + 1):
                for x in range(2):
                    at = key(z, x, half)
                    w = [weights[i, at] for i in range(6)]
                    diag = diags[at]
                    for f in range(3):
                        own, six = neighbours(
                            lambda c, d, e: second[e, f, c * 2 + d], z, x, half, zeros
                        )
                        value = ((first[f, at] - 0.8 * own) + weigh(w, six)) * diag
                        sums[f] = value if sums[f] is None else sums[f] + value
                    share = shares[z, x, half]
                    sums[3] = share if sums[3] is None else sums[3] + share
            for ch in range(4):
                lefts[ch, z4, :, 128 * half : 128 * half + 128] = sums[ch]

    source = iota((256, 128), 0)
    column = ((source % 128) // 16) * 16 + (source // 128) * 8 + (source % 16) // 2
    pool = jnp.where(column == iota((256, 128), 1), 0.125, 0.0)
    level = dot_exact(lefts[...].reshape(128, 256), pool)

    def coarsest(ch, z):
        return level[(ch * 2 + z) * 16 : (ch * 2 + z) * 16 + 16, :]

    masks = [sub > 0, sub < 15, lane > 0, lane < 127]
    resists = [resist(coarsest(3, z)) for z in range(2)]
    gains, ws, ds = [], [], []
    for z in range(2):
        own, other = resists[z], resists[1 - z]
        six = [roll(own, 1, 0), roll(own, -1, 0), roll(own, 1), roll(own, -1)]
        six = [jnp.where(m, s, 0.5) for m, s in zip(masks, six)] + [other, outside]
        gain, w, diag = level_weights(own, six, 0.8)
        gains.append(gain)
        ds.append(diag)
        ws.append([jnp.where(m, v, 0.0) for m, v in zip(masks, w)] + [w[4]])
    whole = jnp.sum(ds[0] + ds[1], keepdims=True)

    def around(values, z):
        own, other = values[z], values[1 - z]
        return weigh(ws[z], (roll(own, 1, 0), roll(own, -1, 0), roll(own, 1), roll(own, -1), other))

    begin = [[256.0 * gains[z] * coarsest(f, z) for z in range(2)] for f in range(3)]
    values = begin
    for step in range(5):
        values = [
            [(0.2 * values[f][z] + begin[f][z]) + around(values[f], z) for z in range(2)] for f in range(3)
        ]
    shifts = []
    for f in range(3):
        change = [(begin[f][z] - 0.8 * values[f][z]) + around(values[f], z) for z in range(2)]
        shifts.append(jnp.sum(1.25 * (change[0] * ds[0] + change[1] * ds[1]), keepdims=True) / whole)
        for z in range(2):
            four[2 * f + z] = values[f][z]

    rows = four.reshape(96, 128)[pl.ds(gx, 6, stride=16), :]
    upper = jnp.concatenate([jnp.broadcast_to(rows[i : i + 1], (4, 128)) for i in range(6)], axis=0)
    flat = second.reshape(768, 128)
    halves = [flat[pl.ds(gx + 384 * half, 24, stride=16), :] for half in range(2)]
    three = turn(jnp.where(first_core, halves[0], halves[1]), -16 * lax.div(gy, 2))
    both = jnp.concatenate([turn(upper, -8 * gy), three], axis=1)
    both = jnp.concatenate([both, jnp.zeros((8, 256), F32)], axis=0)
    source, target = iota((256, 128), 0), iota((256, 128), 1)
    copy = jnp.where(source == jnp.where(source < 128, target // 16, 128 + target // 8), 1.0, 0.0)
    three = dot_exact(both, copy)

    copies = []
    for f in range(3):
        for z in range(4):
            for x in range(2):
                at = f * 8 + z * 2 + x
                value = jnp.broadcast_to(three[at : at + 1] + shifts[f], (8, 128))
                for k in range(8 * z, 8 * z + 8):
                    final[f, k, 8 * x : 8 * x + 8, :] = base[f, k, 8 * x : 8 * x + 8, :] + value
            if z % 2 == 1:
                part = (f, pl.ds(8 * z - 8, 16))
                copy = pltpu.make_async_copy(final.at[part], out.at[part], sems.at[len(copies)])
                copy.start()
                copies.append(copy)
    for copy in copies:
        copy.wait()


def local(labels, guess):
    swap_near = [(i, i ^ 1) for i in range(NY)]
    far_x, far_y = [], []
    for x in range(NX):
        for y in range(NY):
            across_x, across_y = x + 1 if x % 2 else x - 1, y + 1 if y % 2 else y - 1
            to = (across_x, y) if 0 <= across_x < NX else (x, y ^ 1)
            far_x.append((x * NY + y, to[0] * NY + to[1]))
            to = (x, across_y) if 0 <= across_y < NY else (x ^ 1, y)
            far_y.append((x * NY + y, to[0] * NY + to[1]))
    both = ("gx", "gy")
    to_near, to_far, own = call(
        rows_kernel,
        [(12, 32, 128)] * 2 + [(4, 32, 16, 128)],
        [pltpu.VMEM((32, 16, 128), jnp.int32), pltpu.SemaphoreType.DMA((4,))],
        in_specs=[ANY, ANY],
    )(pltpu.with_memory_space_constraint(guess, pltpu.HBM), pltpu.with_memory_space_constraint(labels, pltpu.HBM))
    from_near = lax.ppermute(to_near, "gx", swap_near)
    from_far = lax.ppermute(to_far, both, far_x)
    own_one, own_two, halves, to_right, to_left, edges = call(
        own_kernel,
        [(3, 34, 32, 128)] * 2 + [(4, 16, 16, 128)] + [(4, 4, 16, 128)] * 2 + [(4, 16, 16, 128)],
        [(4, 34, 32, 128), (6, 32, 32, 128), (32, 32, 128)],
        flops=20_000_000,
    )(own)
    to_near, to_far, rim_rows = call(pack_kernel, [(4, 4, 24, 128)] * 2 + [(4, 32, 8, 128)], [])(
        to_right, to_left, from_near, from_far
    )
    from_far = lax.ppermute(to_far, both, far_y)
    from_near = lax.ppermute(to_near, "gy", swap_near)
    two, main, edges_rim = call(
        rows_edge_kernel,
        [(3, 34, 24, 128), (4, 8, 8, 128), (4, 16, 8, 128)],
        [(4, 34, 24, 128), (3, 34, 24, 128), (6, 32, 24, 128), (32, 24, 128)]
        + [(4, 16, 16, 128), (512, 128)],
        flops=10_000_000,
    )(own, rim_rows, own_one, own_two, halves)
    main_near = lax.ppermute(main, "gx", swap_near)
    main_far = lax.ppermute(main, both, far_x)
    rim, rim_one = call(
        rim_kernel,
        [(3, 16, 16, 128), (4, 4, 8, 128)],
        [(3, 18, 32, 128), (18, 32, 128)]
        + [(3, 18, 32, 128)] * 2
        + [(6, 16, 32, 128), (16, 32, 128)]
        + [(4, 8, 16, 128), (256, 128)],
        flops=10_000_000,
    )(edges, edges_rim, from_near, from_far)
    rim_near = lax.ppermute(rim_one, "gx", swap_near)
    rim_far = lax.ppermute(rim_one, both, far_x)
    sent, e_one, e_two = call(
        middle_kernel,
        [(CHIPS, 4, 128), (3, 16, 8, 128), (3, 8, 8, 128)],
        [(16, 24, 128), (18, 32, 128), (3, 16, 32, 128), (3, 18, 32, 128), (3, 18, 32, 128)]
        + [(6, 16, 32, 128), (16, 32, 128), (4, 8, 24, 128), (768, 128)]
        + [(10, 24, 128), (3, 10, 24, 128), (3, 10, 24, 128), (3, 8, 8, 128), (8, 8, 128)]
        + [(7, 8, 16, 128)],
    )(main, main_near, main_far, rim_one, rim_near, rim_far)
    groups = [[i for i in range(NX * NY) if i % 2 == core] for core in range(2)]
    mine = lax.all_to_all(
        sent, ("gx", "gy"), split_axis=0, concat_axis=0, axis_index_groups=groups, tiled=True
    )
    (base,) = call(base_kernel, [(3, 32, 16, 128)], [(192, 128), (3, 16, 16, 128)])(two, rim, e_one, e_two)
    other = lax.ppermute(mine, "gy", swap_near)
    (laid,) = call(lay_kernel, [(4, 128, 128)], [])(mine.reshape(512, 128))
    (out,) = call(
        top_kernel,
        [(3, 32, 16, 128)],
        [(4, 2, 128, 128), (3, 16, 16, 128), (2, 3, 8, 16, 128), (6, 16, 128), (6, 16, 16, 128)]
        + [(16, 16, 128), (4, 2, 16, 256), (3, 32, 16, 128), pltpu.SemaphoreType.DMA((6,))],
        out_specs=[ANY],
    )(laid, other.reshape(512, 128), base)
    return out


def solution(mesh):
    return jax.shard_map(
        local,
        mesh=mesh,
        in_specs=(P(None, "gx", "gy"), P(None, None, "gx", "gy")),
        out_specs=P(None, None, "gx", "gy"),
        check_vma=False,
    )
```

```python
import jax
import jax.numpy as jnp
from jax import lax
from jax.experimental import pallas as pl
from jax.experimental.pallas import tpu as pltpu
from jax.sharding import PartitionSpec as P


F32 = jnp.float32
NX, NY, CHIPS = 16, 16, 128
STEP, WIDE = 16, 32
BETWEEN = 2.0 * 0.1 / 1.1
ANY = pl.BlockSpec(memory_space=pltpu.HBM)


def dot_exact(a, b):
    high = a.astype(jnp.bfloat16)
    low = (a - high.astype(F32)).astype(jnp.bfloat16)
    b = b.astype(jnp.bfloat16)
    return jnp.dot(
        jnp.concatenate([high, low], axis=1), jnp.concatenate([b, b], axis=0), preferred_element_type=F32
    )


def iota(shape, dim):
    return lax.broadcasted_iota(jnp.int32, shape, dim)


def roll(x, shift, axis=1):
    shift = shift % x.shape[axis]
    return x if shift == 0 else pltpu.roll(x, shift, axis)


def turn(x, shift):
    return pltpu.roll(x, lax.rem(shift + 256, 128), 1)


def recip(x):
    guess = pl.reciprocal(x, approx=True)
    return guess * (2.0 - x * guess)


def inner(index):
    return (index > 0) & (index < 15)


def call(kernel, outs, scratch, flops=1_000_000, **kw):
    return pl.pallas_call(
        kernel,
        out_shape=[jax.ShapeDtypeStruct(s, F32) for s in outs],
        scratch_shapes=[pltpu.VMEM(s, F32) if isinstance(s, tuple) else s for s in scratch],
        compiler_params=pltpu.CompilerParams(vmem_limit_bytes=32 * 1024 * 1024),
        cost_estimate=pl.CostEstimate(flops=flops, bytes_accessed=4_000_000, transcendentals=0),
        **kw,
    )


def loop(count, body, unroll=1):
    def step(i, carry):
        body(i)
        return carry

    lax.fori_loop(0, count, step, 0, unroll=unroll)


def weigh(weights, values):
    parts = [w * v for w, v in zip(weights, values)]
    while len(parts) > 1:
        parts = [sum(parts[i : i + 2][1:], parts[i]) for i in range(0, len(parts), 2)]
    return parts[0]


def rows_kernel(guess, labels, near, far, own, phase, sems):
    even = lax.rem(lax.axis_index("gx"), 2) == 0
    near_row, far_row = jnp.where(even, 13, 0), jnp.where(even, 0, 13)
    copies = {}
    for ch in (3, 0, 1, 2):
        source, target = (labels, phase) if ch == 3 else (guess.at[ch], own.at[ch])
        for part in range(4):
            at = pl.ds(8 * part, 8)
            copies[ch, part] = pltpu.make_async_copy(source.at[at], target.at[at], sems.at[4 * ch + part])
            copies[ch, part].start()
    flat = own.reshape(4 * 32 * 16, 128)
    for ch in (3, 0, 1, 2):
        for part in range(4):
            copies[ch, part].wait()
        if ch == 3:
            own[3] = jnp.where(phase[...] == 1, 0.0, 1.0).astype(F32)
        for row in range(3):
            near[3 * ch + row] = flat[pl.ds(512 * ch + near_row + row, 32, stride=16), :]
            far[3 * ch + row] = flat[pl.ds(512 * ch + far_row + row, 32, stride=16), :]


def pack_kernel(to_right, to_left, x_near, x_far, near, far, rim):
    first_core = lax.rem(lax.axis_index("gy"), 2) == 0
    even = lax.rem(lax.axis_index("gx"), 2) == 0
    near_row, far_row = jnp.where(even, 0, 5), jnp.where(even, 5, 0)
    has_far = inner(lax.axis_index("gx"))
    flat = rim.reshape(4 * 32 * 8, 128)
    for ch in range(4):
        for row in range(3):
            flat[pl.ds(256 * ch + near_row + row, 32, stride=8), :] = x_near[3 * ch + row]
            flat[pl.ds(256 * ch + far_row + row, 32, stride=8), :] = jnp.where(has_far, x_far[3 * ch + row], 0.0)

    def some(low):
        for ch in range(4):
            right, left = pack_planes(lambda z: rim[ch, z], low, (8, 128))
            for at, right, left in (
                (slice(0, 16), to_right[ch, low], to_left[ch, low]),
                (slice(16, 24), right, left),
            ):
                near[ch, low, at, :] = jnp.where(first_core, right, left)
                far[ch, low, at, :] = jnp.where(first_core, left, right)

    loop(4, some, 4)


def pack_planes(plane, low, shape):
    group = iota(shape, 1) // 16
    right = left = jnp.zeros(shape, F32)
    for h in range(8):
        moved = roll(plane(4 * h + low), 16 * h + 16)
        right = jnp.where(group == h, moved, right)
        left = jnp.where(group == (h + 1) % 8, moved, left)
    return right, left


def edge_columns(plane, z, shape):
    lane = iota(shape, 1)
    value = jnp.zeros(shape, F32)
    for half in range(2):
        source = plane(z + 16 * half)
        base = 64 * half
        value = jnp.where((lane >= base) & (lane < base + 7), roll(source, base + 7), value)
        value = jnp.where((lane >= base + 57) & (lane < base + 64), roll(source, base + 57), value)
    return value


def six_of(ref, lead, z, first, count):
    own = ref[(*lead, z, pl.ds(first, count), slice(None))]
    return own, (
        ref[(*lead, z, pl.ds(first - 1, count), slice(None))],
        ref[(*lead, z, pl.ds(first + 1, count), slice(None))],
        roll(own, 1),
        roll(own, -1),
        ref[(*lead, z - 1, pl.ds(first, count), slice(None))],
        ref[(*lead, z + 1, pl.ds(first, count), slice(None))],
    )


def block_of(ref, lead, z, planes, first, count):
    rows = pl.ds(first, count)
    own = [ref[(*lead, z + k, rows, slice(None))] for k in range(-1, planes + 1)]
    result = []
    for k in range(planes):
        value = own[k + 1]
        six = (
            ref[(*lead, z + k, pl.ds(first - 1, count), slice(None))],
            ref[(*lead, z + k, pl.ds(first + 1, count), slice(None))],
            roll(value, 1),
            roll(value, -1),
            own[k],
            own[k + 2],
        )
        result.append((value, six))
    return result


def fine_weights(own, six, omega):
    base, slope = 1.0 + (BETWEEN - 1.0) * own, (BETWEEN - 1.0) + (1.1 - 2.0 * BETWEEN) * own
    total = (six[0] + six[1]) + (six[2] + six[3]) + (six[4] + six[5])
    diag = 6.0 * base + slope * total
    gain = omega * recip(diag)
    base, slope = gain * base, gain * slope
    return [base + slope * other for other in six], 1.25 * diag


def fine_sweep(w, f, own, six):
    return (0.2 * own + (w[2 * f + 1] - w[2 * f])) + weigh(w, six)


def fine_left(w, f, own, six, diag):
    return (((w[2 * f + 1] - w[2 * f]) - 0.8 * own) + weigh(w, six)) * diag


def fine_sweeps(planes, windows, start, share, one, two, weights, diags, halves, omega, wrap, keep, size):
    first, count = windows[0]

    def first_sweep(step):
        z = size * step
        w = []
        for k, (own, six) in enumerate(block_of(share, (), z + 1, size, first, count)):
            now, diag = fine_weights(own, six, omega)
            diags[z + k, pl.ds(first, count), :] = diag
            for i in range(6):
                weights[i, z + k, pl.ds(first, count), :] = now[i]
            w.append(now)
        for f in range(3):
            for k, (own, six) in enumerate(block_of(start, (f,), z + 1, size, first, count)):
                one[f, z + k + 1, pl.ds(first, count), :] = fine_sweep(w[k], f, own, six)

    loop(planes // size, first_sweep)
    wrap(one)
    second, count2 = windows[1]

    def second_sweep(step):
        z = size * step
        w = [[weights[i, z + k, pl.ds(second, count2), :] for i in range(6)] for k in range(size)]
        for f in range(3):
            for k, (own, six) in enumerate(block_of(one, (f,), z + 1, size, second, count2)):
                two[f, z + k + 1, pl.ds(second, count2), :] = fine_sweep(w[k], f, own, six)

    loop(planes // size, second_sweep)
    wrap(two)

    def residual(step):
        z = size * step
        w = [[weights[i, z + k, 8:24, :] for i in range(6)] for k in range(size)]
        diag = [diags[z + k, 8:24, :] for k in range(size)]
        for f in range(3):
            values = []
            for k, (own, six) in enumerate(block_of(two, (f,), z + 1, size, 8, 16)):
                if keep is not None:
                    keep[f, z + k] = own
                values.append(fine_left(w[k], f, own, six, diag[k]))
            for pair in range(size // 2):
                halves[f, size // 2 * step + pair] = values[2 * pair] + values[2 * pair + 1]
        for pair in range(size // 2):
            at = z + 2 * pair + 1
            halves[3, size // 2 * step + pair] = share[at, 8:24, :] + share[at + 1, 8:24, :]

    loop(planes // size, residual)


def own_kernel(own, one, two, halves, to_right, to_left, edges, held, weights, diags):
    zero = jnp.zeros((32, 128), F32)
    for z in (0, 33):
        for ch in range(4):
            held[ch, z] = zero
        for ref in (one, two):
            for f in range(3):
                ref[f, z] = zero

    def plane(z):
        for ch in range(4):
            held[ch, z + 1, 8:24, :] = own[ch, z]

    loop(32, plane, 8)
    fine_sweeps(
        32, [(8, 16)] * 2, held, held.at[3], one, two, weights, diags, halves, 0.8, lambda ref: None, None, 8
    )

    def some(low):
        for ch in range(4):
            to_right[ch, low], to_left[ch, low] = pack_planes(lambda z: own[ch, z], low, (16, 128))

    loop(4, some, 2)

    def edge(z):
        for ch in range(4):
            edges[ch, z] = edge_columns(lambda at: own[ch, at], z, (16, 128))

    loop(16, edge, 8)


def rows_edge_kernel(own, rim, own_one, own_two, own_halves, two, packed, edges, start, one, weights, diags, halves, pooled):
    gx = lax.axis_index("gx")
    zero = jnp.zeros((24, 128), F32)
    for z in (0, 33):
        for ch in range(4):
            start[ch, z] = zero
        for ref in (one, two):
            for f in range(3):
                ref[f, z] = zero

    def fill(z):
        for ch in range(4):
            start[ch, z + 1, 0:8, :] = own[ch, z, 8:16, :]
            start[ch, z + 1, 8:16, :] = rim[ch, z]
            start[ch, z + 1, 16:24, :] = own[ch, z, 0:8, :]
        for f in range(3):
            for ref, source in ((one, own_one), (two, own_two)):
                ref[f, z + 1, 0:8, :] = source[f, z + 1, 16:24, :]
                ref[f, z + 1, 16:24, :] = source[f, z + 1, 8:16, :]

    loop(32, fill, 8)
    upper = iota((8, 128), 0) < 4

    def both(ref, lead, step, shift=0):
        high = ref[(*lead, pl.ds(8 - step + shift, 8), slice(None))]
        low = ref[(*lead, pl.ds(8 + step + shift, 8), slice(None))]
        return jnp.where(upper, high, low)

    def block_both(ref, f, z, step):
        own = [both(ref, (f, z + k), step) for k in range(-1, WIDE + 1)]
        result = []
        for k in range(WIDE):
            value = own[k + 1]
            low, high = both(ref, (f, z + k), step, -1), both(ref, (f, z + k), step, 1)
            result.append((value, (low, high, roll(value, 1), roll(value, -1), own[k], own[k + 2])))
        return result

    def put(ref, f, z, step, value):
        ref[f, z, pl.ds(8 - step, 4), :] = value[0:4]
        ref[f, z, pl.ds(12 + step, 4), :] = value[4:8]

    row = iota((16, 128), 0) + 5
    low, high = jnp.where(gx > 0, 1, 0), jnp.where(gx < NX - 1, 1, 0)
    inside = jnp.where((row >= 8) & (row < 12), high, jnp.where((row >= 12) & (row < 16), low, 1))
    omega = 0.8 * inside.astype(F32)

    def weigh_all(step):
        z = WIDE * step
        for k, (value, six) in enumerate(block_of(start, (3,), z + 1, WIDE, 5, 16)):
            w, diag = fine_weights(value, six, omega)
            diags[z + k, 5:21, :] = diag
            for i in range(6):
                weights[i, z + k, 5:21, :] = w[i]

    loop(32 // WIDE, weigh_all)

    for step, source, target in ((1, start, one), (2, one, two)):

        def sweep(block):
            z = WIDE * block
            w = [[both(weights, (i, z + k), step) for i in range(6)] for k in range(WIDE)]
            for f in range(3):
                for k, (value, six) in enumerate(block_both(source, f, z + 1, step)):
                    put(target, f, z + k + 1, step, fine_sweep(w[k], f, value, six))

        loop(32 // WIDE, sweep)

    sub = iota((8, 128), 0)

    def residual(block):
        z = WIDE * block
        w = [[both(weights, (i, z + k), 3) for i in range(6)] for k in range(WIDE)]
        diag = [both(diags, (z + k,), 3) for k in range(WIDE)]
        for f in range(3):
            values = []
            for k, (value, six) in enumerate(block_both(two, f, z + 1, 3)):
                values.append(fine_left(w[k], f, value, six, diag[k]))
            for k in range(WIDE // 2):
                pair = WIDE // 2 * block + k
                value = values[2 * k] + values[2 * k + 1]
                halves[f, pair, 0:8, :] = jnp.where(sub < 3, roll(value, 3, 0), own_halves[f, pair, 0:8, :])
                halves[f, pair, 8:16, :] = jnp.where(sub >= 5, roll(value, 5, 0), own_halves[f, pair, 8:16, :])
        for k in range(WIDE // 2):
            halves[3, WIDE // 2 * block + k] = own_halves[3, WIDE // 2 * block + k]

    loop(32 // WIDE, residual)
    source, target = iota((128, 128), 0), iota((128, 128), 1)
    value = None
    for half in range(2):
        pool = jnp.where(source // 2 + 64 * half == target, 0.125, 0.0)
        part = dot_exact(halves[:, 8 * half : 8 * half + 8].reshape(512, 128), pool)
        value = part if value is None else value + part
    pooled[...] = value
    packed[...] = (pooled[pl.ds(0, 256, stride=2), :] + pooled[pl.ds(1, 256, stride=2), :]).reshape(4, 8, 8, 128)

    def edge(z):
        for ch in range(4):
            edges[ch, z] = edge_columns(lambda at: rim[ch, at], z, (8, 128))

    loop(16, edge, 8)


def rim_kernel(
    edges, edges_rim, near, far, field, packed,
    start, share, one, two, weights, diags, halves, pooled,
):
    gx, gy = lax.axis_index("gx"), lax.axis_index("gy")
    lane = iota((24, 128), 1)
    part = lane % 64
    is_after = (part >= 7) & (part < 22)
    is_before = (part >= 42) & (part < 57)
    first_core = lax.rem(gy, 2) == 0

    def unpack(low):
        for ch in range(4):
            target = start.at[ch] if ch < 3 else share
            from_near, from_far = near[ch, low], jnp.where(inner(gy), far[ch, low], 0.0)
            from_right = jnp.where(first_core, from_near, from_far)
            from_left = jnp.where(first_core, from_far, from_near)
            for h in range(4):
                z = 4 * h + low
                after_y = roll(from_right, 7 - 16 * (h + 1))
                before_y = roll(from_left, 41 - 16 * h)
                own = jnp.concatenate([edges[ch, z], edges_rim[ch, z]], axis=0)
                value = jnp.where(is_after, after_y, jnp.where(is_before, before_y, own))
                target[z + 1, 8:24, :] = value[0:16]
                target[z + 1, 0:8, :] = value[16:24]
                target[z + 1, 24:32, :] = value[16:24]

    loop(4, unpack, 2)

    half_of = iota((32, 128), 1)

    def wrap_one(ref):
        ref[0] = jnp.where(half_of >= 64, roll(ref[16], 64), 0.0)
        ref[17] = jnp.where(half_of < 64, roll(ref[1], 64), 0.0)

    def wrap(ref):
        for f in range(3):
            wrap_one(ref.at[f])

    wrap_one(share)
    wrap(start)
    row = iota((24, 128), 0) + 6
    low, high = jnp.where(gx > 0, 1, 0), jnp.where(gx < NX - 1, 1, 0)
    inside_x = jnp.where(row < 8, low, jnp.where(row >= 24, high, 1))
    inside_y = jnp.where(
        part < 32,
        jnp.where((part < 7) | (gy < NY - 1), 1, 0),
        jnp.where((part >= 57) | (gy > 0), 1, 0),
    )
    omega = 0.8 * (inside_x * inside_y).astype(F32)
    fine_sweeps(
        16, [(6, 24), (7, 24)], start, share, one, two, weights, diags, halves, omega, wrap, field, STEP
    )

    source, target = iota((128, 128), 0), iota((128, 128), 1)
    spot = source % 64
    column = jnp.where(spot < 32, 121 + spot, 71 + spot) // 2
    to = jnp.where(spot < 32, column - 62, column - 48)
    keep = ((spot < 32) & (to >= 0) & (to < 9)) | ((spot >= 32) & (to >= 9) & (to < 18))
    mixed = halves[...].reshape(4, 4, 2, 16, 128)
    value = None
    for odd in range(2):
        pool = jnp.where(keep & (to + 64 * odd + 32 * (source // 64) == target), 0.125, 0.0)
        part = dot_exact(mixed[:, :, odd].reshape(256, 128), pool)
        value = part if value is None else value + part
    pooled[...] = value
    packed[...] = (pooled[pl.ds(0, 128, stride=2), :] + pooled[pl.ds(1, 128, stride=2), :]).reshape(4, 4, 8, 128)


def base_kernel(two, rim, e_one, e_two, base, wide, spread):
    copy = jnp.where(iota((128, 128), 0) == iota((128, 128), 1) // 2, 1.0, 0.0)
    value = dot_exact(e_two[...].reshape(192, 128), copy)
    for block in range(24):
        rows = value[8 * block : 8 * block + 4, :]
        wide[pl.ds(8 * block, 4, stride=2), :] = rows
        wide[pl.ds(8 * block + 1, 4, stride=2), :] = rows
    value = e_one[...].reshape(24, 2, 8, 128) + wide[...].reshape(24, 1, 8, 128)
    value = dot_exact(value.reshape(384, 128), copy)
    flat = spread.reshape(768, 128)
    for block in range(48):
        rows = value[8 * block : 8 * block + 8, :]
        flat[pl.ds(16 * block, 8, stride=2), :] = rows
        flat[pl.ds(16 * block + 1, 8, stride=2), :] = rows
    lane = iota((16, 128), 1)

    def pair(k):
        for f in range(3):
            for z in (2 * k, 2 * k + 1):
                value = rim[f, z]
                for half in range(2):
                    low = roll(value, -57 - 64 * half)
                    high = roll(value, 121 - 64 * half)
                    at = z + 16 * half
                    own = jnp.concatenate([two[f, at + 1, 16:24, :], two[f, at + 1, 0:8, :]], axis=0)
                    own = jnp.where(lane < 3, low, jnp.where(lane >= 125, high, own))
                    base[f, at] = own + spread[f, k + 8 * half]

    loop(8, pair, 4)


def resist(share):
    return recip(2.0 - 1.8 * share)


def level_weights(own, six, omega):
    faces = [recip(own + other) for other in six]
    diag = (faces[0] + faces[1]) + (faces[2] + faces[3]) + (faces[4] + faces[5])
    gain = omega * recip(diag)
    return gain, [gain * w for w in faces], diag


def middle_kernel(
    main, main_near, main_far, rim, rim_near, rim_far, sent, e_one, e_two,
    share, rest, rhs, first, second, weights, diags, halves, pooled,
    rest2, first2, second2, rhs2, share2, weights2,
):
    gx, gy = lax.axis_index("gx"), lax.axis_index("gy")
    low_x, high_x = jnp.where(gx > 0, 1, 0), jnp.where(gx < NX - 1, 1, 0)
    low_y, high_y = jnp.where(gy > 0, 1, 0), jnp.where(gy < NY - 1, 1, 0)

    for f in range(3):
        for ref in (first, second):
            ref[f, 0] = jnp.zeros((32, 128), F32)
            ref[f, 17] = jnp.zeros((32, 128), F32)
    for z in (0, 17):
        rest[z] = jnp.full((32, 128), 0.5, F32)
    lane = iota((8, 128), 1)
    even = lax.rem(gx, 2) == 0
    near_row, far_row = jnp.where(even, 16, 0), jnp.where(even, 0, 16)
    starts = (pl.multiple_of(near_row, 8), pl.multiple_of(far_row, 8), 8)

    sources = zip(starts, ((main_near, rim_near), (main_far, rim_far), (main, rim)))
    sources = list(sources)
    has_far = inner(gx)

    def fill(q):
        for odd in range(2):
            for half in range(2):
                z = 2 * q + odd + 8 * half
                base = 64 * odd + 32 * half
                for at, (middle, outer) in sources:
                    for ch in range(4):
                        edge, body = outer[ch, q], middle[ch, 2 * q + odd]
                        if outer is rim_far:
                            edge, body = jnp.where(has_far, edge, 0.0), jnp.where(has_far, body, 0.0)
                        value = jnp.where(lane < 62, roll(body, 64 * half), roll(edge, 62 - base))
                        value = jnp.where((lane >= 96) | (lane < 2), roll(edge, 112 - base), value)
                        if ch < 3:
                            rhs[ch, z, pl.ds(at, 8), :] = value
                        else:
                            share[z, pl.ds(at, 8), :] = value
                            rest[z + 1, pl.ds(at, 8), :] = resist(value)
                rest[z + 1, 24:32, :] = jnp.full((8, 128), 0.5, F32)

    loop(4, fill, 2)

    row, lane = iota((24, 128), 0) + 1, iota((24, 128), 1)
    in_x = jnp.where(row < 8, low_x, jnp.where(row >= 16, high_x, 1))
    in_y = jnp.where(lane < 64, 1, jnp.where(lane < 96, high_y, low_y))
    omega = 0.8 * (in_x * in_y).astype(F32)

    def start(step):
        z = STEP * step
        for k, (own, six) in enumerate(block_of(rest, (), z + 1, STEP, 1, 24)):
            gain, w, diag = level_weights(own, six, omega)
            for i in range(6):
                weights[i, z + k, 1:25, :] = w[i]
            diags[z + k, 1:25, :] = (1.25 * 0.25) * diag
            for f in range(3):
                first[f, z + k + 1, 1:25, :] = (4.0 * gain) * rhs[f, z + k, 1:25, :]

    loop(16 // STEP, start)

    def sweep(step):
        z = STEP * step
        w = [[weights[i, z + k, 3:27, :] for i in range(6)] for k in range(STEP)]
        for f in range(3):
            for k, (own, six) in enumerate(block_of(first, (f,), z + 1, STEP, 3, 24)):
                second[f, z + k + 1, 3:27, :] = 1.2 * own + weigh(w[k], six)

    loop(16 // STEP, sweep)

    def left(step):
        z = STEP * step
        w = [[weights[i, z + k, 4:20, :] for i in range(6)] for k in range(STEP)]
        diag = [diags[z + k, 4:20, :] for k in range(STEP)]
        for f in range(3):
            values = []
            for k, (own, six) in enumerate(block_of(second, (f,), z + 1, STEP, 4, 16)):
                change = (first[f, z + k + 1, 4:20, :] - 0.8 * own) + weigh(w[k], six)
                values.append(change * diag[k])
                e_one[f, z + k] = second[f, z + k + 1, 8:16, :]
            for k in range(STEP // 2):
                halves[f, STEP // 2 * step + k, 0:16, :] = values[2 * k] + values[2 * k + 1]
                halves[f, STEP // 2 * step + k, 16:24, :] = jnp.zeros((8, 128), F32)
        for k in range(STEP // 2):
            halves[3, STEP // 2 * step + k] = share[z + 2 * k] + share[z + 2 * k + 1]

    loop(16 // STEP, left)

    source, target = iota((128, 128), 0), iota((128, 128), 1)
    pool = jnp.where(source // 2 + jnp.where(source >= 96, 64, 0) == target, 0.125, 0.0)
    pooled[...] = dot_exact(halves[...].reshape(4 * 8 * 24, 128), pool)
    for z in (0, 9):
        rest2[z] = jnp.full((24, 128), 0.5, F32)
        for f in range(3):
            first2[f, z] = jnp.zeros((24, 128), F32)
            second2[f, z] = jnp.zeros((24, 128), F32)
    for z in range(8):
        for f in range(3):
            base = (f * 8 + z) * 24
            rhs2[f, z] = pooled[pl.ds(base, 8, stride=2), :] + pooled[pl.ds(base + 1, 8, stride=2), :]
        base = (3 * 8 + z) * 24
        value = pooled[pl.ds(base + 2, 8, stride=2), :] + pooled[pl.ds(base + 3, 8, stride=2), :]
        rest2[z + 1, 0:8, :] = resist(value)
        value = pooled[pl.ds(base + 8, 8, stride=2), :] + pooled[pl.ds(base + 9, 8, stride=2), :]
        rest2[z + 1, 3:11, :] = resist(value)
        share2[z] = value

    row, lane = iota((8, 128), 0) + 1, iota((8, 128), 1)
    in_x = jnp.where(row < 3, low_x, jnp.where(row >= 7, high_x, 1))
    in_y = jnp.where(lane < 32, 1, jnp.where(lane < 96, high_y, low_y))
    omega2 = 0.8 * (in_x * in_y).astype(F32)

    for z, (own, six) in enumerate(block_of(rest2, (), 1, 8, 1, 8)):
        gain, w, diag = level_weights(own, six, omega2)
        for i in range(6):
            weights2[i, z, 1:9, :] = w[i]
        weights2[6, z, 1:9, :] = (1.25 * 0.0625) * diag
        for f in range(3):
            first2[f, z + 1, 1:9, :] = (16.0 * gain) * rhs2[f, z]
    w = [[weights2[i, z, 2:10, :] for i in range(6)] for z in range(8)]
    for f in range(3):
        for z, (own, six) in enumerate(block_of(first2, (f,), 1, 8, 2, 8)):
            second2[f, z + 1, 2:10, :] = 1.2 * own + weigh(w[z], six)
    w = [[weights2[i, z, 3:11, :] for i in range(7)] for z in range(8)]
    own_row = iota((8, 128), 0) < 4
    parts = [{} for pair in range(4)]
    for f in range(3):
        for z, (own, six) in enumerate(block_of(second2, (f,), 1, 8, 3, 8)):
            e_two[f, z] = own
            change = (first2[f, z + 1, 3:11, :] - 0.8 * own) + weigh(w[z], six)
            value = jnp.where(own_row, change * w[z][6], 0.0)
            sums = parts[z // 2]
            sums[f] = value if z % 2 == 0 else sums[f] + value
    for z in range(8):
        value = jnp.where(own_row, share2[z], 0.0)
        sums = parts[z // 2]
        sums[3] = value if z % 2 == 0 else sums[3] + value

    pool = jnp.where((source < 32) & (source // 2 == target % 16), 0.125, 0.0)
    rows = jnp.concatenate([parts[pair][ch] for ch in range(4) for pair in range(4)], axis=0)
    spread = dot_exact(rows, pool)
    at, to = iota((32, 128), 0), iota((32, 128), 1)
    keep = (at // 8 == to // 32) & ((at % 8) // 2 == (to // 16) % 2)
    result = jnp.concatenate(
        [
            jnp.sum(jnp.where(keep, spread[32 * ch : 32 * ch + 32], 0.0), axis=0, keepdims=True)
            for ch in range(4)
        ],
        axis=0,
    )
    for copy in range(CHIPS):
        sent[copy] = result


def swap_blocks(x):
    sub, group = iota((8, 128), 0), iota((8, 128), 1) // 16
    for bit in (4, 2, 1):
        up = roll(roll(x, -bit, 0), 16 * bit)
        down = up if bit == 4 else roll(roll(x, bit, 0), -16 * bit)
        sub_set, group_set = (sub & bit) != 0, (group & bit) != 0
        x = jnp.where(sub_set == group_set, x, jnp.where(sub_set, down, up))
    return x


def top_kernel(
    mine, other, base, out,
    natural, first, second, four, weights, diags, lefts, final, sems,
):
    gx, gy = lax.axis_index("gx"), lax.axis_index("gy")
    first_core = lax.rem(gy, 2) == 0
    lane, sub = iota((16, 128), 1), iota((16, 128), 0)
    cells = [(z, x, half) for z in range(4) for x in range(2) for half in range(2)]

    def lay(g):
        for ch in range(4):
            rows = pl.ds(32 * g + ch, 8, stride=4)
            pair = mine[rows, :], other[rows, :]
            natural[ch, 0, pl.ds(pl.multiple_of(8 * g, 8), 8), :] = swap_blocks(
                jnp.where(first_core, pair[0], pair[1])
            )
            natural[ch, 1, pl.ds(pl.multiple_of(8 * g, 8), 8), :] = swap_blocks(
                jnp.where(first_core, pair[1], pair[0])
            )

    def lay_some(step):
        for k in range(8):
            lay(8 * step + k)

    loop(2, lay_some)
    flat = natural.reshape(1024, 128)

    def plane(ch, z, x, half):
        return flat[pl.ds((ch * 2 + half) * 128 + z * 2 + x, 16, stride=8), :]

    def neighbours(at, z, x, half, outside):
        own, other = at(z, x, half), at(z, 1 - x, half)
        beside = at(z, x, 1 - half)
        shifted = roll(other, 1 if x == 0 else -1, 0)
        low, high = (shifted, other) if x == 0 else (other, shifted)
        left, right = roll(own, 1), roll(own, -1)
        left = jnp.where(lane % 16 == 0, roll(beside, 1 if half == 0 else -15), left)
        right = jnp.where(lane % 16 == 15, roll(beside, 15 if half == 0 else -1), right)
        down = at(z - 1, x, half) if z > 0 else outside
        up = at(z + 1, x, half) if z < 3 else outside
        return own, [low, high, left, right, down, up]

    def edge_masks(x, half):
        return [
            sub > 0 if x == 0 else None,
            sub < 15 if x == 1 else None,
            lane > 0 if half == 0 else None,
            lane < 127 if half == 1 else None,
            None,
            None,
        ]

    def key(z, x, half):
        return (z * 2 + x) * 2 + half

    shares = {c: plane(3, *c) for c in cells}
    rests = {c: resist(shares[c]) for c in cells}
    outside, zeros = jnp.full((16, 128), 0.5, F32), jnp.zeros((16, 128), F32)
    for z, x, half in cells:
        own, six = neighbours(lambda *c: rests[c], z, x, half, outside)
        masks = edge_masks(x, half)
        six = [s if m is None else jnp.where(m, s, 0.5) for s, m in zip(six, masks)]
        gain, w, diag = level_weights(own, six, 0.8)
        at = key(z, x, half)
        for i in range(6):
            weights[i, at] = w[i] if masks[i] is None else jnp.where(masks[i], w[i], 0.0)
        diags[at] = (1.25 * 0.25**3) * diag
        for f in range(3):
            first[f, at] = (64.0 * gain) * plane(f, z, x, half)

    for z, x, half in cells:
        at = key(z, x, half)
        w = [weights[i, at] for i in range(6)]
        for f in range(3):
            own, six = neighbours(lambda *c: first[f, key(*c)], z, x, half, zeros)
            second[half, f, z * 2 + x] = 1.2 * own + weigh(w, six)

    for z4 in range(2):
        for half in range(2):
            sums = [None] * 4
            for z in (2 * z4, 2 * z4 + 1):
                for x in range(2):
                    at = key(z, x, half)
                    w = [weights[i, at] for i in range(6)]
                    diag = diags[at]
                    for f in range(3):
                        own, six = neighbours(
                            lambda c, d, e: second[e, f, c * 2 + d], z, x, half, zeros
                        )
                        value = ((first[f, at] - 0.8 * own) + weigh(w, six)) * diag
                        sums[f] = value if sums[f] is None else sums[f] + value
                    share = shares[z, x, half]
                    sums[3] = share if sums[3] is None else sums[3] + share
            for ch in range(4):
                lefts[ch, z4, :, 128 * half : 128 * half + 128] = sums[ch]

    source = iota((256, 128), 0)
    column = ((source % 128) // 16) * 16 + (source // 128) * 8 + (source % 16) // 2
    pool = jnp.where(column == iota((256, 128), 1), 0.125, 0.0)
    level = dot_exact(lefts[...].reshape(128, 256), pool)

    def coarsest(ch, z):
        return level[(ch * 2 + z) * 16 : (ch * 2 + z) * 16 + 16, :]

    masks = [sub > 0, sub < 15, lane > 0, lane < 127]
    resists = [resist(coarsest(3, z)) for z in range(2)]
    gains, ws, ds = [], [], []
    for z in range(2):
        own, other = resists[z], resists[1 - z]
        six = [roll(own, 1, 0), roll(own, -1, 0), roll(own, 1), roll(own, -1)]
        six = [jnp.where(m, s, 0.5) for m, s in zip(masks, six)] + [other, outside]
        gain, w, diag = level_weights(own, six, 0.8)
        gains.append(gain)
        ds.append(diag)
        ws.append([jnp.where(m, v, 0.0) for m, v in zip(masks, w)] + [w[4]])
    whole = jnp.sum(ds[0] + ds[1], keepdims=True)

    def around(values, z):
        own, other = values[z], values[1 - z]
        return weigh(ws[z], (roll(own, 1, 0), roll(own, -1, 0), roll(own, 1), roll(own, -1), other))

    begin = [[256.0 * gains[z] * coarsest(f, z) for z in range(2)] for f in range(3)]
    values = begin
    for step in range(5):
        values = [
            [(0.2 * values[f][z] + begin[f][z]) + around(values[f], z) for z in range(2)] for f in range(3)
        ]
    shifts = []
    for f in range(3):
        change = [(begin[f][z] - 0.8 * values[f][z]) + around(values[f], z) for z in range(2)]
        shifts.append(jnp.sum(1.25 * (change[0] * ds[0] + change[1] * ds[1]), keepdims=True) / whole)
        for z in range(2):
            four[2 * f + z] = values[f][z]

    rows = four.reshape(96, 128)[pl.ds(gx, 6, stride=16), :]
    upper = jnp.concatenate([jnp.broadcast_to(rows[i : i + 1], (4, 128)) for i in range(6)], axis=0)
    flat = second.reshape(768, 128)
    halves = [flat[pl.ds(gx + 384 * half, 24, stride=16), :] for half in range(2)]
    three = turn(jnp.where(first_core, halves[0], halves[1]), -16 * lax.div(gy, 2))
    both = jnp.concatenate([turn(upper, -8 * gy), three], axis=1)
    both = jnp.concatenate([both, jnp.zeros((8, 256), F32)], axis=0)
    source, target = iota((256, 128), 0), iota((256, 128), 1)
    copy = jnp.where(source == jnp.where(source < 128, target // 16, 128 + target // 8), 1.0, 0.0)
    three = dot_exact(both, copy)

    copies = []
    for f in range(3):
        for z in range(4):
            for x in range(2):
                at = f * 8 + z * 2 + x
                value = jnp.broadcast_to(three[at : at + 1] + shifts[f], (8, 128))
                for k in range(8 * z, 8 * z + 8):
                    final[f, k, 8 * x : 8 * x + 8, :] = base[f, k, 8 * x : 8 * x + 8, :] + value
            part = (f, pl.ds(8 * z, 8))
            copy = pltpu.make_async_copy(final.at[part], out.at[part], sems.at[len(copies)])
            copy.start()
            copies.append(copy)
    for copy in copies:
        copy.wait()


def local(labels, guess):
    swap_near = [(i, i ^ 1) for i in range(NY)]
    far_x, far_y = [], []
    for x in range(NX):
        for y in range(NY):
            across_x, across_y = x + 1 if x % 2 else x - 1, y + 1 if y % 2 else y - 1
            to = (across_x, y) if 0 <= across_x < NX else (x, y ^ 1)
            far_x.append((x * NY + y, to[0] * NY + to[1]))
            to = (x, across_y) if 0 <= across_y < NY else (x ^ 1, y)
            far_y.append((x * NY + y, to[0] * NY + to[1]))
    both = ("gx", "gy")
    to_near, to_far, own = call(
        rows_kernel,
        [(12, 32, 128)] * 2 + [(4, 32, 16, 128)],
        [pltpu.VMEM((32, 16, 128), jnp.int32), pltpu.SemaphoreType.DMA((16,))],
        in_specs=[ANY, ANY],
    )(pltpu.with_memory_space_constraint(guess, pltpu.HBM), pltpu.with_memory_space_constraint(labels, pltpu.HBM))
    from_near = lax.ppermute(to_near, "gx", swap_near)
    from_far = lax.ppermute(to_far, both, far_x)
    own_one, own_two, halves, to_right, to_left, edges = call(
        own_kernel,
        [(3, 34, 32, 128)] * 2 + [(4, 16, 16, 128)] + [(4, 4, 16, 128)] * 2 + [(4, 16, 16, 128)],
        [(4, 34, 32, 128), (6, 32, 32, 128), (32, 32, 128)],
        flops=20_000_000,
    )(own)
    to_near, to_far, rim_rows = call(pack_kernel, [(4, 4, 24, 128)] * 2 + [(4, 32, 8, 128)], [])(
        to_right, to_left, from_near, from_far
    )
    from_far = lax.ppermute(to_far, both, far_y)
    from_near = lax.ppermute(to_near, "gy", swap_near)
    two, main, edges_rim = call(
        rows_edge_kernel,
        [(3, 34, 24, 128), (4, 8, 8, 128), (4, 16, 8, 128)],
        [(4, 34, 24, 128), (3, 34, 24, 128), (6, 32, 24, 128), (32, 24, 128)]
        + [(4, 16, 16, 128), (512, 128)],
        flops=10_000_000,
    )(own, rim_rows, own_one, own_two, halves)
    main_near = lax.ppermute(main, "gx", swap_near)
    main_far = lax.ppermute(main, both, far_x)
    rim, rim_one = call(
        rim_kernel,
        [(3, 16, 16, 128), (4, 4, 8, 128)],
        [(3, 18, 32, 128), (18, 32, 128)]
        + [(3, 18, 32, 128)] * 2
        + [(6, 16, 32, 128), (16, 32, 128)]
        + [(4, 8, 16, 128), (256, 128)],
        flops=10_000_000,
    )(edges, edges_rim, from_near, from_far)
    rim_near = lax.ppermute(rim_one, "gx", swap_near)
    rim_far = lax.ppermute(rim_one, both, far_x)
    sent, e_one, e_two = call(
        middle_kernel,
        [(CHIPS, 4, 128), (3, 16, 8, 128), (3, 8, 8, 128)],
        [(16, 24, 128), (18, 32, 128), (3, 16, 32, 128), (3, 18, 32, 128), (3, 18, 32, 128)]
        + [(6, 16, 32, 128), (16, 32, 128), (4, 8, 24, 128), (768, 128)]
        + [(10, 24, 128), (3, 10, 24, 128), (3, 10, 24, 128), (3, 8, 8, 128), (8, 8, 128)]
        + [(7, 8, 16, 128)],
    )(main, main_near, main_far, rim_one, rim_near, rim_far)
    groups = [[i for i in range(NX * NY) if i % 2 == core] for core in range(2)]
    mine = lax.all_to_all(
        sent, ("gx", "gy"), split_axis=0, concat_axis=0, axis_index_groups=groups, tiled=True
    )
    (base,) = call(base_kernel, [(3, 32, 16, 128)], [(192, 128), (3, 16, 16, 128)])(two, rim, e_one, e_two)
    other = lax.ppermute(mine, "gy", swap_near)
    (out,) = call(
        top_kernel,
        [(3, 32, 16, 128)],
        [(4, 2, 128, 128), (3, 16, 16, 128), (2, 3, 8, 16, 128), (6, 16, 128), (6, 16, 16, 128)]
        + [(16, 16, 128), (4, 2, 16, 256), (3, 32, 16, 128), pltpu.SemaphoreType.DMA((12,))],
        out_specs=[ANY],
    )(mine.reshape(512, 128), other.reshape(512, 128), base)
    return out


def solution(mesh):
    return jax.shard_map(
        local,
        mesh=mesh,
        in_specs=(P(None, "gx", "gy"), P(None, None, "gx", "gy")),
        out_specs=P(None, None, "gx", "gy"),
        check_vma=False,
    )
```

```python
import jax
import jax.numpy as jnp
from jax import lax
from jax.experimental import pallas as pl
from jax.experimental.pallas import tpu as pltpu
from jax.sharding import PartitionSpec as P


F32 = jnp.float32
NX, NY, CHIPS = 16, 16, 128
STEP, WIDE = 16, 32
BETWEEN = 2.0 * 0.1 / 1.1
ANY = pl.BlockSpec(memory_space=pltpu.HBM)


def dot_exact(a, b):
    high = a.astype(jnp.bfloat16)
    low = (a - high.astype(F32)).astype(jnp.bfloat16)
    b = b.astype(jnp.bfloat16)
    return jnp.dot(
        jnp.concatenate([high, low], axis=1), jnp.concatenate([b, b], axis=0), preferred_element_type=F32
    )


def iota(shape, dim):
    return lax.broadcasted_iota(jnp.int32, shape, dim)


def roll(x, shift, axis=1):
    shift = shift % x.shape[axis]
    return x if shift == 0 else pltpu.roll(x, shift, axis)


def turn(x, shift):
    return pltpu.roll(x, lax.rem(shift + 256, 128), 1)


def recip(x):
    guess = pl.reciprocal(x, approx=True)
    return guess * (2.0 - x * guess)


def inner(index):
    return (index > 0) & (index < 15)


def call(kernel, outs, scratch, flops=1_000_000, **kw):
    return pl.pallas_call(
        kernel,
        out_shape=[jax.ShapeDtypeStruct(s, F32) for s in outs],
        scratch_shapes=[pltpu.VMEM(s, F32) if isinstance(s, tuple) else s for s in scratch],
        compiler_params=pltpu.CompilerParams(vmem_limit_bytes=32 * 1024 * 1024),
        cost_estimate=pl.CostEstimate(flops=flops, bytes_accessed=4_000_000, transcendentals=0),
        **kw,
    )


def loop(count, body, unroll=1):
    def step(i, carry):
        body(i)
        return carry

    lax.fori_loop(0, count, step, 0, unroll=unroll)


def weigh(weights, values):
    parts = [w * v for w, v in zip(weights, values)]
    while len(parts) > 1:
        parts = [sum(parts[i : i + 2][1:], parts[i]) for i in range(0, len(parts), 2)]
    return parts[0]


def rows_kernel(guess, labels, near, far, own, phase, sems):
    even = lax.rem(lax.axis_index("gx"), 2) == 0
    near_row, far_row = jnp.where(even, 13, 0), jnp.where(even, 0, 13)
    copies = [pltpu.make_async_copy(labels, phase, sems.at[3])]
    for f in range(3):
        copies.append(pltpu.make_async_copy(guess.at[f], own.at[f], sems.at[f]))
    for copy in copies:
        copy.start()
    copies[0].wait()
    own[3] = jnp.where(phase[...] == 1, 0.0, 1.0).astype(F32)
    flat = own.reshape(4 * 32 * 16, 128)
    for ch in (3, 0, 1, 2):
        if ch < 3:
            copies[ch + 1].wait()
        for row in range(3):
            near[3 * ch + row] = flat[pl.ds(512 * ch + near_row + row, 32, stride=16), :]
            far[3 * ch + row] = flat[pl.ds(512 * ch + far_row + row, 32, stride=16), :]


def pack_kernel(to_right, to_left, x_near, x_far, near, far, rim):
    first_core = lax.rem(lax.axis_index("gy"), 2) == 0
    even = lax.rem(lax.axis_index("gx"), 2) == 0
    near_row, far_row = jnp.where(even, 0, 5), jnp.where(even, 5, 0)
    has_far = inner(lax.axis_index("gx"))
    flat = rim.reshape(4 * 32 * 8, 128)
    for ch in range(4):
        for row in range(3):
            flat[pl.ds(256 * ch + near_row + row, 32, stride=8), :] = x_near[3 * ch + row]
            flat[pl.ds(256 * ch + far_row + row, 32, stride=8), :] = jnp.where(has_far, x_far[3 * ch + row], 0.0)

    def some(low):
        for ch in range(4):
            right, left = pack_planes(lambda z: rim[ch, z], low, (8, 128))
            for at, right, left in (
                (slice(0, 16), to_right[ch, low], to_left[ch, low]),
                (slice(16, 24), right, left),
            ):
                near[ch, low, at, :] = jnp.where(first_core, right, left)
                far[ch, low, at, :] = jnp.where(first_core, left, right)

    loop(4, some, 4)


def pack_planes(plane, low, shape):
    group = iota(shape, 1) // 16
    right = left = jnp.zeros(shape, F32)
    for h in range(8):
        moved = roll(plane(4 * h + low), 16 * h + 16)
        right = jnp.where(group == h, moved, right)
        left = jnp.where(group == (h + 1) % 8, moved, left)
    return right, left


def edge_columns(plane, z, shape):
    lane = iota(shape, 1)
    value = jnp.zeros(shape, F32)
    for half in range(2):
        source = plane(z + 16 * half)
        base = 64 * half
        value = jnp.where((lane >= base) & (lane < base + 7), roll(source, base + 7), value)
        value = jnp.where((lane >= base + 57) & (lane < base + 64), roll(source, base + 57), value)
    return value


def six_of(ref, lead, z, first, count):
    own = ref[(*lead, z, pl.ds(first, count), slice(None))]
    return own, (
        ref[(*lead, z, pl.ds(first - 1, count), slice(None))],
        ref[(*lead, z, pl.ds(first + 1, count), slice(None))],
        roll(own, 1),
        roll(own, -1),
        ref[(*lead, z - 1, pl.ds(first, count), slice(None))],
        ref[(*lead, z + 1, pl.ds(first, count), slice(None))],
    )


def block_of(ref, lead, z, planes, first, count):
    rows = pl.ds(first, count)
    own = [ref[(*lead, z + k, rows, slice(None))] for k in range(-1, planes + 1)]
    result = []
    for k in range(planes):
        value = own[k + 1]
        six = (
            ref[(*lead, z + k, pl.ds(first - 1, count), slice(None))],
            ref[(*lead, z + k, pl.ds(first + 1, count), slice(None))],
            roll(value, 1),
            roll(value, -1),
            own[k],
            own[k + 2],
        )
        result.append((value, six))
    return result


def fine_weights(own, six, omega):
    base, slope = 1.0 + (BETWEEN - 1.0) * own, (BETWEEN - 1.0) + (1.1 - 2.0 * BETWEEN) * own
    total = (six[0] + six[1]) + (six[2] + six[3]) + (six[4] + six[5])
    diag = 6.0 * base + slope * total
    gain = omega * recip(diag)
    base, slope = gain * base, gain * slope
    return [base + slope * other for other in six], 1.25 * diag


def fine_sweep(w, f, own, six):
    return (0.2 * own + (w[2 * f + 1] - w[2 * f])) + weigh(w, six)


def fine_left(w, f, own, six, diag):
    return (((w[2 * f + 1] - w[2 * f]) - 0.8 * own) + weigh(w, six)) * diag


def fine_sweeps(planes, windows, start, share, one, two, weights, diags, halves, omega, wrap, keep, size):
    first, count = windows[0]

    def first_sweep(step):
        z = size * step
        w = []
        for k, (own, six) in enumerate(block_of(share, (), z + 1, size, first, count)):
            now, diag = fine_weights(own, six, omega)
            diags[z + k, pl.ds(first, count), :] = diag
            for i in range(6):
                weights[i, z + k, pl.ds(first, count), :] = now[i]
            w.append(now)
        for f in range(3):
            for k, (own, six) in enumerate(block_of(start, (f,), z + 1, size, first, count)):
                one[f, z + k + 1, pl.ds(first, count), :] = fine_sweep(w[k], f, own, six)

    loop(planes // size, first_sweep)
    wrap(one)
    second, count2 = windows[1]

    def second_sweep(step):
        z = size * step
        w = [[weights[i, z + k, pl.ds(second, count2), :] for i in range(6)] for k in range(size)]
        for f in range(3):
            for k, (own, six) in enumerate(block_of(one, (f,), z + 1, size, second, count2)):
                two[f, z + k + 1, pl.ds(second, count2), :] = fine_sweep(w[k], f, own, six)

    loop(planes // size, second_sweep)
    wrap(two)

    def residual(step):
        z = size * step
        w = [[weights[i, z + k, 8:24, :] for i in range(6)] for k in range(size)]
        diag = [diags[z + k, 8:24, :] for k in range(size)]
        for f in range(3):
            values = []
            for k, (own, six) in enumerate(block_of(two, (f,), z + 1, size, 8, 16)):
                if keep is not None:
                    keep[f, z + k] = own
                values.append(fine_left(w[k], f, own, six, diag[k]))
            for pair in range(size // 2):
                halves[f, size // 2 * step + pair] = values[2 * pair] + values[2 * pair + 1]
        for pair in range(size // 2):
            at = z + 2 * pair + 1
            halves[3, size // 2 * step + pair] = share[at, 8:24, :] + share[at + 1, 8:24, :]

    loop(planes // size, residual)


def own_kernel(own, one, two, halves, to_right, to_left, edges, held, weights, diags):
    zero = jnp.zeros((32, 128), F32)
    for z in (0, 33):
        for ch in range(4):
            held[ch, z] = zero
        for ref in (one, two):
            for f in range(3):
                ref[f, z] = zero

    def plane(z):
        for ch in range(4):
            held[ch, z + 1, 8:24, :] = own[ch, z]

    loop(32, plane, 8)
    fine_sweeps(
        32, [(8, 16)] * 2, held, held.at[3], one, two, weights, diags, halves, 0.8, lambda ref: None, None, 8
    )

    def some(low):
        for ch in range(4):
            to_right[ch, low], to_left[ch, low] = pack_planes(lambda z: own[ch, z], low, (16, 128))

    loop(4, some, 2)

    def edge(z):
        for ch in range(4):
            edges[ch, z] = edge_columns(lambda at: own[ch, at], z, (16, 128))

    loop(16, edge, 8)


def rows_edge_kernel(own, rim, own_one, own_two, own_halves, two, packed, edges, start, one, weights, diags, halves, pooled):
    gx = lax.axis_index("gx")
    zero = jnp.zeros((24, 128), F32)
    for z in (0, 33):
        for ch in range(4):
            start[ch, z] = zero
        for ref in (one, two):
            for f in range(3):
                ref[f, z] = zero

    def fill(z):
        for ch in range(4):
            start[ch, z + 1, 0:8, :] = own[ch, z, 8:16, :]
            start[ch, z + 1, 8:16, :] = rim[ch, z]
            start[ch, z + 1, 16:24, :] = own[ch, z, 0:8, :]
        for f in range(3):
            for ref, source in ((one, own_one), (two, own_two)):
                ref[f, z + 1, 0:8, :] = source[f, z + 1, 16:24, :]
                ref[f, z + 1, 16:24, :] = source[f, z + 1, 8:16, :]

    loop(32, fill, 8)
    upper = iota((8, 128), 0) < 4

    def both(ref, lead, step, shift=0):
        high = ref[(*lead, pl.ds(8 - step + shift, 8), slice(None))]
        low = ref[(*lead, pl.ds(8 + step + shift, 8), slice(None))]
        return jnp.where(upper, high, low)

    def block_both(ref, f, z, step):
        own = [both(ref, (f, z + k), step) for k in range(-1, WIDE + 1)]
        result = []
        for k in range(WIDE):
            value = own[k + 1]
            low, high = both(ref, (f, z + k), step, -1), both(ref, (f, z + k), step, 1)
            result.append((value, (low, high, roll(value, 1), roll(value, -1), own[k], own[k + 2])))
        return result

    def put(ref, f, z, step, value):
        ref[f, z, pl.ds(8 - step, 4), :] = value[0:4]
        ref[f, z, pl.ds(12 + step, 4), :] = value[4:8]

    row = iota((16, 128), 0) + 5
    low, high = jnp.where(gx > 0, 1, 0), jnp.where(gx < NX - 1, 1, 0)
    inside = jnp.where((row >= 8) & (row < 12), high, jnp.where((row >= 12) & (row < 16), low, 1))
    omega = 0.8 * inside.astype(F32)

    def weigh_all(step):
        z = WIDE * step
        for k, (value, six) in enumerate(block_of(start, (3,), z + 1, WIDE, 5, 16)):
            w, diag = fine_weights(value, six, omega)
            diags[z + k, 5:21, :] = diag
            for i in range(6):
                weights[i, z + k, 5:21, :] = w[i]

    loop(32 // WIDE, weigh_all)

    for step, source, target in ((1, start, one), (2, one, two)):

        def sweep(block):
            z = WIDE * block
            w = [[both(weights, (i, z + k), step) for i in range(6)] for k in range(WIDE)]
            for f in range(3):
                for k, (value, six) in enumerate(block_both(source, f, z + 1, step)):
                    put(target, f, z + k + 1, step, fine_sweep(w[k], f, value, six))

        loop(32 // WIDE, sweep)

    sub = iota((8, 128), 0)

    def residual(block):
        z = WIDE * block
        w = [[both(weights, (i, z + k), 3) for i in range(6)] for k in range(WIDE)]
        diag = [both(diags, (z + k,), 3) for k in range(WIDE)]
        for f in range(3):
            values = []
            for k, (value, six) in enumerate(block_both(two, f, z + 1, 3)):
                values.append(fine_left(w[k], f, value, six, diag[k]))
            for k in range(WIDE // 2):
                pair = WIDE // 2 * block + k
                value = values[2 * k] + values[2 * k + 1]
                halves[f, pair, 0:8, :] = jnp.where(sub < 3, roll(value, 3, 0), own_halves[f, pair, 0:8, :])
                halves[f, pair, 8:16, :] = jnp.where(sub >= 5, roll(value, 5, 0), own_halves[f, pair, 8:16, :])
        for k in range(WIDE // 2):
            halves[3, WIDE // 2 * block + k] = own_halves[3, WIDE // 2 * block + k]

    loop(32 // WIDE, residual)
    source, target = iota((128, 128), 0), iota((128, 128), 1)
    value = None
    for half in range(2):
        pool = jnp.where(source // 2 + 64 * half == target, 0.125, 0.0)
        part = dot_exact(halves[:, 8 * half : 8 * half + 8].reshape(512, 128), pool)
        value = part if value is None else value + part
    pooled[...] = value
    packed[...] = (pooled[pl.ds(0, 256, stride=2), :] + pooled[pl.ds(1, 256, stride=2), :]).reshape(4, 8, 8, 128)

    def edge(z):
        for ch in range(4):
            edges[ch, z] = edge_columns(lambda at: rim[ch, at], z, (8, 128))

    loop(16, edge, 8)


def rim_kernel(
    edges, edges_rim, near, far, field, packed,
    start, share, one, two, weights, diags, halves, pooled,
):
    gx, gy = lax.axis_index("gx"), lax.axis_index("gy")
    lane = iota((24, 128), 1)
    part = lane % 64
    is_after = (part >= 7) & (part < 22)
    is_before = (part >= 42) & (part < 57)
    first_core = lax.rem(gy, 2) == 0

    def unpack(low):
        for ch in range(4):
            target = start.at[ch] if ch < 3 else share
            from_near, from_far = near[ch, low], jnp.where(inner(gy), far[ch, low], 0.0)
            from_right = jnp.where(first_core, from_near, from_far)
            from_left = jnp.where(first_core, from_far, from_near)
            for h in range(4):
                z = 4 * h + low
                after_y = roll(from_right, 7 - 16 * (h + 1))
                before_y = roll(from_left, 41 - 16 * h)
                own = jnp.concatenate([edges[ch, z], edges_rim[ch, z]], axis=0)
                value = jnp.where(is_after, after_y, jnp.where(is_before, before_y, own))
                target[z + 1, 8:24, :] = value[0:16]
                target[z + 1, 0:8, :] = value[16:24]
                target[z + 1, 24:32, :] = value[16:24]

    loop(4, unpack, 2)

    half_of = iota((32, 128), 1)

    def wrap_one(ref):
        ref[0] = jnp.where(half_of >= 64, roll(ref[16], 64), 0.0)
        ref[17] = jnp.where(half_of < 64, roll(ref[1], 64), 0.0)

    def wrap(ref):
        for f in range(3):
            wrap_one(ref.at[f])

    wrap_one(share)
    wrap(start)
    row = iota((24, 128), 0) + 6
    low, high = jnp.where(gx > 0, 1, 0), jnp.where(gx < NX - 1, 1, 0)
    inside_x = jnp.where(row < 8, low, jnp.where(row >= 24, high, 1))
    inside_y = jnp.where(
        part < 32,
        jnp.where((part < 7) | (gy < NY - 1), 1, 0),
        jnp.where((part >= 57) | (gy > 0), 1, 0),
    )
    omega = 0.8 * (inside_x * inside_y).astype(F32)
    fine_sweeps(
        16, [(6, 24), (7, 24)], start, share, one, two, weights, diags, halves, omega, wrap, field, STEP
    )

    source, target = iota((128, 128), 0), iota((128, 128), 1)
    spot = source % 64
    column = jnp.where(spot < 32, 121 + spot, 71 + spot) // 2
    to = jnp.where(spot < 32, column - 62, column - 48)
    keep = ((spot < 32) & (to >= 0) & (to < 9)) | ((spot >= 32) & (to >= 9) & (to < 18))
    mixed = halves[...].reshape(4, 4, 2, 16, 128)
    value = None
    for odd in range(2):
        pool = jnp.where(keep & (to + 64 * odd + 32 * (source // 64) == target), 0.125, 0.0)
        part = dot_exact(mixed[:, :, odd].reshape(256, 128), pool)
        value = part if value is None else value + part
    pooled[...] = value
    packed[...] = (pooled[pl.ds(0, 128, stride=2), :] + pooled[pl.ds(1, 128, stride=2), :]).reshape(4, 4, 8, 128)


def base_kernel(two, rim, e_one, e_two, base, wide, spread):
    copy = jnp.where(iota((128, 128), 0) == iota((128, 128), 1) // 2, 1.0, 0.0)
    value = dot_exact(e_two[...].reshape(192, 128), copy)
    for block in range(24):
        rows = value[8 * block : 8 * block + 4, :]
        wide[pl.ds(8 * block, 4, stride=2), :] = rows
        wide[pl.ds(8 * block + 1, 4, stride=2), :] = rows
    value = e_one[...].reshape(24, 2, 8, 128) + wide[...].reshape(24, 1, 8, 128)
    value = dot_exact(value.reshape(384, 128), copy)
    flat = spread.reshape(768, 128)
    for block in range(48):
        rows = value[8 * block : 8 * block + 8, :]
        flat[pl.ds(16 * block, 8, stride=2), :] = rows
        flat[pl.ds(16 * block + 1, 8, stride=2), :] = rows
    lane = iota((16, 128), 1)

    def pair(k):
        for f in range(3):
            for z in (2 * k, 2 * k + 1):
                value = rim[f, z]
                for half in range(2):
                    low = roll(value, -57 - 64 * half)
                    high = roll(value, 121 - 64 * half)
                    at = z + 16 * half
                    own = jnp.concatenate([two[f, at + 1, 16:24, :], two[f, at + 1, 0:8, :]], axis=0)
                    own = jnp.where(lane < 3, low, jnp.where(lane >= 125, high, own))
                    base[f, at] = own + spread[f, k + 8 * half]

    loop(8, pair, 4)


def resist(share):
    return recip(2.0 - 1.8 * share)


def level_weights(own, six, omega):
    faces = [recip(own + other) for other in six]
    diag = (faces[0] + faces[1]) + (faces[2] + faces[3]) + (faces[4] + faces[5])
    gain = omega * recip(diag)
    return gain, [gain * w for w in faces], diag


def middle_kernel(
    main, main_near, main_far, rim, rim_near, rim_far, sent, e_one, e_two,
    share, rest, rhs, first, second, weights, diags, halves, pooled,
    rest2, first2, second2, rhs2, share2, weights2,
):
    gx, gy = lax.axis_index("gx"), lax.axis_index("gy")
    low_x, high_x = jnp.where(gx > 0, 1, 0), jnp.where(gx < NX - 1, 1, 0)
    low_y, high_y = jnp.where(gy > 0, 1, 0), jnp.where(gy < NY - 1, 1, 0)

    for f in range(3):
        for ref in (first, second):
            ref[f, 0] = jnp.zeros((32, 128), F32)
            ref[f, 17] = jnp.zeros((32, 128), F32)
    for z in (0, 17):
        rest[z] = jnp.full((32, 128), 0.5, F32)
    lane = iota((8, 128), 1)
    even = lax.rem(gx, 2) == 0
    near_row, far_row = jnp.where(even, 16, 0), jnp.where(even, 0, 16)
    starts = (pl.multiple_of(near_row, 8), pl.multiple_of(far_row, 8), 8)

    sources = zip(starts, ((main_near, rim_near), (main_far, rim_far), (main, rim)))
    sources = list(sources)
    has_far = inner(gx)

    def fill(q):
        for odd in range(2):
            for half in range(2):
                z = 2 * q + odd + 8 * half
                base = 64 * odd + 32 * half
                for at, (middle, outer) in sources:
                    for ch in range(4):
                        edge, body = outer[ch, q], middle[ch, 2 * q + odd]
                        if outer is rim_far:
                            edge, body = jnp.where(has_far, edge, 0.0), jnp.where(has_far, body, 0.0)
                        value = jnp.where(lane < 62, roll(body, 64 * half), roll(edge, 62 - base))
                        value = jnp.where((lane >= 96) | (lane < 2), roll(edge, 112 - base), value)
                        if ch < 3:
                            rhs[ch, z, pl.ds(at, 8), :] = value
                        else:
                            share[z, pl.ds(at, 8), :] = value
                            rest[z + 1, pl.ds(at, 8), :] = resist(value)
                rest[z + 1, 24:32, :] = jnp.full((8, 128), 0.5, F32)

    loop(4, fill, 2)

    row, lane = iota((24, 128), 0) + 1, iota((24, 128), 1)
    in_x = jnp.where(row < 8, low_x, jnp.where(row >= 16, high_x, 1))
    in_y = jnp.where(lane < 64, 1, jnp.where(lane < 96, high_y, low_y))
    omega = 0.8 * (in_x * in_y).astype(F32)

    def start(step):
        z = STEP * step
        for k, (own, six) in enumerate(block_of(rest, (), z + 1, STEP, 1, 24)):
            gain, w, diag = level_weights(own, six, omega)
            for i in range(6):
                weights[i, z + k, 1:25, :] = w[i]
            diags[z + k, 1:25, :] = (1.25 * 0.25) * diag
            for f in range(3):
                first[f, z + k + 1, 1:25, :] = (4.0 * gain) * rhs[f, z + k, 1:25, :]

    loop(16 // STEP, start)

    def sweep(step):
        z = STEP * step
        w = [[weights[i, z + k, 3:27, :] for i in range(6)] for k in range(STEP)]
        for f in range(3):
            for k, (own, six) in enumerate(block_of(first, (f,), z + 1, STEP, 3, 24)):
                second[f, z + k + 1, 3:27, :] = 1.2 * own + weigh(w[k], six)

    loop(16 // STEP, sweep)

    def left(step):
        z = STEP * step
        w = [[weights[i, z + k, 4:20, :] for i in range(6)] for k in range(STEP)]
        diag = [diags[z + k, 4:20, :] for k in range(STEP)]
        for f in range(3):
            values = []
            for k, (own, six) in enumerate(block_of(second, (f,), z + 1, STEP, 4, 16)):
                change = (first[f, z + k + 1, 4:20, :] - 0.8 * own) + weigh(w[k], six)
                values.append(change * diag[k])
                e_one[f, z + k] = second[f, z + k + 1, 8:16, :]
            for k in range(STEP // 2):
                halves[f, STEP // 2 * step + k, 0:16, :] = values[2 * k] + values[2 * k + 1]
                halves[f, STEP // 2 * step + k, 16:24, :] = jnp.zeros((8, 128), F32)
        for k in range(STEP // 2):
            halves[3, STEP // 2 * step + k] = share[z + 2 * k] + share[z + 2 * k + 1]

    loop(16 // STEP, left)

    source, target = iota((128, 128), 0), iota((128, 128), 1)
    pool = jnp.where(source // 2 + jnp.where(source >= 96, 64, 0) == target, 0.125, 0.0)
    pooled[...] = dot_exact(halves[...].reshape(4 * 8 * 24, 128), pool)
    for z in (0, 9):
        rest2[z] = jnp.full((24, 128), 0.5, F32)
        for f in range(3):
            first2[f, z] = jnp.zeros((24, 128), F32)
            second2[f, z] = jnp.zeros((24, 128), F32)
    for z in range(8):
        for f in range(3):
            base = (f * 8 + z) * 24
            rhs2[f, z] = pooled[pl.ds(base, 8, stride=2), :] + pooled[pl.ds(base + 1, 8, stride=2), :]
        base = (3 * 8 + z) * 24
        value = pooled[pl.ds(base + 2, 8, stride=2), :] + pooled[pl.ds(base + 3, 8, stride=2), :]
        rest2[z + 1, 0:8, :] = resist(value)
        value = pooled[pl.ds(base + 8, 8, stride=2), :] + pooled[pl.ds(base + 9, 8, stride=2), :]
        rest2[z + 1, 3:11, :] = resist(value)
        share2[z] = value

    row, lane = iota((8, 128), 0) + 1, iota((8, 128), 1)
    in_x = jnp.where(row < 3, low_x, jnp.where(row >= 7, high_x, 1))
    in_y = jnp.where(lane < 32, 1, jnp.where(lane < 96, high_y, low_y))
    omega2 = 0.8 * (in_x * in_y).astype(F32)

    for z, (own, six) in enumerate(block_of(rest2, (), 1, 8, 1, 8)):
        gain, w, diag = level_weights(own, six, omega2)
        for i in range(6):
            weights2[i, z, 1:9, :] = w[i]
        weights2[6, z, 1:9, :] = (1.25 * 0.0625) * diag
        for f in range(3):
            first2[f, z + 1, 1:9, :] = (16.0 * gain) * rhs2[f, z]
    w = [[weights2[i, z, 2:10, :] for i in range(6)] for z in range(8)]
    for f in range(3):
        for z, (own, six) in enumerate(block_of(first2, (f,), 1, 8, 2, 8)):
            second2[f, z + 1, 2:10, :] = 1.2 * own + weigh(w[z], six)
    w = [[weights2[i, z, 3:11, :] for i in range(7)] for z in range(8)]
    own_row = iota((8, 128), 0) < 4
    parts = [{} for pair in range(4)]
    for f in range(3):
        for z, (own, six) in enumerate(block_of(second2, (f,), 1, 8, 3, 8)):
            e_two[f, z] = own
            change = (first2[f, z + 1, 3:11, :] - 0.8 * own) + weigh(w[z], six)
            value = jnp.where(own_row, change * w[z][6], 0.0)
            sums = parts[z // 2]
            sums[f] = value if z % 2 == 0 else sums[f] + value
    for z in range(8):
        value = jnp.where(own_row, share2[z], 0.0)
        sums = parts[z // 2]
        sums[3] = value if z % 2 == 0 else sums[3] + value

    pool = jnp.where((source < 32) & (source // 2 == target % 16), 0.125, 0.0)
    rows = jnp.concatenate([parts[pair][ch] for ch in range(4) for pair in range(4)], axis=0)
    spread = dot_exact(rows, pool)
    at, to = iota((32, 128), 0), iota((32, 128), 1)
    keep = (at // 8 == to // 32) & ((at % 8) // 2 == (to // 16) % 2)
    result = jnp.concatenate(
        [
            jnp.sum(jnp.where(keep, spread[32 * ch : 32 * ch + 32], 0.0), axis=0, keepdims=True)
            for ch in range(4)
        ],
        axis=0,
    )
    for copy in range(CHIPS):
        sent[copy] = result


def swap_blocks(x):
    sub, group = iota((8, 128), 0), iota((8, 128), 1) // 16
    for bit in (4, 2, 1):
        up = roll(roll(x, -bit, 0), 16 * bit)
        down = up if bit == 4 else roll(roll(x, bit, 0), -16 * bit)
        sub_set, group_set = (sub & bit) != 0, (group & bit) != 0
        x = jnp.where(sub_set == group_set, x, jnp.where(sub_set, down, up))
    return x


def top_kernel(
    mine, other, base, out,
    natural, first, second, four, weights, diags, lefts, final, sems,
):
    gx, gy = lax.axis_index("gx"), lax.axis_index("gy")
    first_core = lax.rem(gy, 2) == 0
    lane, sub = iota((16, 128), 1), iota((16, 128), 0)
    cells = [(z, x, half) for z in range(4) for x in range(2) for half in range(2)]

    def lay(g):
        for ch in range(4):
            rows = pl.ds(32 * g + ch, 8, stride=4)
            pair = mine[rows, :], other[rows, :]
            natural[ch, 0, pl.ds(pl.multiple_of(8 * g, 8), 8), :] = swap_blocks(
                jnp.where(first_core, pair[0], pair[1])
            )
            natural[ch, 1, pl.ds(pl.multiple_of(8 * g, 8), 8), :] = swap_blocks(
                jnp.where(first_core, pair[1], pair[0])
            )

    loop(16, lay, 4)
    flat = natural.reshape(1024, 128)

    def plane(ch, z, x, half):
        return flat[pl.ds((ch * 2 + half) * 128 + z * 2 + x, 16, stride=8), :]

    def neighbours(at, z, x, half, outside):
        own, other = at(z, x, half), at(z, 1 - x, half)
        beside = at(z, x, 1 - half)
        shifted = roll(other, 1 if x == 0 else -1, 0)
        low, high = (shifted, other) if x == 0 else (other, shifted)
        left, right = roll(own, 1), roll(own, -1)
        left = jnp.where(lane % 16 == 0, roll(beside, 1 if half == 0 else -15), left)
        right = jnp.where(lane % 16 == 15, roll(beside, 15 if half == 0 else -1), right)
        down = at(z - 1, x, half) if z > 0 else outside
        up = at(z + 1, x, half) if z < 3 else outside
        return own, [low, high, left, right, down, up]

    def edge_masks(x, half):
        return [
            sub > 0 if x == 0 else None,
            sub < 15 if x == 1 else None,
            lane > 0 if half == 0 else None,
            lane < 127 if half == 1 else None,
            None,
            None,
        ]

    def key(z, x, half):
        return (z * 2 + x) * 2 + half

    shares = {c: plane(3, *c) for c in cells}
    rests = {c: resist(shares[c]) for c in cells}
    outside, zeros = jnp.full((16, 128), 0.5, F32), jnp.zeros((16, 128), F32)
    for z, x, half in cells:
        own, six = neighbours(lambda *c: rests[c], z, x, half, outside)
        masks = edge_masks(x, half)
        six = [s if m is None else jnp.where(m, s, 0.5) for s, m in zip(six, masks)]
        gain, w, diag = level_weights(own, six, 0.8)
        at = key(z, x, half)
        for i in range(6):
            weights[i, at] = w[i] if masks[i] is None else jnp.where(masks[i], w[i], 0.0)
        diags[at] = (1.25 * 0.25**3) * diag
        for f in range(3):
            first[f, at] = (64.0 * gain) * plane(f, z, x, half)

    def sweep(f):
        for z, x, half in cells:
            at = key(z, x, half)
            w = [weights[i, at] for i in range(6)]
            own, six = neighbours(lambda *c: first[f, key(*c)], z, x, half, zeros)
            second[half, f, z * 2 + x] = 1.2 * own + weigh(w, six)

    loop(3, sweep)

    def left(f):
        for z4 in range(2):
            for half in range(2):
                total = None
                for z in (2 * z4, 2 * z4 + 1):
                    for x in range(2):
                        at = key(z, x, half)
                        w = [weights[i, at] for i in range(6)]
                        own, six = neighbours(lambda c, d, e: second[e, f, c * 2 + d], z, x, half, zeros)
                        value = ((first[f, at] - 0.8 * own) + weigh(w, six)) * diags[at]
                        total = value if total is None else total + value
                lefts[f, z4, :, 128 * half : 128 * half + 128] = total

    loop(3, left)
    for z4 in range(2):
        for half in range(2):
            total = None
            for z in (2 * z4, 2 * z4 + 1):
                for x in range(2):
                    share = shares[z, x, half]
                    total = share if total is None else total + share
            lefts[3, z4, :, 128 * half : 128 * half + 128] = total

    source = iota((256, 128), 0)
    column = ((source % 128) // 16) * 16 + (source // 128) * 8 + (source % 16) // 2
    pool = jnp.where(column == iota((256, 128), 1), 0.125, 0.0)
    level = dot_exact(lefts[...].reshape(128, 256), pool)

    def coarsest(ch, z):
        return level[(ch * 2 + z) * 16 : (ch * 2 + z) * 16 + 16, :]

    masks = [sub > 0, sub < 15, lane > 0, lane < 127]
    resists = [resist(coarsest(3, z)) for z in range(2)]
    gains, ws, ds = [], [], []
    for z in range(2):
        own, other = resists[z], resists[1 - z]
        six = [roll(own, 1, 0), roll(own, -1, 0), roll(own, 1), roll(own, -1)]
        six = [jnp.where(m, s, 0.5) for m, s in zip(masks, six)] + [other, outside]
        gain, w, diag = level_weights(own, six, 0.8)
        gains.append(gain)
        ds.append(diag)
        ws.append([jnp.where(m, v, 0.0) for m, v in zip(masks, w)] + [w[4]])
    whole = jnp.sum(ds[0] + ds[1], keepdims=True)

    def around(values, z):
        own, other = values[z], values[1 - z]
        return weigh(ws[z], (roll(own, 1, 0), roll(own, -1, 0), roll(own, 1), roll(own, -1), other))

    begin = [[256.0 * gains[z] * coarsest(f, z) for z in range(2)] for f in range(3)]
    values = begin
    for step in range(5):
        values = [
            [(0.2 * values[f][z] + begin[f][z]) + around(values[f], z) for z in range(2)] for f in range(3)
        ]
    shifts = []
    for f in range(3):
        change = [(begin[f][z] - 0.8 * values[f][z]) + around(values[f], z) for z in range(2)]
        shifts.append(jnp.sum(1.25 * (change[0] * ds[0] + change[1] * ds[1]), keepdims=True) / whole)
        for z in range(2):
            four[2 * f + z] = values[f][z]

    rows = four.reshape(96, 128)[pl.ds(gx, 6, stride=16), :]
    upper = jnp.concatenate([jnp.broadcast_to(rows[i : i + 1], (4, 128)) for i in range(6)], axis=0)
    flat = second.reshape(768, 128)
    halves = [flat[pl.ds(gx + 384 * half, 24, stride=16), :] for half in range(2)]
    three = turn(jnp.where(first_core, halves[0], halves[1]), -16 * lax.div(gy, 2))
    both = jnp.concatenate([turn(upper, -8 * gy), three], axis=1)
    both = jnp.concatenate([both, jnp.zeros((8, 256), F32)], axis=0)
    source, target = iota((256, 128), 0), iota((256, 128), 1)
    copy = jnp.where(source == jnp.where(source < 128, target // 16, 128 + target // 8), 1.0, 0.0)
    three = dot_exact(both, copy)

    copies = []
    for f in range(3):
        for z in range(4):
            for x in range(2):
                at = f * 8 + z * 2 + x
                value = jnp.broadcast_to(three[at : at + 1] + shifts[f], (8, 128))
                for k in range(8 * z, 8 * z + 8):
                    final[f, k, 8 * x : 8 * x + 8, :] = base[f, k, 8 * x : 8 * x + 8, :] + value
            if z % 2 == 1:
                part = (f, pl.ds(8 * z - 8, 16))
                copy = pltpu.make_async_copy(final.at[part], out.at[part], sems.at[len(copies)])
                copy.start()
                copies.append(copy)
    for copy in copies:
        copy.wait()


def local(labels, guess):
    swap_near = [(i, i ^ 1) for i in range(NY)]
    far_x, far_y = [], []
    for x in range(NX):
        for y in range(NY):
            across_x, across_y = x + 1 if x % 2 else x - 1, y + 1 if y % 2 else y - 1
            to = (across_x, y) if 0 <= across_x < NX else (x, y ^ 1)
            far_x.append((x * NY + y, to[0] * NY + to[1]))
            to = (x, across_y) if 0 <= across_y < NY else (x ^ 1, y)
            far_y.append((x * NY + y, to[0] * NY + to[1]))
    both = ("gx", "gy")
    to_near, to_far, own = call(
        rows_kernel,
        [(12, 32, 128)] * 2 + [(4, 32, 16, 128)],
        [pltpu.VMEM((32, 16, 128), jnp.int32), pltpu.SemaphoreType.DMA((4,))],
        in_specs=[ANY, ANY],
    )(pltpu.with_memory_space_constraint(guess, pltpu.HBM), pltpu.with_memory_space_constraint(labels, pltpu.HBM))
    from_near = lax.ppermute(to_near, "gx", swap_near)
    from_far = lax.ppermute(to_far, both, far_x)
    own_one, own_two, halves, to_right, to_left, edges = call(
        own_kernel,
        [(3, 34, 32, 128)] * 2 + [(4, 16, 16, 128)] + [(4, 4, 16, 128)] * 2 + [(4, 16, 16, 128)],
        [(4, 34, 32, 128), (6, 32, 32, 128), (32, 32, 128)],
        flops=20_000_000,
    )(own)
    to_near, to_far, rim_rows = call(pack_kernel, [(4, 4, 24, 128)] * 2 + [(4, 32, 8, 128)], [])(
        to_right, to_left, from_near, from_far
    )
    from_far = lax.ppermute(to_far, both, far_y)
    from_near = lax.ppermute(to_near, "gy", swap_near)
    two, main, edges_rim = call(
        rows_edge_kernel,
        [(3, 34, 24, 128), (4, 8, 8, 128), (4, 16, 8, 128)],
        [(4, 34, 24, 128), (3, 34, 24, 128), (6, 32, 24, 128), (32, 24, 128)]
        + [(4, 16, 16, 128), (512, 128)],
        flops=10_000_000,
    )(own, rim_rows, own_one, own_two, halves)
    main_near = lax.ppermute(main, "gx", swap_near)
    main_far = lax.ppermute(main, both, far_x)
    rim, rim_one = call(
        rim_kernel,
        [(3, 16, 16, 128), (4, 4, 8, 128)],
        [(3, 18, 32, 128), (18, 32, 128)]
        + [(3, 18, 32, 128)] * 2
        + [(6, 16, 32, 128), (16, 32, 128)]
        + [(4, 8, 16, 128), (256, 128)],
        flops=10_000_000,
    )(edges, edges_rim, from_near, from_far)
    rim_near = lax.ppermute(rim_one, "gx", swap_near)
    rim_far = lax.ppermute(rim_one, both, far_x)
    sent, e_one, e_two = call(
        middle_kernel,
        [(CHIPS, 4, 128), (3, 16, 8, 128), (3, 8, 8, 128)],
        [(16, 24, 128), (18, 32, 128), (3, 16, 32, 128), (3, 18, 32, 128), (3, 18, 32, 128)]
        + [(6, 16, 32, 128), (16, 32, 128), (4, 8, 24, 128), (768, 128)]
        + [(10, 24, 128), (3, 10, 24, 128), (3, 10, 24, 128), (3, 8, 8, 128), (8, 8, 128)]
        + [(7, 8, 16, 128)],
    )(main, main_near, main_far, rim_one, rim_near, rim_far)
    groups = [[i for i in range(NX * NY) if i % 2 == core] for core in range(2)]
    mine = lax.all_to_all(
        sent, ("gx", "gy"), split_axis=0, concat_axis=0, axis_index_groups=groups, tiled=True
    )
    (base,) = call(base_kernel, [(3, 32, 16, 128)], [(192, 128), (3, 16, 16, 128)])(two, rim, e_one, e_two)
    other = lax.ppermute(mine, "gy", swap_near)
    (out,) = call(
        top_kernel,
        [(3, 32, 16, 128)],
        [(4, 2, 128, 128), (3, 16, 16, 128), (2, 3, 8, 16, 128), (6, 16, 128), (6, 16, 16, 128)]
        + [(16, 16, 128), (4, 2, 16, 256), (3, 32, 16, 128), pltpu.SemaphoreType.DMA((6,))],
        out_specs=[ANY],
    )(mine.reshape(512, 128), other.reshape(512, 128), base)
    return out


def solution(mesh):
    return jax.shard_map(
        local,
        mesh=mesh,
        in_specs=(P(None, "gx", "gy"), P(None, None, "gx", "gy")),
        out_specs=P(None, None, "gx", "gy"),
        check_vma=False,
    )
```

```python
import jax
import jax.numpy as jnp
from jax import lax
from jax.experimental import pallas as pl
from jax.experimental.pallas import tpu as pltpu
from jax.sharding import PartitionSpec as P


F32 = jnp.float32
NX, NY, CHIPS = 16, 16, 128
STEP, WIDE = 16, 32
BETWEEN = 2.0 * 0.1 / 1.1
ANY = pl.BlockSpec(memory_space=pltpu.HBM)


def dot_exact(a, b):
    high = a.astype(jnp.bfloat16)
    low = (a - high.astype(F32)).astype(jnp.bfloat16)
    b = b.astype(jnp.bfloat16)
    return jnp.dot(
        jnp.concatenate([high, low], axis=1), jnp.concatenate([b, b], axis=0), preferred_element_type=F32
    )


def iota(shape, dim):
    return lax.broadcasted_iota(jnp.int32, shape, dim)


def roll(x, shift, axis=1):
    shift = shift % x.shape[axis]
    return x if shift == 0 else pltpu.roll(x, shift, axis)


def turn(x, shift):
    return pltpu.roll(x, lax.rem(shift + 256, 128), 1)


def recip(x):
    guess = pl.reciprocal(x, approx=True)
    return guess * (2.0 - x * guess)


def inner(index):
    return (index > 0) & (index < 15)


def call(kernel, outs, scratch, flops=1_000_000, **kw):
    return pl.pallas_call(
        kernel,
        out_shape=[jax.ShapeDtypeStruct(s, F32) for s in outs],
        scratch_shapes=[pltpu.VMEM(s, F32) if isinstance(s, tuple) else s for s in scratch],
        compiler_params=pltpu.CompilerParams(vmem_limit_bytes=32 * 1024 * 1024),
        cost_estimate=pl.CostEstimate(flops=flops, bytes_accessed=4_000_000, transcendentals=0),
        **kw,
    )


def loop(count, body, unroll=1):
    def step(i, carry):
        body(i)
        return carry

    lax.fori_loop(0, count, step, 0, unroll=unroll)


def weigh(weights, values):
    parts = [w * v for w, v in zip(weights, values)]
    while len(parts) > 1:
        parts = [sum(parts[i : i + 2][1:], parts[i]) for i in range(0, len(parts), 2)]
    return parts[0]


def rows_kernel(guess, labels, near, far, own, phase, sems):
    even = lax.rem(lax.axis_index("gx"), 2) == 0
    near_row, far_row = jnp.where(even, 13, 0), jnp.where(even, 0, 13)
    copies = [pltpu.make_async_copy(labels, phase, sems.at[3])]
    for f in range(3):
        copies.append(pltpu.make_async_copy(guess.at[f], own.at[f], sems.at[f]))
    for copy in copies:
        copy.start()
    copies[0].wait()
    own[3] = jnp.where(phase[...] == 1, 0.0, 1.0).astype(F32)
    flat = own.reshape(4 * 32 * 16, 128)
    for ch in (3, 0, 1, 2):
        if ch < 3:
            copies[ch + 1].wait()
        for row in range(3):
            near[3 * ch + row] = flat[pl.ds(512 * ch + near_row + row, 32, stride=16), :]
            far[3 * ch + row] = flat[pl.ds(512 * ch + far_row + row, 32, stride=16), :]


def pack_kernel(to_right, to_left, x_near, x_far, near, far, rim):
    first_core = lax.rem(lax.axis_index("gy"), 2) == 0
    even = lax.rem(lax.axis_index("gx"), 2) == 0
    near_row, far_row = jnp.where(even, 0, 5), jnp.where(even, 5, 0)
    has_far = inner(lax.axis_index("gx"))
    flat = rim.reshape(4 * 32 * 8, 128)
    for ch in range(4):
        for row in range(3):
            flat[pl.ds(256 * ch + near_row + row, 32, stride=8), :] = x_near[3 * ch + row]
            flat[pl.ds(256 * ch + far_row + row, 32, stride=8), :] = jnp.where(has_far, x_far[3 * ch + row], 0.0)

    def some(low):
        for ch in range(4):
            right, left = pack_planes(lambda z: rim[ch, z], low, (8, 128))
            for at, right, left in (
                (slice(0, 16), to_right[ch, low], to_left[ch, low]),
                (slice(16, 24), right, left),
            ):
                near[ch, low, at, :] = jnp.where(first_core, right, left)
                far[ch, low, at, :] = jnp.where(first_core, left, right)

    loop(4, some, 4)


def pack_planes(plane, low, shape):
    group = iota(shape, 1) // 16
    right = left = jnp.zeros(shape, F32)
    for h in range(8):
        moved = roll(plane(4 * h + low), 16 * h + 16)
        right = jnp.where(group == h, moved, right)
        left = jnp.where(group == (h + 1) % 8, moved, left)
    return right, left


def edge_columns(plane, z, shape):
    lane = iota(shape, 1)
    value = jnp.zeros(shape, F32)
    for half in range(2):
        source = plane(z + 16 * half)
        base = 64 * half
        value = jnp.where((lane >= base) & (lane < base + 7), roll(source, base + 7), value)
        value = jnp.where((lane >= base + 57) & (lane < base + 64), roll(source, base + 57), value)
    return value


def six_of(ref, lead, z, first, count):
    own = ref[(*lead, z, pl.ds(first, count), slice(None))]
    return own, (
        ref[(*lead, z, pl.ds(first - 1, count), slice(None))],
        ref[(*lead, z, pl.ds(first + 1, count), slice(None))],
        roll(own, 1),
        roll(own, -1),
        ref[(*lead, z - 1, pl.ds(first, count), slice(None))],
        ref[(*lead, z + 1, pl.ds(first, count), slice(None))],
    )


def block_of(ref, lead, z, planes, first, count):
    rows = pl.ds(first, count)
    own = [ref[(*lead, z + k, rows, slice(None))] for k in range(-1, planes + 1)]
    result = []
    for k in range(planes):
        value = own[k + 1]
        six = (
            ref[(*lead, z + k, pl.ds(first - 1, count), slice(None))],
            ref[(*lead, z + k, pl.ds(first + 1, count), slice(None))],
            roll(value, 1),
            roll(value, -1),
            own[k],
            own[k + 2],
        )
        result.append((value, six))
    return result


def fine_weights(own, six, omega):
    base, slope = 1.0 + (BETWEEN - 1.0) * own, (BETWEEN - 1.0) + (1.1 - 2.0 * BETWEEN) * own
    total = (six[0] + six[1]) + (six[2] + six[3]) + (six[4] + six[5])
    diag = 6.0 * base + slope * total
    gain = omega * recip(diag)
    base, slope = gain * base, gain * slope
    return [base + slope * other for other in six], 1.25 * diag


def fine_sweep(w, f, own, six):
    return (0.2 * own + (w[2 * f + 1] - w[2 * f])) + weigh(w, six)


def fine_left(w, f, own, six, diag):
    return (((w[2 * f + 1] - w[2 * f]) - 0.8 * own) + weigh(w, six)) * diag


def fine_sweeps(planes, windows, start, share, one, two, weights, diags, halves, omega, wrap, keep, size):
    first, count = windows[0]

    def first_sweep(step):
        z = size * step
        w = []
        for k, (own, six) in enumerate(block_of(share, (), z + 1, size, first, count)):
            now, diag = fine_weights(own, six, omega)
            diags[z + k, pl.ds(first, count), :] = diag
            for i in range(6):
                weights[i, z + k, pl.ds(first, count), :] = now[i]
            w.append(now)
        for f in range(3):
            for k, (own, six) in enumerate(block_of(start, (f,), z + 1, size, first, count)):
                one[f, z + k + 1, pl.ds(first, count), :] = fine_sweep(w[k], f, own, six)

    loop(planes // size, first_sweep)
    wrap(one)
    second, count2 = windows[1]

    def second_sweep(step):
        z = size * step
        w = [[weights[i, z + k, pl.ds(second, count2), :] for i in range(6)] for k in range(size)]
        for f in range(3):
            for k, (own, six) in enumerate(block_of(one, (f,), z + 1, size, second, count2)):
                two[f, z + k + 1, pl.ds(second, count2), :] = fine_sweep(w[k], f, own, six)

    loop(planes // size, second_sweep)
    wrap(two)

    def residual(step):
        z = size * step
        w = [[weights[i, z + k, 8:24, :] for i in range(6)] for k in range(size)]
        diag = [diags[z + k, 8:24, :] for k in range(size)]
        for f in range(3):
            values = []
            for k, (own, six) in enumerate(block_of(two, (f,), z + 1, size, 8, 16)):
                if keep is not None:
                    keep[f, z + k] = own
                values.append(fine_left(w[k], f, own, six, diag[k]))
            for pair in range(size // 2):
                halves[f, size // 2 * step + pair] = values[2 * pair] + values[2 * pair + 1]
        for pair in range(size // 2):
            at = z + 2 * pair + 1
            halves[3, size // 2 * step + pair] = share[at, 8:24, :] + share[at + 1, 8:24, :]

    loop(planes // size, residual)


def own_kernel(own, one, two, halves, to_right, to_left, edges, held, weights, diags):
    zero = jnp.zeros((32, 128), F32)
    for z in (0, 33):
        for ch in range(4):
            held[ch, z] = zero
        for ref in (one, two):
            for f in range(3):
                ref[f, z] = zero

    def plane(z):
        for ch in range(4):
            held[ch, z + 1, 8:24, :] = own[ch, z]

    loop(32, plane, 8)
    fine_sweeps(
        32, [(8, 16)] * 2, held, held.at[3], one, two, weights, diags, halves, 0.8, lambda ref: None, None, 8
    )

    def some(low):
        for ch in range(4):
            to_right[ch, low], to_left[ch, low] = pack_planes(lambda z: own[ch, z], low, (16, 128))

    loop(4, some, 2)

    def edge(z):
        for ch in range(4):
            edges[ch, z] = edge_columns(lambda at: own[ch, at], z, (16, 128))

    loop(16, edge, 8)


def rows_edge_kernel(own, rim, own_one, own_two, own_halves, two, packed, edges, start, one, weights, diags, halves, pooled):
    gx = lax.axis_index("gx")
    zero = jnp.zeros((24, 128), F32)
    for z in (0, 33):
        for ch in range(4):
            start[ch, z] = zero
        for ref in (one, two):
            for f in range(3):
                ref[f, z] = zero

    def fill(z):
        for ch in range(4):
            start[ch, z + 1, 0:8, :] = own[ch, z, 8:16, :]
            start[ch, z + 1, 8:16, :] = rim[ch, z]
            start[ch, z + 1, 16:24, :] = own[ch, z, 0:8, :]
        for f in range(3):
            for ref, source in ((one, own_one), (two, own_two)):
                ref[f, z + 1, 0:8, :] = source[f, z + 1, 16:24, :]
                ref[f, z + 1, 16:24, :] = source[f, z + 1, 8:16, :]

    loop(32, fill, 16)
    upper = iota((8, 128), 0) < 4

    def both(ref, lead, step, shift=0):
        high = ref[(*lead, pl.ds(8 - step + shift, 8), slice(None))]
        low = ref[(*lead, pl.ds(8 + step + shift, 8), slice(None))]
        return jnp.where(upper, high, low)

    def block_both(ref, f, z, step):
        own = [both(ref, (f, z + k), step) for k in range(-1, WIDE + 1)]
        result = []
        for k in range(WIDE):
            value = own[k + 1]
            low, high = both(ref, (f, z + k), step, -1), both(ref, (f, z + k), step, 1)
            result.append((value, (low, high, roll(value, 1), roll(value, -1), own[k], own[k + 2])))
        return result

    def put(ref, f, z, step, value):
        ref[f, z, pl.ds(8 - step, 4), :] = value[0:4]
        ref[f, z, pl.ds(12 + step, 4), :] = value[4:8]

    row = iota((16, 128), 0) + 5
    low, high = jnp.where(gx > 0, 1, 0), jnp.where(gx < NX - 1, 1, 0)
    inside = jnp.where((row >= 8) & (row < 12), high, jnp.where((row >= 12) & (row < 16), low, 1))
    omega = 0.8 * inside.astype(F32)

    def weigh_all(step):
        z = WIDE * step
        for k, (value, six) in enumerate(block_of(start, (3,), z + 1, WIDE, 5, 16)):
            w, diag = fine_weights(value, six, omega)
            diags[z + k, 5:21, :] = diag
            for i in range(6):
                weights[i, z + k, 5:21, :] = w[i]

    loop(32 // WIDE, weigh_all)

    for step, source, target in ((1, start, one), (2, one, two)):

        def sweep(block):
            z = WIDE * block
            w = [[both(weights, (i, z + k), step) for i in range(6)] for k in range(WIDE)]
            for f in range(3):
                for k, (value, six) in enumerate(block_both(source, f, z + 1, step)):
                    put(target, f, z + k + 1, step, fine_sweep(w[k], f, value, six))

        loop(32 // WIDE, sweep)

    sub = iota((8, 128), 0)

    def residual(block):
        z = WIDE * block
        w = [[both(weights, (i, z + k), 3) for i in range(6)] for k in range(WIDE)]
        diag = [both(diags, (z + k,), 3) for k in range(WIDE)]
        for f in range(3):
            values = []
            for k, (value, six) in enumerate(block_both(two, f, z + 1, 3)):
                values.append(fine_left(w[k], f, value, six, diag[k]))
            for k in range(WIDE // 2):
                pair = WIDE // 2 * block + k
                value = values[2 * k] + values[2 * k + 1]
                halves[f, pair, 0:8, :] = jnp.where(sub < 3, roll(value, 3, 0), own_halves[f, pair, 0:8, :])
                halves[f, pair, 8:16, :] = jnp.where(sub >= 5, roll(value, 5, 0), own_halves[f, pair, 8:16, :])
        for k in range(WIDE // 2):
            halves[3, WIDE // 2 * block + k] = own_halves[3, WIDE // 2 * block + k]

    loop(32 // WIDE, residual)
    source, target = iota((128, 128), 0), iota((128, 128), 1)
    value = None
    for half in range(2):
        pool = jnp.where(source // 2 + 64 * half == target, 0.125, 0.0)
        part = dot_exact(halves[:, 8 * half : 8 * half + 8].reshape(512, 128), pool)
        value = part if value is None else value + part
    pooled[...] = value
    packed[...] = (pooled[pl.ds(0, 256, stride=2), :] + pooled[pl.ds(1, 256, stride=2), :]).reshape(4, 8, 8, 128)

    def edge(z):
        for ch in range(4):
            edges[ch, z] = edge_columns(lambda at: rim[ch, at], z, (8, 128))

    loop(16, edge, 16)


def rim_kernel(
    edges, edges_rim, near, far, field, packed,
    start, share, one, two, weights, diags, halves, pooled,
):
    gx, gy = lax.axis_index("gx"), lax.axis_index("gy")
    lane = iota((24, 128), 1)
    part = lane % 64
    is_after = (part >= 7) & (part < 22)
    is_before = (part >= 42) & (part < 57)
    first_core = lax.rem(gy, 2) == 0

    def unpack(low):
        for ch in range(4):
            target = start.at[ch] if ch < 3 else share
            from_near, from_far = near[ch, low], jnp.where(inner(gy), far[ch, low], 0.0)
            from_right = jnp.where(first_core, from_near, from_far)
            from_left = jnp.where(first_core, from_far, from_near)
            for h in range(4):
                z = 4 * h + low
                after_y = roll(from_right, 7 - 16 * (h + 1))
                before_y = roll(from_left, 41 - 16 * h)
                own = jnp.concatenate([edges[ch, z], edges_rim[ch, z]], axis=0)
                value = jnp.where(is_after, after_y, jnp.where(is_before, before_y, own))
                target[z + 1, 8:24, :] = value[0:16]
                target[z + 1, 0:8, :] = value[16:24]
                target[z + 1, 24:32, :] = value[16:24]

    loop(4, unpack, 4)

    half_of = iota((32, 128), 1)

    def wrap_one(ref):
        ref[0] = jnp.where(half_of >= 64, roll(ref[16], 64), 0.0)
        ref[17] = jnp.where(half_of < 64, roll(ref[1], 64), 0.0)

    def wrap(ref):
        for f in range(3):
            wrap_one(ref.at[f])

    wrap_one(share)
    wrap(start)
    row = iota((24, 128), 0) + 6
    low, high = jnp.where(gx > 0, 1, 0), jnp.where(gx < NX - 1, 1, 0)
    inside_x = jnp.where(row < 8, low, jnp.where(row >= 24, high, 1))
    inside_y = jnp.where(
        part < 32,
        jnp.where((part < 7) | (gy < NY - 1), 1, 0),
        jnp.where((part >= 57) | (gy > 0), 1, 0),
    )
    omega = 0.8 * (inside_x * inside_y).astype(F32)
    fine_sweeps(
        16, [(6, 24), (7, 24)], start, share, one, two, weights, diags, halves, omega, wrap, field, STEP
    )

    source, target = iota((128, 128), 0), iota((128, 128), 1)
    spot = source % 64
    column = jnp.where(spot < 32, 121 + spot, 71 + spot) // 2
    to = jnp.where(spot < 32, column - 62, column - 48)
    keep = ((spot < 32) & (to >= 0) & (to < 9)) | ((spot >= 32) & (to >= 9) & (to < 18))
    mixed = halves[...].reshape(4, 4, 2, 16, 128)
    value = None
    for odd in range(2):
        pool = jnp.where(keep & (to + 64 * odd + 32 * (source // 64) == target), 0.125, 0.0)
        part = dot_exact(mixed[:, :, odd].reshape(256, 128), pool)
        value = part if value is None else value + part
    pooled[...] = value
    packed[...] = (pooled[pl.ds(0, 128, stride=2), :] + pooled[pl.ds(1, 128, stride=2), :]).reshape(4, 4, 8, 128)


def base_kernel(two, rim, e_one, e_two, base, wide, spread):
    copy = jnp.where(iota((128, 128), 0) == iota((128, 128), 1) // 2, 1.0, 0.0)
    value = dot_exact(e_two[...].reshape(192, 128), copy)
    for block in range(24):
        rows = value[8 * block : 8 * block + 4, :]
        wide[pl.ds(8 * block, 4, stride=2), :] = rows
        wide[pl.ds(8 * block + 1, 4, stride=2), :] = rows
    value = e_one[...].reshape(24, 2, 8, 128) + wide[...].reshape(24, 1, 8, 128)
    value = dot_exact(value.reshape(384, 128), copy)
    flat = spread.reshape(768, 128)
    for block in range(48):
        rows = value[8 * block : 8 * block + 8, :]
        flat[pl.ds(16 * block, 8, stride=2), :] = rows
        flat[pl.ds(16 * block + 1, 8, stride=2), :] = rows
    lane = iota((16, 128), 1)

    def pair(k):
        for f in range(3):
            for z in (2 * k, 2 * k + 1):
                value = rim[f, z]
                for half in range(2):
                    low = roll(value, -57 - 64 * half)
                    high = roll(value, 121 - 64 * half)
                    at = z + 16 * half
                    own = jnp.concatenate([two[f, at + 1, 16:24, :], two[f, at + 1, 0:8, :]], axis=0)
                    own = jnp.where(lane < 3, low, jnp.where(lane >= 125, high, own))
                    base[f, at] = own + spread[f, k + 8 * half]

    loop(8, pair, 4)


def resist(share):
    return recip(2.0 - 1.8 * share)


def level_weights(own, six, omega):
    faces = [recip(own + other) for other in six]
    diag = (faces[0] + faces[1]) + (faces[2] + faces[3]) + (faces[4] + faces[5])
    gain = omega * recip(diag)
    return gain, [gain * w for w in faces], diag


def middle_kernel(
    main, main_near, main_far, rim, rim_near, rim_far, sent, e_one, e_two,
    share, rest, rhs, first, second, weights, diags, halves, pooled,
    rest2, first2, second2, rhs2, share2, weights2,
):
    gx, gy = lax.axis_index("gx"), lax.axis_index("gy")
    low_x, high_x = jnp.where(gx > 0, 1, 0), jnp.where(gx < NX - 1, 1, 0)
    low_y, high_y = jnp.where(gy > 0, 1, 0), jnp.where(gy < NY - 1, 1, 0)

    for f in range(3):
        for ref in (first, second):
            ref[f, 0] = jnp.zeros((32, 128), F32)
            ref[f, 17] = jnp.zeros((32, 128), F32)
    for z in (0, 17):
        rest[z] = jnp.full((32, 128), 0.5, F32)
    lane = iota((8, 128), 1)
    even = lax.rem(gx, 2) == 0
    near_row, far_row = jnp.where(even, 16, 0), jnp.where(even, 0, 16)
    starts = (pl.multiple_of(near_row, 8), pl.multiple_of(far_row, 8), 8)

    sources = zip(starts, ((main_near, rim_near), (main_far, rim_far), (main, rim)))
    sources = list(sources)
    has_far = inner(gx)

    def fill(q):
        for odd in range(2):
            for half in range(2):
                z = 2 * q + odd + 8 * half
                base = 64 * odd + 32 * half
                for at, (middle, outer) in sources:
                    for ch in range(4):
                        edge, body = outer[ch, q], middle[ch, 2 * q + odd]
                        if outer is rim_far:
                            edge, body = jnp.where(has_far, edge, 0.0), jnp.where(has_far, body, 0.0)
                        value = jnp.where(lane < 62, roll(body, 64 * half), roll(edge, 62 - base))
                        value = jnp.where((lane >= 96) | (lane < 2), roll(edge, 112 - base), value)
                        if ch < 3:
                            rhs[ch, z, pl.ds(at, 8), :] = value
                        else:
                            share[z, pl.ds(at, 8), :] = value
                            rest[z + 1, pl.ds(at, 8), :] = resist(value)
                rest[z + 1, 24:32, :] = jnp.full((8, 128), 0.5, F32)

    loop(4, fill, 4)

    row, lane = iota((24, 128), 0) + 1, iota((24, 128), 1)
    in_x = jnp.where(row < 8, low_x, jnp.where(row >= 16, high_x, 1))
    in_y = jnp.where(lane < 64, 1, jnp.where(lane < 96, high_y, low_y))
    omega = 0.8 * (in_x * in_y).astype(F32)

    def start(step):
        z = STEP * step
        for k, (own, six) in enumerate(block_of(rest, (), z + 1, STEP, 1, 24)):
            gain, w, diag = level_weights(own, six, omega)
            for i in range(6):
                weights[i, z + k, 1:25, :] = w[i]
            diags[z + k, 1:25, :] = (1.25 * 0.25) * diag
            for f in range(3):
                first[f, z + k + 1, 1:25, :] = (4.0 * gain) * rhs[f, z + k, 1:25, :]

    loop(16 // STEP, start)

    def sweep(step):
        z = STEP * step
        w = [[weights[i, z + k, 3:27, :] for i in range(6)] for k in range(STEP)]
        for f in range(3):
            for k, (own, six) in enumerate(block_of(first, (f,), z + 1, STEP, 3, 24)):
                second[f, z + k + 1, 3:27, :] = 1.2 * own + weigh(w[k], six)

    loop(16 // STEP, sweep)

    def left(step):
        z = STEP * step
        w = [[weights[i, z + k, 4:20, :] for i in range(6)] for k in range(STEP)]
        diag = [diags[z + k, 4:20, :] for k in range(STEP)]
        for f in range(3):
            values = []
            for k, (own, six) in enumerate(block_of(second, (f,), z + 1, STEP, 4, 16)):
                change = (first[f, z + k + 1, 4:20, :] - 0.8 * own) + weigh(w[k], six)
                values.append(change * diag[k])
                e_one[f, z + k] = second[f, z + k + 1, 8:16, :]
            for k in range(STEP // 2):
                halves[f, STEP // 2 * step + k, 0:16, :] = values[2 * k] + values[2 * k + 1]
                halves[f, STEP // 2 * step + k, 16:24, :] = jnp.zeros((8, 128), F32)
        for k in range(STEP // 2):
            halves[3, STEP // 2 * step + k] = share[z + 2 * k] + share[z + 2 * k + 1]

    loop(16 // STEP, left)

    source, target = iota((128, 128), 0), iota((128, 128), 1)
    pool = jnp.where(source // 2 + jnp.where(source >= 96, 64, 0) == target, 0.125, 0.0)
    pooled[...] = dot_exact(halves[...].reshape(4 * 8 * 24, 128), pool)
    for z in (0, 9):
        rest2[z] = jnp.full((24, 128), 0.5, F32)
        for f in range(3):
            first2[f, z] = jnp.zeros((24, 128), F32)
            second2[f, z] = jnp.zeros((24, 128), F32)
    for z in range(8):
        for f in range(3):
            base = (f * 8 + z) * 24
            rhs2[f, z] = pooled[pl.ds(base, 8, stride=2), :] + pooled[pl.ds(base + 1, 8, stride=2), :]
        base = (3 * 8 + z) * 24
        value = pooled[pl.ds(base + 2, 8, stride=2), :] + pooled[pl.ds(base + 3, 8, stride=2), :]
        rest2[z + 1, 0:8, :] = resist(value)
        value = pooled[pl.ds(base + 8, 8, stride=2), :] + pooled[pl.ds(base + 9, 8, stride=2), :]
        rest2[z + 1, 3:11, :] = resist(value)
        share2[z] = value

    row, lane = iota((8, 128), 0) + 1, iota((8, 128), 1)
    in_x = jnp.where(row < 3, low_x, jnp.where(row >= 7, high_x, 1))
    in_y = jnp.where(lane < 32, 1, jnp.where(lane < 96, high_y, low_y))
    omega2 = 0.8 * (in_x * in_y).astype(F32)

    for z, (own, six) in enumerate(block_of(rest2, (), 1, 8, 1, 8)):
        gain, w, diag = level_weights(own, six, omega2)
        for i in range(6):
            weights2[i, z, 1:9, :] = w[i]
        weights2[6, z, 1:9, :] = (1.25 * 0.0625) * diag
        for f in range(3):
            first2[f, z + 1, 1:9, :] = (16.0 * gain) * rhs2[f, z]
    w = [[weights2[i, z, 2:10, :] for i in range(6)] for z in range(8)]
    for f in range(3):
        for z, (own, six) in enumerate(block_of(first2, (f,), 1, 8, 2, 8)):
            second2[f, z + 1, 2:10, :] = 1.2 * own + weigh(w[z], six)
    w = [[weights2[i, z, 3:11, :] for i in range(7)] for z in range(8)]
    own_row = iota((8, 128), 0) < 4
    parts = [{} for pair in range(4)]
    for f in range(3):
        for z, (own, six) in enumerate(block_of(second2, (f,), 1, 8, 3, 8)):
            e_two[f, z] = own
            change = (first2[f, z + 1, 3:11, :] - 0.8 * own) + weigh(w[z], six)
            value = jnp.where(own_row, change * w[z][6], 0.0)
            sums = parts[z // 2]
            sums[f] = value if z % 2 == 0 else sums[f] + value
    for z in range(8):
        value = jnp.where(own_row, share2[z], 0.0)
        sums = parts[z // 2]
        sums[3] = value if z % 2 == 0 else sums[3] + value

    pool = jnp.where((source < 32) & (source // 2 == target % 16), 0.125, 0.0)
    rows = jnp.concatenate([parts[pair][ch] for ch in range(4) for pair in range(4)], axis=0)
    spread = dot_exact(rows, pool)
    at, to = iota((32, 128), 0), iota((32, 128), 1)
    keep = (at // 8 == to // 32) & ((at % 8) // 2 == (to // 16) % 2)
    result = jnp.concatenate(
        [
            jnp.sum(jnp.where(keep, spread[32 * ch : 32 * ch + 32], 0.0), axis=0, keepdims=True)
            for ch in range(4)
        ],
        axis=0,
    )
    for copy in range(CHIPS):
        sent[copy] = result


def swap_blocks(x):
    sub, group = iota((8, 128), 0), iota((8, 128), 1) // 16
    for bit in (4, 2, 1):
        up = roll(roll(x, -bit, 0), 16 * bit)
        down = up if bit == 4 else roll(roll(x, bit, 0), -16 * bit)
        sub_set, group_set = (sub & bit) != 0, (group & bit) != 0
        x = jnp.where(sub_set == group_set, x, jnp.where(sub_set, down, up))
    return x


def top_kernel(
    mine, other, base, out,
    natural, first, second, four, weights, diags, lefts, final, sems,
):
    gx, gy = lax.axis_index("gx"), lax.axis_index("gy")
    first_core = lax.rem(gy, 2) == 0
    lane, sub = iota((16, 128), 1), iota((16, 128), 0)
    cells = [(z, x, half) for z in range(4) for x in range(2) for half in range(2)]

    def lay(g):
        for ch in range(4):
            rows = pl.ds(32 * g + ch, 8, stride=4)
            pair = mine[rows, :], other[rows, :]
            natural[ch, 0, pl.ds(pl.multiple_of(8 * g, 8), 8), :] = swap_blocks(
                jnp.where(first_core, pair[0], pair[1])
            )
            natural[ch, 1, pl.ds(pl.multiple_of(8 * g, 8), 8), :] = swap_blocks(
                jnp.where(first_core, pair[1], pair[0])
            )

    loop(16, lay, 4)
    flat = natural.reshape(1024, 128)

    def plane(ch, z, x, half):
        return flat[pl.ds((ch * 2 + half) * 128 + z * 2 + x, 16, stride=8), :]

    def neighbours(at, z, x, half, outside):
        own, other = at(z, x, half), at(z, 1 - x, half)
        beside = at(z, x, 1 - half)
        shifted = roll(other, 1 if x == 0 else -1, 0)
        low, high = (shifted, other) if x == 0 else (other, shifted)
        left, right = roll(own, 1), roll(own, -1)
        left = jnp.where(lane % 16 == 0, roll(beside, 1 if half == 0 else -15), left)
        right = jnp.where(lane % 16 == 15, roll(beside, 15 if half == 0 else -1), right)
        down = at(z - 1, x, half) if z > 0 else outside
        up = at(z + 1, x, half) if z < 3 else outside
        return own, [low, high, left, right, down, up]

    def edge_masks(x, half):
        return [
            sub > 0 if x == 0 else None,
            sub < 15 if x == 1 else None,
            lane > 0 if half == 0 else None,
            lane < 127 if half == 1 else None,
            None,
            None,
        ]

    def key(z, x, half):
        return (z * 2 + x) * 2 + half

    shares = {c: plane(3, *c) for c in cells}
    rests = {c: resist(shares[c]) for c in cells}
    outside, zeros = jnp.full((16, 128), 0.5, F32), jnp.zeros((16, 128), F32)
    for z, x, half in cells:
        own, six = neighbours(lambda *c: rests[c], z, x, half, outside)
        masks = edge_masks(x, half)
        six = [s if m is None else jnp.where(m, s, 0.5) for s, m in zip(six, masks)]
        gain, w, diag = level_weights(own, six, 0.8)
        at = key(z, x, half)
        for i in range(6):
            weights[i, at] = w[i] if masks[i] is None else jnp.where(masks[i], w[i], 0.0)
        diags[at] = (1.25 * 0.25**3) * diag
        for f in range(3):
            first[f, at] = (64.0 * gain) * plane(f, z, x, half)

    for z, x, half in cells:
        at = key(z, x, half)
        w = [weights[i, at] for i in range(6)]
        for f in range(3):
            own, six = neighbours(lambda *c: first[f, key(*c)], z, x, half, zeros)
            second[half, f, z * 2 + x] = 1.2 * own + weigh(w, six)

    for z4 in range(2):
        for half in range(2):
            sums = [None] * 4
            for z in (2 * z4, 2 * z4 + 1):
                for x in range(2):
                    at = key(z, x, half)
                    w = [weights[i, at] for i in range(6)]
                    diag = diags[at]
                    for f in range(3):
                        own, six = neighbours(
                            lambda c, d, e: second[e, f, c * 2 + d], z, x, half, zeros
                        )
                        value = ((first[f, at] - 0.8 * own) + weigh(w, six)) * diag
                        sums[f] = value if sums[f] is None else sums[f] + value
                    share = shares[z, x, half]
                    sums[3] = share if sums[3] is None else sums[3] + share
            for ch in range(4):
                lefts[ch, z4, :, 128 * half : 128 * half + 128] = sums[ch]

    source = iota((256, 128), 0)
    column = ((source % 128) // 16) * 16 + (source // 128) * 8 + (source % 16) // 2
    pool = jnp.where(column == iota((256, 128), 1), 0.125, 0.0)
    level = dot_exact(lefts[...].reshape(128, 256), pool)

    def coarsest(ch, z):
        return level[(ch * 2 + z) * 16 : (ch * 2 + z) * 16 + 16, :]

    masks = [sub > 0, sub < 15, lane > 0, lane < 127]
    resists = [resist(coarsest(3, z)) for z in range(2)]
    gains, ws, ds = [], [], []
    for z in range(2):
        own, other = resists[z], resists[1 - z]
        six = [roll(own, 1, 0), roll(own, -1, 0), roll(own, 1), roll(own, -1)]
        six = [jnp.where(m, s, 0.5) for m, s in zip(masks, six)] + [other, outside]
        gain, w, diag = level_weights(own, six, 0.8)
        gains.append(gain)
        ds.append(diag)
        ws.append([jnp.where(m, v, 0.0) for m, v in zip(masks, w)] + [w[4]])
    whole = jnp.sum(ds[0] + ds[1], keepdims=True)

    def around(values, z):
        own, other = values[z], values[1 - z]
        return weigh(ws[z], (roll(own, 1, 0), roll(own, -1, 0), roll(own, 1), roll(own, -1), other))

    begin = [[256.0 * gains[z] * coarsest(f, z) for z in range(2)] for f in range(3)]
    values = begin
    for step in range(5):
        values = [
            [(0.2 * values[f][z] + begin[f][z]) + around(values[f], z) for z in range(2)] for f in range(3)
        ]
    shifts = []
    for f in range(3):
        change = [(begin[f][z] - 0.8 * values[f][z]) + around(values[f], z) for z in range(2)]
        shifts.append(jnp.sum(1.25 * (change[0] * ds[0] + change[1] * ds[1]), keepdims=True) / whole)
        for z in range(2):
            four[2 * f + z] = values[f][z]

    rows = four.reshape(96, 128)[pl.ds(gx, 6, stride=16), :]
    upper = jnp.concatenate([jnp.broadcast_to(rows[i : i + 1], (4, 128)) for i in range(6)], axis=0)
    flat = second.reshape(768, 128)
    halves = [flat[pl.ds(gx + 384 * half, 24, stride=16), :] for half in range(2)]
    three = turn(jnp.where(first_core, halves[0], halves[1]), -16 * lax.div(gy, 2))
    both = jnp.concatenate([turn(upper, -8 * gy), three], axis=1)
    both = jnp.concatenate([both, jnp.zeros((8, 256), F32)], axis=0)
    source, target = iota((256, 128), 0), iota((256, 128), 1)
    copy = jnp.where(source == jnp.where(source < 128, target // 16, 128 + target // 8), 1.0, 0.0)
    three = dot_exact(both, copy)

    copies = []
    for f in range(3):
        for z in range(4):
            for x in range(2):
                at = f * 8 + z * 2 + x
                value = jnp.broadcast_to(three[at : at + 1] + shifts[f], (8, 128))
                for k in range(8 * z, 8 * z + 8):
                    final[f, k, 8 * x : 8 * x + 8, :] = base[f, k, 8 * x : 8 * x + 8, :] + value
            if z % 2 == 1:
                part = (f, pl.ds(8 * z - 8, 16))
                copy = pltpu.make_async_copy(final.at[part], out.at[part], sems.at[len(copies)])
                copy.start()
                copies.append(copy)
    for copy in copies:
        copy.wait()


def local(labels, guess):
    swap_near = [(i, i ^ 1) for i in range(NY)]
    far_x, far_y = [], []
    for x in range(NX):
        for y in range(NY):
            across_x, across_y = x + 1 if x % 2 else x - 1, y + 1 if y % 2 else y - 1
            to = (across_x, y) if 0 <= across_x < NX else (x, y ^ 1)
            far_x.append((x * NY + y, to[0] * NY + to[1]))
            to = (x, across_y) if 0 <= across_y < NY else (x ^ 1, y)
            far_y.append((x * NY + y, to[0] * NY + to[1]))
    both = ("gx", "gy")
    to_near, to_far, own = call(
        rows_kernel,
        [(12, 32, 128)] * 2 + [(4, 32, 16, 128)],
        [pltpu.VMEM((32, 16, 128), jnp.int32), pltpu.SemaphoreType.DMA((4,))],
        in_specs=[ANY, ANY],
    )(pltpu.with_memory_space_constraint(guess, pltpu.HBM), pltpu.with_memory_space_constraint(labels, pltpu.HBM))
    from_near = lax.ppermute(to_near, "gx", swap_near)
    from_far = lax.ppermute(to_far, both, far_x)
    own_one, own_two, halves, to_right, to_left, edges = call(
        own_kernel,
        [(3, 34, 32, 128)] * 2 + [(4, 16, 16, 128)] + [(4, 4, 16, 128)] * 2 + [(4, 16, 16, 128)],
        [(4, 34, 32, 128), (6, 32, 32, 128), (32, 32, 128)],
        flops=20_000_000,
    )(own)
    to_near, to_far, rim_rows = call(pack_kernel, [(4, 4, 24, 128)] * 2 + [(4, 32, 8, 128)], [])(
        to_right, to_left, from_near, from_far
    )
    from_far = lax.ppermute(to_far, both, far_y)
    from_near = lax.ppermute(to_near, "gy", swap_near)
    two, main, edges_rim = call(
        rows_edge_kernel,
        [(3, 34, 24, 128), (4, 8, 8, 128), (4, 16, 8, 128)],
        [(4, 34, 24, 128), (3, 34, 24, 128), (6, 32, 24, 128), (32, 24, 128)]
        + [(4, 16, 16, 128), (512, 128)],
        flops=10_000_000,
    )(own, rim_rows, own_one, own_two, halves)
    main_near = lax.ppermute(main, "gx", swap_near)
    main_far = lax.ppermute(main, both, far_x)
    rim, rim_one = call(
        rim_kernel,
        [(3, 16, 16, 128), (4, 4, 8, 128)],
        [(3, 18, 32, 128), (18, 32, 128)]
        + [(3, 18, 32, 128)] * 2
        + [(6, 16, 32, 128), (16, 32, 128)]
        + [(4, 8, 16, 128), (256, 128)],
        flops=10_000_000,
    )(edges, edges_rim, from_near, from_far)
    rim_near = lax.ppermute(rim_one, "gx", swap_near)
    rim_far = lax.ppermute(rim_one, both, far_x)
    sent, e_one, e_two = call(
        middle_kernel,
        [(CHIPS, 4, 128), (3, 16, 8, 128), (3, 8, 8, 128)],
        [(16, 24, 128), (18, 32, 128), (3, 16, 32, 128), (3, 18, 32, 128), (3, 18, 32, 128)]
        + [(6, 16, 32, 128), (16, 32, 128), (4, 8, 24, 128), (768, 128)]
        + [(10, 24, 128), (3, 10, 24, 128), (3, 10, 24, 128), (3, 8, 8, 128), (8, 8, 128)]
        + [(7, 8, 16, 128)],
    )(main, main_near, main_far, rim_one, rim_near, rim_far)
    groups = [[i for i in range(NX * NY) if i % 2 == core] for core in range(2)]
    mine = lax.all_to_all(
        sent, ("gx", "gy"), split_axis=0, concat_axis=0, axis_index_groups=groups, tiled=True
    )
    (base,) = call(base_kernel, [(3, 32, 16, 128)], [(192, 128), (3, 16, 16, 128)])(two, rim, e_one, e_two)
    other = lax.ppermute(mine, "gy", swap_near)
    (out,) = call(
        top_kernel,
        [(3, 32, 16, 128)],
        [(4, 2, 128, 128), (3, 16, 16, 128), (2, 3, 8, 16, 128), (6, 16, 128), (6, 16, 16, 128)]
        + [(16, 16, 128), (4, 2, 16, 256), (3, 32, 16, 128), pltpu.SemaphoreType.DMA((6,))],
        out_specs=[ANY],
    )(mine.reshape(512, 128), other.reshape(512, 128), base)
    return out


def solution(mesh):
    return jax.shard_map(
        local,
        mesh=mesh,
        in_specs=(P(None, "gx", "gy"), P(None, None, "gx", "gy")),
        out_specs=P(None, None, "gx", "gy"),
        check_vma=False,
    )
```

```python
import jax
import jax.numpy as jnp
from jax import lax
from jax.experimental import pallas as pl
from jax.experimental.pallas import tpu as pltpu
from jax.sharding import PartitionSpec as P


F32 = jnp.float32
NX, NY, CHIPS = 16, 16, 128
STEP, WIDE = 16, 32
BETWEEN = 2.0 * 0.1 / 1.1
ANY = pl.BlockSpec(memory_space=pltpu.HBM)


def dot_exact(a, b):
    high = a.astype(jnp.bfloat16)
    low = (a - high.astype(F32)).astype(jnp.bfloat16)
    b = b.astype(jnp.bfloat16)
    return jnp.dot(
        jnp.concatenate([high, low], axis=1), jnp.concatenate([b, b], axis=0), preferred_element_type=F32
    )


def iota(shape, dim):
    return lax.broadcasted_iota(jnp.int32, shape, dim)


def roll(x, shift, axis=1):
    shift = shift % x.shape[axis]
    return x if shift == 0 else pltpu.roll(x, shift, axis)


def turn(x, shift):
    return pltpu.roll(x, lax.rem(shift + 256, 128), 1)


def recip(x):
    guess = pl.reciprocal(x, approx=True)
    return guess * (2.0 - x * guess)


def inner(index):
    return (index > 0) & (index < 15)


def call(kernel, outs, scratch, flops=1_000_000, **kw):
    return pl.pallas_call(
        kernel,
        out_shape=[jax.ShapeDtypeStruct(s, F32) for s in outs],
        scratch_shapes=[pltpu.VMEM(s, F32) if isinstance(s, tuple) else s for s in scratch],
        compiler_params=pltpu.CompilerParams(vmem_limit_bytes=32 * 1024 * 1024),
        cost_estimate=pl.CostEstimate(flops=flops, bytes_accessed=4_000_000, transcendentals=0),
        **kw,
    )


def loop(count, body, unroll=1):
    def step(i, carry):
        body(i)
        return carry

    lax.fori_loop(0, count, step, 0, unroll=unroll)


def weigh(weights, values):
    parts = [w * v for w, v in zip(weights, values)]
    while len(parts) > 1:
        parts = [sum(parts[i : i + 2][1:], parts[i]) for i in range(0, len(parts), 2)]
    return parts[0]


def rows_kernel(guess, labels, near, far, own, phase, sems):
    even = lax.rem(lax.axis_index("gx"), 2) == 0
    near_row, far_row = jnp.where(even, 13, 0), jnp.where(even, 0, 13)
    copies = [pltpu.make_async_copy(labels, phase, sems.at[3])]
    for f in range(3):
        copies.append(pltpu.make_async_copy(guess.at[f], own.at[f], sems.at[f]))
    for copy in copies:
        copy.start()
    copies[0].wait()
    own[3] = jnp.where(phase[...] == 1, 0.0, 1.0).astype(F32)
    flat = own.reshape(4 * 32 * 16, 128)
    for ch in (3, 0, 1, 2):
        if ch < 3:
            copies[ch + 1].wait()
        for row in range(3):
            near[3 * ch + row] = flat[pl.ds(512 * ch + near_row + row, 32, stride=16), :]
            far[3 * ch + row] = flat[pl.ds(512 * ch + far_row + row, 32, stride=16), :]


def pack_kernel(to_right, to_left, x_near, x_far, near, far, rim):
    first_core = lax.rem(lax.axis_index("gy"), 2) == 0
    even = lax.rem(lax.axis_index("gx"), 2) == 0
    near_row, far_row = jnp.where(even, 0, 5), jnp.where(even, 5, 0)
    has_far = inner(lax.axis_index("gx"))
    flat = rim.reshape(4 * 32 * 8, 128)
    for ch in range(4):
        for row in range(3):
            flat[pl.ds(256 * ch + near_row + row, 32, stride=8), :] = x_near[3 * ch + row]
            flat[pl.ds(256 * ch + far_row + row, 32, stride=8), :] = jnp.where(has_far, x_far[3 * ch + row], 0.0)

    def some(low):
        for ch in range(4):
            right, left = pack_planes(lambda z: rim[ch, z], low, (8, 128))
            for at, right, left in (
                (slice(0, 16), to_right[ch, low], to_left[ch, low]),
                (slice(16, 24), right, left),
            ):
                near[ch, low, at, :] = jnp.where(first_core, right, left)
                far[ch, low, at, :] = jnp.where(first_core, left, right)

    loop(4, some, 4)


def pack_planes(plane, low, shape):
    group = iota(shape, 1) // 16
    right = left = jnp.zeros(shape, F32)
    for h in range(8):
        moved = roll(plane(4 * h + low), 16 * h + 16)
        right = jnp.where(group == h, moved, right)
        left = jnp.where(group == (h + 1) % 8, moved, left)
    return right, left


def edge_columns(plane, z, shape):
    lane = iota(shape, 1)
    value = jnp.zeros(shape, F32)
    for half in range(2):
        source = plane(z + 16 * half)
        base = 64 * half
        value = jnp.where((lane >= base) & (lane < base + 7), roll(source, base + 7), value)
        value = jnp.where((lane >= base + 57) & (lane < base + 64), roll(source, base + 57), value)
    return value


def six_of(ref, lead, z, first, count):
    own = ref[(*lead, z, pl.ds(first, count), slice(None))]
    return own, (
        ref[(*lead, z, pl.ds(first - 1, count), slice(None))],
        ref[(*lead, z, pl.ds(first + 1, count), slice(None))],
        roll(own, 1),
        roll(own, -1),
        ref[(*lead, z - 1, pl.ds(first, count), slice(None))],
        ref[(*lead, z + 1, pl.ds(first, count), slice(None))],
    )


def block_of(ref, lead, z, planes, first, count):
    rows = pl.ds(first, count)
    own = [ref[(*lead, z + k, rows, slice(None))] for k in range(-1, planes + 1)]
    result = []
    for k in range(planes):
        value = own[k + 1]
        six = (
            ref[(*lead, z + k, pl.ds(first - 1, count), slice(None))],
            ref[(*lead, z + k, pl.ds(first + 1, count), slice(None))],
            roll(value, 1),
            roll(value, -1),
            own[k],
            own[k + 2],
        )
        result.append((value, six))
    return result


def fine_weights(own, six, omega):
    base, slope = 1.0 + (BETWEEN - 1.0) * own, (BETWEEN - 1.0) + (1.1 - 2.0 * BETWEEN) * own
    total = (six[0] + six[1]) + (six[2] + six[3]) + (six[4] + six[5])
    diag = 6.0 * base + slope * total
    gain = omega * recip(diag)
    base, slope = gain * base, gain * slope
    return [base + slope * other for other in six], 1.25 * diag


def fine_sweep(w, f, own, six):
    return (0.2 * own + (w[2 * f + 1] - w[2 * f])) + weigh(w, six)


def fine_left(w, f, own, six, diag):
    return (((w[2 * f + 1] - w[2 * f]) - 0.8 * own) + weigh(w, six)) * diag


def fine_sweeps(planes, windows, start, share, one, two, weights, diags, halves, omega, wrap, keep, size):
    first, count = windows[0]

    def first_sweep(step):
        z = size * step
        w = []
        for k, (own, six) in enumerate(block_of(share, (), z + 1, size, first, count)):
            now, diag = fine_weights(own, six, omega)
            diags[z + k, pl.ds(first, count), :] = diag
            for i in range(6):
                weights[i, z + k, pl.ds(first, count), :] = now[i]
            w.append(now)
        for f in range(3):
            for k, (own, six) in enumerate(block_of(start, (f,), z + 1, size, first, count)):
                one[f, z + k + 1, pl.ds(first, count), :] = fine_sweep(w[k], f, own, six)

    loop(planes // size, first_sweep)
    wrap(one)
    second, count2 = windows[1]

    def second_sweep(step):
        z = size * step
        w = [[weights[i, z + k, pl.ds(second, count2), :] for i in range(6)] for k in range(size)]
        for f in range(3):
            for k, (own, six) in enumerate(block_of(one, (f,), z + 1, size, second, count2)):
                two[f, z + k + 1, pl.ds(second, count2), :] = fine_sweep(w[k], f, own, six)

    loop(planes // size, second_sweep)
    wrap(two)

    def residual(step):
        z = size * step
        w = [[weights[i, z + k, 8:24, :] for i in range(6)] for k in range(size)]
        diag = [diags[z + k, 8:24, :] for k in range(size)]
        for f in range(3):
            values = []
            for k, (own, six) in enumerate(block_of(two, (f,), z + 1, size, 8, 16)):
                if keep is not None:
                    keep[f, z + k] = own
                values.append(fine_left(w[k], f, own, six, diag[k]))
            for pair in range(size // 2):
                halves[f, size // 2 * step + pair] = values[2 * pair] + values[2 * pair + 1]
        for pair in range(size // 2):
            at = z + 2 * pair + 1
            halves[3, size // 2 * step + pair] = share[at, 8:24, :] + share[at + 1, 8:24, :]

    loop(planes // size, residual)


def own_kernel(own, one, two, halves, to_right, to_left, edges, held, weights, diags):
    zero = jnp.zeros((32, 128), F32)
    for z in (0, 33):
        for ch in range(4):
            held[ch, z] = zero
        for ref in (one, two):
            for f in range(3):
                ref[f, z] = zero

    def plane(z):
        for ch in range(4):
            held[ch, z + 1, 8:24, :] = own[ch, z]

    loop(32, plane, 8)
    fine_sweeps(
        32, [(8, 16)] * 2, held, held.at[3], one, two, weights, diags, halves, 0.8, lambda ref: None, None, 8
    )

    def some(low):
        for ch in range(4):
            to_right[ch, low], to_left[ch, low] = pack_planes(lambda z: own[ch, z], low, (16, 128))

    loop(4, some, 2)

    def edge(z):
        for ch in range(4):
            edges[ch, z] = edge_columns(lambda at: own[ch, at], z, (16, 128))

    loop(16, edge, 8)


def rows_edge_kernel(own, rim, own_one, own_two, own_halves, two, packed, edges, start, one, weights, diags, halves, pooled):
    gx = lax.axis_index("gx")
    zero = jnp.zeros((24, 128), F32)
    for z in (0, 33):
        for ch in range(4):
            start[ch, z] = zero
        for ref in (one, two):
            for f in range(3):
                ref[f, z] = zero

    def fill(z):
        for ch in range(4):
            start[ch, z + 1, 0:8, :] = own[ch, z, 8:16, :]
            start[ch, z + 1, 8:16, :] = rim[ch, z]
            start[ch, z + 1, 16:24, :] = own[ch, z, 0:8, :]
        for f in range(3):
            for ref, source in ((one, own_one), (two, own_two)):
                ref[f, z + 1, 0:8, :] = source[f, z + 1, 16:24, :]
                ref[f, z + 1, 16:24, :] = source[f, z + 1, 8:16, :]

    loop(32, fill, 16)
    upper = iota((8, 128), 0) < 4

    def both(ref, lead, step, shift=0):
        high = ref[(*lead, pl.ds(8 - step + shift, 8), slice(None))]
        low = ref[(*lead, pl.ds(8 + step + shift, 8), slice(None))]
        return jnp.where(upper, high, low)

    def block_both(ref, f, z, step):
        own = [both(ref, (f, z + k), step) for k in range(-1, WIDE + 1)]
        result = []
        for k in range(WIDE):
            value = own[k + 1]
            low, high = both(ref, (f, z + k), step, -1), both(ref, (f, z + k), step, 1)
            result.append((value, (low, high, roll(value, 1), roll(value, -1), own[k], own[k + 2])))
        return result

    def put(ref, f, z, step, value):
        ref[f, z, pl.ds(8 - step, 4), :] = value[0:4]
        ref[f, z, pl.ds(12 + step, 4), :] = value[4:8]

    row = iota((16, 128), 0) + 5
    low, high = jnp.where(gx > 0, 1, 0), jnp.where(gx < NX - 1, 1, 0)
    inside = jnp.where((row >= 8) & (row < 12), high, jnp.where((row >= 12) & (row < 16), low, 1))
    omega = 0.8 * inside.astype(F32)

    def weigh_all(step):
        z = WIDE * step
        for k, (value, six) in enumerate(block_of(start, (3,), z + 1, WIDE, 5, 16)):
            w, diag = fine_weights(value, six, omega)
            diags[z + k, 5:21, :] = diag
            for i in range(6):
                weights[i, z + k, 5:21, :] = w[i]

    loop(32 // WIDE, weigh_all)

    for step, source, target in ((1, start, one), (2, one, two)):

        def sweep(block):
            z = WIDE * block
            w = [[both(weights, (i, z + k), step) for i in range(6)] for k in range(WIDE)]
            for f in range(3):
                for k, (value, six) in enumerate(block_both(source, f, z + 1, step)):
                    put(target, f, z + k + 1, step, fine_sweep(w[k], f, value, six))

        loop(32 // WIDE, sweep)

    sub = iota((8, 128), 0)

    def residual(block):
        z = WIDE * block
        w = [[both(weights, (i, z + k), 3) for i in range(6)] for k in range(WIDE)]
        diag = [both(diags, (z + k,), 3) for k in range(WIDE)]
        for f in range(3):
            values = []
            for k, (value, six) in enumerate(block_both(two, f, z + 1, 3)):
                values.append(fine_left(w[k], f, value, six, diag[k]))
            for k in range(WIDE // 2):
                pair = WIDE // 2 * block + k
                value = values[2 * k] + values[2 * k + 1]
                halves[f, pair, 0:8, :] = jnp.where(sub < 3, roll(value, 3, 0), own_halves[f, pair, 0:8, :])
                halves[f, pair, 8:16, :] = jnp.where(sub >= 5, roll(value, 5, 0), own_halves[f, pair, 8:16, :])
        for k in range(WIDE // 2):
            halves[3, WIDE // 2 * block + k] = own_halves[3, WIDE // 2 * block + k]

    loop(32 // WIDE, residual)
    source, target = iota((128, 128), 0), iota((128, 128), 1)
    value = None
    for half in range(2):
        pool = jnp.where(source // 2 + 64 * half == target, 0.125, 0.0)
        part = dot_exact(halves[:, 8 * half : 8 * half + 8].reshape(512, 128), pool)
        value = part if value is None else value + part
    pooled[...] = value
    packed[...] = (pooled[pl.ds(0, 256, stride=2), :] + pooled[pl.ds(1, 256, stride=2), :]).reshape(4, 8, 8, 128)

    def edge(z):
        for ch in range(4):
            edges[ch, z] = edge_columns(lambda at: rim[ch, at], z, (8, 128))

    loop(16, edge, 16)


def rim_kernel(
    edges, edges_rim, near, far, field, packed,
    start, share, one, two, weights, diags, halves, pooled,
):
    gx, gy = lax.axis_index("gx"), lax.axis_index("gy")
    lane = iota((24, 128), 1)
    part = lane % 64
    is_after = (part >= 7) & (part < 22)
    is_before = (part >= 42) & (part < 57)
    first_core = lax.rem(gy, 2) == 0

    def unpack(low):
        for ch in range(4):
            target = start.at[ch] if ch < 3 else share
            from_near, from_far = near[ch, low], jnp.where(inner(gy), far[ch, low], 0.0)
            from_right = jnp.where(first_core, from_near, from_far)
            from_left = jnp.where(first_core, from_far, from_near)
            for h in range(4):
                z = 4 * h + low
                after_y = roll(from_right, 7 - 16 * (h + 1))
                before_y = roll(from_left, 41 - 16 * h)
                own = jnp.concatenate([edges[ch, z], edges_rim[ch, z]], axis=0)
                value = jnp.where(is_after, after_y, jnp.where(is_before, before_y, own))
                target[z + 1, 8:24, :] = value[0:16]
                target[z + 1, 0:8, :] = value[16:24]
                target[z + 1, 24:32, :] = value[16:24]

    loop(4, unpack, 4)

    half_of = iota((32, 128), 1)

    def wrap_one(ref):
        ref[0] = jnp.where(half_of >= 64, roll(ref[16], 64), 0.0)
        ref[17] = jnp.where(half_of < 64, roll(ref[1], 64), 0.0)

    def wrap(ref):
        for f in range(3):
            wrap_one(ref.at[f])

    wrap_one(share)
    wrap(start)
    row = iota((24, 128), 0) + 6
    low, high = jnp.where(gx > 0, 1, 0), jnp.where(gx < NX - 1, 1, 0)
    inside_x = jnp.where(row < 8, low, jnp.where(row >= 24, high, 1))
    inside_y = jnp.where(
        part < 32,
        jnp.where((part < 7) | (gy < NY - 1), 1, 0),
        jnp.where((part >= 57) | (gy > 0), 1, 0),
    )
    omega = 0.8 * (inside_x * inside_y).astype(F32)
    fine_sweeps(
        16, [(6, 24), (7, 24)], start, share, one, two, weights, diags, halves, omega, wrap, field, STEP
    )

    source, target = iota((128, 128), 0), iota((128, 128), 1)
    spot = source % 64
    column = jnp.where(spot < 32, 121 + spot, 71 + spot) // 2
    to = jnp.where(spot < 32, column - 62, column - 48)
    keep = ((spot < 32) & (to >= 0) & (to < 9)) | ((spot >= 32) & (to >= 9) & (to < 18))
    mixed = halves[...].reshape(4, 4, 2, 16, 128)
    value = None
    for odd in range(2):
        pool = jnp.where(keep & (to + 64 * odd + 32 * (source // 64) == target), 0.125, 0.0)
        part = dot_exact(mixed[:, :, odd].reshape(256, 128), pool)
        value = part if value is None else value + part
    pooled[...] = value
    packed[...] = (pooled[pl.ds(0, 128, stride=2), :] + pooled[pl.ds(1, 128, stride=2), :]).reshape(4, 4, 8, 128)


def base_kernel(two, rim, e_one, e_two, base, wide, spread):
    copy = jnp.where(iota((128, 128), 0) == iota((128, 128), 1) // 2, 1.0, 0.0)
    value = dot_exact(e_two[...].reshape(192, 128), copy)
    for block in range(24):
        rows = value[8 * block : 8 * block + 4, :]
        wide[pl.ds(8 * block, 4, stride=2), :] = rows
        wide[pl.ds(8 * block + 1, 4, stride=2), :] = rows
    value = e_one[...].reshape(24, 2, 8, 128) + wide[...].reshape(24, 1, 8, 128)
    value = dot_exact(value.reshape(384, 128), copy)
    flat = spread.reshape(768, 128)
    for block in range(48):
        rows = value[8 * block : 8 * block + 8, :]
        flat[pl.ds(16 * block, 8, stride=2), :] = rows
        flat[pl.ds(16 * block + 1, 8, stride=2), :] = rows
    lane = iota((16, 128), 1)

    def pair(k):
        for f in range(3):
            for z in (2 * k, 2 * k + 1):
                value = rim[f, z]
                for half in range(2):
                    low = roll(value, -57 - 64 * half)
                    high = roll(value, 121 - 64 * half)
                    at = z + 16 * half
                    own = jnp.concatenate([two[f, at + 1, 16:24, :], two[f, at + 1, 0:8, :]], axis=0)
                    own = jnp.where(lane < 3, low, jnp.where(lane >= 125, high, own))
                    base[f, at] = own + spread[f, k + 8 * half]

    loop(8, pair, 4)


def resist(share):
    return recip(2.0 - 1.8 * share)


def level_weights(own, six, omega):
    faces = [recip(own + other) for other in six]
    diag = (faces[0] + faces[1]) + (faces[2] + faces[3]) + (faces[4] + faces[5])
    gain = omega * recip(diag)
    return gain, [gain * w for w in faces], diag


def middle_kernel(
    main, main_near, main_far, rim, rim_near, rim_far, sent, e_one, e_two,
    share, rest, rhs, first, second, weights, diags, halves, pooled,
    rest2, first2, second2, rhs2, share2, weights2,
):
    gx, gy = lax.axis_index("gx"), lax.axis_index("gy")
    low_x, high_x = jnp.where(gx > 0, 1, 0), jnp.where(gx < NX - 1, 1, 0)
    low_y, high_y = jnp.where(gy > 0, 1, 0), jnp.where(gy < NY - 1, 1, 0)

    for f in range(3):
        for ref in (first, second):
            ref[f, 0] = jnp.zeros((32, 128), F32)
            ref[f, 17] = jnp.zeros((32, 128), F32)
    for z in (0, 17):
        rest[z] = jnp.full((32, 128), 0.5, F32)
    lane = iota((8, 128), 1)
    even = lax.rem(gx, 2) == 0
    near_row, far_row = jnp.where(even, 16, 0), jnp.where(even, 0, 16)
    starts = (pl.multiple_of(near_row, 8), pl.multiple_of(far_row, 8), 8)

    sources = zip(starts, ((main_near, rim_near), (main_far, rim_far), (main, rim)))
    sources = list(sources)
    has_far = inner(gx)

    def fill(q):
        for odd in range(2):
            for half in range(2):
                z = 2 * q + odd + 8 * half
                base = 64 * odd + 32 * half
                for at, (middle, outer) in sources:
                    for ch in range(4):
                        edge, body = outer[ch, q], middle[ch, 2 * q + odd]
                        if outer is rim_far:
                            edge, body = jnp.where(has_far, edge, 0.0), jnp.where(has_far, body, 0.0)
                        value = jnp.where(lane < 62, roll(body, 64 * half), roll(edge, 62 - base))
                        value = jnp.where((lane >= 96) | (lane < 2), roll(edge, 112 - base), value)
                        if ch < 3:
                            rhs[ch, z, pl.ds(at, 8), :] = value
                        else:
                            share[z, pl.ds(at, 8), :] = value
                            rest[z + 1, pl.ds(at, 8), :] = resist(value)
                rest[z + 1, 24:32, :] = jnp.full((8, 128), 0.5, F32)

    loop(4, fill, 4)

    row, lane = iota((24, 128), 0) + 1, iota((24, 128), 1)
    in_x = jnp.where(row < 8, low_x, jnp.where(row >= 16, high_x, 1))
    in_y = jnp.where(lane < 64, 1, jnp.where(lane < 96, high_y, low_y))
    omega = 0.8 * (in_x * in_y).astype(F32)

    def start(step):
        z = STEP * step
        for k, (own, six) in enumerate(block_of(rest, (), z + 1, STEP, 1, 24)):
            gain, w, diag = level_weights(own, six, omega)
            for i in range(6):
                weights[i, z + k, 1:25, :] = w[i]
            diags[z + k, 1:25, :] = (1.25 * 0.25) * diag
            for f in range(3):
                first[f, z + k + 1, 1:25, :] = (4.0 * gain) * rhs[f, z + k, 1:25, :]

    loop(16 // STEP, start)

    def sweep(step):
        z = STEP * step
        w = [[weights[i, z + k, 3:27, :] for i in range(6)] for k in range(STEP)]
        for f in range(3):
            for k, (own, six) in enumerate(block_of(first, (f,), z + 1, STEP, 3, 24)):
                second[f, z + k + 1, 3:27, :] = 1.2 * own + weigh(w[k], six)

    loop(16 // STEP, sweep)

    def left(step):
        z = STEP * step
        w = [[weights[i, z + k, 4:20, :] for i in range(6)] for k in range(STEP)]
        diag = [diags[z + k, 4:20, :] for k in range(STEP)]
        for f in range(3):
            values = []
            for k, (own, six) in enumerate(block_of(second, (f,), z + 1, STEP, 4, 16)):
                change = (first[f, z + k + 1, 4:20, :] - 0.8 * own) + weigh(w[k], six)
                values.append(change * diag[k])
                e_one[f, z + k] = second[f, z + k + 1, 8:16, :]
            for k in range(STEP // 2):
                halves[f, STEP // 2 * step + k, 0:16, :] = values[2 * k] + values[2 * k + 1]
                halves[f, STEP // 2 * step + k, 16:24, :] = jnp.zeros((8, 128), F32)
        for k in range(STEP // 2):
            halves[3, STEP // 2 * step + k] = share[z + 2 * k] + share[z + 2 * k + 1]

    loop(16 // STEP, left)

    source, target = iota((128, 128), 0), iota((128, 128), 1)
    pool = jnp.where(source // 2 + jnp.where(source >= 96, 64, 0) == target, 0.125, 0.0)
    pooled[...] = dot_exact(halves[...].reshape(4 * 8 * 24, 128), pool)
    for z in (0, 9):
        rest2[z] = jnp.full((24, 128), 0.5, F32)
        for f in range(3):
            first2[f, z] = jnp.zeros((24, 128), F32)
            second2[f, z] = jnp.zeros((24, 128), F32)
    for z in range(8):
        for f in range(3):
            base = (f * 8 + z) * 24
            rhs2[f, z] = pooled[pl.ds(base, 8, stride=2), :] + pooled[pl.ds(base + 1, 8, stride=2), :]
        base = (3 * 8 + z) * 24
        value = pooled[pl.ds(base + 2, 8, stride=2), :] + pooled[pl.ds(base + 3, 8, stride=2), :]
        rest2[z + 1, 0:8, :] = resist(value)
        value = pooled[pl.ds(base + 8, 8, stride=2), :] + pooled[pl.ds(base + 9, 8, stride=2), :]
        rest2[z + 1, 3:11, :] = resist(value)
        share2[z] = value

    row, lane = iota((8, 128), 0) + 1, iota((8, 128), 1)
    in_x = jnp.where(row < 3, low_x, jnp.where(row >= 7, high_x, 1))
    in_y = jnp.where(lane < 32, 1, jnp.where(lane < 96, high_y, low_y))
    omega2 = 0.8 * (in_x * in_y).astype(F32)

    for z, (own, six) in enumerate(block_of(rest2, (), 1, 8, 1, 8)):
        gain, w, diag = level_weights(own, six, omega2)
        for i in range(6):
            weights2[i, z, 1:9, :] = w[i]
        weights2[6, z, 1:9, :] = (1.25 * 0.0625) * diag
        for f in range(3):
            first2[f, z + 1, 1:9, :] = (16.0 * gain) * rhs2[f, z]
    w = [[weights2[i, z, 2:10, :] for i in range(6)] for z in range(8)]
    for f in range(3):
        for z, (own, six) in enumerate(block_of(first2, (f,), 1, 8, 2, 8)):
            second2[f, z + 1, 2:10, :] = 1.2 * own + weigh(w[z], six)
    w = [[weights2[i, z, 3:11, :] for i in range(7)] for z in range(8)]
    own_row = iota((8, 128), 0) < 4
    parts = [{} for pair in range(4)]
    for f in range(3):
        for z, (own, six) in enumerate(block_of(second2, (f,), 1, 8, 3, 8)):
            e_two[f, z] = own
            change = (first2[f, z + 1, 3:11, :] - 0.8 * own) + weigh(w[z], six)
            value = jnp.where(own_row, change * w[z][6], 0.0)
            sums = parts[z // 2]
            sums[f] = value if z % 2 == 0 else sums[f] + value
    for z in range(8):
        value = jnp.where(own_row, share2[z], 0.0)
        sums = parts[z // 2]
        sums[3] = value if z % 2 == 0 else sums[3] + value

    pool = jnp.where((source < 32) & (source // 2 == target % 16), 0.125, 0.0)
    rows = jnp.concatenate([parts[pair][ch] for ch in range(4) for pair in range(4)], axis=0)
    spread = dot_exact(rows, pool)
    at, to = iota((32, 128), 0), iota((32, 128), 1)
    keep = (at // 8 == to // 32) & ((at % 8) // 2 == (to // 16) % 2)
    result = jnp.concatenate(
        [
            jnp.sum(jnp.where(keep, spread[32 * ch : 32 * ch + 32], 0.0), axis=0, keepdims=True)
            for ch in range(4)
        ],
        axis=0,
    )
    for copy in range(CHIPS):
        sent[copy] = result


def swap_blocks(x):
    apart = (iota((8, 128), 0) - iota((8, 128), 1) // 16) % 8
    moved = [roll(roll(x, d, 0), -16 * d) for d in range(8)]
    while len(moved) > 1:
        bit = 8 // len(moved)
        moved = [
            jnp.where((apart & bit) == 0, even, odd) for even, odd in zip(moved[0::2], moved[1::2])
        ]
    return moved[0]


def top_kernel(
    mine, other, base, out,
    natural, first, second, four, weights, diags, lefts, final, sems,
):
    gx, gy = lax.axis_index("gx"), lax.axis_index("gy")
    first_core = lax.rem(gy, 2) == 0
    lane, sub = iota((16, 128), 1), iota((16, 128), 0)
    cells = [(z, x, half) for z in range(4) for x in range(2) for half in range(2)]

    def lay(g):
        for ch in range(4):
            rows = pl.ds(32 * g + ch, 8, stride=4)
            pair = mine[rows, :], other[rows, :]
            natural[ch, 0, pl.ds(pl.multiple_of(8 * g, 8), 8), :] = swap_blocks(
                jnp.where(first_core, pair[0], pair[1])
            )
            natural[ch, 1, pl.ds(pl.multiple_of(8 * g, 8), 8), :] = swap_blocks(
                jnp.where(first_core, pair[1], pair[0])
            )

    loop(16, lay, 4)
    flat = natural.reshape(1024, 128)

    def plane(ch, z, x, half):
        return flat[pl.ds((ch * 2 + half) * 128 + z * 2 + x, 16, stride=8), :]

    def neighbours(at, z, x, half, outside):
        own, other = at(z, x, half), at(z, 1 - x, half)
        beside = at(z, x, 1 - half)
        shifted = roll(other, 1 if x == 0 else -1, 0)
        low, high = (shifted, other) if x == 0 else (other, shifted)
        left, right = roll(own, 1), roll(own, -1)
        left = jnp.where(lane % 16 == 0, roll(beside, 1 if half == 0 else -15), left)
        right = jnp.where(lane % 16 == 15, roll(beside, 15 if half == 0 else -1), right)
        down = at(z - 1, x, half) if z > 0 else outside
        up = at(z + 1, x, half) if z < 3 else outside
        return own, [low, high, left, right, down, up]

    def edge_masks(x, half):
        return [
            sub > 0 if x == 0 else None,
            sub < 15 if x == 1 else None,
            lane > 0 if half == 0 else None,
            lane < 127 if half == 1 else None,
            None,
            None,
        ]

    def key(z, x, half):
        return (z * 2 + x) * 2 + half

    shares = {c: plane(3, *c) for c in cells}
    rests = {c: resist(shares[c]) for c in cells}
    outside, zeros = jnp.full((16, 128), 0.5, F32), jnp.zeros((16, 128), F32)
    for z, x, half in cells:
        own, six = neighbours(lambda *c: rests[c], z, x, half, outside)
        masks = edge_masks(x, half)
        six = [s if m is None else jnp.where(m, s, 0.5) for s, m in zip(six, masks)]
        gain, w, diag = level_weights(own, six, 0.8)
        at = key(z, x, half)
        for i in range(6):
            weights[i, at] = w[i] if masks[i] is None else jnp.where(masks[i], w[i], 0.0)
        diags[at] = (1.25 * 0.25**3) * diag
        for f in range(3):
            first[f, at] = (64.0 * gain) * plane(f, z, x, half)

    for z, x, half in cells:
        at = key(z, x, half)
        w = [weights[i, at] for i in range(6)]
        for f in range(3):
            own, six = neighbours(lambda *c: first[f, key(*c)], z, x, half, zeros)
            second[half, f, z * 2 + x] = 1.2 * own + weigh(w, six)

    for z4 in range(2):
        for half in range(2):
            sums = [None] * 4
            for z in (2 * z4, 2 * z4 + 1):
                for x in range(2):
                    at = key(z, x, half)
                    w = [weights[i, at] for i in range(6)]
                    diag = diags[at]
                    for f in range(3):
                        own, six = neighbours(
                            lambda c, d, e: second[e, f, c * 2 + d], z, x, half, zeros
                        )
                        value = ((first[f, at] - 0.8 * own) + weigh(w, six)) * diag
                        sums[f] = value if sums[f] is None else sums[f] + value
                    share = shares[z, x, half]
                    sums[3] = share if sums[3] is None else sums[3] + share
            for ch in range(4):
                lefts[ch, z4, :, 128 * half : 128 * half + 128] = sums[ch]

    source = iota((256, 128), 0)
    column = ((source % 128) // 16) * 16 + (source // 128) * 8 + (source % 16) // 2
    pool = jnp.where(column == iota((256, 128), 1), 0.125, 0.0)
    level = dot_exact(lefts[...].reshape(128, 256), pool)

    def coarsest(ch, z):
        return level[(ch * 2 + z) * 16 : (ch * 2 + z) * 16 + 16, :]

    masks = [sub > 0, sub < 15, lane > 0, lane < 127]
    resists = [resist(coarsest(3, z)) for z in range(2)]
    gains, ws, ds = [], [], []
    for z in range(2):
        own, other = resists[z], resists[1 - z]
        six = [roll(own, 1, 0), roll(own, -1, 0), roll(own, 1), roll(own, -1)]
        six = [jnp.where(m, s, 0.5) for m, s in zip(masks, six)] + [other, outside]
        gain, w, diag = level_weights(own, six, 0.8)
        gains.append(gain)
        ds.append(diag)
        ws.append([jnp.where(m, v, 0.0) for m, v in zip(masks, w)] + [w[4]])
    whole = jnp.sum(ds[0] + ds[1], keepdims=True)

    def around(values, z):
        own, other = values[z], values[1 - z]
        return weigh(ws[z], (roll(own, 1, 0), roll(own, -1, 0), roll(own, 1), roll(own, -1), other))

    begin = [[256.0 * gains[z] * coarsest(f, z) for z in range(2)] for f in range(3)]
    values = begin
    for step in range(5):
        values = [
            [(0.2 * values[f][z] + begin[f][z]) + around(values[f], z) for z in range(2)] for f in range(3)
        ]
    shifts = []
    for f in range(3):
        change = [(begin[f][z] - 0.8 * values[f][z]) + around(values[f], z) for z in range(2)]
        shifts.append(jnp.sum(1.25 * (change[0] * ds[0] + change[1] * ds[1]), keepdims=True) / whole)
        for z in range(2):
            four[2 * f + z] = values[f][z]

    rows = four.reshape(96, 128)[pl.ds(gx, 6, stride=16), :]
    upper = jnp.concatenate([jnp.broadcast_to(rows[i : i + 1], (4, 128)) for i in range(6)], axis=0)
    flat = second.reshape(768, 128)
    halves = [flat[pl.ds(gx + 384 * half, 24, stride=16), :] for half in range(2)]
    three = turn(jnp.where(first_core, halves[0], halves[1]), -16 * lax.div(gy, 2))
    both = jnp.concatenate([turn(upper, -8 * gy), three], axis=1)
    both = jnp.concatenate([both, jnp.zeros((8, 256), F32)], axis=0)
    source, target = iota((256, 128), 0), iota((256, 128), 1)
    copy = jnp.where(source == jnp.where(source < 128, target // 16, 128 + target // 8), 1.0, 0.0)
    three = dot_exact(both, copy)

    copies = []
    for f in range(3):
        for z in range(4):
            for x in range(2):
                at = f * 8 + z * 2 + x
                value = jnp.broadcast_to(three[at : at + 1] + shifts[f], (8, 128))
                for k in range(8 * z, 8 * z + 8):
                    final[f, k, 8 * x : 8 * x + 8, :] = base[f, k, 8 * x : 8 * x + 8, :] + value
            if z % 2 == 1:
                part = (f, pl.ds(8 * z - 8, 16))
                copy = pltpu.make_async_copy(final.at[part], out.at[part], sems.at[len(copies)])
                copy.start()
                copies.append(copy)
    for copy in copies:
        copy.wait()


def local(labels, guess):
    swap_near = [(i, i ^ 1) for i in range(NY)]
    far_x, far_y = [], []
    for x in range(NX):
        for y in range(NY):
            across_x, across_y = x + 1 if x % 2 else x - 1, y + 1 if y % 2 else y - 1
            to = (across_x, y) if 0 <= across_x < NX else (x, y ^ 1)
            far_x.append((x * NY + y, to[0] * NY + to[1]))
            to = (x, across_y) if 0 <= across_y < NY else (x ^ 1, y)
            far_y.append((x * NY + y, to[0] * NY + to[1]))
    both = ("gx", "gy")
    to_near, to_far, own = call(
        rows_kernel,
        [(12, 32, 128)] * 2 + [(4, 32, 16, 128)],
        [pltpu.VMEM((32, 16, 128), jnp.int32), pltpu.SemaphoreType.DMA((4,))],
        in_specs=[ANY, ANY],
    )(pltpu.with_memory_space_constraint(guess, pltpu.HBM), pltpu.with_memory_space_constraint(labels, pltpu.HBM))
    from_near = lax.ppermute(to_near, "gx", swap_near)
    from_far = lax.ppermute(to_far, both, far_x)
    own_one, own_two, halves, to_right, to_left, edges = call(
        own_kernel,
        [(3, 34, 32, 128)] * 2 + [(4, 16, 16, 128)] + [(4, 4, 16, 128)] * 2 + [(4, 16, 16, 128)],
        [(4, 34, 32, 128), (6, 32, 32, 128), (32, 32, 128)],
        flops=20_000_000,
    )(own)
    to_near, to_far, rim_rows = call(pack_kernel, [(4, 4, 24, 128)] * 2 + [(4, 32, 8, 128)], [])(
        to_right, to_left, from_near, from_far
    )
    from_far = lax.ppermute(to_far, both, far_y)
    from_near = lax.ppermute(to_near, "gy", swap_near)
    two, main, edges_rim = call(
        rows_edge_kernel,
        [(3, 34, 24, 128), (4, 8, 8, 128), (4, 16, 8, 128)],
        [(4, 34, 24, 128), (3, 34, 24, 128), (6, 32, 24, 128), (32, 24, 128)]
        + [(4, 16, 16, 128), (512, 128)],
        flops=10_000_000,
    )(own, rim_rows, own_one, own_two, halves)
    main_near = lax.ppermute(main, "gx", swap_near)
    main_far = lax.ppermute(main, both, far_x)
    rim, rim_one = call(
        rim_kernel,
        [(3, 16, 16, 128), (4, 4, 8, 128)],
        [(3, 18, 32, 128), (18, 32, 128)]
        + [(3, 18, 32, 128)] * 2
        + [(6, 16, 32, 128), (16, 32, 128)]
        + [(4, 8, 16, 128), (256, 128)],
        flops=10_000_000,
    )(edges, edges_rim, from_near, from_far)
    rim_near = lax.ppermute(rim_one, "gx", swap_near)
    rim_far = lax.ppermute(rim_one, both, far_x)
    sent, e_one, e_two = call(
        middle_kernel,
        [(CHIPS, 4, 128), (3, 16, 8, 128), (3, 8, 8, 128)],
        [(16, 24, 128), (18, 32, 128), (3, 16, 32, 128), (3, 18, 32, 128), (3, 18, 32, 128)]
        + [(6, 16, 32, 128), (16, 32, 128), (4, 8, 24, 128), (768, 128)]
        + [(10, 24, 128), (3, 10, 24, 128), (3, 10, 24, 128), (3, 8, 8, 128), (8, 8, 128)]
        + [(7, 8, 16, 128)],
    )(main, main_near, main_far, rim_one, rim_near, rim_far)
    groups = [[i for i in range(NX * NY) if i % 2 == core] for core in range(2)]
    mine = lax.all_to_all(
        sent, ("gx", "gy"), split_axis=0, concat_axis=0, axis_index_groups=groups, tiled=True
    )
    (base,) = call(base_kernel, [(3, 32, 16, 128)], [(192, 128), (3, 16, 16, 128)])(two, rim, e_one, e_two)
    other = lax.ppermute(mine, "gy", swap_near)
    (out,) = call(
        top_kernel,
        [(3, 32, 16, 128)],
        [(4, 2, 128, 128), (3, 16, 16, 128), (2, 3, 8, 16, 128), (6, 16, 128), (6, 16, 16, 128)]
        + [(16, 16, 128), (4, 2, 16, 256), (3, 32, 16, 128), pltpu.SemaphoreType.DMA((6,))],
        out_specs=[ANY],
    )(mine.reshape(512, 128), other.reshape(512, 128), base)
    return out


def solution(mesh):
    return jax.shard_map(
        local,
        mesh=mesh,
        in_specs=(P(None, "gx", "gy"), P(None, None, "gx", "gy")),
        out_specs=P(None, None, "gx", "gy"),
        check_vma=False,
    )
```

```python
import jax
import jax.numpy as jnp
from jax import lax
from jax.experimental import pallas as pl
from jax.experimental.pallas import tpu as pltpu
from jax.sharding import PartitionSpec as P


F32 = jnp.float32
NX, NY, CHIPS = 16, 16, 128
STEP, WIDE = 16, 32
BETWEEN = 2.0 * 0.1 / 1.1
ANY = pl.BlockSpec(memory_space=pltpu.HBM)


def dot_exact(a, b):
    high = a.astype(jnp.bfloat16)
    low = (a - high.astype(F32)).astype(jnp.bfloat16)
    b = b.astype(jnp.bfloat16)
    return jnp.dot(
        jnp.concatenate([high, low], axis=1), jnp.concatenate([b, b], axis=0), preferred_element_type=F32
    )


def iota(shape, dim):
    return lax.broadcasted_iota(jnp.int32, shape, dim)


def roll(x, shift, axis=1):
    shift = shift % x.shape[axis]
    return x if shift == 0 else pltpu.roll(x, shift, axis)


def turn(x, shift):
    return pltpu.roll(x, lax.rem(shift + 256, 128), 1)


def recip(x):
    guess = pl.reciprocal(x, approx=True)
    return guess * (2.0 - x * guess)


def inner(index):
    return (index > 0) & (index < 15)


def call(kernel, outs, scratch, flops=1_000_000, **kw):
    return pl.pallas_call(
        kernel,
        out_shape=[jax.ShapeDtypeStruct(s, F32) for s in outs],
        scratch_shapes=[pltpu.VMEM(s, F32) if isinstance(s, tuple) else s for s in scratch],
        compiler_params=pltpu.CompilerParams(vmem_limit_bytes=32 * 1024 * 1024),
        cost_estimate=pl.CostEstimate(flops=flops, bytes_accessed=4_000_000, transcendentals=0),
        **kw,
    )


def loop(count, body, unroll=1):
    def step(i, carry):
        body(i)
        return carry

    lax.fori_loop(0, count, step, 0, unroll=unroll)


def weigh(weights, values):
    parts = [w * v for w, v in zip(weights, values)]
    while len(parts) > 1:
        parts = [sum(parts[i : i + 2][1:], parts[i]) for i in range(0, len(parts), 2)]
    return parts[0]


def rows_kernel(guess, labels, near, far, own, phase, sems):
    even = lax.rem(lax.axis_index("gx"), 2) == 0
    near_row, far_row = jnp.where(even, 13, 0), jnp.where(even, 0, 13)
    copies = [pltpu.make_async_copy(labels, phase, sems.at[3])]
    for f in range(3):
        copies.append(pltpu.make_async_copy(guess.at[f], own.at[f], sems.at[f]))
    for copy in copies:
        copy.start()
    copies[0].wait()
    own[3] = jnp.where(phase[...] == 1, 0.0, 1.0).astype(F32)
    flat = own.reshape(4 * 32 * 16, 128)
    for ch in (3, 0, 1, 2):
        if ch < 3:
            copies[ch + 1].wait()
        for row in range(3):
            near[3 * ch + row] = flat[pl.ds(512 * ch + near_row + row, 32, stride=16), :]
            far[3 * ch + row] = flat[pl.ds(512 * ch + far_row + row, 32, stride=16), :]


def pack_kernel(to_right, to_left, x_near, x_far, near, far, rim):
    first_core = lax.rem(lax.axis_index("gy"), 2) == 0
    even = lax.rem(lax.axis_index("gx"), 2) == 0
    near_row, far_row = jnp.where(even, 0, 5), jnp.where(even, 5, 0)
    has_far = inner(lax.axis_index("gx"))
    flat = rim.reshape(4 * 32 * 8, 128)
    for ch in range(4):
        for row in range(3):
            flat[pl.ds(256 * ch + near_row + row, 32, stride=8), :] = x_near[3 * ch + row]
            flat[pl.ds(256 * ch + far_row + row, 32, stride=8), :] = jnp.where(has_far, x_far[3 * ch + row], 0.0)

    def some(low):
        for ch in range(4):
            right, left = pack_planes(lambda z: rim[ch, z], low, (8, 128))
            for at, right, left in (
                (slice(0, 16), to_right[ch, low], to_left[ch, low]),
                (slice(16, 24), right, left),
            ):
                near[ch, low, at, :] = jnp.where(first_core, right, left)
                far[ch, low, at, :] = jnp.where(first_core, left, right)

    loop(4, some, 4)


def pack_planes(plane, low, shape):
    group = iota(shape, 1) // 16
    right = left = jnp.zeros(shape, F32)
    for h in range(8):
        moved = roll(plane(4 * h + low), 16 * h + 16)
        right = jnp.where(group == h, moved, right)
        left = jnp.where(group == (h + 1) % 8, moved, left)
    return right, left


def edge_columns(plane, z, shape):
    lane = iota(shape, 1)
    value = jnp.zeros(shape, F32)
    for half in range(2):
        source = plane(z + 16 * half)
        base = 64 * half
        value = jnp.where((lane >= base) & (lane < base + 7), roll(source, base + 7), value)
        value = jnp.where((lane >= base + 57) & (lane < base + 64), roll(source, base + 57), value)
    return value


def six_of(ref, lead, z, first, count):
    own = ref[(*lead, z, pl.ds(first, count), slice(None))]
    return own, (
        ref[(*lead, z, pl.ds(first - 1, count), slice(None))],
        ref[(*lead, z, pl.ds(first + 1, count), slice(None))],
        roll(own, 1),
        roll(own, -1),
        ref[(*lead, z - 1, pl.ds(first, count), slice(None))],
        ref[(*lead, z + 1, pl.ds(first, count), slice(None))],
    )


def block_of(ref, lead, z, planes, first, count):
    rows = pl.ds(first, count)
    own = [ref[(*lead, z + k, rows, slice(None))] for k in range(-1, planes + 1)]
    result = []
    for k in range(planes):
        value = own[k + 1]
        six = (
            ref[(*lead, z + k, pl.ds(first - 1, count), slice(None))],
            ref[(*lead, z + k, pl.ds(first + 1, count), slice(None))],
            roll(value, 1),
            roll(value, -1),
            own[k],
            own[k + 2],
        )
        result.append((value, six))
    return result


def fine_weights(own, six, omega):
    base, slope = 1.0 + (BETWEEN - 1.0) * own, (BETWEEN - 1.0) + (1.1 - 2.0 * BETWEEN) * own
    total = (six[0] + six[1]) + (six[2] + six[3]) + (six[4] + six[5])
    diag = 6.0 * base + slope * total
    gain = omega * recip(diag)
    base, slope = gain * base, gain * slope
    return [base + slope * other for other in six], 1.25 * diag


def fine_sweep(w, f, own, six):
    return (0.2 * own + (w[2 * f + 1] - w[2 * f])) + weigh(w, six)


def fine_left(w, f, own, six, diag):
    return (((w[2 * f + 1] - w[2 * f]) - 0.8 * own) + weigh(w, six)) * diag


def fine_sweeps(planes, windows, start, share, one, two, weights, diags, halves, omega, wrap, keep, size):
    first, count = windows[0]

    def first_sweep(step):
        z = size * step
        w = []
        for k, (own, six) in enumerate(block_of(share, (), z + 1, size, first, count)):
            now, diag = fine_weights(own, six, omega)
            diags[z + k, pl.ds(first, count), :] = diag
            for i in range(6):
                weights[i, z + k, pl.ds(first, count), :] = now[i]
            w.append(now)
        for f in range(3):
            for k, (own, six) in enumerate(block_of(start, (f,), z + 1, size, first, count)):
                one[f, z + k + 1, pl.ds(first, count), :] = fine_sweep(w[k], f, own, six)

    loop(planes // size, first_sweep)
    wrap(one)
    second, count2 = windows[1]

    def second_sweep(step):
        z = size * step
        w = [[weights[i, z + k, pl.ds(second, count2), :] for i in range(6)] for k in range(size)]
        for f in range(3):
            for k, (own, six) in enumerate(block_of(one, (f,), z + 1, size, second, count2)):
                two[f, z + k + 1, pl.ds(second, count2), :] = fine_sweep(w[k], f, own, six)

    loop(planes // size, second_sweep)
    wrap(two)

    def residual(step):
        z = size * step
        w = [[weights[i, z + k, 8:24, :] for i in range(6)] for k in range(size)]
        diag = [diags[z + k, 8:24, :] for k in range(size)]
        for f in range(3):
            values = []
            for k, (own, six) in enumerate(block_of(two, (f,), z + 1, size, 8, 16)):
                if keep is not None:
                    keep[f, z + k] = own
                values.append(fine_left(w[k], f, own, six, diag[k]))
            for pair in range(size // 2):
                halves[f, size // 2 * step + pair] = values[2 * pair] + values[2 * pair + 1]
        for pair in range(size // 2):
            at = z + 2 * pair + 1
            halves[3, size // 2 * step + pair] = share[at, 8:24, :] + share[at + 1, 8:24, :]

    loop(planes // size, residual)


def own_kernel(own, one, two, halves, to_right, to_left, edges, held, weights, diags):
    zero = jnp.zeros((32, 128), F32)
    for z in (0, 33):
        for ch in range(4):
            held[ch, z] = zero
        for ref in (one, two):
            for f in range(3):
                ref[f, z] = zero

    def plane(z):
        for ch in range(4):
            held[ch, z + 1, 8:24, :] = own[ch, z]

    loop(32, plane, 8)
    fine_sweeps(
        32, [(8, 16)] * 2, held, held.at[3], one, two, weights, diags, halves, 0.8, lambda ref: None, None, 8
    )

    def some(low):
        for ch in range(4):
            to_right[ch, low], to_left[ch, low] = pack_planes(lambda z: own[ch, z], low, (16, 128))

    loop(4, some, 2)

    def edge(z):
        for ch in range(4):
            edges[ch, z] = edge_columns(lambda at: own[ch, at], z, (16, 128))

    loop(16, edge, 8)


def rows_edge_kernel(own, rim, own_one, own_two, own_halves, two, packed, edges, start, one, weights, diags, halves, pooled):
    gx = lax.axis_index("gx")
    zero = jnp.zeros((24, 128), F32)
    for z in (0, 33):
        for ch in range(4):
            start[ch, z] = zero
        for ref in (one, two):
            for f in range(3):
                ref[f, z] = zero

    def fill(z):
        for ch in range(4):
            start[ch, z + 1, 0:8, :] = own[ch, z, 8:16, :]
            start[ch, z + 1, 8:16, :] = rim[ch, z]
            start[ch, z + 1, 16:24, :] = own[ch, z, 0:8, :]
        for f in range(3):
            for ref, source in ((one, own_one), (two, own_two)):
                ref[f, z + 1, 0:8, :] = source[f, z + 1, 16:24, :]
                ref[f, z + 1, 16:24, :] = source[f, z + 1, 8:16, :]

    loop(32, fill, 32)
    upper = iota((8, 128), 0) < 4

    def both(ref, lead, step, shift=0):
        high = ref[(*lead, pl.ds(8 - step + shift, 8), slice(None))]
        low = ref[(*lead, pl.ds(8 + step + shift, 8), slice(None))]
        return jnp.where(upper, high, low)

    def block_both(ref, f, z, step):
        own = [both(ref, (f, z + k), step) for k in range(-1, WIDE + 1)]
        result = []
        for k in range(WIDE):
            value = own[k + 1]
            low, high = both(ref, (f, z + k), step, -1), both(ref, (f, z + k), step, 1)
            result.append((value, (low, high, roll(value, 1), roll(value, -1), own[k], own[k + 2])))
        return result

    def put(ref, f, z, step, value):
        ref[f, z, pl.ds(8 - step, 4), :] = value[0:4]
        ref[f, z, pl.ds(12 + step, 4), :] = value[4:8]

    row = iota((16, 128), 0) + 5
    low, high = jnp.where(gx > 0, 1, 0), jnp.where(gx < NX - 1, 1, 0)
    inside = jnp.where((row >= 8) & (row < 12), high, jnp.where((row >= 12) & (row < 16), low, 1))
    omega = 0.8 * inside.astype(F32)

    def weigh_all(step):
        z = WIDE * step
        for k, (value, six) in enumerate(block_of(start, (3,), z + 1, WIDE, 5, 16)):
            w, diag = fine_weights(value, six, omega)
            diags[z + k, 5:21, :] = diag
            for i in range(6):
                weights[i, z + k, 5:21, :] = w[i]

    loop(32 // WIDE, weigh_all)

    for step, source, target in ((1, start, one), (2, one, two)):

        def sweep(block):
            z = WIDE * block
            w = [[both(weights, (i, z + k), step) for i in range(6)] for k in range(WIDE)]
            for f in range(3):
                for k, (value, six) in enumerate(block_both(source, f, z + 1, step)):
                    put(target, f, z + k + 1, step, fine_sweep(w[k], f, value, six))

        loop(32 // WIDE, sweep)

    sub = iota((8, 128), 0)

    def residual(block):
        z = WIDE * block
        w = [[both(weights, (i, z + k), 3) for i in range(6)] for k in range(WIDE)]
        diag = [both(diags, (z + k,), 3) for k in range(WIDE)]
        for f in range(3):
            values = []
            for k, (value, six) in enumerate(block_both(two, f, z + 1, 3)):
                values.append(fine_left(w[k], f, value, six, diag[k]))
            for k in range(WIDE // 2):
                pair = WIDE // 2 * block + k
                value = values[2 * k] + values[2 * k + 1]
                halves[f, pair, 0:8, :] = jnp.where(sub < 3, roll(value, 3, 0), own_halves[f, pair, 0:8, :])
                halves[f, pair, 8:16, :] = jnp.where(sub >= 5, roll(value, 5, 0), own_halves[f, pair, 8:16, :])
        for k in range(WIDE // 2):
            halves[3, WIDE // 2 * block + k] = own_halves[3, WIDE // 2 * block + k]

    loop(32 // WIDE, residual)
    source, target = iota((128, 128), 0), iota((128, 128), 1)
    value = None
    for half in range(2):
        pool = jnp.where(source // 2 + 64 * half == target, 0.125, 0.0)
        part = dot_exact(halves[:, 8 * half : 8 * half + 8].reshape(512, 128), pool)
        value = part if value is None else value + part
    pooled[...] = value
    packed[...] = (pooled[pl.ds(0, 256, stride=2), :] + pooled[pl.ds(1, 256, stride=2), :]).reshape(4, 8, 8, 128)

    def edge(z):
        for ch in range(4):
            edges[ch, z] = edge_columns(lambda at: rim[ch, at], z, (8, 128))

    loop(16, edge, 16)


def rim_kernel(
    edges, edges_rim, near, far, field, packed,
    start, share, one, two, weights, diags, halves, pooled,
):
    gx, gy = lax.axis_index("gx"), lax.axis_index("gy")
    lane = iota((24, 128), 1)
    part = lane % 64
    is_after = (part >= 7) & (part < 22)
    is_before = (part >= 42) & (part < 57)
    first_core = lax.rem(gy, 2) == 0

    def unpack(low):
        for ch in range(4):
            target = start.at[ch] if ch < 3 else share
            from_near, from_far = near[ch, low], jnp.where(inner(gy), far[ch, low], 0.0)
            from_right = jnp.where(first_core, from_near, from_far)
            from_left = jnp.where(first_core, from_far, from_near)
            for h in range(4):
                z = 4 * h + low
                after_y = roll(from_right, 7 - 16 * (h + 1))
                before_y = roll(from_left, 41 - 16 * h)
                own = jnp.concatenate([edges[ch, z], edges_rim[ch, z]], axis=0)
                value = jnp.where(is_after, after_y, jnp.where(is_before, before_y, own))
                target[z + 1, 8:24, :] = value[0:16]
                target[z + 1, 0:8, :] = value[16:24]
                target[z + 1, 24:32, :] = value[16:24]

    loop(4, unpack, 4)

    half_of = iota((32, 128), 1)

    def wrap_one(ref):
        ref[0] = jnp.where(half_of >= 64, roll(ref[16], 64), 0.0)
        ref[17] = jnp.where(half_of < 64, roll(ref[1], 64), 0.0)

    def wrap(ref):
        for f in range(3):
            wrap_one(ref.at[f])

    wrap_one(share)
    wrap(start)
    row = iota((24, 128), 0) + 6
    low, high = jnp.where(gx > 0, 1, 0), jnp.where(gx < NX - 1, 1, 0)
    inside_x = jnp.where(row < 8, low, jnp.where(row >= 24, high, 1))
    inside_y = jnp.where(
        part < 32,
        jnp.where((part < 7) | (gy < NY - 1), 1, 0),
        jnp.where((part >= 57) | (gy > 0), 1, 0),
    )
    omega = 0.8 * (inside_x * inside_y).astype(F32)
    fine_sweeps(
        16, [(6, 24), (7, 24)], start, share, one, two, weights, diags, halves, omega, wrap, field, STEP
    )

    source, target = iota((128, 128), 0), iota((128, 128), 1)
    spot = source % 64
    column = jnp.where(spot < 32, 121 + spot, 71 + spot) // 2
    to = jnp.where(spot < 32, column - 62, column - 48)
    keep = ((spot < 32) & (to >= 0) & (to < 9)) | ((spot >= 32) & (to >= 9) & (to < 18))
    mixed = halves[...].reshape(4, 4, 2, 16, 128)
    value = None
    for odd in range(2):
        pool = jnp.where(keep & (to + 64 * odd + 32 * (source // 64) == target), 0.125, 0.0)
        part = dot_exact(mixed[:, :, odd].reshape(256, 128), pool)
        value = part if value is None else value + part
    pooled[...] = value
    packed[...] = (pooled[pl.ds(0, 128, stride=2), :] + pooled[pl.ds(1, 128, stride=2), :]).reshape(4, 4, 8, 128)


def base_kernel(two, rim, e_one, e_two, base, wide, spread):
    copy = jnp.where(iota((128, 128), 0) == iota((128, 128), 1) // 2, 1.0, 0.0)
    value = dot_exact(e_two[...].reshape(192, 128), copy)
    for block in range(24):
        rows = value[8 * block : 8 * block + 4, :]
        wide[pl.ds(8 * block, 4, stride=2), :] = rows
        wide[pl.ds(8 * block + 1, 4, stride=2), :] = rows
    value = e_one[...].reshape(24, 2, 8, 128) + wide[...].reshape(24, 1, 8, 128)
    value = dot_exact(value.reshape(384, 128), copy)
    flat = spread.reshape(768, 128)
    for block in range(48):
        rows = value[8 * block : 8 * block + 8, :]
        flat[pl.ds(16 * block, 8, stride=2), :] = rows
        flat[pl.ds(16 * block + 1, 8, stride=2), :] = rows
    lane = iota((16, 128), 1)

    def pair(k):
        for f in range(3):
            for z in (2 * k, 2 * k + 1):
                value = rim[f, z]
                for half in range(2):
                    low = roll(value, -57 - 64 * half)
                    high = roll(value, 121 - 64 * half)
                    at = z + 16 * half
                    own = jnp.concatenate([two[f, at + 1, 16:24, :], two[f, at + 1, 0:8, :]], axis=0)
                    own = jnp.where(lane < 3, low, jnp.where(lane >= 125, high, own))
                    base[f, at] = own + spread[f, k + 8 * half]

    loop(8, pair, 8)


def resist(share):
    return recip(2.0 - 1.8 * share)


def level_weights(own, six, omega):
    faces = [recip(own + other) for other in six]
    diag = (faces[0] + faces[1]) + (faces[2] + faces[3]) + (faces[4] + faces[5])
    gain = omega * recip(diag)
    return gain, [gain * w for w in faces], diag


def middle_kernel(
    main, main_near, main_far, rim, rim_near, rim_far, sent, e_one, e_two,
    share, rest, rhs, first, second, weights, diags, halves, pooled,
    rest2, first2, second2, rhs2, share2, weights2,
):
    gx, gy = lax.axis_index("gx"), lax.axis_index("gy")
    low_x, high_x = jnp.where(gx > 0, 1, 0), jnp.where(gx < NX - 1, 1, 0)
    low_y, high_y = jnp.where(gy > 0, 1, 0), jnp.where(gy < NY - 1, 1, 0)

    for f in range(3):
        for ref in (first, second):
            ref[f, 0] = jnp.zeros((32, 128), F32)
            ref[f, 17] = jnp.zeros((32, 128), F32)
    for z in (0, 17):
        rest[z] = jnp.full((32, 128), 0.5, F32)
    lane = iota((8, 128), 1)
    even = lax.rem(gx, 2) == 0
    near_row, far_row = jnp.where(even, 16, 0), jnp.where(even, 0, 16)
    starts = (pl.multiple_of(near_row, 8), pl.multiple_of(far_row, 8), 8)

    sources = zip(starts, ((main_near, rim_near), (main_far, rim_far), (main, rim)))
    sources = list(sources)
    has_far = inner(gx)

    def fill(q):
        for odd in range(2):
            for half in range(2):
                z = 2 * q + odd + 8 * half
                base = 64 * odd + 32 * half
                for at, (middle, outer) in sources:
                    for ch in range(4):
                        edge, body = outer[ch, q], middle[ch, 2 * q + odd]
                        if outer is rim_far:
                            edge, body = jnp.where(has_far, edge, 0.0), jnp.where(has_far, body, 0.0)
                        value = jnp.where(lane < 62, roll(body, 64 * half), roll(edge, 62 - base))
                        value = jnp.where((lane >= 96) | (lane < 2), roll(edge, 112 - base), value)
                        if ch < 3:
                            rhs[ch, z, pl.ds(at, 8), :] = value
                        else:
                            share[z, pl.ds(at, 8), :] = value
                            rest[z + 1, pl.ds(at, 8), :] = resist(value)
                rest[z + 1, 24:32, :] = jnp.full((8, 128), 0.5, F32)

    loop(4, fill, 4)

    row, lane = iota((24, 128), 0) + 1, iota((24, 128), 1)
    in_x = jnp.where(row < 8, low_x, jnp.where(row >= 16, high_x, 1))
    in_y = jnp.where(lane < 64, 1, jnp.where(lane < 96, high_y, low_y))
    omega = 0.8 * (in_x * in_y).astype(F32)

    def start(step):
        z = STEP * step
        for k, (own, six) in enumerate(block_of(rest, (), z + 1, STEP, 1, 24)):
            gain, w, diag = level_weights(own, six, omega)
            for i in range(6):
                weights[i, z + k, 1:25, :] = w[i]
            diags[z + k, 1:25, :] = (1.25 * 0.25) * diag
            for f in range(3):
                first[f, z + k + 1, 1:25, :] = (4.0 * gain) * rhs[f, z + k, 1:25, :]

    loop(16 // STEP, start)

    def sweep(step):
        z = STEP * step
        w = [[weights[i, z + k, 3:27, :] for i in range(6)] for k in range(STEP)]
        for f in range(3):
            for k, (own, six) in enumerate(block_of(first, (f,), z + 1, STEP, 3, 24)):
                second[f, z + k + 1, 3:27, :] = 1.2 * own + weigh(w[k], six)

    loop(16 // STEP, sweep)

    def left(step):
        z = STEP * step
        w = [[weights[i, z + k, 4:20, :] for i in range(6)] for k in range(STEP)]
        diag = [diags[z + k, 4:20, :] for k in range(STEP)]
        for f in range(3):
            values = []
            for k, (own, six) in enumerate(block_of(second, (f,), z + 1, STEP, 4, 16)):
                change = (first[f, z + k + 1, 4:20, :] - 0.8 * own) + weigh(w[k], six)
                values.append(change * diag[k])
                e_one[f, z + k] = second[f, z + k + 1, 8:16, :]
            for k in range(STEP // 2):
                halves[f, STEP // 2 * step + k, 0:16, :] = values[2 * k] + values[2 * k + 1]
                halves[f, STEP // 2 * step + k, 16:24, :] = jnp.zeros((8, 128), F32)
        for k in range(STEP // 2):
            halves[3, STEP // 2 * step + k] = share[z + 2 * k] + share[z + 2 * k + 1]

    loop(16 // STEP, left)

    source, target = iota((128, 128), 0), iota((128, 128), 1)
    pool = jnp.where(source // 2 + jnp.where(source >= 96, 64, 0) == target, 0.125, 0.0)
    pooled[...] = dot_exact(halves[...].reshape(4 * 8 * 24, 128), pool)
    for z in (0, 9):
        rest2[z] = jnp.full((24, 128), 0.5, F32)
        for f in range(3):
            first2[f, z] = jnp.zeros((24, 128), F32)
            second2[f, z] = jnp.zeros((24, 128), F32)
    for z in range(8):
        for f in range(3):
            base = (f * 8 + z) * 24
            rhs2[f, z] = pooled[pl.ds(base, 8, stride=2), :] + pooled[pl.ds(base + 1, 8, stride=2), :]
        base = (3 * 8 + z) * 24
        value = pooled[pl.ds(base + 2, 8, stride=2), :] + pooled[pl.ds(base + 3, 8, stride=2), :]
        rest2[z + 1, 0:8, :] = resist(value)
        value = pooled[pl.ds(base + 8, 8, stride=2), :] + pooled[pl.ds(base + 9, 8, stride=2), :]
        rest2[z + 1, 3:11, :] = resist(value)
        share2[z] = value

    row, lane = iota((8, 128), 0) + 1, iota((8, 128), 1)
    in_x = jnp.where(row < 3, low_x, jnp.where(row >= 7, high_x, 1))
    in_y = jnp.where(lane < 32, 1, jnp.where(lane < 96, high_y, low_y))
    omega2 = 0.8 * (in_x * in_y).astype(F32)

    for z, (own, six) in enumerate(block_of(rest2, (), 1, 8, 1, 8)):
        gain, w, diag = level_weights(own, six, omega2)
        for i in range(6):
            weights2[i, z, 1:9, :] = w[i]
        weights2[6, z, 1:9, :] = (1.25 * 0.0625) * diag
        for f in range(3):
            first2[f, z + 1, 1:9, :] = (16.0 * gain) * rhs2[f, z]
    w = [[weights2[i, z, 2:10, :] for i in range(6)] for z in range(8)]
    for f in range(3):
        for z, (own, six) in enumerate(block_of(first2, (f,), 1, 8, 2, 8)):
            second2[f, z + 1, 2:10, :] = 1.2 * own + weigh(w[z], six)
    w = [[weights2[i, z, 3:11, :] for i in range(7)] for z in range(8)]
    own_row = iota((8, 128), 0) < 4
    parts = [{} for pair in range(4)]
    for f in range(3):
        for z, (own, six) in enumerate(block_of(second2, (f,), 1, 8, 3, 8)):
            e_two[f, z] = own
            change = (first2[f, z + 1, 3:11, :] - 0.8 * own) + weigh(w[z], six)
            value = jnp.where(own_row, change * w[z][6], 0.0)
            sums = parts[z // 2]
            sums[f] = value if z % 2 == 0 else sums[f] + value
    for z in range(8):
        value = jnp.where(own_row, share2[z], 0.0)
        sums = parts[z // 2]
        sums[3] = value if z % 2 == 0 else sums[3] + value

    pool = jnp.where((source < 32) & (source // 2 == target % 16), 0.125, 0.0)
    rows = jnp.concatenate([parts[pair][ch] for ch in range(4) for pair in range(4)], axis=0)
    spread = dot_exact(rows, pool)
    at, to = iota((32, 128), 0), iota((32, 128), 1)
    keep = (at // 8 == to // 32) & ((at % 8) // 2 == (to // 16) % 2)
    result = jnp.concatenate(
        [
            jnp.sum(jnp.where(keep, spread[32 * ch : 32 * ch + 32], 0.0), axis=0, keepdims=True)
            for ch in range(4)
        ],
        axis=0,
    )
    for copy in range(CHIPS):
        sent[copy] = result


def swap_blocks(x):
    sub, group = iota((8, 128), 0), iota((8, 128), 1) // 16
    for bit in (4, 2, 1):
        up = roll(roll(x, -bit, 0), 16 * bit)
        down = up if bit == 4 else roll(roll(x, bit, 0), -16 * bit)
        sub_set, group_set = (sub & bit) != 0, (group & bit) != 0
        x = jnp.where(sub_set == group_set, x, jnp.where(sub_set, down, up))
    return x


def top_kernel(
    mine, other, base, out,
    natural, first, second, four, weights, diags, lefts, final, sems,
):
    gx, gy = lax.axis_index("gx"), lax.axis_index("gy")
    first_core = lax.rem(gy, 2) == 0
    lane, sub = iota((16, 128), 1), iota((16, 128), 0)
    cells = [(z, x, half) for z in range(4) for x in range(2) for half in range(2)]

    def lay(g):
        for ch in range(4):
            rows = pl.ds(32 * g + ch, 8, stride=4)
            pair = mine[rows, :], other[rows, :]
            natural[ch, 0, pl.ds(pl.multiple_of(8 * g, 8), 8), :] = swap_blocks(
                jnp.where(first_core, pair[0], pair[1])
            )
            natural[ch, 1, pl.ds(pl.multiple_of(8 * g, 8), 8), :] = swap_blocks(
                jnp.where(first_core, pair[1], pair[0])
            )

    loop(16, lay, 4)
    flat = natural.reshape(1024, 128)

    def plane(ch, z, x, half):
        return flat[pl.ds((ch * 2 + half) * 128 + z * 2 + x, 16, stride=8), :]

    def neighbours(at, z, x, half, outside):
        own, other = at(z, x, half), at(z, 1 - x, half)
        beside = at(z, x, 1 - half)
        shifted = roll(other, 1 if x == 0 else -1, 0)
        low, high = (shifted, other) if x == 0 else (other, shifted)
        left, right = roll(own, 1), roll(own, -1)
        left = jnp.where(lane % 16 == 0, roll(beside, 1 if half == 0 else -15), left)
        right = jnp.where(lane % 16 == 15, roll(beside, 15 if half == 0 else -1), right)
        down = at(z - 1, x, half) if z > 0 else outside
        up = at(z + 1, x, half) if z < 3 else outside
        return own, [low, high, left, right, down, up]

    def edge_masks(x, half):
        return [
            sub > 0 if x == 0 else None,
            sub < 15 if x == 1 else None,
            lane > 0 if half == 0 else None,
            lane < 127 if half == 1 else None,
            None,
            None,
        ]

    def key(z, x, half):
        return (z * 2 + x) * 2 + half

    shares = {c: plane(3, *c) for c in cells}
    rests = {c: resist(shares[c]) for c in cells}
    outside, zeros = jnp.full((16, 128), 0.5, F32), jnp.zeros((16, 128), F32)
    for z, x, half in cells:
        own, six = neighbours(lambda *c: rests[c], z, x, half, outside)
        masks = edge_masks(x, half)
        six = [s if m is None else jnp.where(m, s, 0.5) for s, m in zip(six, masks)]
        gain, w, diag = level_weights(own, six, 0.8)
        at = key(z, x, half)
        for i in range(6):
            weights[i, at] = w[i] if masks[i] is None else jnp.where(masks[i], w[i], 0.0)
        diags[at] = (1.25 * 0.25**3) * diag
        for f in range(3):
            first[f, at] = (64.0 * gain) * plane(f, z, x, half)

    for z, x, half in cells:
        at = key(z, x, half)
        w = [weights[i, at] for i in range(6)]
        for f in range(3):
            own, six = neighbours(lambda *c: first[f, key(*c)], z, x, half, zeros)
            second[half, f, z * 2 + x] = 1.2 * own + weigh(w, six)

    for z4 in range(2):
        for half in range(2):
            sums = [None] * 4
            for z in (2 * z4, 2 * z4 + 1):
                for x in range(2):
                    at = key(z, x, half)
                    w = [weights[i, at] for i in range(6)]
                    diag = diags[at]
                    for f in range(3):
                        own, six = neighbours(
                            lambda c, d, e: second[e, f, c * 2 + d], z, x, half, zeros
                        )
                        value = ((first[f, at] - 0.8 * own) + weigh(w, six)) * diag
                        sums[f] = value if sums[f] is None else sums[f] + value
                    share = shares[z, x, half]
                    sums[3] = share if sums[3] is None else sums[3] + share
            for ch in range(4):
                lefts[ch, z4, :, 128 * half : 128 * half + 128] = sums[ch]

    source = iota((256, 128), 0)
    column = ((source % 128) // 16) * 16 + (source // 128) * 8 + (source % 16) // 2
    pool = jnp.where(column == iota((256, 128), 1), 0.125, 0.0)
    level = dot_exact(lefts[...].reshape(128, 256), pool)

    def coarsest(ch, z):
        return level[(ch * 2 + z) * 16 : (ch * 2 + z) * 16 + 16, :]

    masks = [sub > 0, sub < 15, lane > 0, lane < 127]
    resists = [resist(coarsest(3, z)) for z in range(2)]
    gains, ws, ds = [], [], []
    for z in range(2):
        own, other = resists[z], resists[1 - z]
        six = [roll(own, 1, 0), roll(own, -1, 0), roll(own, 1), roll(own, -1)]
        six = [jnp.where(m, s, 0.5) for m, s in zip(masks, six)] + [other, outside]
        gain, w, diag = level_weights(own, six, 0.8)
        gains.append(gain)
        ds.append(diag)
        ws.append([jnp.where(m, v, 0.0) for m, v in zip(masks, w)] + [w[4]])
    whole = jnp.sum(ds[0] + ds[1], keepdims=True)

    def around(values, z):
        own, other = values[z], values[1 - z]
        return weigh(ws[z], (roll(own, 1, 0), roll(own, -1, 0), roll(own, 1), roll(own, -1), other))

    begin = [[256.0 * gains[z] * coarsest(f, z) for z in range(2)] for f in range(3)]
    values = begin
    for step in range(5):
        values = [
            [(0.2 * values[f][z] + begin[f][z]) + around(values[f], z) for z in range(2)] for f in range(3)
        ]
    shifts = []
    for f in range(3):
        change = [(begin[f][z] - 0.8 * values[f][z]) + around(values[f], z) for z in range(2)]
        shifts.append(jnp.sum(1.25 * (change[0] * ds[0] + change[1] * ds[1]), keepdims=True) / whole)
        for z in range(2):
            four[2 * f + z] = values[f][z]

    rows = four.reshape(96, 128)[pl.ds(gx, 6, stride=16), :]
    upper = jnp.concatenate([jnp.broadcast_to(rows[i : i + 1], (4, 128)) for i in range(6)], axis=0)
    flat = second.reshape(768, 128)
    halves = [flat[pl.ds(gx + 384 * half, 24, stride=16), :] for half in range(2)]
    three = turn(jnp.where(first_core, halves[0], halves[1]), -16 * lax.div(gy, 2))
    both = jnp.concatenate([turn(upper, -8 * gy), three], axis=1)
    both = jnp.concatenate([both, jnp.zeros((8, 256), F32)], axis=0)
    source, target = iota((256, 128), 0), iota((256, 128), 1)
    copy = jnp.where(source == jnp.where(source < 128, target // 16, 128 + target // 8), 1.0, 0.0)
    three = dot_exact(both, copy)

    copies = []
    for f in range(3):
        for z in range(4):
            for x in range(2):
                at = f * 8 + z * 2 + x
                value = jnp.broadcast_to(three[at : at + 1] + shifts[f], (8, 128))
                for k in range(8 * z, 8 * z + 8):
                    final[f, k, 8 * x : 8 * x + 8, :] = base[f, k, 8 * x : 8 * x + 8, :] + value
            if z % 2 == 1:
                part = (f, pl.ds(8 * z - 8, 16))
                copy = pltpu.make_async_copy(final.at[part], out.at[part], sems.at[len(copies)])
                copy.start()
                copies.append(copy)
    for copy in copies:
        copy.wait()


def local(labels, guess):
    swap_near = [(i, i ^ 1) for i in range(NY)]
    far_x, far_y = [], []
    for x in range(NX):
        for y in range(NY):
            across_x, across_y = x + 1 if x % 2 else x - 1, y + 1 if y % 2 else y - 1
            to = (across_x, y) if 0 <= across_x < NX else (x, y ^ 1)
            far_x.append((x * NY + y, to[0] * NY + to[1]))
            to = (x, across_y) if 0 <= across_y < NY else (x ^ 1, y)
            far_y.append((x * NY + y, to[0] * NY + to[1]))
    both = ("gx", "gy")
    to_near, to_far, own = call(
        rows_kernel,
        [(12, 32, 128)] * 2 + [(4, 32, 16, 128)],
        [pltpu.VMEM((32, 16, 128), jnp.int32), pltpu.SemaphoreType.DMA((4,))],
        in_specs=[ANY, ANY],
    )(pltpu.with_memory_space_constraint(guess, pltpu.HBM), pltpu.with_memory_space_constraint(labels, pltpu.HBM))
    from_near = lax.ppermute(to_near, "gx", swap_near)
    from_far = lax.ppermute(to_far, both, far_x)
    own_one, own_two, halves, to_right, to_left, edges = call(
        own_kernel,
        [(3, 34, 32, 128)] * 2 + [(4, 16, 16, 128)] + [(4, 4, 16, 128)] * 2 + [(4, 16, 16, 128)],
        [(4, 34, 32, 128), (6, 32, 32, 128), (32, 32, 128)],
        flops=20_000_000,
    )(own)
    to_near, to_far, rim_rows = call(pack_kernel, [(4, 4, 24, 128)] * 2 + [(4, 32, 8, 128)], [])(
        to_right, to_left, from_near, from_far
    )
    from_far = lax.ppermute(to_far, both, far_y)
    from_near = lax.ppermute(to_near, "gy", swap_near)
    two, main, edges_rim = call(
        rows_edge_kernel,
        [(3, 34, 24, 128), (4, 8, 8, 128), (4, 16, 8, 128)],
        [(4, 34, 24, 128), (3, 34, 24, 128), (6, 32, 24, 128), (32, 24, 128)]
        + [(4, 16, 16, 128), (512, 128)],
        flops=10_000_000,
    )(own, rim_rows, own_one, own_two, halves)
    main_near = lax.ppermute(main, "gx", swap_near)
    main_far = lax.ppermute(main, both, far_x)
    rim, rim_one = call(
        rim_kernel,
        [(3, 16, 16, 128), (4, 4, 8, 128)],
        [(3, 18, 32, 128), (18, 32, 128)]
        + [(3, 18, 32, 128)] * 2
        + [(6, 16, 32, 128), (16, 32, 128)]
        + [(4, 8, 16, 128), (256, 128)],
        flops=10_000_000,
    )(edges, edges_rim, from_near, from_far)
    rim_near = lax.ppermute(rim_one, "gx", swap_near)
    rim_far = lax.ppermute(rim_one, both, far_x)
    sent, e_one, e_two = call(
        middle_kernel,
        [(CHIPS, 4, 128), (3, 16, 8, 128), (3, 8, 8, 128)],
        [(16, 24, 128), (18, 32, 128), (3, 16, 32, 128), (3, 18, 32, 128), (3, 18, 32, 128)]
        + [(6, 16, 32, 128), (16, 32, 128), (4, 8, 24, 128), (768, 128)]
        + [(10, 24, 128), (3, 10, 24, 128), (3, 10, 24, 128), (3, 8, 8, 128), (8, 8, 128)]
        + [(7, 8, 16, 128)],
    )(main, main_near, main_far, rim_one, rim_near, rim_far)
    groups = [[i for i in range(NX * NY) if i % 2 == core] for core in range(2)]
    mine = lax.all_to_all(
        sent, ("gx", "gy"), split_axis=0, concat_axis=0, axis_index_groups=groups, tiled=True
    )
    (base,) = call(base_kernel, [(3, 32, 16, 128)], [(192, 128), (3, 16, 16, 128)])(two, rim, e_one, e_two)
    other = lax.ppermute(mine, "gy", swap_near)
    (out,) = call(
        top_kernel,
        [(3, 32, 16, 128)],
        [(4, 2, 128, 128), (3, 16, 16, 128), (2, 3, 8, 16, 128), (6, 16, 128), (6, 16, 16, 128)]
        + [(16, 16, 128), (4, 2, 16, 256), (3, 32, 16, 128), pltpu.SemaphoreType.DMA((6,))],
        out_specs=[ANY],
    )(mine.reshape(512, 128), other.reshape(512, 128), base)
    return out


def solution(mesh):
    return jax.shard_map(
        local,
        mesh=mesh,
        in_specs=(P(None, "gx", "gy"), P(None, None, "gx", "gy")),
        out_specs=P(None, None, "gx", "gy"),
        check_vma=False,
    )
```
